32 devices in a mesh: fsdp: 4 (over x, core), dp: 8 (over z, y).
Axes of the slice: x: 2, y: 2, z: 4, core: 2. Of those that a mesh axis runs over, the one named last changes fastest.
Arguments:
- tokens: bfloat16 [32, 1024, 768], P(('fsdp', 'dp')), may hold values from -6 to 6
- lengths: int32 [32], P(('fsdp', 'dp')), may hold values from 256 to 1024, as said below
- neighbours: bfloat16 [1024, 128, 768], P(('fsdp', 'dp')), may hold values from -6 to 6
- neighbour_ids: int32 [32, 16, 2], P(('fsdp', 'dp')), may hold values from 0 to 31
- neighbour_lengths: int32 [1024], P(('fsdp', 'dp')), may hold values from 32 to 128
- first_gain: bfloat16 [768], P(('fsdp', 'dp')), may hold values from 0.5 to 1.5
- first_shift: bfloat16 [768], P(('fsdp', 'dp')), may hold values from -3 to 3
- self_input: bfloat16 [768, 2304], P(('fsdp', 'dp')), may hold values from -0.21875 to 0.21875
- self_output: bfloat16 [768, 768], P(('fsdp', 'dp')), may hold values from -3.5 to 3.5
- second_gain: bfloat16 [768], P(('fsdp', 'dp')), may hold values from 0.5 to 1.5
- second_shift: bfloat16 [768], P(('fsdp', 'dp')), may hold values from -3 to 3
- cross_query: bfloat16 [768, 768], P(('fsdp', 'dp')), may hold values from -0.21875 to 0.21875
- cross_keyval: bfloat16 [768, 1536], P(('fsdp', 'dp')), may hold values from -0.21875 to 0.21875
- cross_output: bfloat16 [768, 768], P(('fsdp', 'dp')), may hold values from -2.5 to 2.5
- third_gain: bfloat16 [768], P(('fsdp', 'dp')), may hold values from 0.5 to 1.5
- third_shift: bfloat16 [768], P(('fsdp', 'dp')), may hold values from -3 to 3
- feed_up: bfloat16 [768, 3072], P(('fsdp', 'dp')), may hold values from -0.21875 to 0.21875
- feed_down: bfloat16 [3072, 768], P(('fsdp', 'dp')), may hold values from -0.109375 to 0.109375
- cotangent: bfloat16 [32, 1024, 768], P(('fsdp', 'dp')), may hold values from -6 to 6
Outputs:
- block_out: bfloat16 [32, 1024, 768], P(('fsdp', 'dp'))
- tokens_grad: float32 [32, 1024, 768], P(('fsdp', 'dp'))
- neighbours_grad: float32 [1024, 128, 768], P(('fsdp', 'dp'))
- firstgain_grad: float32 [768], P(('fsdp', 'dp'))
- firstshift_grad: float32 [768], P(('fsdp', 'dp'))
- selfinput_grad: float32 [768, 2304], P(('fsdp', 'dp'))
- selfoutput_grad: float32 [768, 768], P(('fsdp', 'dp'))
- secondgain_grad: float32 [768], P(('fsdp', 'dp'))
- secondshift_grad: float32 [768], P(('fsdp', 'dp'))
- crossquery_grad: float32 [768, 768], P(('fsdp', 'dp'))
- crosskeyval_grad: float32 [768, 1536], P(('fsdp', 'dp'))
- crossoutput_grad: float32 [768, 768], P(('fsdp', 'dp'))
- thirdgain_grad: float32 [768], P(('fsdp', 'dp'))
- thirdshift_grad: float32 [768], P(('fsdp', 'dp'))
- feedup_grad: float32 [768, 3072], P(('fsdp', 'dp'))
- feeddown_grad: float32 [3072, 768], P(('fsdp', 'dp'))
The draws below stay inside these ranges and needn't reach their ends.
Inputs may be any that keep to these rules, and one draw needn't show every extreme that they name: `lengths`: positions at or past a sequence's length are padding; some sequence has all 1024 tokens. Slot j of span c of sequence s is filled by row (s) * 32 + neighbour_ids[s, c, j] of neighbours, held with the sequence; an encoded neighbour may fill several slots or none.
All inputs are finite; a program needn't handle non-finite values.
Results may differ from the reference program's by a relative error of at most 0.017.
Values may be sent and summed in bfloat16 or wider, within the bound.
No kernel may reach another device: no remote copies, remote signals or barrier semaphores. Data moves between devices by JAX's collectives and lax.ppermute only.
A program may use at most 384 MiB of HBM per device.

```python
import jax
import jax.numpy as jnp
from jax import lax

D = 768
HEADS = 12
HEAD = 64
FF = 3072
SPAN = 64
NEIGH = 2
NLEN = 128
SEQ = 1024
SEQ_DEV = 1
SPANS = 16
SEQS = 32
POOL_DEV = 32
POOL = 1024


def draw_lengths(key, part):
    key = jax.random.fold_in(key, 11)
    first_key, second_key = jax.random.split(key)
    drawn = jax.random.randint(first_key, (SEQS,), SEQ // 4, SEQ + 1)
    chosen = jax.random.randint(second_key, (), 0, SEQS)
    return jnp.where(jnp.arange(SEQS) == chosen, SEQ, drawn).astype(jnp.int32)


def set_ends(array, stream_key, low, high):
    extent = array.shape
    spot = [jax.random.randint(jax.random.fold_in(stream_key, axis), (), 0, extent[axis]) for axis in range(len(extent))]
    array = array.at[tuple(spot)].set(low)
    longest = extent.index(max(extent))
    spot[longest] = (spot[longest] + 1) % extent[longest]
    return array.at[tuple(spot)].set(high)


def shard_levels(own_key, dims, shards, low, largest):
    level = 1.0
    for axis_at, blocks in shards:
        draws = jax.random.uniform(jax.random.fold_in(jax.random.fold_in(own_key, 6), axis_at), (blocks,), jnp.float32, low / len(shards), largest / len(shards))
        level = level * jnp.repeat(jnp.exp(draws), dims[axis_at] // blocks).reshape((-1,) + (1,) * (len(dims) - 1 - axis_at))
    return level


def gaussian(stream_key, dims, scale, reach, cuts=(), held_as=jnp.bfloat16):
    array = jax.random.normal(stream_key, dims, jnp.float32) * scale
    if len(cuts) > 0:
        array = shard_levels(stream_key, dims, cuts, -0.22, 0.18) * array
    return jnp.clip(array, min=-reach, max=reach).astype(held_as)


def setup_inputs(seed: int = 0) -> dict:
    key_of = jax.random.split(jax.random.key(seed), 20)
    return {
        "tokens": gaussian(key_of[0], (SEQS, SEQ, D), 1.0, 6.0, ((0, 32),)),
        "lengths": draw_lengths(jax.random.fold_in(key_of[19], 71), 0),
        "neighbours": gaussian(key_of[2], (POOL, NLEN, D), 1.0, 6.0, ((0, 32),)),
        "neighbour_ids": set_ends(jax.random.randint(key_of[3], (SEQS, SPANS, NEIGH), 0, POOL_DEV), jax.random.fold_in(key_of[3], 1), 0, POOL_DEV - 1).astype(jnp.int32),
        "neighbour_lengths": set_ends(jax.random.randint(key_of[4], (POOL,), NLEN // 4, NLEN + 1), jax.random.fold_in(key_of[4], 1), NLEN // 4, NLEN).astype(jnp.int32),
        "first_gain": jnp.clip(1.0 + 0.1 * jax.random.normal(key_of[5], (D,), jnp.float32), 0.5, 1.5).astype(jnp.bfloat16),
        "first_shift": gaussian(key_of[6], (D,), 0.5, 3.0, ((0, 32),)),
        "self_input": gaussian(key_of[7], (D, 3 * D), D ** -0.5, 0.21875, ((0, 32),)),
        "self_output": gaussian(key_of[8], (D, D), (max(D // 256, 1)) ** -0.5, 3.5, ((0, 32),)),
        "second_gain": jnp.clip(1.0 + 0.1 * jax.random.normal(key_of[9], (D,), jnp.float32), 0.5, 1.5).astype(jnp.bfloat16),
        "second_shift": gaussian(key_of[10], (D,), 0.5, 3.0, ((0, 32),)),
        "cross_query": gaussian(key_of[11], (D, D), D ** -0.5, 0.21875, ((0, 32),)),
        "cross_keyval": gaussian(key_of[12], (D, 2 * D), D ** -0.5, 0.21875, ((0, 32),)),
        "cross_output": gaussian(key_of[13], (D, D), (max(D // 128, 1)) ** -0.5, 2.5, ((0, 32),)),
        "third_gain": jnp.clip(1.0 + 0.1 * jax.random.normal(key_of[14], (D,), jnp.float32), 0.5, 1.5).astype(jnp.bfloat16),
        "third_shift": gaussian(key_of[15], (D,), 0.5, 3.0, ((0, 32),)),
        "feed_up": gaussian(key_of[16], (D, FF), D ** -0.5, 0.21875, ((0, 32),)),
        "feed_down": gaussian(key_of[17], (FF, D), FF ** -0.5, 0.109375, ((0, 32),)),
        "cotangent": gaussian(key_of[18], (SEQS, SEQ, D), 1.0, 6.0, ((0, 32),)),
    }


EPSILON = 1e-05
SCALE = 0.125
NEGATIVE = -1e+30
PRECISION_MAX = lax.Precision.HIGHEST

@jax.custom_vjp
def lowered_input(v):
    return lax.optimization_barrier(v.astype(jnp.bfloat16)).astype(jnp.float32)

@jax.custom_vjp
def lowered_backward(v):
    return v

def low_keep(v):
    return (lowered_input(v), None)

def low_pass(kept, grad):
    return (grad,)

def back_keep(v):
    return (v, None)

def back_low(kept, grad):
    return (lowered_input(grad),)
lowered_input.defvjp(low_keep, low_pass)
lowered_backward.defvjp(back_keep, back_low)

def norm_apply(values, gain, shift):
    centre = lax.optimization_barrier(jnp.mean(values, axis=-1, keepdims=True))
    centred = values - centre
    spread = lax.optimization_barrier(jnp.mean(centred * centred, axis=-1, keepdims=True))
    return centred * lax.rsqrt(spread + EPSILON) * gain + shift

def split_heads(matrix):
    return matrix.reshape(matrix.shape[:-1] + (HEADS, HEAD))

def masked_softmax(scores, allowed):
    masked = jnp.where(allowed, scores, NEGATIVE)
    top = lax.optimization_barrier(jnp.max(masked, axis=-1, keepdims=True))
    expo = jnp.exp(masked - top)
    return expo / lax.optimization_barrier(jnp.sum(expo, axis=-1, keepdims=True))

def forward(residual_stream, encoded, weights, seq_lengths, span_ids, encoded_lengths):
    gain_one, shift_one, self_attention_input, self_attention_output, gain_two, shift_two, cross_query_weight, keyval_cross, cross_attention_output, gain_three, shift_three, up_projection_weight, down_projection_weight = weights
    seq_count = residual_stream.shape[0]
    first_norm_input = lowered_input(norm_apply(residual_stream, gain_one, shift_one))
    projected_rows = jnp.einsum('zjx,xc->zjc', first_norm_input, self_attention_input, precision=PRECISION_MAX)
    query_heads = split_heads(lowered_input(lowered_backward(projected_rows[..., :D])))
    key_heads = split_heads(lowered_input(lowered_backward(projected_rows[..., D:2 * D])))
    value_heads = split_heads(lowered_input(lowered_backward(projected_rows[..., 2 * D:])))
    valid = jnp.arange(SEQ, dtype=jnp.int32)[None, :] < seq_lengths[:, None]
    block = min(512, SEQ)

    def self_block(index):
        start = index * block
        query_block = lax.dynamic_slice_in_dim(query_heads, start, block, 1)
        raw = jnp.einsum('sqhe,skhe->shqk', query_block, key_heads, precision=PRECISION_MAX)
        scores = lowered_backward(raw * SCALE)
        rows = start + jnp.arange(block, dtype=jnp.int32)
        columns = jnp.arange(SEQ, dtype=jnp.int32)
        allowed = (columns[None, :] <= rows[:, None])[None, None] & valid[:, None, None, :]
        probs = masked_softmax(scores, allowed)
        return jnp.einsum('shqk,skhe->sqhe', lowered_input(probs), value_heads, precision=PRECISION_MAX)
    mixed = lax.map(jax.checkpoint(self_block), jnp.arange(SEQ // block, dtype=jnp.int32))
    self_attended = lowered_input(lowered_backward(jnp.moveaxis(mixed, 0, 1).reshape(seq_count, SEQ, D)))
    self_residual_sum = residual_stream + lowered_backward(jnp.einsum('zjx,xc->zjc', self_attended, self_attention_output, precision=PRECISION_MAX))
    second_norm_input = lowered_input(norm_apply(self_residual_sum, gain_two, shift_two))
    pool_keyval = lowered_input(lowered_backward(jnp.einsum('pnd,de->pne', encoded, keyval_cross, precision=PRECISION_MAX)))
    span_keyval = jnp.take(pool_keyval, span_ids, axis=0).reshape(seq_count, SPANS, NEIGH * NLEN, 2 * D)
    span_keys = split_heads(span_keyval[..., :D])
    span_values = split_heads(span_keyval[..., D:])
    slot_lengths = jnp.take(encoded_lengths, span_ids, axis=0)
    span_valid = (jnp.arange(NLEN, dtype=jnp.int32) < slot_lengths[..., None]).reshape(seq_count, SPANS, NEIGH * NLEN)
    cross_query_rows = lowered_input(lowered_backward(jnp.einsum('zjx,xc->zjc', second_norm_input, cross_query_weight, precision=PRECISION_MAX)))
    cross_query_rows = split_heads(cross_query_rows.reshape(seq_count, SPANS, SPAN, D))
    raw = jnp.einsum('scqhe,sckhe->schqk', cross_query_rows, span_keys, precision=PRECISION_MAX)
    cross_probs = masked_softmax(lowered_backward(raw * SCALE), span_valid[:, :, None, None, :])
    cross_attended = jnp.einsum('schqk,sckhe->scqhe', lowered_input(cross_probs), span_values, precision=PRECISION_MAX)
    cross_attended = lowered_input(lowered_backward(cross_attended.reshape(seq_count, SEQ, D)))
    cross_residual_sum = self_residual_sum + lowered_backward(jnp.einsum('zjx,xc->zjc', cross_attended, cross_attention_output, precision=PRECISION_MAX))
    third_norm_input = lowered_input(norm_apply(cross_residual_sum, gain_three, shift_three))
    hidden_preactivation = lowered_backward(jnp.einsum('vtc,cz->vtz', third_norm_input, up_projection_weight, precision=PRECISION_MAX))
    hidden_activations = lowered_input(jax.nn.gelu(hidden_preactivation, approximate=True))
    return cross_residual_sum + lowered_backward(jnp.einsum('iew,wm->iem', hidden_activations, down_projection_weight, precision=PRECISION_MAX))

def reference(tokens, lengths, neighbours, neighbour_ids, neighbour_lengths, first_gain, first_shift, self_input, self_output, second_gain, second_shift, cross_query, cross_keyval, cross_output, third_gain, third_shift, feed_up, feed_down, cotangent):
    params = tuple((weight.astype(jnp.float32) for weight in (first_gain, first_shift, self_input, self_output, second_gain, second_shift, cross_query, cross_keyval, cross_output, third_gain, third_shift, feed_up, feed_down)))
    device_count = SEQS // SEQ_DEV
    pieces = (tokens.reshape(device_count, SEQ_DEV, SEQ, D), cotangent.reshape(device_count, SEQ_DEV, SEQ, D), neighbours.reshape(device_count, POOL_DEV, NLEN, D), lengths.reshape(device_count, SEQ_DEV), neighbour_ids.reshape(device_count, SEQ_DEV, SPANS, NEIGH), neighbour_lengths.reshape(device_count, POOL_DEV))

    def one_device(totals, slabs):
        token_piece, cotangent_piece, encoded_piece, length_piece, ident_piece, encoded_counts = slabs

        def localized(residual_stream, encoded, weights):
            return forward(residual_stream, encoded, weights, length_piece, ident_piece, encoded_counts)
        result, pullback = jax.vjp(localized, token_piece.astype(jnp.float32), encoded_piece.astype(jnp.float32), params)
        token_grad, encoded_grad, weight_grads = pullback(cotangent_piece.astype(jnp.float32))
        totals = jax.tree.map(jnp.add, totals, weight_grads)
        return (totals, (result.astype(jnp.bfloat16), token_grad, encoded_grad))
    zeroes = jax.tree.map(jnp.zeros_like, params)
    totals, stacked = lax.scan(one_device, zeroes, pieces)
    outputs, token_grads, encoded_grads = stacked
    grad_gainone, grad_shiftone, grad_selfin, grad_selfout, grad_gaintwo, grad_shifttwo, grad_crossq, grad_crosskv, grad_crossout, grad_gainthree, grad_shiftthree, grad_feedup, grad_feeddown = totals
    return (outputs.reshape(SEQS, SEQ, D), token_grads.reshape(SEQS, SEQ, D), encoded_grads.reshape(POOL, NLEN, D), grad_gainone, grad_shiftone, grad_selfin, grad_selfout, grad_gaintwo, grad_shifttwo, grad_crossq, grad_crosskv, grad_crossout, grad_gainthree, grad_shiftthree, grad_feedup, grad_feeddown)
```

```python
import functools

import jax
import jax.numpy as jnp
from jax import lax
from jax.experimental import pallas as pl
from jax.experimental.pallas import tpu as pltpu
from jax.sharding import PartitionSpec as P

HEADS = 12
SPAN = 64
NEIGH = 2
LANES = 128
WIDE = 256
QBLOCK = 256

EPSILON = 1e-05
SCALE = 0.125
NEGATIVE = -1e30
BF16 = jnp.bfloat16
F32 = jnp.float32
NT = (((1,), (1,)), ((), ()))
NN = (((1,), (0,)), ((), ()))
TN = (((0,), (0,)), ((), ()))


def dot(left, right, dims=NN):
    return lax.dot_general(left, right, dims, preferred_element_type=F32)


def iota(shape, axis):
    return lax.broadcasted_iota(jnp.int32, shape, axis)


def split_three(values):
    high = values.astype(BF16)
    rest = values - high.astype(F32)
    middle = rest.astype(BF16)
    low = (rest - middle.astype(F32)).astype(BF16)
    return (high, middle, low)


def self_forward_kernel(length_ref, query_ref, key_ref, value_ref, mixed_ref, exact_ref, logsum_ref):
    seq_len = query_ref.shape[0]
    length = length_ref[0]
    lane = iota((1, LANES), 1)
    first = lane < 64
    padded = jnp.where(iota((seq_len, 1), 0) < length, 0.0, NEGATIVE).astype(BF16)
    keys = key_ref[...]
    values = value_ref[...]
    one = jnp.ones((), BF16)
    keys_by_head = (
        jnp.where(first, keys, jnp.where(lane == 64, padded, 0)),
        jnp.where(first, jnp.where(lane == 0, padded, 0), keys),
    )
    values_by_head = (jnp.where(first, values, one), jnp.where(first, one, values))
    causal = iota((QBLOCK, QBLOCK), 1) <= iota((QBLOCK, QBLOCK), 0)
    for block in range(seq_len // QBLOCK):
        start = block * QBLOCK
        query = query_ref[start : start + QBLOCK] * jnp.asarray(SCALE, BF16)
        queries = (
            jnp.where(first, query, jnp.where(lane == 64, one, 0)),
            jnp.where(first, jnp.where(lane == 0, one, 0), query),
        )
        outs = []
        tops = []
        for head in range(2):
            diagonal = dot(queries[head], keys_by_head[head][start : start + QBLOCK], NT)
            diagonal = jnp.where(causal, diagonal, NEGATIVE)
            top = jnp.max(diagonal, axis=-1, keepdims=True)
            if block:
                before = dot(queries[head], keys_by_head[head][:start], NT)
                top = jnp.maximum(top, jnp.max(before, axis=-1, keepdims=True))
            out = dot(
                jnp.exp(diagonal - top).astype(BF16),
                values_by_head[head][start : start + QBLOCK],
            )
            if block:
                out = out + dot(jnp.exp(before - top).astype(BF16), values_by_head[head][:start])
            outs.append(out)
            tops.append(top)
        total = pltpu.roll(jnp.where(first, outs[1], outs[0]), 64, 1)
        mixed = jnp.where(first, outs[0], outs[1]) / total
        mixed_ref[start : start + QBLOCK] = mixed.astype(BF16)
        exact_ref[start : start + QBLOCK] = mixed
        logsum = (jnp.where(first, tops[0], tops[1]) + jnp.log(total)).T
        logsum_ref[0, 0:1, start : start + QBLOCK] = logsum[0:1]
        logsum_ref[0, 1:2, start : start + QBLOCK] = logsum[64:65]


def self_forward(projected, lengths):
    seq_len = projected.shape[0]
    width = projected.shape[1] // 3
    pairs = width // LANES
    column = lambda offset: pl.BlockSpec((seq_len, LANES), lambda p: (0, p + offset))
    return pl.pallas_call(
        self_forward_kernel,
        grid=(pairs,),
        in_specs=[
            pl.BlockSpec(memory_space=pltpu.SMEM),
            column(0),
            column(pairs),
            column(2 * pairs),
        ],
        out_specs=[
            column(0),
            column(0),
            pl.BlockSpec((1, 8, seq_len), lambda p: (p, 0, 0)),
        ],
        out_shape=[
            jax.ShapeDtypeStruct((seq_len, width), BF16),
            jax.ShapeDtypeStruct((seq_len, width), F32),
            jax.ShapeDtypeStruct((pairs, 8, seq_len), F32),
        ],
        compiler_params=pltpu.CompilerParams(vmem_limit_bytes=48 * 2**20),
        name="self_forward",
    )(lengths, projected, projected, projected)


def self_backward_kernel(
    length_ref,
    query_ref,
    key_ref,
    value_ref,
    grad_ref,
    exact_ref,
    logsum_ref,
    out_ref,
    key_grad_ref,
    value_grad_ref,
):
    seq_len = query_ref.shape[0]
    length = length_ref[0]
    lane = iota((1, LANES), 1)
    first = lane < 64
    row = iota((LANES, 1), 0)
    top_rows = row < 64
    padded = jnp.where(iota((seq_len, 1), 0) < length, 0.0, NEGATIVE).astype(BF16)
    keys = key_ref[...]
    values = value_ref[...]
    zero = jnp.zeros((), BF16)
    minus = -jnp.ones((), BF16)

    def beside(offset, head_lane):
        kept = (lane > head_lane) & (lane < head_lane + 4)
        return jnp.where(lane == head_lane, offset, jnp.where(kept, minus, zero))

    keys_by_head = (
        jnp.where(first, keys, beside(padded, 64)),
        jnp.where(first, beside(padded, 0), keys),
    )
    values_by_head = (
        jnp.where(first, values, beside(zero, 64)),
        jnp.where(first, beside(zero, 0), values),
    )
    keys_turned = keys.T
    turned_by_head = (
        jnp.where(top_rows, keys_turned, zero),
        jnp.where(top_rows, zero, keys_turned),
    )
    causal = iota((QBLOCK, QBLOCK), 0) <= iota((QBLOCK, QBLOCK), 1)

    def fill(turned, head, lead, parts):
        base = 64 if head == 0 else 0
        other = jnp.where(row == base, lead, zero)
        for place, part in enumerate(parts):
            other = jnp.where(row == base + 1 + place, part, other)
        own = top_rows if head == 0 else ~top_rows
        return jnp.where(own, turned, other)

    count = seq_len // QBLOCK
    for block in reversed(range(count)):
        start = block * QBLOCK
        stop = start + QBLOCK
        query = query_ref[start:stop] * jnp.asarray(SCALE, BF16)
        grad = grad_ref[start:stop]
        query_turned = query.T
        grad_turned = grad.T
        weighted = (grad.astype(F32) * exact_ref[start:stop]).T
        probs_all = []
        scores_all = []
        query_grad = None
        for head in range(2):
            delta = jnp.sum(weighted[head * 64 : head * 64 + 64], axis=0, keepdims=True)
            logsum = logsum_ref[0, head : head + 1, start:stop]
            score = dot(
                keys_by_head[head][:stop],
                fill(query_turned, head, jnp.ones((), BF16), split_three(logsum)),
            )
            prob = jnp.exp(score)
            last = jnp.where(causal, prob[start:], 0.0)
            prob = jnp.concatenate([prob[:start], last], axis=0) if block else last
            centred = dot(
                values_by_head[head][:stop], fill(grad_turned, head, zero, split_three(delta))
            )
            score_grad = (prob * centred).astype(BF16)
            scores_all.append(score_grad)
            probs_all.append(prob.astype(BF16))
            part = dot(turned_by_head[head][:, :stop], score_grad)
            query_grad = part if query_grad is None else query_grad + part
        out_ref[0, start:stop] = (query_grad.T * SCALE).astype(BF16)
        own_query = jnp.concatenate(
            [jnp.where(first, query, zero), jnp.where(first, zero, query)], axis=0
        )
        own_grad = jnp.concatenate(
            [jnp.where(first, grad, zero), jnp.where(first, zero, grad)], axis=0
        )
        key_part = dot(jnp.concatenate(scores_all, axis=1), own_query)
        value_part = dot(jnp.concatenate(probs_all, axis=1), own_grad)
        if block == count - 1:
            key_grad_ref[...] = key_part
            value_grad_ref[...] = value_part
        else:
            key_grad_ref[:stop] += key_part
            value_grad_ref[:stop] += value_part
    out_ref[1] = key_grad_ref[...].astype(BF16)
    out_ref[2] = value_grad_ref[...].astype(BF16)


def self_backward(projected, lengths, grad, exact, logsum):
    seq_len = projected.shape[0]
    width = projected.shape[1] // 3
    pairs = width // LANES
    column = lambda offset: pl.BlockSpec((seq_len, LANES), lambda p: (0, p + offset))
    return pl.pallas_call(
        self_backward_kernel,
        grid=(pairs,),
        in_specs=[
            pl.BlockSpec(memory_space=pltpu.SMEM),
            column(0),
            column(pairs),
            column(2 * pairs),
            column(0),
            column(0),
            pl.BlockSpec((1, 8, seq_len), lambda p: (p, 0, 0)),
        ],
        out_specs=pl.BlockSpec((3, seq_len, LANES), lambda p: (0, 0, p)),
        out_shape=jax.ShapeDtypeStruct((3, seq_len, width), BF16),
        scratch_shapes=[pltpu.VMEM((seq_len, LANES), F32), pltpu.VMEM((seq_len, LANES), F32)],
        compiler_params=pltpu.CompilerParams(vmem_limit_bytes=48 * 2**20),
        name="self_backward",
    )(lengths, projected, projected, projected, grad, exact, logsum)


def block_diagonal(rows):
    lane = iota((1, WIDE), 1)
    return jnp.concatenate(
        [jnp.where((lane >= h * 64) & (lane < h * 64 + 64), rows, 0) for h in range(4)], axis=0
    )


def take_diagonal(stacked):
    lane = iota((1, WIDE), 1)
    result = stacked[:SPAN]
    for h in range(1, 4):
        result = jnp.where(lane >= h * 64, stacked[h * SPAN : (h + 1) * SPAN], result)
    return result


def slot_bias(ids_ref, neighbour_lengths_ref, span, neigh_len, axis):
    shape = (1, NEIGH * neigh_len) if axis else (NEIGH * neigh_len, 1)
    place = iota(shape, axis)
    first = neighbour_lengths_ref[ids_ref[span * NEIGH]]
    second = neighbour_lengths_ref[ids_ref[span * NEIGH + 1]]
    limit = jnp.where(place < neigh_len, first, neigh_len + second)
    return jnp.where(place < limit, 0.0, NEGATIVE)


def cross_forward_kernel(
    ids_ref, neighbour_lengths_ref, query_ref, first_ref, second_ref, mixed_ref
):
    span = pl.program_id(0)
    neigh_len = first_ref.shape[1]
    width = query_ref.shape[1]
    bias = slot_bias(ids_ref, neighbour_lengths_ref, span, neigh_len, 1)
    for group in range(width // WIDE):
        place = slice(group * WIDE, (group + 1) * WIDE)
        value_place = slice(width + group * WIDE, width + (group + 1) * WIDE)
        queries = block_diagonal(query_ref[:, place] * jnp.asarray(SCALE, BF16))
        keys = jnp.concatenate([first_ref[0, :, place], second_ref[0, :, place]], axis=0)
        values = jnp.concatenate(
            [first_ref[0, :, value_place], second_ref[0, :, value_place]], axis=0
        )
        score = dot(queries, keys, NT) + bias
        expo = jnp.exp(score - jnp.max(score, axis=-1, keepdims=True))
        total = jnp.sum(expo, axis=-1, keepdims=True)
        out = dot(expo.astype(BF16), values) / total
        mixed_ref[:, place] = take_diagonal(out).astype(BF16)


def cross_forward(queries, pool_keyval, ids, neighbour_lengths):
    seq_len, width = queries.shape
    neigh_len, both = pool_keyval.shape[1:]
    spans = seq_len // SPAN
    rows = pl.BlockSpec((SPAN, width), lambda c, ids, lens: (c, 0))
    slot = lambda j: pl.BlockSpec(
        (1, neigh_len, both), lambda c, ids, lens: (ids[c * NEIGH + j], 0, 0)
    )
    return pl.pallas_call(
        cross_forward_kernel,
        grid_spec=pltpu.PrefetchScalarGridSpec(
            num_scalar_prefetch=2,
            grid=(spans,),
            in_specs=[rows, slot(0), slot(1)],
            out_specs=rows,
        ),
        out_shape=jax.ShapeDtypeStruct((seq_len, width), BF16),
        compiler_params=pltpu.CompilerParams(vmem_limit_bytes=48 * 2**20),
        name="cross_forward",
    )(ids, neighbour_lengths, queries, pool_keyval, pool_keyval)


def cross_backward_kernel(
    ids_ref,
    neighbour_lengths_ref,
    query_ref,
    grad_ref,
    first_key_ref,
    second_key_ref,
    first_value_ref,
    second_value_ref,
    query_grad_ref,
    key_out_ref,
    value_out_ref,
    key_total,
    value_total,
):
    span = pl.program_id(1)
    spans = pl.num_programs(1)
    neigh_len = first_key_ref.shape[1]

    @pl.when(span == 0)
    def _():
        key_total[...] = jnp.zeros_like(key_total)
        value_total[...] = jnp.zeros_like(value_total)

    bias = slot_bias(ids_ref, neighbour_lengths_ref, span, neigh_len, 0)
    queries = block_diagonal(query_ref[...] * jnp.asarray(SCALE, BF16))
    grads = block_diagonal(grad_ref[...])
    keys = jnp.concatenate([first_key_ref[0], second_key_ref[0]], axis=0)
    values = jnp.concatenate([first_value_ref[0], second_value_ref[0]], axis=0)
    score = dot(keys, queries, NT) + bias
    expo = jnp.exp(score - jnp.max(score, axis=0, keepdims=True))
    prob = expo * (1.0 / jnp.sum(expo, axis=0, keepdims=True))
    prob_grad = dot(values, grads, NT)
    centred = prob_grad - jnp.sum(prob * prob_grad, axis=0, keepdims=True)
    score_grad = (prob * centred).astype(BF16)
    value_part = dot(prob.astype(BF16), grads)
    key_part = dot(score_grad, queries)
    query_part = dot(score_grad, keys, TN)
    query_grad_ref[...] = (take_diagonal(query_part) * SCALE).astype(BF16)
    for slot in range(NEIGH):
        ident = ids_ref[span * NEIGH + slot]
        rows = slice(slot * neigh_len, (slot + 1) * neigh_len)
        key_total[ident] += key_part[rows]
        value_total[ident] += value_part[rows]

    @pl.when(span == spans - 1)
    def _():
        key_out_ref[...] = key_total[...].astype(BF16)
        value_out_ref[...] = value_total[...].astype(BF16)


def cross_backward(queries, grads, pool_keyval, ids, neighbour_lengths):
    seq_len, width = queries.shape
    pool_count, neigh_len, _ = pool_keyval.shape
    spans = seq_len // SPAN
    groups = width // WIDE
    rows = pl.BlockSpec((SPAN, WIDE), lambda g, c, ids, lens: (c, g))
    slot = lambda j, offset: pl.BlockSpec(
        (1, neigh_len, WIDE), lambda g, c, ids, lens: (ids[c * NEIGH + j], 0, g + offset)
    )
    pool = pl.BlockSpec((pool_count, neigh_len, WIDE), lambda g, c, ids, lens: (0, 0, g))
    pool_shape = jax.ShapeDtypeStruct((pool_count, neigh_len, width), BF16)
    return pl.pallas_call(
        cross_backward_kernel,
        grid_spec=pltpu.PrefetchScalarGridSpec(
            num_scalar_prefetch=2,
            grid=(groups, spans),
            in_specs=[rows, rows, slot(0, 0), slot(1, 0), slot(0, groups), slot(1, groups)],
            out_specs=[rows, pool, pool],
            scratch_shapes=[
                pltpu.VMEM((pool_count, neigh_len, WIDE), F32),
                pltpu.VMEM((pool_count, neigh_len, WIDE), F32),
            ],
        ),
        out_shape=[jax.ShapeDtypeStruct((seq_len, width), BF16), pool_shape, pool_shape],
        compiler_params=pltpu.CompilerParams(vmem_limit_bytes=56 * 2**20),
        name="cross_backward",
    )(ids, neighbour_lengths, queries, grads, pool_keyval, pool_keyval, pool_keyval, pool_keyval)


def norm_parts(values):
    centre = jnp.mean(values, axis=-1, keepdims=True)
    centred = values - centre
    spread = jnp.mean(centred * centred, axis=-1, keepdims=True)
    inverse = lax.rsqrt(spread + EPSILON)
    return (centred * inverse, inverse)


def norm_apply(values, gain, shift):
    return norm_parts(values)[0] * gain + shift


def norm_back(values, gain, upstream):
    unit, inverse = norm_parts(values)
    gain_term = jnp.sum(upstream * unit, axis=0)
    shift_term = jnp.sum(upstream, axis=0)
    inner = upstream * gain
    mean_inner = jnp.mean(inner, axis=-1, keepdims=True)
    mean_both = jnp.mean(inner * unit, axis=-1, keepdims=True)
    return (inverse * (inner - mean_inner - unit * mean_both), gain_term, shift_term)


def gelu_tanh(values):
    return jax.nn.gelu(values, approximate=True)


AXES = ("fsdp", "dp")


def local(
    tokens,
    lengths,
    neighbours,
    neighbour_ids,
    neighbour_lengths,
    first_gain,
    first_shift,
    self_input,
    self_output,
    second_gain,
    second_shift,
    cross_query,
    cross_keyval,
    cross_output,
    third_gain,
    third_shift,
    feed_up,
    feed_down,
    cotangent,
):
    _, seq_len, width = tokens.shape
    pool_count, neigh_len = neighbours.shape[:2]
    rows = self_input.shape[0]
    vectors = (first_gain, first_shift, second_gain, second_shift, third_gain, third_shift)
    vector_pack = jnp.pad(jnp.stack(vectors, axis=1), ((0, 0), (0, LANES - len(vectors))))
    packed = jnp.concatenate(
        [cross_keyval, self_input, self_output, cross_query, cross_output, vector_pack], axis=1
    )
    gathered = lax.all_gather(packed, AXES, axis=0, tiled=True)
    sizes = (2 * width, 3 * width, width, width, width)
    weights = []
    offset = 0
    for size in sizes:
        weights.append(gathered[:, offset : offset + size])
        offset = offset + size
    w_keyval, w_self_in, w_self_out, w_query, w_cross_out = weights
    gains = gathered[:, offset : offset + len(vectors)].astype(F32).T
    w_up = lax.all_gather(feed_up, AXES, axis=0, tiled=True)
    w_down = lax.all_gather(feed_down, AXES, axis=0, tiled=True)

    stream = tokens[0].astype(F32)
    encoded = neighbours.reshape(pool_count * neigh_len, width)
    ids = neighbour_ids.reshape(-1)
    pool_keyval = dot(encoded, w_keyval).astype(BF16).reshape(pool_count, neigh_len, 2 * width)
    first_in = norm_apply(stream, gains[0], gains[1]).astype(BF16)
    projected = dot(first_in, w_self_in).astype(BF16)
    self_mixed, self_exact, logsum = self_forward(projected, lengths)
    after_self = stream + dot(self_mixed, w_self_out)
    second_in = norm_apply(after_self, gains[2], gains[3]).astype(BF16)
    cross_queries = dot(second_in, w_query).astype(BF16)
    cross_mixed = cross_forward(cross_queries, pool_keyval, ids, neighbour_lengths)
    after_cross = after_self + dot(cross_mixed, w_cross_out)
    third_in = norm_apply(after_cross, gains[4], gains[5]).astype(BF16)
    hidden_pre = dot(third_in, w_up)
    hidden, gelu_back = jax.vjp(gelu_tanh, hidden_pre)
    hidden = hidden.astype(BF16)
    block_out = (after_cross + dot(hidden, w_down)).astype(BF16)

    down_in = cotangent[0]
    feeddown_term = dot(hidden, down_in, TN).astype(BF16)
    hidden_grad = gelu_back(dot(down_in, w_down, NT))[0].astype(BF16)
    feedup_term = dot(third_in, hidden_grad, TN).astype(BF16)
    third_back = dot(hidden_grad, w_up, NT)
    back, gain_three, shift_three = norm_back(after_cross, gains[4], third_back)
    after_cross_grad = down_in.astype(F32) + back
    cross_out_in = after_cross_grad.astype(BF16)
    crossout_term = dot(cross_mixed, cross_out_in, TN)
    mixed_grad = dot(cross_out_in, w_cross_out, NT).astype(BF16)
    query_grad, pool_key_grad, pool_value_grad = cross_backward(
        cross_queries, mixed_grad, pool_keyval, ids, neighbour_lengths
    )
    query_term = dot(second_in, query_grad, TN)
    second_back = dot(query_grad, w_query, NT)
    back, gain_two, shift_two = norm_back(after_self, gains[2], second_back)
    after_self_grad = after_cross_grad + back
    self_out_in = after_self_grad.astype(BF16)
    selfout_term = dot(self_mixed, self_out_in, TN)
    attend_grad = dot(self_out_in, w_self_out, NT).astype(BF16)
    projected_grad = self_backward(projected, lengths, attend_grad, self_exact, logsum)
    projected_grad = jnp.concatenate([projected_grad[i] for i in range(3)], axis=1)
    selfin_term = dot(first_in, projected_grad, TN)
    first_back = dot(projected_grad, w_self_in, NT)
    back, gain_one, shift_one = norm_back(stream, gains[0], first_back)
    tokens_grad = after_self_grad + back

    pool_grad = jnp.concatenate([pool_key_grad, pool_value_grad], axis=-1)
    pool_grad = pool_grad.reshape(pool_count * neigh_len, 2 * width)
    keyval_term = dot(encoded, pool_grad, TN)
    neighbours_grad = dot(pool_grad, w_keyval, NT).reshape(neighbours.shape)

    vector_terms = jnp.stack([gain_one, shift_one, gain_two, shift_two, gain_three, shift_three], axis=1)
    vector_terms = jnp.pad(vector_terms, ((0, 0), (0, LANES - len(vectors))))
    packed_terms = jnp.concatenate(
        [
            term.astype(BF16)
            for term in (keyval_term, selfin_term, selfout_term, query_term, crossout_term, vector_terms)
        ],
        axis=1,
    )

    def scatter(term):
        return lax.psum_scatter(term, AXES, scatter_dimension=0, tiled=True).astype(F32)

    feeddown_grad = scatter(feeddown_term)
    feedup_grad = scatter(feedup_term)
    summed = scatter(packed_terms)
    pieces = []
    offset = 0
    for size in sizes:
        pieces.append(summed[:, offset : offset + size])
        offset = offset + size
    vector_grads = [summed[:, offset + i] for i in range(len(vectors))]
    return (
        block_out[None],
        tokens_grad[None],
        neighbours_grad,
        vector_grads[0],
        vector_grads[1],
        pieces[1],
        pieces[2],
        vector_grads[2],
        vector_grads[3],
        pieces[3],
        pieces[0],
        pieces[4],
        vector_grads[4],
        vector_grads[5],
        feedup_grad,
        feeddown_grad,
    )


def solution(mesh):
    placed = (
        P(("fsdp", "dp"), None, None),
        P(("fsdp", "dp")),
        P(("fsdp", "dp"), None, None),
        P(("fsdp", "dp"), None, None),
        P(("fsdp", "dp")),
        P(("fsdp", "dp")),
        P(("fsdp", "dp")),
        P(("fsdp", "dp"), None),
        P(("fsdp", "dp"), None),
        P(("fsdp", "dp")),
        P(("fsdp", "dp")),
        P(("fsdp", "dp"), None),
        P(("fsdp", "dp"), None),
        P(("fsdp", "dp"), None),
        P(("fsdp", "dp")),
        P(("fsdp", "dp")),
        P(("fsdp", "dp"), None),
        P(("fsdp", "dp"), None),
        P(("fsdp", "dp"), None, None),
    )
    return jax.shard_map(
        local,
        mesh=mesh,
        in_specs=placed,
        out_specs=(
            P(("fsdp", "dp"), None, None),
            P(("fsdp", "dp"), None, None),
            P(("fsdp", "dp"), None, None),
            P(("fsdp", "dp")),
            P(("fsdp", "dp")),
            P(("fsdp", "dp"), None),
            P(("fsdp", "dp"), None),
            P(("fsdp", "dp")),
            P(("fsdp", "dp")),
            P(("fsdp", "dp"), None),
            P(("fsdp", "dp"), None),
            P(("fsdp", "dp"), None),
            P(("fsdp", "dp")),
            P(("fsdp", "dp")),
            P(("fsdp", "dp"), None),
            P(("fsdp", "dp"), None),
        ),
        check_vma=False,
    )
```

```python
import functools

import jax
import jax.numpy as jnp
from jax import lax
from jax.experimental import pallas as pl
from jax.experimental.pallas import tpu as pltpu
from jax.sharding import PartitionSpec as P

HEADS = 12
SPAN = 64
NEIGH = 2
LANES = 128
WIDE = 256
QBLOCK = 256

EPSILON = 1e-05
SCALE = 0.125
NEGATIVE = -1e30
BF16 = jnp.bfloat16
F32 = jnp.float32
NT = (((1,), (1,)), ((), ()))
NN = (((1,), (0,)), ((), ()))
TN = (((0,), (0,)), ((), ()))


def dot(left, right, dims=NN):
    return lax.dot_general(left, right, dims, preferred_element_type=F32)


def iota(shape, axis):
    return lax.broadcasted_iota(jnp.int32, shape, axis)


def split_three(values):
    high = values.astype(BF16)
    rest = values - high.astype(F32)
    middle = rest.astype(BF16)
    low = (rest - middle.astype(F32)).astype(BF16)
    return (high, middle, low)


def self_forward_kernel(length_ref, query_ref, key_ref, value_ref, mixed_ref, exact_ref, logsum_ref):
    seq_len = query_ref.shape[0]
    length = length_ref[0]
    lane = iota((1, LANES), 1)
    first = lane < 64
    padded = jnp.where(iota((seq_len, 1), 0) < length, 0.0, NEGATIVE).astype(BF16)
    keys = key_ref[...]
    values = value_ref[...]
    one = jnp.ones((), BF16)
    keys_by_head = (
        jnp.where(first, keys, jnp.where(lane == 64, padded, 0)),
        jnp.where(first, jnp.where(lane == 0, padded, 0), keys),
    )
    values_by_head = (jnp.where(first, values, one), jnp.where(first, one, values))
    causal = iota((QBLOCK, QBLOCK), 1) <= iota((QBLOCK, QBLOCK), 0)
    for block in range(seq_len // QBLOCK):
        start = block * QBLOCK
        query = query_ref[start : start + QBLOCK] * jnp.asarray(SCALE, BF16)
        queries = (
            jnp.where(first, query, jnp.where(lane == 64, one, 0)),
            jnp.where(first, jnp.where(lane == 0, one, 0), query),
        )
        outs = []
        tops = []
        for head in range(2):
            diagonal = dot(queries[head], keys_by_head[head][start : start + QBLOCK], NT)
            diagonal = jnp.where(causal, diagonal, NEGATIVE)
            top = jnp.max(diagonal, axis=-1, keepdims=True)
            if block:
                before = dot(queries[head], keys_by_head[head][:start], NT)
                top = jnp.maximum(top, jnp.max(before, axis=-1, keepdims=True))
            out = dot(
                jnp.exp(diagonal - top).astype(BF16),
                values_by_head[head][start : start + QBLOCK],
            )
            if block:
                out = out + dot(jnp.exp(before - top).astype(BF16), values_by_head[head][:start])
            outs.append(out)
            tops.append(top)
        total = pltpu.roll(jnp.where(first, outs[1], outs[0]), 64, 1)
        mixed = jnp.where(first, outs[0], outs[1]) / total
        mixed_ref[start : start + QBLOCK] = mixed.astype(BF16)
        exact_ref[start : start + QBLOCK] = mixed
        logsum = (jnp.where(first, tops[0], tops[1]) + jnp.log(total)).T
        logsum_ref[0, 0:1, start : start + QBLOCK] = logsum[0:1]
        logsum_ref[0, 1:2, start : start + QBLOCK] = logsum[64:65]


def self_forward(projected, lengths):
    seq_len = projected.shape[0]
    width = projected.shape[1] // 3
    pairs = width // LANES
    column = lambda offset: pl.BlockSpec((seq_len, LANES), lambda p: (0, p + offset))
    return pl.pallas_call(
        self_forward_kernel,
        grid=(pairs,),
        in_specs=[
            pl.BlockSpec(memory_space=pltpu.SMEM),
            column(0),
            column(pairs),
            column(2 * pairs),
        ],
        out_specs=[
            column(0),
            column(0),
            pl.BlockSpec((1, 8, seq_len), lambda p: (p, 0, 0)),
        ],
        out_shape=[
            jax.ShapeDtypeStruct((seq_len, width), BF16),
            jax.ShapeDtypeStruct((seq_len, width), F32),
            jax.ShapeDtypeStruct((pairs, 8, seq_len), F32),
        ],
        compiler_params=pltpu.CompilerParams(vmem_limit_bytes=48 * 2**20),
        name="self_forward",
    )(lengths, projected, projected, projected)


def self_backward_kernel(
    length_ref,
    query_ref,
    key_ref,
    value_ref,
    grad_ref,
    exact_ref,
    logsum_ref,
    out_ref,
    key_grad_ref,
    value_grad_ref,
):
    seq_len = query_ref.shape[0]
    length = length_ref[0]
    lane = iota((1, LANES), 1)
    first = lane < 64
    row = iota((LANES, 1), 0)
    top_rows = row < 64
    padded = jnp.where(iota((seq_len, 1), 0) < length, 0.0, NEGATIVE).astype(BF16)
    keys = key_ref[...]
    values = value_ref[...]
    zero = jnp.zeros((), BF16)
    minus = -jnp.ones((), BF16)

    def beside(offset, head_lane):
        kept = (lane > head_lane) & (lane < head_lane + 4)
        return jnp.where(lane == head_lane, offset, jnp.where(kept, minus, zero))

    keys_by_head = (
        jnp.where(first, keys, beside(padded, 64)),
        jnp.where(first, beside(padded, 0), keys),
    )
    values_by_head = (
        jnp.where(first, values, beside(zero, 64)),
        jnp.where(first, beside(zero, 0), values),
    )
    keys_turned = keys.T
    turned_by_head = (
        jnp.where(top_rows, keys_turned, zero),
        jnp.where(top_rows, zero, keys_turned),
    )
    causal = iota((QBLOCK, QBLOCK), 0) <= iota((QBLOCK, QBLOCK), 1)

    def fill(turned, head, lead, parts):
        base = 64 if head == 0 else 0
        other = jnp.where(row == base, lead, zero)
        for place, part in enumerate(parts):
            other = jnp.where(row == base + 1 + place, part, other)
        own = top_rows if head == 0 else ~top_rows
        return jnp.where(own, turned, other)

    count = seq_len // QBLOCK
    for block in reversed(range(count)):
        start = block * QBLOCK
        stop = start + QBLOCK
        query = query_ref[start:stop] * jnp.asarray(SCALE, BF16)
        grad = grad_ref[start:stop]
        query_turned = query.T
        grad_turned = grad.T
        weighted = (grad.astype(F32) * exact_ref[start:stop]).T
        probs_all = []
        scores_all = []
        query_grad = None
        for head in range(2):
            delta = jnp.sum(weighted[head * 64 : head * 64 + 64], axis=0, keepdims=True)
            logsum = logsum_ref[0, head : head + 1, start:stop]
            score = dot(
                keys_by_head[head][:stop],
                fill(query_turned, head, jnp.ones((), BF16), split_three(logsum)),
            )
            prob = jnp.exp(score)
            last = jnp.where(causal, prob[start:], 0.0)
            prob = jnp.concatenate([prob[:start], last], axis=0) if block else last
            centred = dot(
                values_by_head[head][:stop], fill(grad_turned, head, zero, split_three(delta))
            )
            score_grad = (prob * centred).astype(BF16)
            scores_all.append(score_grad)
            probs_all.append(prob.astype(BF16))
            part = dot(turned_by_head[head][:, :stop], score_grad)
            query_grad = part if query_grad is None else query_grad + part
        out_ref[0, start:stop] = (query_grad.T * SCALE).astype(BF16)
        own_query = jnp.concatenate(
            [jnp.where(first, query, zero), jnp.where(first, zero, query)], axis=0
        )
        own_grad = jnp.concatenate(
            [jnp.where(first, grad, zero), jnp.where(first, zero, grad)], axis=0
        )
        key_part = dot(jnp.concatenate(scores_all, axis=1), own_query)
        value_part = dot(jnp.concatenate(probs_all, axis=1), own_grad)
        if block == count - 1:
            key_grad_ref[...] = key_part
            value_grad_ref[...] = value_part
        else:
            key_grad_ref[:stop] += key_part
            value_grad_ref[:stop] += value_part
    out_ref[1] = key_grad_ref[...].astype(BF16)
    out_ref[2] = value_grad_ref[...].astype(BF16)


def self_backward(projected, lengths, grad, exact, logsum):
    seq_len = projected.shape[0]
    width = projected.shape[1] // 3
    pairs = width // LANES
    column = lambda offset: pl.BlockSpec((seq_len, LANES), lambda p: (0, p + offset))
    return pl.pallas_call(
        self_backward_kernel,
        grid=(pairs,),
        in_specs=[
            pl.BlockSpec(memory_space=pltpu.SMEM),
            column(0),
            column(pairs),
            column(2 * pairs),
            column(0),
            column(0),
            pl.BlockSpec((1, 8, seq_len), lambda p: (p, 0, 0)),
        ],
        out_specs=pl.BlockSpec((3, seq_len, LANES), lambda p: (0, 0, p)),
        out_shape=jax.ShapeDtypeStruct((3, seq_len, width), BF16),
        scratch_shapes=[pltpu.VMEM((seq_len, LANES), F32), pltpu.VMEM((seq_len, LANES), F32)],
        compiler_params=pltpu.CompilerParams(vmem_limit_bytes=48 * 2**20),
        name="self_backward",
    )(lengths, projected, projected, projected, grad, exact, logsum)


def block_diagonal(rows):
    lane = iota((1, WIDE), 1)
    return jnp.concatenate(
        [jnp.where((lane >= h * 64) & (lane < h * 64 + 64), rows, 0) for h in range(4)], axis=0
    )


def take_diagonal(stacked):
    lane = iota((1, WIDE), 1)
    result = stacked[:SPAN]
    for h in range(1, 4):
        result = jnp.where(lane >= h * 64, stacked[h * SPAN : (h + 1) * SPAN], result)
    return result


def slot_bias(ids_ref, neighbour_lengths_ref, span, neigh_len, axis):
    shape = (1, NEIGH * neigh_len) if axis else (NEIGH * neigh_len, 1)
    place = iota(shape, axis)
    first = neighbour_lengths_ref[ids_ref[span * NEIGH]]
    second = neighbour_lengths_ref[ids_ref[span * NEIGH + 1]]
    limit = jnp.where(place < neigh_len, first, neigh_len + second)
    return jnp.where(place < limit, 0.0, NEGATIVE)


def cross_forward_kernel(
    ids_ref, neighbour_lengths_ref, query_ref, first_ref, second_ref, mixed_ref
):
    span = pl.program_id(0)
    neigh_len = first_ref.shape[1]
    width = query_ref.shape[1]
    bias = slot_bias(ids_ref, neighbour_lengths_ref, span, neigh_len, 1)
    for group in range(width // WIDE):
        place = slice(group * WIDE, (group + 1) * WIDE)
        value_place = slice(width + group * WIDE, width + (group + 1) * WIDE)
        queries = block_diagonal(query_ref[:, place] * jnp.asarray(SCALE, BF16))
        keys = jnp.concatenate([first_ref[0, :, place], second_ref[0, :, place]], axis=0)
        values = jnp.concatenate(
            [first_ref[0, :, value_place], second_ref[0, :, value_place]], axis=0
        )
        score = dot(queries, keys, NT) + bias
        expo = jnp.exp(score - jnp.max(score, axis=-1, keepdims=True))
        total = jnp.sum(expo, axis=-1, keepdims=True)
        out = dot(expo.astype(BF16), values) / total
        mixed_ref[:, place] = take_diagonal(out).astype(BF16)


def cross_forward(queries, pool_keyval, ids, neighbour_lengths):
    seq_len, width = queries.shape
    neigh_len, both = pool_keyval.shape[1:]
    spans = seq_len // SPAN
    rows = pl.BlockSpec((SPAN, width), lambda c, ids, lens: (c, 0))
    slot = lambda j: pl.BlockSpec(
        (1, neigh_len, both), lambda c, ids, lens: (ids[c * NEIGH + j], 0, 0)
    )
    return pl.pallas_call(
        cross_forward_kernel,
        grid_spec=pltpu.PrefetchScalarGridSpec(
            num_scalar_prefetch=2,
            grid=(spans,),
            in_specs=[rows, slot(0), slot(1)],
            out_specs=rows,
        ),
        out_shape=jax.ShapeDtypeStruct((seq_len, width), BF16),
        compiler_params=pltpu.CompilerParams(vmem_limit_bytes=48 * 2**20),
        name="cross_forward",
    )(ids, neighbour_lengths, queries, pool_keyval, pool_keyval)


def cross_backward_kernel(
    ids_ref,
    neighbour_lengths_ref,
    query_ref,
    grad_ref,
    first_key_ref,
    second_key_ref,
    first_value_ref,
    second_value_ref,
    query_grad_ref,
    key_out_ref,
    value_out_ref,
    key_total,
    value_total,
):
    span = pl.program_id(1)
    spans = pl.num_programs(1)
    neigh_len = first_key_ref.shape[1]

    @pl.when(span == 0)
    def _():
        key_total[...] = jnp.zeros_like(key_total)
        value_total[...] = jnp.zeros_like(value_total)

    bias = slot_bias(ids_ref, neighbour_lengths_ref, span, neigh_len, 0)
    queries = block_diagonal(query_ref[...] * jnp.asarray(SCALE, BF16))
    grads = block_diagonal(grad_ref[...])
    keys = jnp.concatenate([first_key_ref[0], second_key_ref[0]], axis=0)
    values = jnp.concatenate([first_value_ref[0], second_value_ref[0]], axis=0)
    score = dot(keys, queries, NT) + bias
    expo = jnp.exp(score - jnp.max(score, axis=0, keepdims=True))
    prob = expo * (1.0 / jnp.sum(expo, axis=0, keepdims=True))
    prob_grad = dot(values, grads, NT)
    centred = prob_grad - jnp.sum(prob * prob_grad, axis=0, keepdims=True)
    score_grad = (prob * centred).astype(BF16)
    value_part = dot(prob.astype(BF16), grads)
    key_part = dot(score_grad, queries)
    query_part = dot(score_grad, keys, TN)
    query_grad_ref[...] = (take_diagonal(query_part) * SCALE).astype(BF16)
    for slot in range(NEIGH):
        ident = ids_ref[span * NEIGH + slot]
        rows = slice(slot * neigh_len, (slot + 1) * neigh_len)
        key_total[ident] += key_part[rows]
        value_total[ident] += value_part[rows]

    @pl.when(span == spans - 1)
    def _():
        key_out_ref[...] = key_total[...].astype(BF16)
        value_out_ref[...] = value_total[...].astype(BF16)


def cross_backward(queries, grads, pool_keyval, ids, neighbour_lengths):
    seq_len, width = queries.shape
    pool_count, neigh_len, _ = pool_keyval.shape
    spans = seq_len // SPAN
    groups = width // WIDE
    rows = pl.BlockSpec((SPAN, WIDE), lambda g, c, ids, lens: (c, g))
    slot = lambda j, offset: pl.BlockSpec(
        (1, neigh_len, WIDE), lambda g, c, ids, lens: (ids[c * NEIGH + j], 0, g + offset)
    )
    pool = pl.BlockSpec((pool_count, neigh_len, WIDE), lambda g, c, ids, lens: (0, 0, g))
    pool_shape = jax.ShapeDtypeStruct((pool_count, neigh_len, width), BF16)
    return pl.pallas_call(
        cross_backward_kernel,
        grid_spec=pltpu.PrefetchScalarGridSpec(
            num_scalar_prefetch=2,
            grid=(groups, spans),
            in_specs=[rows, rows, slot(0, 0), slot(1, 0), slot(0, groups), slot(1, groups)],
            out_specs=[rows, pool, pool],
            scratch_shapes=[
                pltpu.VMEM((pool_count, neigh_len, WIDE), F32),
                pltpu.VMEM((pool_count, neigh_len, WIDE), F32),
            ],
        ),
        out_shape=[jax.ShapeDtypeStruct((seq_len, width), BF16), pool_shape, pool_shape],
        compiler_params=pltpu.CompilerParams(vmem_limit_bytes=56 * 2**20),
        name="cross_backward",
    )(ids, neighbour_lengths, queries, grads, pool_keyval, pool_keyval, pool_keyval, pool_keyval)

AXES = ("fsdp", "dp")


def bits_of(size):
    return [1 << i for i in range(size.bit_length() - 1)]


def index_bits(count):
    return [1 << i for i in range(count.bit_length() - 2, -1, -1)]


def place(side, own, other):
    return jnp.stack([jnp.where(side == 0, own, other), jnp.where(side == 0, other, own)])


class Plan:
    def __init__(self, rows):
        self.inner = lax.axis_size("dp")
        self.outer = lax.axis_size("fsdp")
        self.count = self.inner * self.outer
        self.rows = rows
        self.core = [self.inner] if self.outer > 1 else []
        self.halves = 2 if self.core else 1
        self.across = self.outer // self.halves
        self.stripe = self.inner * rows
        self.half_rows = self.across * self.stripe
        self.me = lax.axis_index(AXES)
        across = [bit * self.inner for bit in bits_of(self.outer)[1:]]
        along = bits_of(self.inner)
        near, far = along[: len(across)], along[len(across) :]
        self.orders = (far + near + across, far + across + near)
        self.natural = [mask for mask in index_bits(self.count) if mask not in self.core]
        self.odd = self.bit(self.core[0]) if self.core else jnp.zeros((), jnp.int32)
        self.odd_word = self.odd.reshape(1)

    def steps(self):
        return list(zip(*self.orders))

    def bit(self, mask):
        return (self.me // mask) % 2

    def side(self, masks):
        even, odd = masks
        return jnp.where(self.odd == 0, self.bit(even), self.bit(odd))

    def exchange(self, values, masks):
        even, odd = masks
        pairs = []
        for index in range(self.count):
            is_odd = bool(self.core) and (index // self.core[0]) % 2 == 1
            pairs.append((index, index ^ (odd if is_odd else even)))
        return lax.ppermute(values, AXES, pairs)

    def swap(self, values):
        return self.exchange(values, (self.core[0], self.core[0])) if self.core else values


def reorder_kernel(moves, odd_ref, in_ref, out_ref, buffer, sems):
    for parity, pairs in enumerate(moves):

        @pl.when(odd_ref[0] == parity)
        def _():
            for source, target in pairs:
                pltpu.make_async_copy(
                    in_ref.at[source], buffer.at[target], sems.at[source]
                ).start()
            for source, target in pairs:
                pltpu.make_async_copy(
                    in_ref.at[source], buffer.at[target], sems.at[source]
                ).wait()

    pltpu.sync_copy(buffer, out_ref)


def reorder(plan, held):
    blocks = held.shape[0]
    moves = []
    for order in plan.orders[: plan.halves]:
        pairs = []
        for source in range(blocks):
            target = 0
            for place_at, mask in enumerate(order):
                if (source >> place_at) & 1:
                    target += 1 << (len(plan.natural) - 1 - plan.natural.index(mask))
            pairs.append((source, target))
        moves.append(pairs)
    return pl.pallas_call(
        functools.partial(reorder_kernel, moves),
        in_specs=[pl.BlockSpec(memory_space=pltpu.SMEM), pl.BlockSpec(memory_space=pl.ANY)],
        out_specs=pl.BlockSpec(memory_space=pl.ANY),
        out_shape=jax.ShapeDtypeStruct(held.shape, held.dtype),
        scratch_shapes=[pltpu.VMEM(held.shape, held.dtype), pltpu.SemaphoreType.DMA((blocks,))],
        compiler_params=pltpu.CompilerParams(vmem_limit_bytes=32 * 2**20),
        name="reorder_blocks",
    )(plan.odd_word, held)


def gather_halves(plan, shard):
    columns = shard.shape[1]
    held = shard
    for masks in plan.steps():
        other = plan.exchange(held, masks)
        held = place(plan.side(masks), held, other)
    held = reorder(plan, held.reshape((-1,) + shard.shape))
    other = plan.swap(held)
    shape = (plan.half_rows, columns)
    return (held.reshape(shape), other.reshape(shape))


def scatter_halves(plan, keep, send):
    columns = keep.shape[1]
    shape = (2,) * len(plan.natural) + (plan.rows, columns)
    blocks = [keep.reshape(shape)]
    if plan.core:
        blocks.append(plan.swap(send).reshape(shape))

    def add(parts):
        total = parts[0].astype(F32)
        for part in parts[1:]:
            total = total + part.astype(F32)
        return total.astype(BF16)

    def pick(parts, axes, index):
        chosen = []
        for part in parts:
            even, odd = [lax.dynamic_index_in_dim(part, index, axis, False) for axis in axes]
            chosen.append(even if axes[0] == axes[1] else jnp.where(plan.odd == 0, even, odd))
        return add(chosen)

    layouts = [list(plan.natural), list(plan.natural)]
    for masks in plan.steps()[::-1]:
        axes = tuple(layouts[parity].index(masks[parity]) for parity in range(2))
        side = plan.side(masks)
        sent = pick(blocks, axes, 1 - side)
        kept = pick(blocks, axes, side)
        blocks = [kept, plan.exchange(sent, masks)]
        for parity in range(2):
            layouts[parity].pop(axes[parity])
    total = blocks[0].astype(F32)
    for part in blocks[1:]:
        total = total + part.astype(F32)
    return total.reshape(plan.rows, columns)


def column_copies(plan, odd, held_ref, other_ref, target, sems, start, width):
    copies = []
    for across in range(plan.across):
        source_rows = pl.ds(across * plan.stripe, plan.stripe)
        for turn, ref in enumerate((held_ref, other_ref)[: plan.halves]):
            half = odd if turn == 0 else 1 - odd
            first = across * plan.halves * plan.stripe + half * plan.stripe
            if plan.halves == 1:
                first = across * plan.stripe
            elif plan.stripe % 16 == 0:
                first = pl.multiple_of(first, 16)
            copies.append(
                pltpu.make_async_copy(
                    ref.at[source_rows, pl.ds(start, width)],
                    target.at[pl.ds(first, plan.stripe), :],
                    sems.at[across * plan.halves + turn],
                )
            )
    return copies


def store_halves(plan, odd, result, keep_ref, send_ref, columns):
    for across in range(plan.across):
        rows = slice(across * plan.stripe, (across + 1) * plan.stripe)
        for half in range(plan.halves):
            first = (across * plan.halves + half) * plan.stripe
            part = result[first : first + plan.stripe]
            if plan.halves == 1:
                keep_ref[rows, columns] = part
                continue

            @pl.when(odd == half)
            def _():
                keep_ref[rows, columns] = part

            @pl.when(odd != half)
            def _():
                send_ref[rows, columns] = part

ROWS = 256
MEBI = 2**20
ANYWHERE = pl.BlockSpec(memory_space=pl.ANY)
SCALAR = pl.BlockSpec(memory_space=pltpu.SMEM)


def norm_parts(values):
    centre = jnp.mean(values, axis=-1, keepdims=True)
    centred = values - centre
    spread = jnp.mean(centred * centred, axis=-1, keepdims=True)
    inverse = lax.rsqrt(spread + EPSILON)
    return (centred * inverse, inverse)


def norm_back(values, gain, upstream):
    unit, inverse = norm_parts(values)
    gain_term = jnp.sum(upstream * unit, axis=0, keepdims=True)
    shift_term = jnp.sum(upstream, axis=0, keepdims=True)
    inner = upstream * gain
    mean_inner = jnp.mean(inner, axis=-1, keepdims=True)
    mean_both = jnp.mean(inner * unit, axis=-1, keepdims=True)
    return (inverse * (inner - mean_inner - unit * mean_both), gain_term, shift_term)


def add_terms(step, target_ref, gain_term, shift_term):
    @pl.when(step == 0)
    def _():
        target_ref[...] = jnp.zeros_like(target_ref)

    target_ref[0:1] += gain_term
    target_ref[1:2] += shift_term


def start_all(copies):
    for copy in copies:
        copy.start()


def wait_all(copies):
    for copy in copies:
        copy.wait()


def row_block(columns, last=None):
    if last is None:
        return pl.BlockSpec((ROWS, columns), lambda i: (i, 0))
    return pl.BlockSpec((ROWS, columns), lambda i: (jnp.minimum(i, last), 0))


def params(megabytes):
    return pltpu.CompilerParams(vmem_limit_bytes=megabytes * MEBI)


def copy_sems(plan, *sets):
    return pltpu.SemaphoreType.DMA(sets + (plan.across * plan.halves,))


def pool_kernel(plan, odd_ref, rows_ref, held_ref, other_ref, out_ref, weight, sems):
    width = weight.shape[1]

    @pl.when(pl.program_id(0) == 0)
    def _():
        copies = column_copies(plan, odd_ref[0], held_ref, other_ref, weight, sems, 0, width)
        start_all(copies)
        wait_all(copies)

    out_ref[...] = dot(rows_ref[...], weight[...]).astype(BF16)


def pool_project(plan, encoded, halves):
    rows, width = encoded.shape
    block = 512
    return pl.pallas_call(
        functools.partial(pool_kernel, plan),
        grid=(rows // block,),
        in_specs=[SCALAR, pl.BlockSpec((block, width), lambda i: (i, 0)), ANYWHERE, ANYWHERE],
        out_specs=pl.BlockSpec((block, 2 * width), lambda i: (i, 0)),
        out_shape=jax.ShapeDtypeStruct((rows, 2 * width), BF16),
        scratch_shapes=[pltpu.VMEM((width, 2 * width), BF16), copy_sems(plan)],
        compiler_params=params(40),
        name="pool_project",
    )(plan.odd_word, encoded, *halves)


def project_kernel(
    plan,
    odd_ref,
    tokens_ref,
    held_ref,
    other_ref,
    first_in_ref,
    projected_ref,
    vectors_ref,
    weight,
    pack,
    sems,
):
    width = tokens_ref.shape[1]

    @pl.when(pl.program_id(0) == 0)
    def _():
        copies = column_copies(plan, odd_ref[0], held_ref, other_ref, weight, sems.at[0], 0, 3 * width)
        copies += column_copies(
            plan, odd_ref[0], held_ref, other_ref, pack, sems.at[1], 3 * width, LANES
        )
        start_all(copies)
        wait_all(copies)
        vectors_ref[...] = pack[...].astype(F32).T[:8]

    unit = norm_parts(tokens_ref[...].astype(F32))[0]
    first_in = (unit * vectors_ref[0:1] + vectors_ref[1:2]).astype(BF16)
    first_in_ref[...] = first_in
    projected_ref[...] = dot(first_in, weight[...]).astype(BF16)


def project(plan, tokens, halves):
    rows, width = tokens.shape
    return pl.pallas_call(
        functools.partial(project_kernel, plan),
        grid=(rows // ROWS,),
        in_specs=[SCALAR, row_block(width), ANYWHERE, ANYWHERE],
        out_specs=[
            row_block(width),
            row_block(3 * width),
            pl.BlockSpec((8, width), lambda i: (0, 0)),
        ],
        out_shape=[
            jax.ShapeDtypeStruct((rows, width), BF16),
            jax.ShapeDtypeStruct((rows, 3 * width), BF16),
            jax.ShapeDtypeStruct((8, width), F32),
        ],
        scratch_shapes=[
            pltpu.VMEM((width, 3 * width), BF16),
            pltpu.VMEM((width, LANES), BF16),
            copy_sems(plan, 2),
        ],
        compiler_params=params(40),
        name="project",
    )(plan.odd_word, tokens, *halves)


def middle_kernel(
    plan,
    starts,
    odd_ref,
    tokens_ref,
    mixed_ref,
    vectors_ref,
    held_ref,
    other_ref,
    after_ref,
    second_in_ref,
    queries_ref,
    out_weight,
    query_weight,
    sems,
):
    width = tokens_ref.shape[1]

    @pl.when(pl.program_id(0) == 0)
    def _():
        copies = []
        for place_at, target in enumerate((out_weight, query_weight)):
            copies += column_copies(
                plan, odd_ref[0], held_ref, other_ref, target, sems.at[place_at], starts[place_at], width
            )
        start_all(copies)
        wait_all(copies)

    after = tokens_ref[...].astype(F32) + dot(mixed_ref[...], out_weight[...])
    after_ref[...] = after
    unit = norm_parts(after)[0]
    second_in = (unit * vectors_ref[2:3] + vectors_ref[3:4]).astype(BF16)
    second_in_ref[...] = second_in
    queries_ref[...] = dot(second_in, query_weight[...]).astype(BF16)


def middle(plan, starts, tokens, mixed, vectors, halves):
    rows, width = tokens.shape
    return pl.pallas_call(
        functools.partial(middle_kernel, plan, starts),
        grid=(rows // ROWS,),
        in_specs=[
            SCALAR,
            row_block(width),
            row_block(width),
            pl.BlockSpec((8, width), lambda i: (0, 0)),
            ANYWHERE,
            ANYWHERE,
        ],
        out_specs=[row_block(width)] * 3,
        out_shape=[
            jax.ShapeDtypeStruct((rows, width), F32),
            jax.ShapeDtypeStruct((rows, width), BF16),
            jax.ShapeDtypeStruct((rows, width), BF16),
        ],
        scratch_shapes=[
            pltpu.VMEM((width, width), BF16),
            pltpu.VMEM((width, width), BF16),
            copy_sems(plan, 2),
        ],
        compiler_params=params(40),
        name="middle",
    )(plan.odd_word, tokens, mixed, vectors, *halves)


GELU_SCALE = 0.7978845608028654
GELU_CUBE = 0.044715


def gelu_both(values):
    square = values * values
    bent = jnp.tanh(values * (GELU_SCALE + (GELU_SCALE * GELU_CUBE) * square))
    half = 0.5 + 0.5 * bent
    slope = GELU_SCALE + (3.0 * GELU_SCALE * GELU_CUBE) * square
    return (values * half, half + (0.5 * values) * (1.0 - bent * bent) * slope)


def feed_kernel(
    plan,
    out_start,
    row_steps,
    odd_ref,
    after_ref,
    mixed_ref,
    cotangent_ref,
    vectors_ref,
    feed_held_ref,
    feed_other_ref,
    held_ref,
    other_ref,
    block_ref,
    grad_ref,
    mixed_grad_ref,
    terms_ref,
    keep_ref,
    send_ref,
    weights,
    lefts,
    rights,
    sems,
):
    step = pl.program_id(0)
    width = after_ref.shape[1]
    parts = (weights.shape[0] - 1) // 2

    def copies(index):
        if index == 2 * parts:
            return column_copies(
                plan, odd_ref[0], held_ref, other_ref, weights.at[index], sems.at[index], out_start, width
            )
        return column_copies(
            plan,
            odd_ref[0],
            feed_held_ref,
            feed_other_ref,
            weights.at[index],
            sems.at[index],
            index * width,
            width,
        )

    @pl.when(step == 0)
    def _():
        order = [2 * parts]
        for part in range(parts):
            order += [part, parts + part]
        for index in order:
            start_all(copies(index))

    def ready(index):
        @pl.when(step == 0)
        def _():
            wait_all(copies(index))

        return weights[index]

    @pl.when(step < row_steps)
    def _():
        place_at = pl.ds(pl.multiple_of(step * ROWS, ROWS), ROWS)
        mixed = mixed_ref[...]
        cotangent = cotangent_ref[...]
        out_weight = ready(2 * parts)
        after_cross = after_ref[...] + dot(mixed, out_weight)
        unit, inverse = norm_parts(after_cross)
        gain = vectors_ref[4:5]
        third_in = (unit * gain + vectors_ref[5:6]).astype(BF16)
        lefts[parts, :, place_at] = third_in.T
        lefts[parts + 1, :, place_at] = mixed.T
        rights[0, place_at] = cotangent
        result = after_cross
        upstream = jnp.zeros_like(after_cross)
        for part in range(parts):
            up = ready(part)
            hidden, slope = gelu_both(dot(third_in, up))
            hidden = hidden.astype(BF16)
            lefts[part, :, place_at] = hidden.T
            down = ready(parts + part)
            result = result + dot(hidden, down)
            hidden_grad = (slope * dot(cotangent, down, NT)).astype(BF16)
            rights[1 + part, place_at] = hidden_grad
            upstream = upstream + dot(hidden_grad, up, NT)
        block_ref[...] = result.astype(BF16)
        inner = upstream * gain
        mean_inner = jnp.mean(inner, axis=-1, keepdims=True)
        mean_both = jnp.mean(inner * unit, axis=-1, keepdims=True)
        grad = cotangent.astype(F32) + inverse * (inner - mean_inner - unit * mean_both)
        add_terms(
            step,
            terms_ref,
            jnp.sum(upstream * unit, axis=0, keepdims=True),
            jnp.sum(upstream, axis=0, keepdims=True),
        )
        grad_ref[...] = grad
        rounded = grad.astype(BF16)
        rights[parts + 1, place_at] = rounded
        mixed_grad_ref[...] = dot(rounded, out_weight, NT).astype(BF16)

    @pl.when(step >= row_steps)
    def _():
        term = step - row_steps
        left = jnp.where(term < parts, term, jnp.where(term < 2 * parts, parts, parts + 1))
        right = jnp.where(term < parts, 0, term - parts + 1)
        result = dot(lefts[left], rights[right]).astype(BF16)
        store_halves(plan, odd_ref[0], result, keep_ref, send_ref, slice(0, width))


def feed(plan, out_start, after, mixed, cotangent, vectors, feed_halves, halves):
    rows, width = after.shape
    parts = feed_halves[0].shape[1] // width // 2
    terms = 2 * parts + 1
    steps = rows // ROWS
    last = steps - 1
    rows_in = row_block(width, last)
    whole = pl.BlockSpec((8, width), lambda i: (0, 0))
    slab = pl.BlockSpec((plan.half_rows, width), lambda i: (0, jnp.maximum(i - steps, 0)))
    slab_shape = jax.ShapeDtypeStruct((plan.half_rows, terms * width), BF16)
    return pl.pallas_call(
        functools.partial(feed_kernel, plan, out_start, steps),
        grid=(steps + terms,),
        in_specs=[SCALAR, rows_in, rows_in, rows_in, whole] + [ANYWHERE] * 4,
        out_specs=[rows_in, rows_in, rows_in, whole, slab, slab],
        out_shape=[
            jax.ShapeDtypeStruct((rows, width), BF16),
            jax.ShapeDtypeStruct((rows, width), F32),
            jax.ShapeDtypeStruct((rows, width), BF16),
            jax.ShapeDtypeStruct((8, width), F32),
            slab_shape,
            slab_shape,
        ],
        scratch_shapes=[
            pltpu.VMEM((terms, width, width), BF16),
            pltpu.VMEM((parts + 2, width, rows), BF16),
            pltpu.VMEM((parts + 2, rows, width), BF16),
            copy_sems(plan, terms),
        ],
        compiler_params=params(60),
        name="feed_forward",
    )(plan.odd_word, after, mixed, cotangent, vectors, *feed_halves, *halves)


def second_kernel(
    plan,
    starts,
    row_steps,
    odd_ref,
    after_ref,
    grad_in_ref,
    query_grad_ref,
    second_in_ref,
    mixed_ref,
    vectors_ref,
    held_ref,
    other_ref,
    grad_ref,
    attend_ref,
    terms_ref,
    keep_ref,
    send_ref,
    out_weight,
    query_weight,
    lefts,
    rights,
    sems,
):
    step = pl.program_id(0)
    width = after_ref.shape[1]

    @pl.when(step == 0)
    def _():
        copies = []
        for place_at, target in enumerate((out_weight, query_weight)):
            copies += column_copies(
                plan, odd_ref[0], held_ref, other_ref, target, sems.at[place_at], starts[place_at], width
            )
        start_all(copies)
        wait_all(copies)

    @pl.when(step < row_steps)
    def _():
        place_at = pl.ds(pl.multiple_of(step * ROWS, ROWS), ROWS)
        query_grad = query_grad_ref[...]
        back, gain_term, shift_term = norm_back(
            after_ref[...], vectors_ref[2:3], dot(query_grad, query_weight[...], NT)
        )
        add_terms(step, terms_ref, gain_term, shift_term)
        grad = grad_in_ref[...] + back
        grad_ref[...] = grad
        rounded = grad.astype(BF16)
        attend_ref[...] = dot(rounded, out_weight[...], NT).astype(BF16)
        lefts[0, :, place_at] = second_in_ref[...].T
        lefts[1, :, place_at] = mixed_ref[...].T
        rights[0, place_at] = query_grad
        rights[1, place_at] = rounded

    @pl.when(step >= row_steps)
    def _():
        term = step - row_steps
        result = dot(lefts[term], rights[term]).astype(BF16)
        store_halves(plan, odd_ref[0], result, keep_ref, send_ref, slice(0, width))


def second_back(plan, starts, after, grad_in, query_grad, second_in, mixed, vectors, halves):
    rows, width = after.shape
    steps = rows // ROWS
    rows_in = row_block(width, steps - 1)
    whole = pl.BlockSpec((8, width), lambda i: (0, 0))
    slab = pl.BlockSpec((plan.half_rows, width), lambda i: (0, jnp.maximum(i - steps, 0)))
    slab_shape = jax.ShapeDtypeStruct((plan.half_rows, 2 * width), BF16)
    return pl.pallas_call(
        functools.partial(second_kernel, plan, starts, steps),
        grid=(steps + 2,),
        in_specs=[SCALAR] + [rows_in] * 5 + [whole, ANYWHERE, ANYWHERE],
        out_specs=[rows_in, rows_in, whole, slab, slab],
        out_shape=[
            jax.ShapeDtypeStruct((rows, width), F32),
            jax.ShapeDtypeStruct((rows, width), BF16),
            jax.ShapeDtypeStruct((8, width), F32),
            slab_shape,
            slab_shape,
        ],
        scratch_shapes=[
            pltpu.VMEM((width, width), BF16),
            pltpu.VMEM((width, width), BF16),
            pltpu.VMEM((2, width, rows), BF16),
            pltpu.VMEM((2, rows, width), BF16),
            copy_sems(plan, 2),
        ],
        compiler_params=params(48),
        name="second_back",
    )(plan.odd_word, after, grad_in, query_grad, second_in, mixed, vectors, *halves)


def first_kernel(
    plan,
    row_steps,
    odd_ref,
    tokens_ref,
    grad_in_ref,
    projected_grad_ref,
    first_in_ref,
    vectors_ref,
    second_terms_ref,
    third_terms_ref,
    held_ref,
    other_ref,
    grad_ref,
    keep_ref,
    send_ref,
    weight,
    terms,
    left,
    rights,
    sems,
):
    step = pl.program_id(0)
    width = tokens_ref.shape[1]

    @pl.when(step == 0)
    def _():
        copies = column_copies(plan, odd_ref[0], held_ref, other_ref, weight, sems, 0, 3 * width)
        start_all(copies)
        wait_all(copies)

    place_at = pl.ds(pl.multiple_of(step * ROWS, ROWS), ROWS)
    upstream = None
    for part in range(3):
        grads = projected_grad_ref[part]
        rights[part, place_at] = grads
        product = dot(grads, weight[:, part * width : (part + 1) * width], NT)
        upstream = product if upstream is None else upstream + product
    back, gain_term, shift_term = norm_back(
        tokens_ref[...].astype(F32), vectors_ref[0:1], upstream
    )
    add_terms(step, terms, gain_term, shift_term)
    grad_ref[...] = grad_in_ref[...] + back
    left[:, place_at] = first_in_ref[...].T

    @pl.when(step == row_steps - 1)
    def _():
        for part in range(3):
            result = dot(left[...], rights[part]).astype(BF16)
            columns = slice(part * width, (part + 1) * width)
            store_halves(plan, odd_ref[0], result, keep_ref, send_ref, columns)
        rows = jnp.concatenate(
            [
                terms[0:2],
                second_terms_ref[0:2],
                third_terms_ref[0:2],
                jnp.zeros((LANES - 6, width), F32),
            ],
            axis=0,
        )
        columns = slice(3 * width, 3 * width + LANES)
        store_halves(plan, odd_ref[0], rows.T.astype(BF16), keep_ref, send_ref, columns)


def first_back(
    plan, tokens, grad_in, projected_grad, first_in, vectors, second_terms, third_terms, halves
):
    rows, width = tokens.shape
    steps = rows // ROWS
    rows_in = row_block(width)
    whole = pl.BlockSpec((8, width), lambda i: (0, 0))
    columns = 3 * width + LANES
    slab = pl.BlockSpec((plan.half_rows, columns), lambda i: (0, 0))
    slab_shape = jax.ShapeDtypeStruct((plan.half_rows, columns), BF16)
    return pl.pallas_call(
        functools.partial(first_kernel, plan, steps),
        grid=(steps,),
        in_specs=[
            SCALAR,
            rows_in,
            rows_in,
            pl.BlockSpec((3, ROWS, width), lambda i: (0, i, 0)),
            rows_in,
            whole,
            whole,
            whole,
            ANYWHERE,
            ANYWHERE,
        ],
        out_specs=[rows_in, slab, slab],
        out_shape=[jax.ShapeDtypeStruct((rows, width), F32), slab_shape, slab_shape],
        scratch_shapes=[
            pltpu.VMEM((width, 3 * width), BF16),
            pltpu.VMEM((8, width), F32),
            pltpu.VMEM((width, rows), BF16),
            pltpu.VMEM((3, rows, width), BF16),
            copy_sems(plan),
        ],
        compiler_params=params(56),
        name="first_back",
    )(
        plan.odd_word,
        tokens,
        grad_in,
        projected_grad,
        first_in,
        vectors,
        second_terms,
        third_terms,
        *halves,
    )


def keyval_kernel(
    plan, odd_ref, rows_ref, key_ref, value_ref, keep_ref, send_ref, key_total, value_total
):
    step = pl.program_id(0)
    width = rows_ref.shape[1]
    turned = rows_ref[...].T
    key_part = dot(turned, key_ref[...])
    value_part = dot(turned, value_ref[...])

    @pl.when(step == 0)
    def _():
        key_total[...] = key_part
        value_total[...] = value_part

    @pl.when(step > 0)
    def _():
        key_total[...] += key_part
        value_total[...] += value_part

    @pl.when(step == pl.num_programs(0) - 1)
    def _():
        for place_at, total in enumerate((key_total, value_total)):
            columns = slice(place_at * width, (place_at + 1) * width)
            store_halves(plan, odd_ref[0], total[...].astype(BF16), keep_ref, send_ref, columns)


def keyval_terms(plan, encoded, pool_keys, pool_values):
    rows, width = encoded.shape
    block = 1024
    rows_in = pl.BlockSpec((block, width), lambda i: (i, 0))
    slab = pl.BlockSpec((plan.half_rows, 2 * width), lambda i: (0, 0))
    slab_shape = jax.ShapeDtypeStruct((plan.half_rows, 2 * width), BF16)
    return pl.pallas_call(
        functools.partial(keyval_kernel, plan),
        grid=(rows // block,),
        in_specs=[SCALAR, rows_in, rows_in, rows_in],
        out_specs=[slab, slab],
        out_shape=[slab_shape, slab_shape],
        scratch_shapes=[pltpu.VMEM((width, width), F32), pltpu.VMEM((width, width), F32)],
        compiler_params=params(48),
        name="keyval_terms",
    )(plan.odd_word, encoded, pool_keys, pool_values)


def neighbours_kernel(
    plan, odd_ref, key_ref, value_ref, held_ref, other_ref, out_ref, weight, sems
):
    width = key_ref.shape[1]

    @pl.when(pl.program_id(0) == 0)
    def _():
        copies = column_copies(plan, odd_ref[0], held_ref, other_ref, weight, sems, 0, 2 * width)
        start_all(copies)
        wait_all(copies)

    out_ref[...] = dot(key_ref[...], weight[:, :width], NT) + dot(
        value_ref[...], weight[:, width:], NT
    )


def neighbours_back(plan, pool_keys, pool_values, halves):
    rows, width = pool_keys.shape
    block = 512
    rows_in = pl.BlockSpec((block, width), lambda i: (i, 0))
    return pl.pallas_call(
        functools.partial(neighbours_kernel, plan),
        grid=(rows // block,),
        in_specs=[SCALAR, rows_in, rows_in, ANYWHERE, ANYWHERE],
        out_specs=rows_in,
        out_shape=jax.ShapeDtypeStruct((rows, width), F32),
        scratch_shapes=[pltpu.VMEM((width, 2 * width), BF16), copy_sems(plan)],
        compiler_params=params(40),
        name="neighbours_back",
    )(plan.odd_word, pool_keys, pool_values, *halves)

def local(
    tokens,
    lengths,
    neighbours,
    neighbour_ids,
    neighbour_lengths,
    first_gain,
    first_shift,
    self_input,
    self_output,
    second_gain,
    second_shift,
    cross_query,
    cross_keyval,
    cross_output,
    third_gain,
    third_shift,
    feed_up,
    feed_down,
    cotangent,
):
    rows, width = cross_query.shape
    plan = Plan(rows)
    parts = feed_down.shape[0] // rows
    pool_count, neigh_len = neighbours.shape[:2]
    vectors = (first_gain, first_shift, second_gain, second_shift, third_gain, third_shift)
    vector_pack = jnp.pad(jnp.stack(vectors, axis=1), ((0, 0), (0, LANES - len(vectors))))
    up_shard = feed_up.reshape(rows, plan.count, parts, rows).swapaxes(1, 2).reshape(feed_up.shape)
    down_shard = feed_down.reshape(parts, rows, width).swapaxes(0, 1).reshape(rows, parts * width)

    keyval_halves = gather_halves(plan, cross_keyval)
    project_halves = gather_halves(plan, jnp.concatenate([self_input, vector_pack], axis=1))
    middle_halves = gather_halves(
        plan, jnp.concatenate([self_output, cross_query, cross_output], axis=1)
    )
    feed_halves = gather_halves(plan, jnp.concatenate([up_shard, down_shard], axis=1))

    rows_in = tokens[0]
    encoded = neighbours.reshape(pool_count * neigh_len, width)
    ids = neighbour_ids.reshape(-1)
    pool_keyval = pool_project(plan, encoded, keyval_halves)
    pool_keyval = pool_keyval.reshape(pool_count, neigh_len, 2 * width)
    first_in, projected, vector_rows = project(plan, rows_in, project_halves)
    self_mixed, self_exact, logsum = self_forward(projected, lengths)
    after_self, second_in, cross_queries = middle(
        plan, (0, width), rows_in, self_mixed, vector_rows, middle_halves
    )
    cross_mixed = cross_forward(cross_queries, pool_keyval, ids, neighbour_lengths)
    block_out, after_cross_grad, mixed_grad, third_terms, feed_keep, feed_send = feed(
        plan,
        2 * width,
        after_self,
        cross_mixed,
        cotangent[0],
        vector_rows,
        feed_halves,
        middle_halves,
    )
    feed_sum = scatter_halves(plan, feed_keep, feed_send)

    query_grad, pool_keys, pool_values = cross_backward(
        cross_queries, mixed_grad, pool_keyval, ids, neighbour_lengths
    )
    pool_keys = pool_keys.reshape(pool_count * neigh_len, width)
    pool_values = pool_values.reshape(pool_count * neigh_len, width)
    keyval_keep, keyval_send = keyval_terms(plan, encoded, pool_keys, pool_values)
    after_self_grad, attend_grad, second_terms, second_keep, second_send = second_back(
        plan,
        (0, width),
        after_self,
        after_cross_grad,
        query_grad,
        second_in,
        self_mixed,
        vector_rows,
        middle_halves,
    )
    middle_sum = scatter_halves(
        plan,
        jnp.concatenate([keyval_keep, second_keep], axis=1),
        jnp.concatenate([keyval_send, second_send], axis=1),
    )
    projected_grad = self_backward(projected, lengths, attend_grad, self_exact, logsum)
    tokens_grad, first_keep, first_send = first_back(
        plan,
        rows_in,
        after_self_grad,
        projected_grad,
        first_in,
        vector_rows,
        second_terms,
        third_terms,
        project_halves,
    )
    first_sum = scatter_halves(plan, first_keep, first_send)
    neighbours_grad = neighbours_back(plan, pool_keys, pool_values, keyval_halves)

    down_grad = feed_sum[:, : parts * width].reshape(rows, parts, width).swapaxes(0, 1)
    up_grad = feed_sum[:, parts * width : 2 * parts * width]
    up_grad = up_grad.reshape(rows, parts, plan.count, rows).swapaxes(1, 2)
    vector_grads = [first_sum[:, 3 * width + i] for i in range(len(vectors))]
    return (
        block_out[None],
        tokens_grad[None],
        neighbours_grad.reshape(neighbours.shape),
        vector_grads[0],
        vector_grads[1],
        first_sum[:, : 3 * width],
        middle_sum[:, 3 * width :],
        vector_grads[2],
        vector_grads[3],
        middle_sum[:, 2 * width : 3 * width],
        middle_sum[:, : 2 * width],
        feed_sum[:, 2 * parts * width :],
        vector_grads[4],
        vector_grads[5],
        up_grad.reshape(feed_up.shape),
        down_grad.reshape(feed_down.shape),
    )


def solution(mesh):
    placed = (
        P(("fsdp", "dp"), None, None),
        P(("fsdp", "dp")),
        P(("fsdp", "dp"), None, None),
        P(("fsdp", "dp"), None, None),
        P(("fsdp", "dp")),
        P(("fsdp", "dp")),
        P(("fsdp", "dp")),
        P(("fsdp", "dp"), None),
        P(("fsdp", "dp"), None),
        P(("fsdp", "dp")),
        P(("fsdp", "dp")),
        P(("fsdp", "dp"), None),
        P(("fsdp", "dp"), None),
        P(("fsdp", "dp"), None),
        P(("fsdp", "dp")),
        P(("fsdp", "dp")),
        P(("fsdp", "dp"), None),
        P(("fsdp", "dp"), None),
        P(("fsdp", "dp"), None, None),
    )
    return jax.shard_map(
        local,
        mesh=mesh,
        in_specs=placed,
        out_specs=(
            P(("fsdp", "dp"), None, None),
            P(("fsdp", "dp"), None, None),
            P(("fsdp", "dp"), None, None),
            P(("fsdp", "dp")),
            P(("fsdp", "dp")),
            P(("fsdp", "dp"), None),
            P(("fsdp", "dp"), None),
            P(("fsdp", "dp")),
            P(("fsdp", "dp")),
            P(("fsdp", "dp"), None),
            P(("fsdp", "dp"), None),
            P(("fsdp", "dp"), None),
            P(("fsdp", "dp")),
            P(("fsdp", "dp")),
            P(("fsdp", "dp"), None),
            P(("fsdp", "dp"), None),
        ),
        check_vma=False,
    )
```

```python
import functools

import jax
import jax.numpy as jnp
from jax import lax
from jax.experimental import pallas as pl
from jax.experimental.pallas import tpu as pltpu
from jax.sharding import PartitionSpec as P

HEADS = 12
SPAN = 64
NEIGH = 2
LANES = 128
WIDE = 256
QBLOCK = 256

EPSILON = 1e-05
SCALE = 0.125
NEGATIVE = -1e30
BF16 = jnp.bfloat16
F32 = jnp.float32
NT = (((1,), (1,)), ((), ()))
NN = (((1,), (0,)), ((), ()))
TN = (((0,), (0,)), ((), ()))


def dot(left, right, dims=NN):
    return lax.dot_general(left, right, dims, preferred_element_type=F32)


def iota(shape, axis):
    return lax.broadcasted_iota(jnp.int32, shape, axis)


def cost(microseconds):
    return pl.CostEstimate(flops=int(microseconds * 1.1e9), bytes_accessed=0, transcendentals=0)


def passing(kernel, before, given, *refs):
    return kernel(*refs[:before], *refs[before + given :])


def split_three(values):
    high = values.astype(BF16)
    rest = values - high.astype(F32)
    middle = rest.astype(BF16)
    low = (rest - middle.astype(F32)).astype(BF16)
    return (high, middle, low)


def self_forward_kernel(length_ref, query_ref, key_ref, value_ref, mixed_ref, exact_ref, logsum_ref):
    seq_len = query_ref.shape[0]
    length = length_ref[0]
    lane = iota((1, LANES), 1)
    first = lane < 64
    padded = jnp.where(iota((seq_len, 1), 0) < length, 0.0, NEGATIVE).astype(BF16)
    keys = key_ref[...]
    values = value_ref[...]
    one = jnp.ones((), BF16)
    keys_by_head = (
        jnp.where(first, keys, jnp.where(lane == 64, padded, 0)),
        jnp.where(first, jnp.where(lane == 0, padded, 0), keys),
    )
    values_by_head = (jnp.where(first, values, one), jnp.where(first, one, values))
    causal = iota((QBLOCK, QBLOCK), 1) <= iota((QBLOCK, QBLOCK), 0)
    for block in range(seq_len // QBLOCK):
        start = block * QBLOCK
        query = query_ref[start : start + QBLOCK] * jnp.asarray(SCALE, BF16)
        queries = (
            jnp.where(first, query, jnp.where(lane == 64, one, 0)),
            jnp.where(first, jnp.where(lane == 0, one, 0), query),
        )
        outs = []
        tops = []
        for head in range(2):
            diagonal = dot(queries[head], keys_by_head[head][start : start + QBLOCK], NT)
            diagonal = jnp.where(causal, diagonal, NEGATIVE)
            top = jnp.max(diagonal, axis=-1, keepdims=True)
            if block:
                before = dot(queries[head], keys_by_head[head][:start], NT)
                top = jnp.maximum(top, jnp.max(before, axis=-1, keepdims=True))
            out = dot(
                jnp.exp(diagonal - top).astype(BF16),
                values_by_head[head][start : start + QBLOCK],
            )
            if block:
                out = out + dot(jnp.exp(before - top).astype(BF16), values_by_head[head][:start])
            outs.append(out)
            tops.append(top)
        total = pltpu.roll(jnp.where(first, outs[1], outs[0]), 64, 1)
        mixed = jnp.where(first, outs[0], outs[1]) / total
        mixed_ref[start : start + QBLOCK] = mixed.astype(BF16)
        exact_ref[start : start + QBLOCK] = mixed
        logsum = (jnp.where(first, tops[0], tops[1]) + jnp.log(total)).T
        logsum_ref[0, 0:1, start : start + QBLOCK] = logsum[0:1]
        logsum_ref[0, 1:2, start : start + QBLOCK] = logsum[64:65]


def self_forward(projected, lengths):
    seq_len = projected.shape[0]
    width = projected.shape[1] // 3
    pairs = width // LANES
    column = lambda offset: pl.BlockSpec((seq_len, LANES), lambda p: (0, p + offset))
    return pl.pallas_call(
        self_forward_kernel,
        grid=(pairs,),
        in_specs=[
            pl.BlockSpec(memory_space=pltpu.SMEM),
            column(0),
            column(pairs),
            column(2 * pairs),
        ],
        out_specs=[
            column(0),
            column(0),
            pl.BlockSpec((1, 8, seq_len), lambda p: (p, 0, 0)),
        ],
        out_shape=[
            jax.ShapeDtypeStruct((seq_len, width), BF16),
            jax.ShapeDtypeStruct((seq_len, width), F32),
            jax.ShapeDtypeStruct((pairs, 8, seq_len), F32),
        ],
        compiler_params=pltpu.CompilerParams(vmem_limit_bytes=48 * 2**20),
        cost_estimate=cost(22),
        name="self_forward",
    )(lengths, projected, projected, projected)


def self_backward_kernel(
    length_ref,
    query_ref,
    key_ref,
    value_ref,
    grad_ref,
    exact_ref,
    logsum_ref,
    out_ref,
    key_grad_ref,
    value_grad_ref,
):
    seq_len = query_ref.shape[0]
    length = length_ref[0]
    lane = iota((1, LANES), 1)
    first = lane < 64
    row = iota((LANES, 1), 0)
    top_rows = row < 64
    padded = jnp.where(iota((seq_len, 1), 0) < length, 0.0, NEGATIVE).astype(BF16)
    keys = key_ref[...]
    values = value_ref[...]
    zero = jnp.zeros((), BF16)
    minus = -jnp.ones((), BF16)

    def beside(offset, head_lane):
        kept = (lane > head_lane) & (lane < head_lane + 4)
        return jnp.where(lane == head_lane, offset, jnp.where(kept, minus, zero))

    keys_by_head = (
        jnp.where(first, keys, beside(padded, 64)),
        jnp.where(first, beside(padded, 0), keys),
    )
    values_by_head = (
        jnp.where(first, values, beside(zero, 64)),
        jnp.where(first, beside(zero, 0), values),
    )
    keys_turned = keys.T
    turned_by_head = (
        jnp.where(top_rows, keys_turned, zero),
        jnp.where(top_rows, zero, keys_turned),
    )
    causal = iota((QBLOCK, QBLOCK), 0) <= iota((QBLOCK, QBLOCK), 1)

    def fill(turned, head, lead, parts):
        base = 64 if head == 0 else 0
        other = jnp.where(row == base, lead, zero)
        for place, part in enumerate(parts):
            other = jnp.where(row == base + 1 + place, part, other)
        own = top_rows if head == 0 else ~top_rows
        return jnp.where(own, turned, other)

    count = seq_len // QBLOCK
    for block in reversed(range(count)):
        start = block * QBLOCK
        stop = start + QBLOCK
        query = query_ref[start:stop] * jnp.asarray(SCALE, BF16)
        grad = grad_ref[start:stop]
        query_turned = query.T
        grad_turned = grad.T
        weighted = (grad.astype(F32) * exact_ref[start:stop]).T
        probs_all = []
        scores_all = []
        query_grad = None
        for head in range(2):
            delta = jnp.sum(weighted[head * 64 : head * 64 + 64], axis=0, keepdims=True)
            logsum = logsum_ref[0, head : head + 1, start:stop]
            score = dot(
                keys_by_head[head][:stop],
                fill(query_turned, head, jnp.ones((), BF16), split_three(logsum)),
            )
            prob = jnp.exp(score)
            last = jnp.where(causal, prob[start:], 0.0)
            prob = jnp.concatenate([prob[:start], last], axis=0) if block else last
            centred = dot(
                values_by_head[head][:stop], fill(grad_turned, head, zero, split_three(delta))
            )
            score_grad = (prob * centred).astype(BF16)
            scores_all.append(score_grad)
            probs_all.append(prob.astype(BF16))
            part = dot(turned_by_head[head][:, :stop], score_grad)
            query_grad = part if query_grad is None else query_grad + part
        out_ref[0, start:stop] = (query_grad.T * SCALE).astype(BF16)
        own_query = jnp.concatenate(
            [jnp.where(first, query, zero), jnp.where(first, zero, query)], axis=0
        )
        own_grad = jnp.concatenate(
            [jnp.where(first, grad, zero), jnp.where(first, zero, grad)], axis=0
        )
        key_part = dot(jnp.concatenate(scores_all, axis=1), own_query)
        value_part = dot(jnp.concatenate(probs_all, axis=1), own_grad)
        if block == count - 1:
            key_grad_ref[...] = key_part
            value_grad_ref[...] = value_part
        else:
            key_grad_ref[:stop] += key_part
            value_grad_ref[:stop] += value_part
    out_ref[1] = key_grad_ref[...].astype(BF16)
    out_ref[2] = value_grad_ref[...].astype(BF16)


def self_backward(projected, lengths, grad, exact, logsum, first, count, earlier):
    seq_len = projected.shape[0]
    width = projected.shape[1] // 3
    pairs = width // LANES
    column = lambda offset: pl.BlockSpec((seq_len, LANES), lambda p: (0, p + offset))
    given = [] if earlier is None else [earlier]
    return pl.pallas_call(
        functools.partial(passing, self_backward_kernel, 7, len(given)),
        grid=(count,),
        in_specs=[
            pl.BlockSpec(memory_space=pltpu.SMEM),
            column(first),
            column(pairs + first),
            column(2 * pairs + first),
            column(first),
            column(first),
            pl.BlockSpec((1, 8, seq_len), lambda p: (p + first, 0, 0)),
        ]
        + [pl.BlockSpec(memory_space=pl.ANY)] * len(given),
        out_specs=pl.BlockSpec((3, seq_len, LANES), lambda p: (0, 0, p + first)),
        out_shape=jax.ShapeDtypeStruct((3, seq_len, width), BF16),
        scratch_shapes=[pltpu.VMEM((seq_len, LANES), F32), pltpu.VMEM((seq_len, LANES), F32)],
        input_output_aliases={7: 0} if given else {},
        compiler_params=pltpu.CompilerParams(vmem_limit_bytes=48 * 2**20),
        cost_estimate=cost(25),
        name="self_backward",
    )(lengths, projected, projected, projected, grad, exact, logsum, *given)


def block_diagonal(rows):
    lane = iota((1, WIDE), 1)
    return jnp.concatenate(
        [jnp.where((lane >= h * 64) & (lane < h * 64 + 64), rows, 0) for h in range(4)], axis=0
    )


def take_diagonal(stacked):
    lane = iota((1, WIDE), 1)
    result = stacked[:SPAN]
    for h in range(1, 4):
        result = jnp.where(lane >= h * 64, stacked[h * SPAN : (h + 1) * SPAN], result)
    return result


def slot_bias(ids_ref, neighbour_lengths_ref, span, neigh_len, axis):
    shape = (1, NEIGH * neigh_len) if axis else (NEIGH * neigh_len, 1)
    place = iota(shape, axis)
    first = neighbour_lengths_ref[ids_ref[span * NEIGH]]
    second = neighbour_lengths_ref[ids_ref[span * NEIGH + 1]]
    limit = jnp.where(place < neigh_len, first, neigh_len + second)
    return jnp.where(place < limit, 0.0, NEGATIVE)


def cross_forward_kernel(
    ids_ref, neighbour_lengths_ref, query_ref, first_ref, second_ref, mixed_ref
):
    span = pl.program_id(0)
    neigh_len = first_ref.shape[1]
    width = query_ref.shape[1]
    bias = slot_bias(ids_ref, neighbour_lengths_ref, span, neigh_len, 1)
    for group in range(width // WIDE):
        place = slice(group * WIDE, (group + 1) * WIDE)
        value_place = slice(width + group * WIDE, width + (group + 1) * WIDE)
        queries = block_diagonal(query_ref[:, place] * jnp.asarray(SCALE, BF16))
        keys = jnp.concatenate([first_ref[0, :, place], second_ref[0, :, place]], axis=0)
        values = jnp.concatenate(
            [first_ref[0, :, value_place], second_ref[0, :, value_place]], axis=0
        )
        score = dot(queries, keys, NT) + bias
        expo = jnp.exp(score - jnp.max(score, axis=-1, keepdims=True))
        total = jnp.sum(expo, axis=-1, keepdims=True)
        out = dot(expo.astype(BF16), values) / total
        mixed_ref[:, place] = take_diagonal(out).astype(BF16)


def cross_forward(queries, pool_keyval, ids, neighbour_lengths):
    seq_len, width = queries.shape
    neigh_len, both = pool_keyval.shape[1:]
    spans = seq_len // SPAN
    rows = pl.BlockSpec((SPAN, width), lambda c, ids, lens: (c, 0))
    slot = lambda j: pl.BlockSpec(
        (1, neigh_len, both), lambda c, ids, lens: (ids[c * NEIGH + j], 0, 0)
    )
    return pl.pallas_call(
        cross_forward_kernel,
        grid_spec=pltpu.PrefetchScalarGridSpec(
            num_scalar_prefetch=2,
            grid=(spans,),
            in_specs=[rows, slot(0), slot(1)],
            out_specs=rows,
        ),
        out_shape=jax.ShapeDtypeStruct((seq_len, width), BF16),
        compiler_params=pltpu.CompilerParams(vmem_limit_bytes=48 * 2**20),
        cost_estimate=cost(17),
        name="cross_forward",
    )(ids, neighbour_lengths, queries, pool_keyval, pool_keyval)


def cross_backward_kernel(
    ids_ref,
    neighbour_lengths_ref,
    query_ref,
    grad_ref,
    first_key_ref,
    second_key_ref,
    first_value_ref,
    second_value_ref,
    query_grad_ref,
    key_out_ref,
    value_out_ref,
    key_total,
    value_total,
):
    span = pl.program_id(0)
    spans = pl.num_programs(0)
    neigh_len = first_key_ref.shape[1]

    @pl.when(span == 0)
    def _():
        key_total[...] = jnp.zeros_like(key_total)
        value_total[...] = jnp.zeros_like(value_total)

    bias = slot_bias(ids_ref, neighbour_lengths_ref, span, neigh_len, 0)
    queries = block_diagonal(query_ref[...] * jnp.asarray(SCALE, BF16))
    grads = block_diagonal(grad_ref[...])
    keys = jnp.concatenate([first_key_ref[0], second_key_ref[0]], axis=0)
    values = jnp.concatenate([first_value_ref[0], second_value_ref[0]], axis=0)
    score = dot(keys, queries, NT) + bias
    expo = jnp.exp(score - jnp.max(score, axis=0, keepdims=True))
    prob = expo * (1.0 / jnp.sum(expo, axis=0, keepdims=True))
    prob_grad = dot(values, grads, NT)
    centred = prob_grad - jnp.sum(prob * prob_grad, axis=0, keepdims=True)
    score_grad = (prob * centred).astype(BF16)
    value_part = dot(prob.astype(BF16), grads)
    key_part = dot(score_grad, queries)
    query_part = dot(score_grad, keys, TN)
    query_grad_ref[...] = (take_diagonal(query_part) * SCALE).astype(BF16)
    for slot in range(NEIGH):
        ident = ids_ref[span * NEIGH + slot]
        rows = slice(slot * neigh_len, (slot + 1) * neigh_len)
        key_total[ident] += key_part[rows]
        value_total[ident] += value_part[rows]

    @pl.when(span == spans - 1)
    def _():
        key_out_ref[...] = key_total[...].astype(BF16)
        value_out_ref[...] = value_total[...].astype(BF16)


def cross_backward(queries, grads, pool_keyval, ids, neighbour_lengths, group, earlier):
    seq_len, width = queries.shape
    pool_count, neigh_len, _ = pool_keyval.shape
    spans = seq_len // SPAN
    groups = width // WIDE
    rows = pl.BlockSpec((SPAN, WIDE), lambda c, ids, lens: (c, group))
    slot = lambda j, offset: pl.BlockSpec(
        (1, neigh_len, WIDE), lambda c, ids, lens: (ids[c * NEIGH + j], 0, group + offset)
    )
    pool = pl.BlockSpec((pool_count, neigh_len, WIDE), lambda c, ids, lens: (0, 0, group))
    pool_shape = jax.ShapeDtypeStruct((pool_count, neigh_len, width), BF16)
    given = [] if earlier is None else list(earlier)
    return pl.pallas_call(
        functools.partial(passing, cross_backward_kernel, 8, len(given)),
        grid_spec=pltpu.PrefetchScalarGridSpec(
            num_scalar_prefetch=2,
            grid=(spans,),
            in_specs=[rows, rows, slot(0, 0), slot(1, 0), slot(0, groups), slot(1, groups)]
            + [pl.BlockSpec(memory_space=pl.ANY)] * len(given),
            out_specs=[rows, pool, pool],
            scratch_shapes=[
                pltpu.VMEM((pool_count, neigh_len, WIDE), F32),
                pltpu.VMEM((pool_count, neigh_len, WIDE), F32),
            ],
        ),
        out_shape=[jax.ShapeDtypeStruct((seq_len, width), BF16), pool_shape, pool_shape],
        input_output_aliases={8 + i: i for i in range(len(given))},
        compiler_params=pltpu.CompilerParams(vmem_limit_bytes=56 * 2**20),
        cost_estimate=cost(48),
        name="cross_backward",
    )(ids, neighbour_lengths, queries, grads, *[pool_keyval] * 4, *given)

AXES = ("fsdp", "dp")


def bits_of(size):
    return [1 << i for i in range(size.bit_length() - 1)]


def index_bits(count):
    return [1 << i for i in range(count.bit_length() - 2, -1, -1)]


class Line:
    def __init__(self):
        self.noted = []

    def note(self, *values):
        self.noted = [values[0]]

    def also(self, value):
        self.noted.append(value)

    def after(self, value):
        if not self.noted:
            return value
        return lax.optimization_barrier((value, *self.noted))[0]


class Plan:
    def __init__(self, rows, line):
        self.line = line
        self.inner = lax.axis_size("dp")
        self.outer = lax.axis_size("fsdp")
        self.count = self.inner * self.outer
        self.rows = rows
        self.core = [self.inner] if self.outer > 1 else []
        self.halves = 2 if self.core else 1
        self.across = self.outer // self.halves
        self.stripe = self.inner * rows
        self.half_rows = self.across * self.stripe
        self.me = lax.axis_index(AXES)
        across = [bit * self.inner for bit in bits_of(self.outer)[1:]]
        along = bits_of(self.inner)
        near, far = along[: len(across)], along[len(across) :]
        self.orders = (far + near + across, far + across + near)
        self.natural = [mask for mask in index_bits(self.count) if mask not in self.core]
        self.odd = self.bit(self.core[0]) if self.core else jnp.zeros((), jnp.int32)
        self.odd_word = self.odd.reshape(1)
        self.steps = list(zip(*self.orders))
        self.places = self.arrival_places()

    def bit(self, mask):
        return (self.me // mask) % 2

    def by_core(self, even, odd):
        return jnp.where(self.odd == 0, even, odd)

    def exchange(self, values, masks):
        even, odd = masks
        pairs = []
        for index in range(self.count):
            is_odd = bool(self.core) and (index // self.core[0]) % 2 == 1
            pairs.append((index, index ^ (odd if is_odd else even)))
        return lax.ppermute(values, AXES, pairs)

    def swap(self, values):
        return self.exchange(values, (self.core[0], self.core[0])) if self.core else values

    def weight_of(self, mask):
        return 1 << (len(self.natural) - 1 - self.natural.index(mask))

    def arrival_places(self):
        blocks = jnp.arange(1 << len(self.natural), dtype=jnp.int32)
        found = []
        for order in self.orders:
            target = jnp.zeros_like(blocks)
            for place_at, mask in enumerate(order):
                flag = ((blocks >> place_at) & 1) ^ self.bit(mask)
                target = target + flag * self.weight_of(mask)
            found.append(target)
        return self.by_core(found[0], found[1])

    def fold_places(self, step):
        found = []
        for order in self.orders:
            gone = order[::-1][:step]
            left = [mask for mask in self.natural if mask not in gone]
            mask = order[::-1][step]
            high = 1 << (len(left) - 1 - left.index(mask))
            index = jnp.arange(1 << (len(left) - 1), dtype=jnp.int32)
            kept = (index // high) * (2 * high) + index % high
            own = self.bit(mask)
            found.append((kept + (1 - own) * high, kept + own * high))
        return tuple(self.by_core(found[0][i], found[1][i]) for i in range(2))


def reorder_kernel(places_ref, in_ref, out_ref, buffer, sems):
    blocks = in_ref.shape[0]

    def copies(block):
        return pltpu.make_async_copy(
            in_ref.at[block], buffer.at[places_ref[block]], sems.at[block]
        )

    for block in range(blocks):
        copies(block).start()
    for block in range(blocks):
        copies(block).wait()
    pltpu.sync_copy(buffer, out_ref)


def reorder(plan, held):
    blocks = held.shape[0]
    return pl.pallas_call(
        reorder_kernel,
        in_specs=[pl.BlockSpec(memory_space=pltpu.SMEM), pl.BlockSpec(memory_space=pl.ANY)],
        out_specs=pl.BlockSpec(memory_space=pl.ANY),
        out_shape=jax.ShapeDtypeStruct(held.shape, held.dtype),
        scratch_shapes=[pltpu.VMEM(held.shape, held.dtype), pltpu.SemaphoreType.DMA((blocks,))],
        compiler_params=pltpu.CompilerParams(vmem_limit_bytes=32 * 2**20),
        name="reorder_blocks",
    )(plan.places, held)


class Gather:
    def __init__(self, plan, shard):
        self.plan = plan
        self.held = shard[None]
        self.at = 0
        self.other = None
        self.halves = None

    def launch(self):
        plan = self.plan
        self.held = plan.line.after(self.held)
        plan.line.also(self.held)
        if self.at < len(plan.steps):
            self.other = plan.exchange(self.held, plan.steps[self.at])
        else:
            self.other = plan.swap(self.held)

    def land(self):
        plan = self.plan
        other = plan.line.after(self.other)
        if self.at < len(plan.steps):
            self.held = jnp.concatenate([self.held, other], axis=0)
            self.at += 1
            if self.at == len(plan.steps):
                self.held = reorder(plan, self.held)
            plan.line.note(self.held)
        else:
            plan.line.note(other)
            shape = (plan.half_rows, self.held.shape[-1])
            self.halves = (self.held.reshape(shape), other.reshape(shape))

    def step(self):
        if self.halves is None:
            self.land()
            if self.halves is None:
                self.launch()

    def finish(self):
        while self.halves is None:
            self.step()
        return self.halves


def fold_kernel(sent_places, kept_places, *refs):
    half = len(refs) // 2 - 1
    sent_in, kept_in, (sent_ref, kept_ref) = refs[:half], refs[half : 2 * half], refs[2 * half :]
    for source, target in ((sent_in, sent_ref), (kept_in, kept_ref)):
        total = source[0][...].astype(F32)
        for part in source[1:]:
            total = total + part[...].astype(F32)
        target[...] = total.astype(BF16)


def fold(places, parts):
    blocks, rows, columns = parts[0].shape
    shape = jax.ShapeDtypeStruct((blocks // 2, rows, columns), BF16)
    out = pl.BlockSpec((1, rows, columns), lambda i, sent, kept: (i, 0, 0))
    sent = pl.BlockSpec((1, rows, columns), lambda i, sent, kept: (sent[i], 0, 0))
    kept = pl.BlockSpec((1, rows, columns), lambda i, sent, kept: (kept[i], 0, 0))
    return pl.pallas_call(
        fold_kernel,
        grid_spec=pltpu.PrefetchScalarGridSpec(
            num_scalar_prefetch=2,
            grid=(blocks // 2,),
            in_specs=[sent] * len(parts) + [kept] * len(parts),
            out_specs=[out, out],
        ),
        out_shape=[shape, shape],
        compiler_params=pltpu.CompilerParams(vmem_limit_bytes=32 * 2**20),
        name="fold_blocks",
    )(*places, *parts, *parts)


class Scatter:
    def __init__(self, plan, keep, send):
        self.plan = plan
        self.columns = keep.shape[1]
        shape = (1 << len(plan.natural), plan.rows, self.columns)
        self.kept = keep.reshape(shape)
        self.sent = send.reshape(shape) if plan.core else None
        self.at = -1
        self.other = None
        self.total = None

    def launch(self):
        plan = self.plan
        if self.sent is None:
            return
        self.sent = plan.line.after(self.sent)
        plan.line.also(self.sent)
        if self.at < 0:
            self.other = plan.swap(self.sent)
        else:
            self.other = plan.exchange(self.sent, plan.steps[::-1][self.at])

    def land(self):
        plan = self.plan
        parts = [self.kept] if self.other is None else [self.kept, plan.line.after(self.other)]
        self.at += 1
        if self.at < len(plan.steps):
            self.sent, self.kept = fold(plan.fold_places(self.at), parts)
            plan.line.note(self.sent)
        else:
            total = parts[0].astype(F32)
            for part in parts[1:]:
                total = total + part.astype(F32)
            self.total = total.reshape(plan.rows, self.columns)
            plan.line.note(self.total)

    def step(self):
        if self.total is None:
            self.land()
            if self.total is None:
                self.launch()

    def finish(self):
        while self.total is None:
            self.step()
        return self.total


def column_copies(plan, odd, held_ref, other_ref, target, sems, start, width):
    copies = []
    for across in range(plan.across):
        source_rows = pl.ds(across * plan.stripe, plan.stripe)
        for turn, ref in enumerate((held_ref, other_ref)[: plan.halves]):
            half = odd if turn == 0 else 1 - odd
            first = across * plan.halves * plan.stripe + half * plan.stripe
            if plan.halves == 1:
                first = across * plan.stripe
            elif plan.stripe % 16 == 0:
                first = pl.multiple_of(first, 16)
            copies.append(
                pltpu.make_async_copy(
                    ref.at[source_rows, pl.ds(start, width)],
                    target.at[pl.ds(first, plan.stripe), :],
                    sems.at[across * plan.halves + turn],
                )
            )
    return copies


def store_halves(plan, odd, result, keep_ref, send_ref, columns):
    for across in range(plan.across):
        rows = slice(across * plan.stripe, (across + 1) * plan.stripe)
        for half in range(plan.halves):
            first = (across * plan.halves + half) * plan.stripe
            part = result[first : first + plan.stripe]
            if plan.halves == 1:
                keep_ref[rows, columns] = part
                continue

            @pl.when(odd == half)
            def _():
                keep_ref[rows, columns] = part

            @pl.when(odd != half)
            def _():
                send_ref[rows, columns] = part

ROWS = 256
MEBI = 2**20
ANYWHERE = pl.BlockSpec(memory_space=pl.ANY)
SCALAR = pl.BlockSpec(memory_space=pltpu.SMEM)


def norm_parts(values):
    centre = jnp.mean(values, axis=-1, keepdims=True)
    centred = values - centre
    spread = jnp.mean(centred * centred, axis=-1, keepdims=True)
    inverse = lax.rsqrt(spread + EPSILON)
    return (centred * inverse, inverse)


def norm_back(values, gain, upstream):
    unit, inverse = norm_parts(values)
    gain_term = jnp.sum(upstream * unit, axis=0, keepdims=True)
    shift_term = jnp.sum(upstream, axis=0, keepdims=True)
    inner = upstream * gain
    mean_inner = jnp.mean(inner, axis=-1, keepdims=True)
    mean_both = jnp.mean(inner * unit, axis=-1, keepdims=True)
    return (inverse * (inner - mean_inner - unit * mean_both), gain_term, shift_term)


def add_terms(step, target_ref, gain_term, shift_term):
    @pl.when(step == 0)
    def _():
        target_ref[...] = jnp.zeros_like(target_ref)

    target_ref[0:1] += gain_term
    target_ref[1:2] += shift_term


def start_all(copies):
    for copy in copies:
        copy.start()


def wait_all(copies):
    for copy in copies:
        copy.wait()


def row_block(columns, last=None):
    if last is None:
        return pl.BlockSpec((ROWS, columns), lambda i: (i, 0))
    return pl.BlockSpec((ROWS, columns), lambda i: (jnp.minimum(i, last), 0))


def params(megabytes):
    return pltpu.CompilerParams(vmem_limit_bytes=megabytes * MEBI)


def copy_sems(plan, *sets):
    return pltpu.SemaphoreType.DMA(sets + (plan.across * plan.halves,))


def pool_kernel(plan, odd_ref, rows_ref, held_ref, other_ref, out_ref, weight, sems):
    width = weight.shape[1]

    @pl.when(pl.program_id(0) == 0)
    def _():
        copies = column_copies(plan, odd_ref[0], held_ref, other_ref, weight, sems, 0, width)
        start_all(copies)
        wait_all(copies)

    out_ref[...] = dot(rows_ref[...], weight[...]).astype(BF16)


def pool_project(plan, encoded, halves):
    rows, width = encoded.shape
    block = 512
    return pl.pallas_call(
        functools.partial(pool_kernel, plan),
        grid=(rows // block,),
        in_specs=[SCALAR, pl.BlockSpec((block, width), lambda i: (i, 0)), ANYWHERE, ANYWHERE],
        out_specs=pl.BlockSpec((block, 2 * width), lambda i: (i, 0)),
        out_shape=jax.ShapeDtypeStruct((rows, 2 * width), BF16),
        scratch_shapes=[pltpu.VMEM((width, 2 * width), BF16), copy_sems(plan)],
        compiler_params=params(40),
        cost_estimate=cost(13),
        name="pool_project",
    )(plan.odd_word, encoded, *halves)


def project_kernel(
    plan,
    odd_ref,
    tokens_ref,
    held_ref,
    other_ref,
    first_in_ref,
    projected_ref,
    vectors_ref,
    weight,
    pack,
    sems,
):
    width = tokens_ref.shape[1]

    @pl.when(pl.program_id(0) == 0)
    def _():
        copies = column_copies(plan, odd_ref[0], held_ref, other_ref, weight, sems.at[0], 0, 3 * width)
        copies += column_copies(
            plan, odd_ref[0], held_ref, other_ref, pack, sems.at[1], 3 * width, LANES
        )
        start_all(copies)
        wait_all(copies)
        vectors_ref[...] = pack[...].astype(F32).T[:8]

    unit = norm_parts(tokens_ref[...].astype(F32))[0]
    first_in = (unit * vectors_ref[0:1] + vectors_ref[1:2]).astype(BF16)
    first_in_ref[...] = first_in
    projected_ref[...] = dot(first_in, weight[...]).astype(BF16)


def project(plan, tokens, halves):
    rows, width = tokens.shape
    return pl.pallas_call(
        functools.partial(project_kernel, plan),
        grid=(rows // ROWS,),
        in_specs=[SCALAR, row_block(width), ANYWHERE, ANYWHERE],
        out_specs=[
            row_block(width),
            row_block(3 * width),
            pl.BlockSpec((8, width), lambda i: (0, 0)),
        ],
        out_shape=[
            jax.ShapeDtypeStruct((rows, width), BF16),
            jax.ShapeDtypeStruct((rows, 3 * width), BF16),
            jax.ShapeDtypeStruct((8, width), F32),
        ],
        scratch_shapes=[
            pltpu.VMEM((width, 3 * width), BF16),
            pltpu.VMEM((width, LANES), BF16),
            copy_sems(plan, 2),
        ],
        compiler_params=params(40),
        cost_estimate=cost(6),
        name="project",
    )(plan.odd_word, tokens, *halves)


def middle_kernel(
    plan,
    starts,
    odd_ref,
    tokens_ref,
    mixed_ref,
    vectors_ref,
    held_ref,
    other_ref,
    after_ref,
    second_in_ref,
    queries_ref,
    out_weight,
    query_weight,
    sems,
):
    width = tokens_ref.shape[1]

    @pl.when(pl.program_id(0) == 0)
    def _():
        copies = []
        for place_at, target in enumerate((out_weight, query_weight)):
            copies += column_copies(
                plan, odd_ref[0], held_ref, other_ref, target, sems.at[place_at], starts[place_at], width
            )
        start_all(copies)
        wait_all(copies)

    after = tokens_ref[...].astype(F32) + dot(mixed_ref[...], out_weight[...])
    after_ref[...] = after
    unit = norm_parts(after)[0]
    second_in = (unit * vectors_ref[2:3] + vectors_ref[3:4]).astype(BF16)
    second_in_ref[...] = second_in
    queries_ref[...] = dot(second_in, query_weight[...]).astype(BF16)


def middle(plan, starts, tokens, mixed, vectors, halves):
    rows, width = tokens.shape
    return pl.pallas_call(
        functools.partial(middle_kernel, plan, starts),
        grid=(rows // ROWS,),
        in_specs=[
            SCALAR,
            row_block(width),
            row_block(width),
            pl.BlockSpec((8, width), lambda i: (0, 0)),
            ANYWHERE,
            ANYWHERE,
        ],
        out_specs=[row_block(width)] * 3,
        out_shape=[
            jax.ShapeDtypeStruct((rows, width), F32),
            jax.ShapeDtypeStruct((rows, width), BF16),
            jax.ShapeDtypeStruct((rows, width), BF16),
        ],
        scratch_shapes=[
            pltpu.VMEM((width, width), BF16),
            pltpu.VMEM((width, width), BF16),
            copy_sems(plan, 2),
        ],
        compiler_params=params(40),
        cost_estimate=cost(6),
        name="middle",
    )(plan.odd_word, tokens, mixed, vectors, *halves)


GELU_SCALE = 0.7978845608028654
GELU_CUBE = 0.044715


def gelu_both(values):
    square = values * values
    bent = jnp.tanh(values * (GELU_SCALE + (GELU_SCALE * GELU_CUBE) * square))
    half = 0.5 + 0.5 * bent
    slope = GELU_SCALE + (3.0 * GELU_SCALE * GELU_CUBE) * square
    return (values * half, half + (0.5 * values) * (1.0 - bent * bent) * slope)


def feed_kernel(
    plan,
    out_start,
    row_steps,
    odd_ref,
    after_ref,
    mixed_ref,
    cotangent_ref,
    vectors_ref,
    up_held_ref,
    up_other_ref,
    down_held_ref,
    down_other_ref,
    held_ref,
    other_ref,
    block_ref,
    grad_ref,
    mixed_grad_ref,
    terms_ref,
    keep_ref,
    send_ref,
    weights,
    lefts,
    rights,
    sems,
):
    step = pl.program_id(0)
    width = after_ref.shape[1]
    parts = (weights.shape[0] - 1) // 2

    def copies(index):
        if index == 2 * parts:
            return column_copies(
                plan, odd_ref[0], held_ref, other_ref, weights.at[index], sems.at[index], out_start, width
            )
        is_up = index < parts
        return column_copies(
            plan,
            odd_ref[0],
            up_held_ref if is_up else down_held_ref,
            up_other_ref if is_up else down_other_ref,
            weights.at[index],
            sems.at[index],
            (index if is_up else index - parts) * width,
            width,
        )

    @pl.when(step == 0)
    def _():
        order = [2 * parts]
        for part in range(parts):
            order += [part, parts + part]
        for index in order:
            start_all(copies(index))

    def ready(index):
        @pl.when(step == 0)
        def _():
            wait_all(copies(index))

        return weights[index]

    @pl.when(step < row_steps)
    def _():
        place_at = pl.ds(pl.multiple_of(step * ROWS, ROWS), ROWS)
        mixed = mixed_ref[...]
        cotangent = cotangent_ref[...]
        out_weight = ready(2 * parts)
        after_cross = after_ref[...] + dot(mixed, out_weight)
        unit, inverse = norm_parts(after_cross)
        gain = vectors_ref[4:5]
        third_in = (unit * gain + vectors_ref[5:6]).astype(BF16)
        lefts[parts, :, place_at] = third_in.T
        lefts[parts + 1, :, place_at] = mixed.T
        rights[0, place_at] = cotangent
        result = after_cross
        upstream = jnp.zeros_like(after_cross)
        for part in range(parts):
            up = ready(part)
            hidden, slope = gelu_both(dot(third_in, up))
            hidden = hidden.astype(BF16)
            lefts[part, :, place_at] = hidden.T
            down = ready(parts + part)
            result = result + dot(hidden, down)
            hidden_grad = (slope * dot(cotangent, down, NT)).astype(BF16)
            rights[1 + part, place_at] = hidden_grad
            upstream = upstream + dot(hidden_grad, up, NT)
        block_ref[...] = result.astype(BF16)
        inner = upstream * gain
        mean_inner = jnp.mean(inner, axis=-1, keepdims=True)
        mean_both = jnp.mean(inner * unit, axis=-1, keepdims=True)
        grad = cotangent.astype(F32) + inverse * (inner - mean_inner - unit * mean_both)
        add_terms(
            step,
            terms_ref,
            jnp.sum(upstream * unit, axis=0, keepdims=True),
            jnp.sum(upstream, axis=0, keepdims=True),
        )
        grad_ref[...] = grad
        rounded = grad.astype(BF16)
        rights[parts + 1, place_at] = rounded
        mixed_grad_ref[...] = dot(rounded, out_weight, NT).astype(BF16)

    @pl.when(step >= row_steps)
    def _():
        term = step - row_steps
        left = jnp.where(term < parts, term, jnp.where(term < 2 * parts, parts, parts + 1))
        right = jnp.where(term < parts, 0, term - parts + 1)
        result = dot(lefts[left], rights[right]).astype(BF16)
        store_halves(plan, odd_ref[0], result, keep_ref, send_ref, slice(0, width))


def feed(plan, out_start, after, mixed, cotangent, vectors, up_halves, down_halves, halves):
    rows, width = after.shape
    parts = up_halves[0].shape[1] // width
    terms = 2 * parts + 1
    steps = rows // ROWS
    last = steps - 1
    rows_in = row_block(width, last)
    whole = pl.BlockSpec((8, width), lambda i: (0, 0))
    slab = pl.BlockSpec((plan.half_rows, width), lambda i: (0, jnp.maximum(i - steps, 0)))
    slab_shape = jax.ShapeDtypeStruct((plan.half_rows, terms * width), BF16)
    return pl.pallas_call(
        functools.partial(feed_kernel, plan, out_start, steps),
        grid=(steps + terms,),
        in_specs=[SCALAR, rows_in, rows_in, rows_in, whole] + [ANYWHERE] * 6,
        out_specs=[rows_in, rows_in, rows_in, whole, slab, slab],
        out_shape=[
            jax.ShapeDtypeStruct((rows, width), BF16),
            jax.ShapeDtypeStruct((rows, width), F32),
            jax.ShapeDtypeStruct((rows, width), BF16),
            jax.ShapeDtypeStruct((8, width), F32),
            slab_shape,
            slab_shape,
        ],
        scratch_shapes=[
            pltpu.VMEM((terms, width, width), BF16),
            pltpu.VMEM((parts + 2, width, rows), BF16),
            pltpu.VMEM((parts + 2, rows, width), BF16),
            copy_sems(plan, terms),
        ],
        compiler_params=params(60),
        cost_estimate=cost(58),
        name="feed_forward",
    )(plan.odd_word, after, mixed, cotangent, vectors, *up_halves, *down_halves, *halves)


def second_kernel(
    plan,
    starts,
    row_steps,
    odd_ref,
    after_ref,
    grad_in_ref,
    query_grad_ref,
    second_in_ref,
    mixed_ref,
    vectors_ref,
    held_ref,
    other_ref,
    grad_ref,
    attend_ref,
    terms_ref,
    keep_ref,
    send_ref,
    out_weight,
    query_weight,
    lefts,
    rights,
    sems,
):
    step = pl.program_id(0)
    width = after_ref.shape[1]

    @pl.when(step == 0)
    def _():
        copies = []
        for place_at, target in enumerate((out_weight, query_weight)):
            copies += column_copies(
                plan, odd_ref[0], held_ref, other_ref, target, sems.at[place_at], starts[place_at], width
            )
        start_all(copies)
        wait_all(copies)

    @pl.when(step < row_steps)
    def _():
        place_at = pl.ds(pl.multiple_of(step * ROWS, ROWS), ROWS)
        query_grad = query_grad_ref[...]
        back, gain_term, shift_term = norm_back(
            after_ref[...], vectors_ref[2:3], dot(query_grad, query_weight[...], NT)
        )
        add_terms(step, terms_ref, gain_term, shift_term)
        grad = grad_in_ref[...] + back
        grad_ref[...] = grad
        rounded = grad.astype(BF16)
        attend_ref[...] = dot(rounded, out_weight[...], NT).astype(BF16)
        lefts[0, :, place_at] = second_in_ref[...].T
        lefts[1, :, place_at] = mixed_ref[...].T
        rights[0, place_at] = query_grad
        rights[1, place_at] = rounded

    @pl.when(step >= row_steps)
    def _():
        term = step - row_steps
        result = dot(lefts[term], rights[term]).astype(BF16)
        store_halves(plan, odd_ref[0], result, keep_ref, send_ref, slice(0, width))


def second_back(plan, starts, after, grad_in, query_grad, second_in, mixed, vectors, halves):
    rows, width = after.shape
    steps = rows // ROWS
    rows_in = row_block(width, steps - 1)
    whole = pl.BlockSpec((8, width), lambda i: (0, 0))
    slab = pl.BlockSpec((plan.half_rows, width), lambda i: (0, jnp.maximum(i - steps, 0)))
    slab_shape = jax.ShapeDtypeStruct((plan.half_rows, 2 * width), BF16)
    return pl.pallas_call(
        functools.partial(second_kernel, plan, starts, steps),
        grid=(steps + 2,),
        in_specs=[SCALAR] + [rows_in] * 5 + [whole, ANYWHERE, ANYWHERE],
        out_specs=[rows_in, rows_in, whole, slab, slab],
        out_shape=[
            jax.ShapeDtypeStruct((rows, width), F32),
            jax.ShapeDtypeStruct((rows, width), BF16),
            jax.ShapeDtypeStruct((8, width), F32),
            slab_shape,
            slab_shape,
        ],
        scratch_shapes=[
            pltpu.VMEM((width, width), BF16),
            pltpu.VMEM((width, width), BF16),
            pltpu.VMEM((2, width, rows), BF16),
            pltpu.VMEM((2, rows, width), BF16),
            copy_sems(plan, 2),
        ],
        compiler_params=params(48),
        cost_estimate=cost(14),
        name="second_back",
    )(plan.odd_word, after, grad_in, query_grad, second_in, mixed, vectors, *halves)


def first_kernel(
    plan,
    row_steps,
    odd_ref,
    tokens_ref,
    grad_in_ref,
    projected_grad_ref,
    first_in_ref,
    vectors_ref,
    second_terms_ref,
    third_terms_ref,
    held_ref,
    other_ref,
    grad_ref,
    keep_ref,
    send_ref,
    weight,
    terms,
    left,
    rights,
    sems,
):
    step = pl.program_id(0)
    width = tokens_ref.shape[1]

    @pl.when(step == 0)
    def _():
        copies = column_copies(plan, odd_ref[0], held_ref, other_ref, weight, sems, 0, 3 * width)
        start_all(copies)
        wait_all(copies)

    place_at = pl.ds(pl.multiple_of(step * ROWS, ROWS), ROWS)
    upstream = None
    for part in range(3):
        grads = projected_grad_ref[part]
        rights[part, place_at] = grads
        product = dot(grads, weight[:, part * width : (part + 1) * width], NT)
        upstream = product if upstream is None else upstream + product
    back, gain_term, shift_term = norm_back(
        tokens_ref[...].astype(F32), vectors_ref[0:1], upstream
    )
    add_terms(step, terms, gain_term, shift_term)
    grad_ref[...] = grad_in_ref[...] + back
    left[:, place_at] = first_in_ref[...].T

    @pl.when(step == row_steps - 1)
    def _():
        for part in range(3):
            result = dot(left[...], rights[part]).astype(BF16)
            columns = slice(part * width, (part + 1) * width)
            store_halves(plan, odd_ref[0], result, keep_ref, send_ref, columns)
        rows = jnp.concatenate(
            [
                terms[0:2],
                second_terms_ref[0:2],
                third_terms_ref[0:2],
                jnp.zeros((LANES - 6, width), F32),
            ],
            axis=0,
        )
        columns = slice(3 * width, 3 * width + LANES)
        store_halves(plan, odd_ref[0], rows.T.astype(BF16), keep_ref, send_ref, columns)


def first_back(
    plan, tokens, grad_in, projected_grad, first_in, vectors, second_terms, third_terms, halves
):
    rows, width = tokens.shape
    steps = rows // ROWS
    rows_in = row_block(width)
    whole = pl.BlockSpec((8, width), lambda i: (0, 0))
    columns = 3 * width + LANES
    slab = pl.BlockSpec((plan.half_rows, columns), lambda i: (0, 0))
    slab_shape = jax.ShapeDtypeStruct((plan.half_rows, columns), BF16)
    return pl.pallas_call(
        functools.partial(first_kernel, plan, steps),
        grid=(steps,),
        in_specs=[
            SCALAR,
            rows_in,
            rows_in,
            pl.BlockSpec((3, ROWS, width), lambda i: (0, i, 0)),
            rows_in,
            whole,
            whole,
            whole,
            ANYWHERE,
            ANYWHERE,
        ],
        out_specs=[rows_in, slab, slab],
        out_shape=[jax.ShapeDtypeStruct((rows, width), F32), slab_shape, slab_shape],
        scratch_shapes=[
            pltpu.VMEM((width, 3 * width), BF16),
            pltpu.VMEM((8, width), F32),
            pltpu.VMEM((width, rows), BF16),
            pltpu.VMEM((3, rows, width), BF16),
            copy_sems(plan),
        ],
        compiler_params=params(56),
        cost_estimate=cost(18),
        name="first_back",
    )(
        plan.odd_word,
        tokens,
        grad_in,
        projected_grad,
        first_in,
        vectors,
        second_terms,
        third_terms,
        *halves,
    )


def keyval_kernel(
    plan, odd_ref, rows_ref, key_ref, value_ref, keep_ref, send_ref, key_total, value_total
):
    step = pl.program_id(0)
    width = rows_ref.shape[1]
    turned = rows_ref[...].T
    key_part = dot(turned, key_ref[...])
    value_part = dot(turned, value_ref[...])

    @pl.when(step == 0)
    def _():
        key_total[...] = key_part
        value_total[...] = value_part

    @pl.when(step > 0)
    def _():
        key_total[...] += key_part
        value_total[...] += value_part

    @pl.when(step == pl.num_programs(0) - 1)
    def _():
        for place_at, total in enumerate((key_total, value_total)):
            columns = slice(place_at * width, (place_at + 1) * width)
            store_halves(plan, odd_ref[0], total[...].astype(BF16), keep_ref, send_ref, columns)


def keyval_terms(plan, encoded, pool_keys, pool_values):
    rows, width = encoded.shape
    block = 1024
    rows_in = pl.BlockSpec((block, width), lambda i: (i, 0))
    slab = pl.BlockSpec((plan.half_rows, 2 * width), lambda i: (0, 0))
    slab_shape = jax.ShapeDtypeStruct((plan.half_rows, 2 * width), BF16)
    return pl.pallas_call(
        functools.partial(keyval_kernel, plan),
        grid=(rows // block,),
        in_specs=[SCALAR, rows_in, rows_in, rows_in],
        out_specs=[slab, slab],
        out_shape=[slab_shape, slab_shape],
        scratch_shapes=[pltpu.VMEM((width, width), F32), pltpu.VMEM((width, width), F32)],
        compiler_params=params(48),
        cost_estimate=cost(15),
        name="keyval_terms",
    )(plan.odd_word, encoded, pool_keys, pool_values)


def neighbours_kernel(
    plan, odd_ref, key_ref, value_ref, held_ref, other_ref, out_ref, weight, sems
):
    width = key_ref.shape[1]

    @pl.when(pl.program_id(0) == 0)
    def _():
        copies = column_copies(plan, odd_ref[0], held_ref, other_ref, weight, sems, 0, 2 * width)
        start_all(copies)
        wait_all(copies)

    out_ref[...] = dot(key_ref[...], weight[:, :width], NT) + dot(
        value_ref[...], weight[:, width:], NT
    )


def neighbours_back(plan, pool_keys, pool_values, halves, first, count, earlier):
    rows, width = pool_keys.shape
    block = 512
    rows_in = pl.BlockSpec((block, width), lambda i: (i + first, 0))
    given = [] if earlier is None else [earlier]
    return pl.pallas_call(
        functools.partial(passing, functools.partial(neighbours_kernel, plan), 5, len(given)),
        grid=(count,),
        in_specs=[SCALAR, rows_in, rows_in, ANYWHERE, ANYWHERE] + [ANYWHERE] * len(given),
        out_specs=rows_in,
        out_shape=jax.ShapeDtypeStruct((rows, width), F32),
        scratch_shapes=[pltpu.VMEM((width, 2 * width), BF16), copy_sems(plan)],
        input_output_aliases={5: 0} if given else {},
        compiler_params=params(40),
        cost_estimate=cost(15),
        name="neighbours_back",
    )(plan.odd_word, pool_keys, pool_values, *halves, *given)

def local(
    tokens,
    lengths,
    neighbours,
    neighbour_ids,
    neighbour_lengths,
    first_gain,
    first_shift,
    self_input,
    self_output,
    second_gain,
    second_shift,
    cross_query,
    cross_keyval,
    cross_output,
    third_gain,
    third_shift,
    feed_up,
    feed_down,
    cotangent,
):
    rows, width = cross_query.shape
    line = Line()
    plan = Plan(rows, line)
    steps = len(plan.steps)
    parts = feed_down.shape[0] // rows
    pool_count, neigh_len = neighbours.shape[:2]
    vectors = (first_gain, first_shift, second_gain, second_shift, third_gain, third_shift)
    vector_pack = jnp.pad(jnp.stack(vectors, axis=1), ((0, 0), (0, LANES - len(vectors))))
    up_shard = feed_up.reshape(rows, plan.count, parts, rows).swapaxes(1, 2).reshape(feed_up.shape)
    down_shard = feed_down.reshape(parts, rows, width).swapaxes(0, 1).reshape(rows, parts * width)
    rows_in = tokens[0]
    encoded = neighbours.reshape(pool_count * neigh_len, width)
    ids = neighbour_ids.reshape(-1)

    def advance(*chunks):
        for chunk in chunks:
            chunk.step()

    def run(kernel, first, *rest):
        results = kernel(line.after(first), *rest)
        line.note(results[0] if isinstance(results, (tuple, list)) else results)
        return results

    keyval = Gather(plan, cross_keyval)
    start = Gather(plan, jnp.concatenate([self_input, vector_pack], axis=1))
    middle_part = Gather(plan, jnp.concatenate([self_output, cross_query, cross_output], axis=1))
    up = Gather(plan, up_shard)
    down = Gather(plan, down_shard)

    keyval.launch()
    start.launch()
    advance(keyval)
    advance(keyval, start)
    middle_part.launch()
    up.launch()
    down.launch()
    advance(keyval, start)
    advance(keyval, start, middle_part)
    advance(start, middle_part, up)
    keyval_halves = keyval.finish()
    pool_keyval = run(functools.partial(pool_project, plan), encoded, keyval_halves)
    pool_keyval = pool_keyval.reshape(pool_count, neigh_len, 2 * width)
    start_halves = start.finish()
    advance(middle_part, up, down)
    first_in, projected, vector_rows = run(
        lambda values: project(plan, values, start_halves), rows_in
    )
    advance(middle_part, up, down)
    self_mixed, self_exact, logsum = run(self_forward, projected, lengths)
    middle_halves = middle_part.finish()
    advance(up, down)
    after_self, second_in, cross_queries = run(
        lambda values: middle(plan, (0, width), rows_in, values, vector_rows, middle_halves),
        self_mixed,
    )
    up_halves = up.finish()
    cross_mixed = run(cross_forward, cross_queries, pool_keyval, ids, neighbour_lengths)
    down_halves = down.finish()
    block_out, after_cross_grad, mixed_grad, third_terms, feed_keep, feed_send = run(
        lambda values: feed(
            plan,
            2 * width,
            after_self,
            values,
            cotangent[0],
            vector_rows,
            up_halves,
            down_halves,
            middle_halves,
        ),
        cross_mixed,
    )
    feed_sum = Scatter(plan, feed_keep, feed_send)
    feed_sum.launch()

    crossed = None
    for group in range(width // WIDE):
        crossed = run(
            cross_backward,
            cross_queries,
            mixed_grad,
            pool_keyval,
            ids,
            neighbour_lengths,
            group,
            crossed,
        )
        if group == 0:
            advance(feed_sum)
    advance(feed_sum)
    query_grad, pool_keys, pool_values = crossed
    pool_keys = pool_keys.reshape(pool_count * neigh_len, width)
    pool_values = pool_values.reshape(pool_count * neigh_len, width)
    keyval_keep, keyval_send = run(
        lambda values: keyval_terms(plan, encoded, values, pool_values), pool_keys
    )
    advance(feed_sum)
    after_self_grad, attend_grad, second_terms, second_keep, second_send = run(
        lambda values: second_back(
            plan,
            (0, width),
            after_self,
            after_cross_grad,
            values,
            second_in,
            self_mixed,
            vector_rows,
            middle_halves,
        ),
        query_grad,
    )
    middle_sum = Scatter(
        plan,
        jnp.concatenate([keyval_keep, second_keep], axis=1),
        jnp.concatenate([keyval_send, second_send], axis=1),
    )
    middle_sum.launch()
    pairs = width // LANES
    projected_grad = None
    for turn in range(2):
        projected_grad = run(
            lambda values: self_backward(
                projected,
                lengths,
                values,
                self_exact,
                logsum,
                turn * (pairs // 2),
                pairs // 2,
                projected_grad,
            ),
            attend_grad,
        )
        advance(middle_sum, feed_sum)
    tokens_grad, first_keep, first_send = run(
        lambda values: first_back(
            plan,
            rows_in,
            after_self_grad,
            values,
            first_in,
            vector_rows,
            second_terms,
            third_terms,
            start_halves,
        ),
        projected_grad,
    )
    first_sum = Scatter(plan, first_keep, first_send)
    first_sum.launch()
    advance(middle_sum)
    blocks = pool_keys.shape[0] // 512
    neighbours_grad = None
    for turn in range(2):
        advance(first_sum)
        neighbours_grad = run(
            lambda values: neighbours_back(
                plan,
                values,
                pool_values,
                keyval_halves,
                turn * (blocks // 2),
                blocks // 2,
                neighbours_grad,
            ),
            pool_keys,
        )
        advance(middle_sum)
    feed_total = feed_sum.finish()
    middle_total = middle_sum.finish()
    first_total = first_sum.finish()

    down_grad = feed_total[:, : parts * width].reshape(rows, parts, width).swapaxes(0, 1)
    up_grad = feed_total[:, parts * width : 2 * parts * width]
    up_grad = up_grad.reshape(rows, parts, plan.count, rows).swapaxes(1, 2)
    vector_grads = [first_total[:, 3 * width + i] for i in range(len(vectors))]
    return (
        block_out[None],
        tokens_grad[None],
        neighbours_grad.reshape(neighbours.shape),
        vector_grads[0],
        vector_grads[1],
        first_total[:, : 3 * width],
        middle_total[:, 3 * width :],
        vector_grads[2],
        vector_grads[3],
        middle_total[:, 2 * width : 3 * width],
        middle_total[:, : 2 * width],
        feed_total[:, 2 * parts * width :],
        vector_grads[4],
        vector_grads[5],
        up_grad.reshape(feed_up.shape),
        down_grad.reshape(feed_down.shape),
    )


def solution(mesh):
    placed = (
        P(("fsdp", "dp"), None, None),
        P(("fsdp", "dp")),
        P(("fsdp", "dp"), None, None),
        P(("fsdp", "dp"), None, None),
        P(("fsdp", "dp")),
        P(("fsdp", "dp")),
        P(("fsdp", "dp")),
        P(("fsdp", "dp"), None),
        P(("fsdp", "dp"), None),
        P(("fsdp", "dp")),
        P(("fsdp", "dp")),
        P(("fsdp", "dp"), None),
        P(("fsdp", "dp"), None),
        P(("fsdp", "dp"), None),
        P(("fsdp", "dp")),
        P(("fsdp", "dp")),
        P(("fsdp", "dp"), None),
        P(("fsdp", "dp"), None),
        P(("fsdp", "dp"), None, None),
    )
    return jax.shard_map(
        local,
        mesh=mesh,
        in_specs=placed,
        out_specs=(
            P(("fsdp", "dp"), None, None),
            P(("fsdp", "dp"), None, None),
            P(("fsdp", "dp"), None, None),
            P(("fsdp", "dp")),
            P(("fsdp", "dp")),
            P(("fsdp", "dp"), None),
            P(("fsdp", "dp"), None),
            P(("fsdp", "dp")),
            P(("fsdp", "dp")),
            P(("fsdp", "dp"), None),
            P(("fsdp", "dp"), None),
            P(("fsdp", "dp"), None),
            P(("fsdp", "dp")),
            P(("fsdp", "dp")),
            P(("fsdp", "dp"), None),
            P(("fsdp", "dp"), None),
        ),
        check_vma=False,
    )
```

```python
import functools

import jax
import jax.numpy as jnp
from jax import lax
from jax.experimental import pallas as pl
from jax.experimental.pallas import tpu as pltpu
from jax.sharding import PartitionSpec as P

HEADS = 12
SPAN = 64
NEIGH = 2
LANES = 128
WIDE = 256
QBLOCK = 256

EPSILON = 1e-05
SCALE = 0.125
NEGATIVE = -1e30
BF16 = jnp.bfloat16
F32 = jnp.float32
NT = (((1,), (1,)), ((), ()))
NN = (((1,), (0,)), ((), ()))
TN = (((0,), (0,)), ((), ()))


def dot(left, right, dims=NN):
    return lax.dot_general(left, right, dims, preferred_element_type=F32)


def iota(shape, axis):
    return lax.broadcasted_iota(jnp.int32, shape, axis)


def cost(microseconds):
    return pl.CostEstimate(
        flops=int(microseconds * 1100000000.0), bytes_accessed=0, transcendentals=0
    )


def passing(kernel, before, given, *refs):
    return kernel(*refs[:before], *refs[before + given :])


def split_three(values):
    high = values.astype(BF16)
    rest = values - high.astype(F32)
    middle = rest.astype(BF16)
    low = (rest - middle.astype(F32)).astype(BF16)
    return (high, middle, low)


def self_forward_kernel(length_ref, query_ref, key_ref, value_ref, mixed_ref, exact_ref, logsum_ref):
    seq_len = query_ref.shape[0]
    length = length_ref[0]
    lane = iota((1, LANES), 1)
    first = lane < 64
    padded = jnp.where(iota((seq_len, 1), 0) < length, 0.0, NEGATIVE).astype(BF16)
    keys = key_ref[...]
    values = value_ref[...]
    one = jnp.ones((), BF16)
    keys_by_head = (
        jnp.where(first, keys, jnp.where(lane == 64, padded, 0)),
        jnp.where(first, jnp.where(lane == 0, padded, 0), keys),
    )
    values_by_head = (jnp.where(first, values, one), jnp.where(first, one, values))
    causal = iota((QBLOCK, QBLOCK), 1) <= iota((QBLOCK, QBLOCK), 0)

    def scores(block, head):
        start = block * QBLOCK
        query = query_ref[start : start + QBLOCK] * jnp.asarray(SCALE, BF16)
        if head == 0:
            query = jnp.where(first, query, jnp.where(lane == 64, one, 0))
        else:
            query = jnp.where(first, jnp.where(lane == 0, one, 0), query)
        diagonal = dot(query, keys_by_head[head][start : start + QBLOCK], NT)
        before = dot(query, keys_by_head[head][:start], NT) if block else None
        return (jnp.where(causal, diagonal, NEGATIVE), before)

    units = [(block, head) for block in reversed(range(seq_len // QBLOCK)) for head in range(2)]
    ahead = [scores(*unit) for unit in units[:AHEAD]]
    outs = []
    tops = []
    for place_at, (block, head) in enumerate(units):
        if place_at + AHEAD < len(units):
            ahead.append(scores(*units[place_at + AHEAD]))
        start = block * QBLOCK
        diagonal, before = ahead.pop(0)
        top = jnp.max(diagonal, axis=-1, keepdims=True)
        if block:
            top = jnp.maximum(top, jnp.max(before, axis=-1, keepdims=True))
        out = dot(
            jnp.exp(diagonal - top).astype(BF16), values_by_head[head][start : start + QBLOCK]
        )
        if block:
            out = out + dot(jnp.exp(before - top).astype(BF16), values_by_head[head][:start])
        outs.append(out)
        tops.append(top)
        if head == 0:
            continue
        total = pltpu.roll(jnp.where(first, outs[1], outs[0]), 64, 1)
        mixed = jnp.where(first, outs[0], outs[1]) / total
        mixed_ref[start : start + QBLOCK] = mixed.astype(BF16)
        exact_ref[start : start + QBLOCK] = mixed
        logsum = (jnp.where(first, tops[0], tops[1]) + jnp.log(total)).T
        logsum_ref[0, 0:1, start : start + QBLOCK] = logsum[0:1]
        logsum_ref[0, 1:2, start : start + QBLOCK] = logsum[64:65]
        outs = []
        tops = []


def self_forward(projected, lengths, first, count, earlier):
    seq_len = projected.shape[0]
    width = projected.shape[1] // 3
    pairs = width // LANES
    column = lambda offset: pl.BlockSpec((seq_len, LANES), lambda p: (0, p + offset))
    given = [] if earlier is None else list(earlier)
    return pl.pallas_call(
        functools.partial(passing, self_forward_kernel, 4, len(given)),
        grid=(count,),
        in_specs=[
            pl.BlockSpec(memory_space=pltpu.SMEM),
            column(first),
            column(pairs + first),
            column(2 * pairs + first),
        ]
        + [pl.BlockSpec(memory_space=pl.ANY)] * len(given),
        out_specs=[
            column(first),
            column(first),
            pl.BlockSpec((1, 8, seq_len), lambda p: (p + first, 0, 0)),
        ],
        out_shape=[
            jax.ShapeDtypeStruct((seq_len, width), BF16),
            jax.ShapeDtypeStruct((seq_len, width), F32),
            jax.ShapeDtypeStruct((pairs, 8, seq_len), F32),
        ],
        input_output_aliases={4 + i: i for i in range(len(given))},
        compiler_params=pltpu.CompilerParams(vmem_limit_bytes=48 * 2**20),
        cost_estimate=cost(8),
        name="self_forward",
    )(lengths, projected, projected, projected, *given)


AHEAD = 1
AHEAD_BACK = 2
AHEAD_CROSS = 2
SPANS_STEP = 8


def self_backward_kernel(
    length_ref,
    query_ref,
    key_ref,
    value_ref,
    grad_ref,
    exact_ref,
    logsum_ref,
    out_ref,
    key_grad_ref,
    value_grad_ref,
):
    seq_len = query_ref.shape[0]
    length = length_ref[0]
    lane = iota((1, LANES), 1)
    first = lane < 64
    row = iota((LANES, 1), 0)
    top_rows = row < 64
    padded = jnp.where(iota((seq_len, 1), 0) < length, 0.0, NEGATIVE).astype(BF16)
    keys = key_ref[...]
    values = value_ref[...]
    zero = jnp.zeros((), BF16)
    minus = -jnp.ones((), BF16)

    def beside(offset, head_lane):
        kept = (lane > head_lane) & (lane < head_lane + 4)
        return jnp.where(lane == head_lane, offset, jnp.where(kept, minus, zero))

    keys_by_head = (
        jnp.where(first, keys, beside(padded, 64)),
        jnp.where(first, beside(padded, 0), keys),
    )
    values_by_head = (
        jnp.where(first, values, beside(zero, 64)),
        jnp.where(first, beside(zero, 0), values),
    )
    keys_turned = keys.T
    turned_by_head = (
        jnp.where(top_rows, keys_turned, zero),
        jnp.where(top_rows, zero, keys_turned),
    )
    causal = iota((QBLOCK, QBLOCK), 0) <= iota((QBLOCK, QBLOCK), 1)

    def fill(turned, head, lead, parts):
        base = 64 if head == 0 else 0
        other = jnp.where(row == base, lead, zero)
        for place, part in enumerate(parts):
            other = jnp.where(row == base + 1 + place, part, other)
        own = top_rows if head == 0 else ~top_rows
        return jnp.where(own, turned, other)

    count = seq_len // QBLOCK
    units = [(block, head) for block in reversed(range(count)) for head in range(2)]
    loaded = {}

    def load(block):
        start = block * QBLOCK
        stop = start + QBLOCK
        query = query_ref[start:stop] * jnp.asarray(SCALE, BF16)
        grad = grad_ref[start:stop]
        weighted = (grad.astype(F32) * exact_ref[start:stop]).T
        return (query, grad, query.T, grad.T, weighted)

    def products(block, head):
        if head == 0:
            loaded[block] = load(block)
        _, _, query_turned, grad_turned, weighted = loaded[block]
        start = block * QBLOCK
        stop = start + QBLOCK
        delta = jnp.sum(weighted[head * 64 : head * 64 + 64], axis=0, keepdims=True)
        logsum = logsum_ref[0, head : head + 1, start:stop]
        score = dot(
            keys_by_head[head][:stop],
            fill(query_turned, head, jnp.ones((), BF16), split_three(logsum)),
        )
        centred = dot(
            values_by_head[head][:stop], fill(grad_turned, head, zero, split_three(delta))
        )
        return (score, centred)

    ahead = [products(*unit) for unit in units[:AHEAD_BACK]]
    probs_all = []
    scores_all = []
    query_grad = None
    for place_at, (block, head) in enumerate(units):
        if place_at + AHEAD_BACK < len(units):
            ahead.append(products(*units[place_at + AHEAD_BACK]))
        start = block * QBLOCK
        stop = start + QBLOCK
        score, centred = ahead.pop(0)
        prob = jnp.exp(score)
        last = jnp.where(causal, prob[start:], 0.0)
        prob = jnp.concatenate([prob[:start], last], axis=0) if block else last
        score_grad = (prob * centred).astype(BF16)
        scores_all.append(score_grad)
        probs_all.append(prob.astype(BF16))
        part = dot(turned_by_head[head][:, :stop], score_grad)
        query_grad = part if query_grad is None else query_grad + part
        if head == 0:
            continue
        query, grad = loaded[block][:2]
        out_ref[0, start:stop] = (query_grad.T * SCALE).astype(BF16)
        own_query = jnp.concatenate(
            [jnp.where(first, query, zero), jnp.where(first, zero, query)], axis=0
        )
        own_grad = jnp.concatenate(
            [jnp.where(first, grad, zero), jnp.where(first, zero, grad)], axis=0
        )
        key_part = dot(jnp.concatenate(scores_all, axis=1), own_query)
        value_part = dot(jnp.concatenate(probs_all, axis=1), own_grad)
        if block == count - 1:
            key_grad_ref[...] = key_part
            value_grad_ref[...] = value_part
        else:
            key_grad_ref[:stop] += key_part
            value_grad_ref[:stop] += value_part
        probs_all = []
        scores_all = []
        query_grad = None
    out_ref[1] = key_grad_ref[...].astype(BF16)
    out_ref[2] = value_grad_ref[...].astype(BF16)


def self_backward(projected, lengths, grad, exact, logsum, first, count, earlier):
    seq_len = projected.shape[0]
    width = projected.shape[1] // 3
    pairs = width // LANES
    column = lambda offset: pl.BlockSpec((seq_len, LANES), lambda p: (0, p + offset))
    given = [] if earlier is None else [earlier]
    return pl.pallas_call(
        functools.partial(passing, self_backward_kernel, 7, len(given)),
        grid=(count,),
        in_specs=[
            pl.BlockSpec(memory_space=pltpu.SMEM),
            column(first),
            column(pairs + first),
            column(2 * pairs + first),
            column(first),
            column(first),
            pl.BlockSpec((1, 8, seq_len), lambda p: (p + first, 0, 0)),
        ]
        + [pl.BlockSpec(memory_space=pl.ANY)] * len(given),
        out_specs=pl.BlockSpec((3, seq_len, LANES), lambda p: (0, 0, p + first)),
        out_shape=jax.ShapeDtypeStruct((3, seq_len, width), BF16),
        scratch_shapes=[pltpu.VMEM((seq_len, LANES), F32), pltpu.VMEM((seq_len, LANES), F32)],
        input_output_aliases={7: 0} if given else {},
        compiler_params=pltpu.CompilerParams(vmem_limit_bytes=48 * 2**20),
        cost_estimate=cost(12),
        name="self_backward",
    )(lengths, projected, projected, projected, grad, exact, logsum, *given)


def block_diagonal(rows):
    lane = iota((1, WIDE), 1)
    return jnp.concatenate(
        [jnp.where((lane >= h * 64) & (lane < h * 64 + 64), rows, 0) for h in range(4)], axis=0
    )


def take_diagonal(stacked):
    lane = iota((1, WIDE), 1)
    result = stacked[:SPAN]
    for h in range(1, 4):
        result = jnp.where(lane >= h * 64, stacked[h * SPAN : (h + 1) * SPAN], result)
    return result


def slot_bias(ids_ref, neighbour_lengths_ref, span, neigh_len, axis):
    shape = (1, NEIGH * neigh_len) if axis else (NEIGH * neigh_len, 1)
    place = iota(shape, axis)
    first = neighbour_lengths_ref[ids_ref[span * NEIGH]]
    second = neighbour_lengths_ref[ids_ref[span * NEIGH + 1]]
    limit = jnp.where(place < neigh_len, first, neigh_len + second)
    return jnp.where(place < limit, 0.0, NEGATIVE)


def cross_forward_kernel(ids_ref, neighbour_lengths_ref, query_ref, *refs):
    slots, mixed_ref = refs[:-1], refs[-1]
    step = pl.program_id(0)
    neigh_len = slots[0].shape[1]
    width = query_ref.shape[1]
    units = [(span, group) for span in range(SPANS_STEP) for group in range(width // WIDE)]

    def scores(span, group):
        rows = slice(span * SPAN, (span + 1) * SPAN)
        place = slice(group * WIDE, (group + 1) * WIDE)
        queries = block_diagonal(query_ref[rows, place] * jnp.asarray(SCALE, BF16))
        keys = jnp.concatenate([ref[0, :, place] for ref in slots[span * NEIGH :][:NEIGH]], axis=0)
        return dot(queries, keys, NT)

    ahead = [scores(*unit) for unit in units[:AHEAD_CROSS]]
    for place_at, (span, group) in enumerate(units):
        if place_at + AHEAD_CROSS < len(units):
            ahead.append(scores(*units[place_at + AHEAD_CROSS]))
        if group == 0:
            bias = slot_bias(
                ids_ref, neighbour_lengths_ref, step * SPANS_STEP + span, neigh_len, 1
            )
        score = ahead.pop(0) + bias
        expo = jnp.exp(score - jnp.max(score, axis=-1, keepdims=True))
        total = jnp.sum(expo, axis=-1, keepdims=True)
        place = slice(width + group * WIDE, width + (group + 1) * WIDE)
        values = jnp.concatenate(
            [ref[0, :, place] for ref in slots[span * NEIGH :][:NEIGH]], axis=0
        )
        out = dot(expo.astype(BF16), values) / total
        rows = slice(span * SPAN, (span + 1) * SPAN)
        mixed_ref[rows, group * WIDE : (group + 1) * WIDE] = take_diagonal(out).astype(BF16)


def cross_forward(queries, pool_keyval, ids, neighbour_lengths):
    seq_len, width = queries.shape
    neigh_len, both = pool_keyval.shape[1:]
    spans = seq_len // SPAN
    slots = SPANS_STEP * NEIGH
    rows = pl.BlockSpec((SPANS_STEP * SPAN, width), lambda c, ids, lens: (c, 0))
    slot = lambda j: pl.BlockSpec(
        (1, neigh_len, both), lambda c, ids, lens: (ids[c * slots + j], 0, 0)
    )
    return pl.pallas_call(
        cross_forward_kernel,
        grid_spec=pltpu.PrefetchScalarGridSpec(
            num_scalar_prefetch=2,
            grid=(spans // SPANS_STEP,),
            in_specs=[rows] + [slot(j) for j in range(slots)],
            out_specs=rows,
        ),
        out_shape=jax.ShapeDtypeStruct((seq_len, width), BF16),
        compiler_params=pltpu.CompilerParams(vmem_limit_bytes=56 * 2**20),
        cost_estimate=cost(12),
        name="cross_forward",
    )(ids, neighbour_lengths, queries, *[pool_keyval] * slots)


def cross_backward_kernel(
    ids_ref,
    neighbour_lengths_ref,
    query_ref,
    grad_ref,
    key_ref,
    value_ref,
    query_grad_ref,
    key_out_ref,
    value_out_ref,
    key_total,
    value_total,
):
    step = pl.program_id(1)
    neigh_len = key_ref.shape[1]

    @pl.when(step == 0)
    def _():
        key_total[...] = jnp.zeros_like(key_total)
        value_total[...] = jnp.zeros_like(value_total)

    def slots_of(span):
        place = (step * SPANS_STEP + span) * NEIGH
        return [ids_ref[place + slot] for slot in range(NEIGH)]

    def products(span):
        rows = slice(span * SPAN, (span + 1) * SPAN)
        queries = block_diagonal(query_ref[rows] * jnp.asarray(SCALE, BF16))
        grads = block_diagonal(grad_ref[rows])
        keys = jnp.concatenate([key_ref[ident] for ident in slots_of(span)], axis=0)
        values = jnp.concatenate([value_ref[ident] for ident in slots_of(span)], axis=0)
        return (queries, grads, keys, dot(keys, queries, NT), dot(values, grads, NT))

    ahead = [products(span) for span in range(AHEAD_CROSS)]
    for span in range(SPANS_STEP):
        if span + AHEAD_CROSS < SPANS_STEP:
            ahead.append(products(span + AHEAD_CROSS))
        queries, grads, keys, score, prob_grad = ahead.pop(0)
        bias = slot_bias(ids_ref, neighbour_lengths_ref, step * SPANS_STEP + span, neigh_len, 0)
        score = score + bias
        expo = jnp.exp(score - jnp.max(score, axis=0, keepdims=True))
        prob = expo * (1.0 / jnp.sum(expo, axis=0, keepdims=True))
        weighted = prob * prob_grad
        score_grad = (weighted - prob * jnp.sum(weighted, axis=0, keepdims=True)).astype(BF16)
        value_part = dot(prob.astype(BF16), grads)
        key_part = dot(score_grad, queries)
        query_part = dot(score_grad, keys, TN)
        rows = slice(span * SPAN, (span + 1) * SPAN)
        query_grad_ref[rows] = (take_diagonal(query_part) * SCALE).astype(BF16)
        for slot, ident in enumerate(slots_of(span)):
            part = slice(slot * neigh_len, (slot + 1) * neigh_len)
            key_total[ident] += key_part[part]
            value_total[ident] += value_part[part]

    @pl.when(step == pl.num_programs(1) - 1)
    def _():
        key_out_ref[...] = key_total[...].astype(BF16)
        value_out_ref[...] = value_total[...].astype(BF16)


def cross_backward(queries, grads, pool_keyval, ids, neighbour_lengths, first, count, earlier):
    seq_len, width = queries.shape
    pool_count, neigh_len, _ = pool_keyval.shape
    spans = seq_len // SPAN
    groups = width // WIDE
    rows = pl.BlockSpec((SPANS_STEP * SPAN, WIDE), lambda g, c, ids, lens: (c, g + first))
    pool = lambda offset: pl.BlockSpec(
        (pool_count, neigh_len, WIDE), lambda g, c, ids, lens: (0, 0, g + first + offset)
    )
    pool_shape = jax.ShapeDtypeStruct((pool_count, neigh_len, width), BF16)
    given = [] if earlier is None else list(earlier)
    return pl.pallas_call(
        functools.partial(passing, cross_backward_kernel, 6, len(given)),
        grid_spec=pltpu.PrefetchScalarGridSpec(
            num_scalar_prefetch=2,
            grid=(count, spans // SPANS_STEP),
            in_specs=[rows, rows, pool(0), pool(groups)]
            + [pl.BlockSpec(memory_space=pl.ANY)] * len(given),
            out_specs=[rows, pool(0), pool(0)],
            scratch_shapes=[
                pltpu.VMEM((pool_count, neigh_len, WIDE), F32),
                pltpu.VMEM((pool_count, neigh_len, WIDE), F32),
            ],
        ),
        out_shape=[jax.ShapeDtypeStruct((seq_len, width), BF16), pool_shape, pool_shape],
        input_output_aliases={6 + i: i for i in range(len(given))},
        compiler_params=pltpu.CompilerParams(vmem_limit_bytes=56 * 2**20),
        cost_estimate=cost(15),
        name="cross_backward",
    )(ids, neighbour_lengths, queries, grads, pool_keyval, pool_keyval, *given)

AXES = ("fsdp", "dp")
PIECES = 2
COPY_ROWS = 48
VMEM_FOLD = 32


def bits_of(size):
    return [1 << i for i in range(size.bit_length() - 1)]


def index_bits(count):
    return [1 << i for i in range(count.bit_length() - 2, -1, -1)]


class Line:
    def __init__(self):
        self.noted = []

    def note(self, *values):
        self.noted = [values[0]]

    def also(self, value):
        self.noted.append(value)

    def after(self, value):
        return self.after_all([value])[0]

    def after_all(self, values):
        if not self.noted:
            return values
        return lax.optimization_barrier((*values, *self.noted))[: len(values)]


class Plan:
    def __init__(self, rows, line):
        self.line = line
        self.inner = lax.axis_size("dp")
        self.outer = lax.axis_size("fsdp")
        self.count = self.inner * self.outer
        self.rows = rows
        self.core = [self.inner] if self.outer > 1 else []
        self.halves = 2 if self.core else 1
        self.across = self.outer // self.halves
        self.stripe = self.inner * rows
        self.half_rows = self.across * self.stripe
        self.pieces = PIECES if self.core else 1
        self.piece = self.half_rows // self.pieces
        self.copy_rows = min(self.stripe, COPY_ROWS)
        self.me = lax.axis_index(AXES)
        across = [bit * self.inner for bit in bits_of(self.outer)[1:]]
        along = bits_of(self.inner)
        near, far = along[: len(across)], along[len(across) :]
        self.orders = (far + near + across, far + across + near)
        self.natural = [mask for mask in index_bits(self.count) if mask not in self.core]
        self.odd = self.bit(self.core[0]) if self.core else jnp.zeros((), jnp.int32)
        self.odd_word = self.odd.reshape(1)
        self.steps = list(zip(*self.orders))
        self.places = self.arrival_places()

    def bit(self, mask):
        return (self.me // mask) % 2

    def by_core(self, even, odd):
        return jnp.where(self.odd == 0, even, odd)

    def exchange(self, values, masks):
        even, odd = masks
        pairs = []
        for index in range(self.count):
            is_odd = bool(self.core) and (index // self.core[0]) % 2 == 1
            pairs.append((index, index ^ (odd if is_odd else even)))
        return lax.ppermute(values, AXES, pairs)

    def swap(self, values):
        return self.exchange(values, (self.core[0], self.core[0])) if self.core else values

    def weight_of(self, mask):
        return 1 << (len(self.natural) - 1 - self.natural.index(mask))

    def arrival_places(self):
        blocks = jnp.arange(1 << len(self.natural), dtype=jnp.int32)
        found = []
        for order in self.orders:
            target = jnp.zeros_like(blocks)
            for place_at, mask in enumerate(order):
                flag = ((blocks >> place_at) & 1) ^ self.bit(mask)
                target = target + flag * self.weight_of(mask)
            found.append(target)
        return self.by_core(found[0], found[1])

    def fold_places(self, step):
        found = []
        for order in self.orders:
            gone = order[::-1][:step]
            left = [mask for mask in self.natural if mask not in gone]
            mask = order[::-1][step]
            high = 1 << (len(left) - 1 - left.index(mask))
            index = jnp.arange(1 << (len(left) - 1), dtype=jnp.int32)
            kept = (index // high) * (2 * high) + index % high
            own = self.bit(mask)
            found.append((kept + (1 - own) * high, kept + own * high))
        return tuple(self.by_core(found[0][i], found[1][i]) for i in range(2))


def reorder_kernel(places_ref, in_ref, out_ref, buffer, sems):
    blocks = in_ref.shape[0]

    def copies(block):
        return pltpu.make_async_copy(
            in_ref.at[block], buffer.at[places_ref[block]], sems.at[block]
        )

    for block in range(blocks):
        copies(block).start()
    for block in range(blocks):
        copies(block).wait()
    pltpu.sync_copy(buffer, out_ref)


def reorder(plan, held):
    blocks = held.shape[0]
    return pl.pallas_call(
        reorder_kernel,
        in_specs=[pl.BlockSpec(memory_space=pltpu.SMEM), pl.BlockSpec(memory_space=pl.ANY)],
        out_specs=pl.BlockSpec(memory_space=pl.ANY),
        out_shape=jax.ShapeDtypeStruct(held.shape, held.dtype),
        scratch_shapes=[pltpu.VMEM(held.shape, held.dtype), pltpu.SemaphoreType.DMA((blocks,))],
        compiler_params=pltpu.CompilerParams(vmem_limit_bytes=VMEM_FOLD * 2**20),
        cost_estimate=cost(0.1),
        name="reorder_blocks",
    )(plan.places, held)


class Gather:
    def __init__(self, plan, shard):
        self.plan = plan
        self.held = shard[None]
        self.at = 0
        self.other = None
        self.halves = None

    def launch(self):
        plan = self.plan
        self.held = plan.line.after(self.held)
        plan.line.also(self.held)
        if self.at < len(plan.steps):
            self.other = plan.exchange(self.held, plan.steps[self.at])
        else:
            blocks = self.held.shape[0] // plan.pieces
            self.other = [
                plan.swap(self.held[i * blocks : (i + 1) * blocks]) for i in range(plan.pieces)
            ]

    def land(self):
        plan = self.plan
        if self.at < len(plan.steps):
            other = plan.line.after(self.other)
            self.held = jnp.concatenate([self.held, other], axis=0)
            self.at += 1
            if self.at == len(plan.steps):
                self.held = reorder(plan, self.held)
            plan.line.note(self.held)
        else:
            others = plan.line.after_all(self.other)
            plan.line.note(others[0])
            columns = self.held.shape[-1]
            self.halves = [self.held.reshape(plan.half_rows, columns)]
            self.halves += [other.reshape(plan.piece, columns) for other in others]

    def done(self):
        return self.halves is not None

    def finish(self):
        while not self.done():
            self.land()
            if not self.done():
                self.launch()
        return self.halves


def fold_kernel(sent_places, kept_places, *refs):
    half = len(refs) // 2 - 1
    sent_in, kept_in, (sent_ref, kept_ref) = refs[:half], refs[half : 2 * half], refs[2 * half :]
    for source, target in ((sent_in, sent_ref), (kept_in, kept_ref)):
        total = source[0][...].astype(F32)
        for part in source[1:]:
            total = total + part[...].astype(F32)
        target[...] = total.astype(BF16)


def fold(places, parts):
    blocks, rows, columns = parts[0].shape
    shape = jax.ShapeDtypeStruct((blocks // 2, rows, columns), BF16)
    out = pl.BlockSpec((1, rows, columns), lambda i, sent, kept: (i, 0, 0))
    sent = pl.BlockSpec((1, rows, columns), lambda i, sent, kept: (sent[i], 0, 0))
    kept = pl.BlockSpec((1, rows, columns), lambda i, sent, kept: (kept[i], 0, 0))
    return pl.pallas_call(
        fold_kernel,
        grid_spec=pltpu.PrefetchScalarGridSpec(
            num_scalar_prefetch=2,
            grid=(blocks // 2,),
            in_specs=[sent] * len(parts) + [kept] * len(parts),
            out_specs=[out, out],
        ),
        out_shape=[shape, shape],
        compiler_params=pltpu.CompilerParams(vmem_limit_bytes=VMEM_FOLD * 2**20),
        cost_estimate=cost(0.1),
        name="fold_blocks",
    )(*places, *parts, *parts)


class Scatter:
    def __init__(self, plan, keep, send):
        self.plan = plan
        self.columns = keep.shape[1]
        shape = (1 << len(plan.natural), plan.rows, self.columns)
        self.kept = keep.reshape(shape)
        self.sent = send.reshape(shape) if plan.core else None
        self.at = -1
        self.other = None
        self.total = None

    def launch(self):
        plan = self.plan
        if self.sent is None:
            return
        self.sent = plan.line.after(self.sent)
        plan.line.also(self.sent)
        if self.at < 0:
            self.other = plan.swap(self.sent)
        else:
            self.other = plan.exchange(self.sent, plan.steps[::-1][self.at])

    def land(self):
        plan = self.plan
        parts = [self.kept] if self.other is None else [self.kept, plan.line.after(self.other)]
        self.at += 1
        if self.at < len(plan.steps):
            self.sent, self.kept = fold(plan.fold_places(self.at), parts)
            plan.line.note(self.sent)
        else:
            total = parts[0].astype(F32)
            for part in parts[1:]:
                total = total + part.astype(F32)
            self.total = total.reshape(plan.rows, self.columns)
            plan.line.note(self.total)

    def done(self):
        return self.total is not None

    def finish(self):
        while not self.done():
            self.land()
            if not self.done():
                self.launch()
        return self.total


def bundled(kernel, plan, *places):
    def call(*refs):
        refs = list(refs)
        for place in sorted(places, reverse=True):
            refs[place : place + plan.pieces] = [tuple(refs[place : place + plan.pieces])]
        return kernel(*refs)

    return call


def column_copies(plan, odd, held_ref, other_refs, target, sems, start, width, rows=None):
    copies = []

    def add(ref, at, rows, first, half):
        across, rest = divmod(first, plan.stripe)
        place = across * plan.halves * plan.stripe + rest
        if plan.halves > 1:
            place = place + half * plan.stripe
            if plan.stripe % 16 == 0 and rest % 16 == 0:
                place = pl.multiple_of(place, 16)
        copies.append(
            pltpu.make_async_copy(
                ref.at[pl.ds(at, rows), pl.ds(start, width)],
                target.at[pl.ds(place, rows), :],
                sems.at[len(copies)],
            )
        )

    rows = rows or plan.copy_rows
    for first in range(0, plan.half_rows, rows):
        add(held_ref, first, rows, first, odd)
    if plan.halves > 1:
        for first in range(0, plan.half_rows, rows):
            add(other_refs[first // plan.piece], first % plan.piece, rows, first, 1 - odd)
    return copies


def store_halves(plan, odd, result, keep_ref, send_ref, columns):
    for across in range(plan.across):
        rows = slice(across * plan.stripe, (across + 1) * plan.stripe)
        parts = []
        for half in range(plan.halves):
            first = (across * plan.halves + half) * plan.stripe
            parts.append(result[first : first + plan.stripe])
        if plan.halves == 1:
            keep_ref[rows, columns] = parts[0].astype(BF16)
        else:
            keep_ref[rows, columns] = jnp.where(odd == 0, parts[0], parts[1]).astype(BF16)
            send_ref[rows, columns] = jnp.where(odd == 0, parts[1], parts[0]).astype(BF16)

ROWS = 512
FEED_ROWS = 256
POOL_BLOCK = 1024
MEBI = 2**20
ANYWHERE = pl.BlockSpec(memory_space=pl.ANY)
SCALAR = pl.BlockSpec(memory_space=pltpu.SMEM)


def norm_parts(values):
    centre = jnp.mean(values, axis=-1, keepdims=True)
    centred = values - centre
    spread = jnp.mean(centred * centred, axis=-1, keepdims=True)
    inverse = lax.rsqrt(spread + EPSILON)
    return (centred * inverse, inverse)


def norm_back(values, gain, upstream):
    unit, inverse = norm_parts(values)
    gain_term = jnp.sum(upstream * unit, axis=0, keepdims=True)
    shift_term = jnp.sum(upstream, axis=0, keepdims=True)
    inner = upstream * gain
    mean_inner = jnp.mean(inner, axis=-1, keepdims=True)
    mean_both = jnp.mean(inner * unit, axis=-1, keepdims=True)
    return (inverse * (inner - mean_inner - unit * mean_both), gain_term, shift_term)


def add_terms(step, target_ref, gain_term, shift_term):
    @pl.when(step == 0)
    def _():
        target_ref[...] = jnp.zeros_like(target_ref)

    target_ref[0:1] += gain_term
    target_ref[1:2] += shift_term


def start_all(copies):
    for copy in copies:
        copy.start()


def wait_all(copies):
    for copy in copies:
        copy.wait()


def row_block(columns, last=None, block=ROWS):
    if last is None:
        return pl.BlockSpec((block, columns), lambda i: (i, 0))
    return pl.BlockSpec((block, columns), lambda i: (jnp.minimum(i, last), 0))


def params(megabytes):
    return pltpu.CompilerParams(vmem_limit_bytes=megabytes * MEBI)


def copy_sems(plan, *sets):
    return pltpu.SemaphoreType.DMA(sets + (plan.halves * plan.half_rows // plan.copy_rows,))


def pool_kernel(plan, odd_ref, rows_ref, held_ref, other_ref, out_ref, weight, sems):
    width = weight.shape[1]

    @pl.when(pl.program_id(0) == 0)
    def _():
        copies = column_copies(plan, odd_ref[0], held_ref, other_ref, weight, sems, 0, width)
        start_all(copies)
        wait_all(copies)

    out_ref[...] = dot(rows_ref[...], weight[...]).astype(BF16)


def pool_project(plan, encoded, halves):
    rows, width = encoded.shape
    block = 1024
    return pl.pallas_call(
        bundled(functools.partial(pool_kernel, plan), plan, 3),
        grid=(rows // block,),
        in_specs=[SCALAR, pl.BlockSpec((block, width), lambda i: (i, 0))]
        + [ANYWHERE] * len(halves),
        out_specs=pl.BlockSpec((block, 2 * width), lambda i: (i, 0)),
        out_shape=jax.ShapeDtypeStruct((rows, 2 * width), BF16),
        scratch_shapes=[pltpu.VMEM((width, 2 * width), BF16), copy_sems(plan)],
        compiler_params=params(40),
        cost_estimate=cost(12),
        name="pool_project",
    )(plan.odd_word, encoded, *halves)


def project_kernel(
    plan,
    odd_ref,
    tokens_ref,
    held_ref,
    other_ref,
    unit_ref,
    projected_ref,
    vectors_ref,
    columns_ref,
    weight,
    pack,
    sems,
):
    width = tokens_ref.shape[1]

    @pl.when(pl.program_id(0) == 0)
    def _():
        copies = column_copies(plan, odd_ref[0], held_ref, other_ref, weight, sems.at[0], 0, 3 * width)
        copies += column_copies(
            plan, odd_ref[0], held_ref, other_ref, pack, sems.at[1], 3 * width, LANES
        )
        start_all(copies)
        wait_all(copies)
        columns_ref[...] = pack[...].astype(F32)
        vectors_ref[...] = columns_ref[...].T[:8]

    unit = norm_parts(tokens_ref[...].astype(F32))[0]
    first_in = (unit * vectors_ref[0:1] + vectors_ref[1:2]).astype(BF16)
    unit_ref[...] = unit.astype(BF16)
    projected_ref[...] = dot(first_in, weight[...]).astype(BF16)


def project(plan, tokens, halves):
    rows, width = tokens.shape
    return pl.pallas_call(
        bundled(functools.partial(project_kernel, plan), plan, 3),
        grid=(rows // ROWS,),
        in_specs=[SCALAR, row_block(width)] + [ANYWHERE] * len(halves),
        out_specs=[
            row_block(width),
            row_block(3 * width),
            pl.BlockSpec((8, width), lambda i: (0, 0)),
            pl.BlockSpec((width, LANES), lambda i: (0, 0)),
        ],
        out_shape=[
            jax.ShapeDtypeStruct((rows, width), BF16),
            jax.ShapeDtypeStruct((rows, 3 * width), BF16),
            jax.ShapeDtypeStruct((8, width), F32),
            jax.ShapeDtypeStruct((width, LANES), F32),
        ],
        scratch_shapes=[
            pltpu.VMEM((width, 3 * width), BF16),
            pltpu.VMEM((width, LANES), BF16),
            copy_sems(plan, 2),
        ],
        compiler_params=params(40),
        cost_estimate=cost(5),
        name="project",
    )(plan.odd_word, tokens, *halves)


def middle_kernel(
    plan,
    starts,
    odd_ref,
    tokens_ref,
    mixed_ref,
    vectors_ref,
    held_ref,
    other_ref,
    after_ref,
    second_in_ref,
    queries_ref,
    out_weight,
    query_weight,
    sems,
):
    width = tokens_ref.shape[1]

    @pl.when(pl.program_id(0) == 0)
    def _():
        copies = []
        for place_at, target in enumerate((out_weight, query_weight)):
            copies += column_copies(
                plan, odd_ref[0], held_ref, other_ref, target, sems.at[place_at], starts[place_at], width
            )
        start_all(copies)
        wait_all(copies)

    after = tokens_ref[...].astype(F32) + dot(mixed_ref[...], out_weight[...])
    after_ref[...] = after
    unit = norm_parts(after)[0]
    second_in = (unit * vectors_ref[2:3] + vectors_ref[3:4]).astype(BF16)
    second_in_ref[...] = second_in
    queries_ref[...] = dot(second_in, query_weight[...]).astype(BF16)


def middle(plan, starts, tokens, mixed, vectors, halves):
    rows, width = tokens.shape
    return pl.pallas_call(
        bundled(functools.partial(middle_kernel, plan, starts), plan, 5),
        grid=(rows // ROWS,),
        in_specs=[
            SCALAR,
            row_block(width),
            row_block(width),
            pl.BlockSpec((8, width), lambda i: (0, 0)),
        ]
        + [ANYWHERE] * len(halves),
        out_specs=[row_block(width)] * 3,
        out_shape=[
            jax.ShapeDtypeStruct((rows, width), F32),
            jax.ShapeDtypeStruct((rows, width), BF16),
            jax.ShapeDtypeStruct((rows, width), BF16),
        ],
        scratch_shapes=[
            pltpu.VMEM((width, width), BF16),
            pltpu.VMEM((width, width), BF16),
            copy_sems(plan, 2),
        ],
        compiler_params=params(40),
        cost_estimate=cost(5),
        name="middle",
    )(plan.odd_word, tokens, mixed, vectors, *halves)


def segments_kernel(moves, in_ref, out_ref):
    lane = iota((1, LANES), 1)
    tiles = {}
    for place in range(out_ref.shape[1] // LANES):
        result = None
        for source, shift, first, last in moves[place]:
            if source not in tiles:
                tiles[source] = in_ref[:, source * LANES : (source + 1) * LANES].astype(F32)
            tile = pltpu.roll(tiles[source], shift, 1) if shift else tiles[source]
            if result is None:
                result = tile
            else:
                result = jnp.where((lane >= first) & (lane < last), tile, result)
        out_ref[:, place * LANES : (place + 1) * LANES] = result.astype(out_ref.dtype)


def swap_segments(matrix, outer, inner, size):
    rows, columns = matrix.shape
    moves = [[] for _ in range(columns // LANES)]
    for i in range(outer):
        for j in range(inner):
            source = (i * inner + j) * size
            target = (j * outer + i) * size
            done = 0
            while done < size:
                at, to = source + done, target + done
                count = min(size - done, LANES - at % LANES, LANES - to % LANES)
                shift = (to - at) % LANES
                moves[to // LANES].append((at // LANES, shift, to % LANES, to % LANES + count))
                done += count
    return pl.pallas_call(
        functools.partial(segments_kernel, moves),
        in_specs=[pl.BlockSpec(memory_space=pltpu.VMEM)],
        out_specs=pl.BlockSpec(memory_space=pltpu.VMEM),
        out_shape=jax.ShapeDtypeStruct((rows, columns), matrix.dtype),
        compiler_params=params(24),
        cost_estimate=cost(2),
        name="swap_segments",
    )(matrix)


GELU_SCALE = 0.7978845608028654
GELU_CUBE = 0.044715
TERMS_STEP = 3


def gelu_both(values):
    square = values * values
    bent = jnp.tanh(values * (GELU_SCALE + (GELU_SCALE * GELU_CUBE) * square))
    half = 0.5 + 0.5 * bent
    result = values * half
    slope = 2.0 * GELU_SCALE + (6.0 * GELU_SCALE * GELU_CUBE) * square
    return (result, half * (1.0 + (values - result) * slope))


def feed_kernel(
    plan,
    out_start,
    row_steps,
    odd_ref,
    after_ref,
    mixed_ref,
    cotangent_ref,
    vectors_ref,
    feed_held_ref,
    feed_other_ref,
    held_ref,
    other_ref,
    block_ref,
    grad_ref,
    mixed_grad_ref,
    terms_ref,
    keep_ref,
    send_ref,
    out_matrix,
    weights,
    lefts,
    rights,
    sems,
):
    step = pl.program_id(0)
    width = after_ref.shape[1]
    parts = weights.shape[1] // width // 2

    def copies():
        return column_copies(
            plan,
            odd_ref[0],
            held_ref,
            other_ref,
            out_matrix,
            sems.at[0],
            out_start,
            width,
            plan.stripe,
        ) + column_copies(
            plan,
            odd_ref[0],
            feed_held_ref,
            feed_other_ref,
            weights,
            sems.at[1],
            0,
            2 * parts * width,
            plan.stripe,
        )

    def ready(index):
        if index == 2 * parts:
            return out_matrix[...]
        return weights[:, index * width : (index + 1) * width]

    def rows_of(place_at):
        mixed = mixed_ref[...]
        cotangent = cotangent_ref[...]
        out_weight = ready(2 * parts)
        after_cross = after_ref[...] + dot(mixed, out_weight)
        unit, inverse = norm_parts(after_cross)
        gain = vectors_ref[4:5]
        third_in = (unit * gain + vectors_ref[5:6]).astype(BF16)
        up = ready(0)
        before = dot(third_in, up)
        lefts[parts, :, place_at] = third_in.T
        lefts[parts + 1, :, place_at] = mixed.T
        rights[0, place_at] = cotangent
        result = after_cross
        upstream = jnp.zeros_like(after_cross)
        for part in range(parts):
            down = ready(parts + part)
            back = dot(cotangent, down, NT)
            hidden, slope = gelu_both(before)
            hidden = hidden.astype(BF16)
            if part + 1 < parts:
                next_up = ready(part + 1)
                before = dot(third_in, next_up)
            result = result + dot(hidden, down)
            lefts[part, :, place_at] = hidden.T
            hidden_grad = (slope * back).astype(BF16)
            rights[1 + part, place_at] = hidden_grad
            upstream = upstream + dot(hidden_grad, up, NT)
            if part + 1 < parts:
                up = next_up
        block_ref[...] = result.astype(BF16)
        inner = upstream * gain
        mean_inner = jnp.mean(inner, axis=-1, keepdims=True)
        mean_both = jnp.mean(inner * unit, axis=-1, keepdims=True)
        grad = cotangent.astype(F32) + inverse * (inner - mean_inner - unit * mean_both)
        add_terms(
            step,
            terms_ref,
            jnp.sum(upstream * unit, axis=0, keepdims=True),
            jnp.sum(upstream, axis=0, keepdims=True),
        )
        grad_ref[...] = grad
        rounded = grad.astype(BF16)
        rights[parts + 1, place_at] = rounded
        mixed_grad_ref[...] = dot(rounded, out_weight, NT).astype(BF16)

    @pl.when(step == 0)
    def _():
        start_all(copies())
        wait_all(copies())

    @pl.when(step < row_steps)
    def _():
        rows_of(pl.ds(pl.multiple_of(step * FEED_ROWS, FEED_ROWS), FEED_ROWS))

    @pl.when(step >= row_steps)
    def _():
        for turn in range(TERMS_STEP):
            term = (step - row_steps) * TERMS_STEP + turn
            left = jnp.where(term < parts, term, jnp.where(term < 2 * parts, parts, parts + 1))
            right = jnp.where(term < parts, 0, term - parts + 1)
            result = dot(lefts[left], rights[right])
            columns = slice(turn * width, (turn + 1) * width)
            store_halves(plan, odd_ref[0], result, keep_ref, send_ref, columns)


def feed(plan, out_start, after, mixed, cotangent, vectors, feed_halves, halves):
    rows, width = after.shape
    parts = feed_halves[0].shape[1] // width // 2
    terms = 2 * parts + 1
    steps = rows // FEED_ROWS
    last = steps - 1
    rows_in = row_block(width, last, FEED_ROWS)
    whole = pl.BlockSpec((8, width), lambda i: (0, 0))
    slab = pl.BlockSpec(
        (plan.half_rows, TERMS_STEP * width), lambda i: (0, jnp.maximum(i - steps, 0))
    )
    slab_shape = jax.ShapeDtypeStruct((plan.half_rows, terms * width), BF16)
    return pl.pallas_call(
        bundled(
            functools.partial(feed_kernel, plan, out_start, steps), plan, 6, 7 + plan.pieces
        ),
        grid=(steps + terms // TERMS_STEP,),
        in_specs=[SCALAR, rows_in, rows_in, rows_in, whole]
        + [ANYWHERE] * (len(feed_halves) + len(halves)),
        out_specs=[rows_in, rows_in, rows_in, whole, slab, slab],
        out_shape=[
            jax.ShapeDtypeStruct((rows, width), BF16),
            jax.ShapeDtypeStruct((rows, width), F32),
            jax.ShapeDtypeStruct((rows, width), BF16),
            jax.ShapeDtypeStruct((8, width), F32),
            slab_shape,
            slab_shape,
        ],
        scratch_shapes=[
            pltpu.VMEM((width, width), BF16),
            pltpu.VMEM((width, 2 * parts * width), BF16),
            pltpu.VMEM((parts + 2, width, rows), BF16),
            pltpu.VMEM((parts + 2, rows, width), BF16),
            copy_sems(plan, 2),
        ],
        compiler_params=params(60),
        cost_estimate=cost(50),
        name="feed_forward",
    )(plan.odd_word, after, mixed, cotangent, vectors, *feed_halves, *halves)


def second_kernel(
    plan,
    starts,
    row_steps,
    odd_ref,
    after_ref,
    grad_in_ref,
    query_grad_ref,
    second_in_ref,
    mixed_ref,
    vectors_ref,
    held_ref,
    other_ref,
    grad_ref,
    attend_ref,
    terms_ref,
    keep_ref,
    send_ref,
    out_weight,
    query_weight,
    lefts,
    rights,
    sems,
):
    step = pl.program_id(0)
    width = after_ref.shape[1]

    @pl.when(step == 0)
    def _():
        copies = []
        for place_at, target in enumerate((out_weight, query_weight)):
            copies += column_copies(
                plan, odd_ref[0], held_ref, other_ref, target, sems.at[place_at], starts[place_at], width
            )
        start_all(copies)
        wait_all(copies)

    place_at = pl.ds(pl.multiple_of(step * ROWS, ROWS), ROWS)
    query_grad = query_grad_ref[...]
    back, gain_term, shift_term = norm_back(
        after_ref[...], vectors_ref[2:3], dot(query_grad, query_weight[...], NT)
    )
    lefts[0, :, place_at] = second_in_ref[...].T
    lefts[1, :, place_at] = mixed_ref[...].T
    rights[0, place_at] = query_grad
    add_terms(step, terms_ref, gain_term, shift_term)
    grad = grad_in_ref[...] + back
    grad_ref[...] = grad
    rounded = grad.astype(BF16)
    attend_ref[...] = dot(rounded, out_weight[...], NT).astype(BF16)
    rights[1, place_at] = rounded

    @pl.when(step == row_steps - 1)
    def _():
        for term in range(2):
            result = dot(lefts[term], rights[term])
            columns = slice(term * width, (term + 1) * width)
            store_halves(plan, odd_ref[0], result, keep_ref, send_ref, columns)


def second_back(plan, starts, after, grad_in, query_grad, second_in, mixed, vectors, halves):
    rows, width = after.shape
    steps = rows // ROWS
    rows_in = row_block(width)
    whole = pl.BlockSpec((8, width), lambda i: (0, 0))
    slab = pl.BlockSpec((plan.half_rows, 2 * width), lambda i: (0, 0))
    slab_shape = jax.ShapeDtypeStruct((plan.half_rows, 2 * width), BF16)
    return pl.pallas_call(
        bundled(functools.partial(second_kernel, plan, starts, steps), plan, 8),
        grid=(steps,),
        in_specs=[SCALAR] + [rows_in] * 5 + [whole] + [ANYWHERE] * len(halves),
        out_specs=[rows_in, rows_in, whole, slab, slab],
        out_shape=[
            jax.ShapeDtypeStruct((rows, width), F32),
            jax.ShapeDtypeStruct((rows, width), BF16),
            jax.ShapeDtypeStruct((8, width), F32),
            slab_shape,
            slab_shape,
        ],
        scratch_shapes=[
            pltpu.VMEM((width, width), BF16),
            pltpu.VMEM((width, width), BF16),
            pltpu.VMEM((2, width, rows), BF16),
            pltpu.VMEM((2, rows, width), BF16),
            copy_sems(plan, 2),
        ],
        compiler_params=params(48),
        cost_estimate=cost(12),
        name="second_back",
    )(plan.odd_word, after, grad_in, query_grad, second_in, mixed, vectors, *halves)


def first_terms_kernel(
    plan,
    odd_ref,
    unit_ref,
    projected_grad_ref,
    columns_ref,
    second_terms_ref,
    third_terms_ref,
    held_ref,
    other_ref,
    keep_ref,
    send_ref,
    weight,
    terms,
    sems,
):
    part = pl.program_id(0)
    width = unit_ref.shape[1]

    def copies(index):
        return column_copies(
            plan, odd_ref[0], held_ref, other_ref, weight.at[index], sems.at[index], index * width, width
        )

    @pl.when(part == 0)
    def _():
        for index in range(3):
            start_all(copies(index))
        terms[...] = jnp.zeros_like(terms)

    for index in range(3):

        @pl.when(part == index)
        def _():
            wait_all(copies(index))

    grads = projected_grad_ref[0]
    plain = dot(unit_ref[...], grads, TN)
    sums = jnp.sum(grads.astype(F32), axis=0, keepdims=True)
    gain = columns_ref[:, 0:1]
    shift = columns_ref[:, 1:2]
    place = pl.ds(pl.multiple_of(part * width, LANES), width)
    store_halves(plan, odd_ref[0], gain * plain + shift * sums, keep_ref, send_ref, place)
    matrix = weight[part].astype(F32)
    terms[:, 0:1] += jnp.sum(matrix * plain, axis=1, keepdims=True)
    terms[:, 1:2] += jnp.sum(matrix * sums, axis=1, keepdims=True)

    @pl.when(part == 2)
    def _():
        rows = jnp.concatenate(
            [
                jnp.zeros((2, width), F32),
                second_terms_ref[0:2],
                third_terms_ref[0:2],
                jnp.zeros((LANES - 6, width), F32),
            ],
            axis=0,
        )
        lane = iota((1, LANES), 1)
        result = jnp.where(lane < 2, terms[...], rows.T)
        place = slice(3 * width, 3 * width + LANES)
        store_halves(plan, odd_ref[0], result, keep_ref, send_ref, place)


def first_terms(plan, unit, projected_grad, columns, second_terms, third_terms, halves):
    rows, width = unit.shape
    whole = pl.BlockSpec((8, width), lambda i: (0, 0))
    slab = pl.BlockSpec((plan.half_rows, 3 * width + LANES), lambda i: (0, 0))
    slab_shape = jax.ShapeDtypeStruct((plan.half_rows, 3 * width + LANES), BF16)
    return pl.pallas_call(
        bundled(functools.partial(first_terms_kernel, plan), plan, 7),
        grid=(3,),
        in_specs=[
            SCALAR,
            pl.BlockSpec((rows, width), lambda i: (0, 0)),
            pl.BlockSpec((1, rows, width), lambda i: (i, 0, 0)),
            pl.BlockSpec((width, LANES), lambda i: (0, 0)),
            whole,
            whole,
        ]
        + [ANYWHERE] * len(halves),
        out_specs=[slab, slab],
        out_shape=[slab_shape, slab_shape],
        scratch_shapes=[
            pltpu.VMEM((3, width, width), BF16),
            pltpu.VMEM((width, LANES), F32),
            copy_sems(plan, 3),
        ],
        compiler_params=params(56),
        cost_estimate=cost(8),
        name="first_terms",
    )(plan.odd_word, unit, projected_grad, columns, second_terms, third_terms, *halves)


def first_rows_kernel(
    plan,
    odd_ref,
    tokens_ref,
    grad_in_ref,
    projected_grad_ref,
    vectors_ref,
    held_ref,
    other_ref,
    grad_ref,
    weight,
    sems,
):
    width = tokens_ref.shape[1]

    @pl.when(pl.program_id(0) == 0)
    def _():
        copies = column_copies(plan, odd_ref[0], held_ref, other_ref, weight, sems, 0, 3 * width)
        start_all(copies)
        wait_all(copies)

    upstream = None
    for part in range(3):
        product = dot(projected_grad_ref[part], weight[:, part * width : (part + 1) * width], NT)
        upstream = product if upstream is None else upstream + product
    unit, inverse = norm_parts(tokens_ref[...].astype(F32))
    inner = upstream * vectors_ref[0:1]
    mean_inner = jnp.mean(inner, axis=-1, keepdims=True)
    mean_both = jnp.mean(inner * unit, axis=-1, keepdims=True)
    grad_ref[...] = grad_in_ref[...] + inverse * (inner - mean_inner - unit * mean_both)


def first_rows(plan, tokens, grad_in, projected_grad, vectors, halves):
    rows, width = tokens.shape
    rows_in = row_block(width, None, FEED_ROWS)
    return pl.pallas_call(
        bundled(functools.partial(first_rows_kernel, plan), plan, 6),
        grid=(rows // FEED_ROWS,),
        in_specs=[
            SCALAR,
            rows_in,
            rows_in,
            pl.BlockSpec((3, FEED_ROWS, width), lambda i: (0, i, 0)),
            pl.BlockSpec((8, width), lambda i: (0, 0)),
        ]
        + [ANYWHERE] * len(halves),
        out_specs=rows_in,
        out_shape=jax.ShapeDtypeStruct((rows, width), F32),
        scratch_shapes=[pltpu.VMEM((width, 3 * width), BF16), copy_sems(plan)],
        compiler_params=params(52),
        cost_estimate=cost(8),
        name="first_rows",
    )(plan.odd_word, tokens, grad_in, projected_grad, vectors, *halves)


def keyval_kernel(
    plan, odd_ref, rows_ref, key_ref, value_ref, keep_ref, send_ref, key_total, value_total
):
    step = pl.program_id(0)
    width = rows_ref.shape[1]
    turned = rows_ref[...].T
    key_part = dot(turned, key_ref[...])
    value_part = dot(turned, value_ref[...])

    @pl.when(step == 0)
    def _():
        key_total[...] = key_part
        value_total[...] = value_part

    @pl.when(step > 0)
    def _():
        key_total[...] += key_part
        value_total[...] += value_part

    @pl.when(step == pl.num_programs(0) - 1)
    def _():
        for place_at, total in enumerate((key_total, value_total)):
            columns = slice(place_at * width, (place_at + 1) * width)
            store_halves(plan, odd_ref[0], total[...], keep_ref, send_ref, columns)


def keyval_terms(plan, encoded, pool_keys, pool_values):
    rows, width = encoded.shape
    block = 2048
    rows_in = pl.BlockSpec((block, width), lambda i: (i, 0))
    slab = pl.BlockSpec((plan.half_rows, 2 * width), lambda i: (0, 0))
    slab_shape = jax.ShapeDtypeStruct((plan.half_rows, 2 * width), BF16)
    return pl.pallas_call(
        functools.partial(keyval_kernel, plan),
        grid=(rows // block,),
        in_specs=[SCALAR, rows_in, rows_in, rows_in],
        out_specs=[slab, slab],
        out_shape=[slab_shape, slab_shape],
        scratch_shapes=[pltpu.VMEM((width, width), F32), pltpu.VMEM((width, width), F32)],
        compiler_params=params(48),
        cost_estimate=cost(14),
        name="keyval_terms",
    )(plan.odd_word, encoded, pool_keys, pool_values)


def neighbours_kernel(
    plan, odd_ref, key_ref, value_ref, held_ref, other_ref, out_ref, weight, sems
):
    width = key_ref.shape[1]

    @pl.when(pl.program_id(0) == 0)
    def _():
        copies = column_copies(plan, odd_ref[0], held_ref, other_ref, weight, sems, 0, 2 * width)
        start_all(copies)
        wait_all(copies)

    out_ref[...] = dot(key_ref[...], weight[:, :width], NT) + dot(
        value_ref[...], weight[:, width:], NT
    )


def neighbours_back(plan, pool_keys, pool_values, halves, first, count, earlier):
    rows, width = pool_keys.shape
    block = POOL_BLOCK
    rows_in = pl.BlockSpec((block, width), lambda i: (i + first, 0))
    given = [] if earlier is None else [earlier]
    return pl.pallas_call(
        functools.partial(
            passing,
            bundled(functools.partial(neighbours_kernel, plan), plan, 4),
            4 + plan.pieces,
            len(given),
        ),
        grid=(count,),
        in_specs=[SCALAR, rows_in, rows_in] + [ANYWHERE] * (len(halves) + len(given)),
        out_specs=rows_in,
        out_shape=jax.ShapeDtypeStruct((rows, width), F32),
        scratch_shapes=[pltpu.VMEM((width, 2 * width), BF16), copy_sems(plan)],
        input_output_aliases={4 + plan.pieces: 0} if given else {},
        compiler_params=params(52),
        cost_estimate=cost(5),
        name="neighbours_back",
    )(plan.odd_word, pool_keys, pool_values, *halves, *given)

def local(
    tokens,
    lengths,
    neighbours,
    neighbour_ids,
    neighbour_lengths,
    first_gain,
    first_shift,
    self_input,
    self_output,
    second_gain,
    second_shift,
    cross_query,
    cross_keyval,
    cross_output,
    third_gain,
    third_shift,
    feed_up,
    feed_down,
    cotangent,
):
    rows, width = cross_query.shape
    line = Line()
    plan = Plan(rows, line)
    steps = len(plan.steps)
    parts = feed_down.shape[0] // rows
    pool_count, neigh_len = neighbours.shape[:2]
    vectors = (first_gain, first_shift, second_gain, second_shift, third_gain, third_shift)
    vector_pack = jnp.pad(jnp.stack(vectors, axis=1), ((0, 0), (0, LANES - len(vectors))))
    rows_in = tokens[0]
    encoded = neighbours.reshape(pool_count * neigh_len, width)
    ids = neighbour_ids.reshape(-1)
    pairs = width // LANES

    def advance(*chunks, after=()):
        moving = [chunk for chunk in chunks if not chunk.done()]
        for chunk in moving:
            chunk.land()
        for chunk in moving + list(after):
            if not chunk.done():
                chunk.launch()

    def run(kernel, first, *rest):
        results = kernel(line.after(first), *rest)
        line.note(results[0] if isinstance(results, (tuple, list)) else results)
        return results

    start = Gather(plan, jnp.concatenate([self_input, vector_pack], axis=1))
    start.launch()
    middle_part = Gather(
        plan,
        jnp.concatenate(
            [line.after(cross_keyval), self_output, cross_query, cross_output], axis=1
        ),
    )
    advance(start, after=[middle_part])
    up_shard = swap_segments(line.after(feed_up), plan.count, parts, rows)
    down_shard = line.after(feed_down).reshape(parts, rows, width)
    down_shard = down_shard.swapaxes(0, 1).reshape(rows, parts * width)
    feed_part = Gather(plan, jnp.concatenate([up_shard, down_shard], axis=1))
    advance(start)
    advance(start, middle_part, after=[feed_part])
    advance(start)
    start_halves = start.finish()
    unit, projected, vector_rows, vector_columns = run(
        lambda values: project(plan, values, start_halves), rows_in
    )
    advance(middle_part, feed_part)
    attended = None
    for turn in range(2):
        attended = run(self_forward, projected, lengths, turn * (pairs // 2), pairs // 2, attended)
        if turn == 0:
            advance(middle_part)
    advance(middle_part, feed_part)
    self_mixed, self_exact, logsum = attended
    middle_halves = middle_part.finish()
    after_self, second_in, cross_queries = run(
        lambda values: middle(
            plan, (2 * width, 3 * width), rows_in, values, vector_rows, middle_halves
        ),
        self_mixed,
    )
    advance(feed_part)
    pool_keyval = run(functools.partial(pool_project, plan), encoded, middle_halves)
    pool_keyval = pool_keyval.reshape(pool_count, neigh_len, 2 * width)
    cross_mixed = run(cross_forward, cross_queries, pool_keyval, ids, neighbour_lengths)
    advance(feed_part)
    feed_halves = feed_part.finish()
    block_out, after_cross_grad, mixed_grad, third_terms, feed_keep, feed_send = run(
        lambda values: feed(
            plan,
            4 * width,
            after_self,
            values,
            cotangent[0],
            vector_rows,
            feed_halves,
            middle_halves,
        ),
        cross_mixed,
    )
    feed_sum = Scatter(plan, feed_keep, feed_send)
    feed_sum.launch()

    groups = width // WIDE
    crossed = None
    for first, count in ((0, 1), (1, groups - 1)):
        crossed = run(
            cross_backward,
            cross_queries,
            mixed_grad,
            pool_keyval,
            ids,
            neighbour_lengths,
            first,
            count,
            crossed,
        )
        if first == 0:
            advance(feed_sum)
    query_grad, pool_keys, pool_values = crossed
    pool_keys = pool_keys.reshape(pool_count * neigh_len, width)
    pool_values = pool_values.reshape(pool_count * neigh_len, width)
    keyval_keep, keyval_send = run(
        lambda values: keyval_terms(plan, encoded, values, pool_values), pool_keys
    )
    advance(feed_sum)
    after_self_grad, attend_grad, second_terms, second_keep, second_send = run(
        lambda values: second_back(
            plan,
            (2 * width, 3 * width),
            after_self,
            after_cross_grad,
            values,
            second_in,
            self_mixed,
            vector_rows,
            middle_halves,
        ),
        query_grad,
    )
    middle_sum = Scatter(
        plan,
        jnp.concatenate([keyval_keep, second_keep], axis=1),
        jnp.concatenate([keyval_send, second_send], axis=1),
    )
    advance(feed_sum, after=[middle_sum])
    projected_grad = None
    for turn in range(2):
        projected_grad = run(
            lambda values: self_backward(
                projected,
                lengths,
                values,
                self_exact,
                logsum,
                turn * (pairs // 2),
                pairs // 2,
                projected_grad,
            ),
            attend_grad,
        )
        if turn == 0:
            advance(middle_sum)
    first_keep, first_send = run(
        lambda values: first_terms(
            plan, unit, values, vector_columns, second_terms, third_terms, start_halves
        ),
        projected_grad,
    )
    first_sum = Scatter(plan, first_keep, first_send)
    advance(feed_sum, middle_sum, after=[first_sum])
    blocks = pool_keys.shape[0] // POOL_BLOCK
    quarter = blocks // 4
    neighbours_grad = None

    def neighbours_turn(first, count, earlier):
        return run(
            lambda values: neighbours_back(
                plan,
                values,
                pool_values,
                middle_halves,
                first,
                count,
                earlier,
            ),
            pool_keys,
        )

    neighbours_grad = neighbours_turn(0, quarter, neighbours_grad)
    advance(feed_sum, middle_sum, first_sum)
    tokens_grad = run(
        lambda values: first_rows(
            plan, rows_in, after_self_grad, values, vector_rows, start_halves
        ),
        projected_grad,
    )
    advance(middle_sum, first_sum)
    neighbours_grad = neighbours_turn(quarter, quarter, neighbours_grad)
    advance(middle_sum, first_sum)
    neighbours_grad = neighbours_turn(2 * quarter, blocks - 2 * quarter, neighbours_grad)
    feed_total = feed_sum.finish()
    middle_total = middle_sum.finish()
    first_total = first_sum.finish()

    down_grad = feed_total[:, : parts * width].reshape(rows, parts, width).swapaxes(0, 1)
    up_grad = swap_segments(
        feed_total[:, parts * width : 2 * parts * width], parts, plan.count, rows
    )
    vector_grads = [first_total[:, 3 * width + i] for i in range(len(vectors))]
    return (
        block_out[None],
        tokens_grad[None],
        neighbours_grad.reshape(neighbours.shape),
        vector_grads[0],
        vector_grads[1],
        first_total[:, : 3 * width],
        middle_total[:, 3 * width :],
        vector_grads[2],
        vector_grads[3],
        middle_total[:, 2 * width : 3 * width],
        middle_total[:, : 2 * width],
        feed_total[:, 2 * parts * width :],
        vector_grads[4],
        vector_grads[5],
        up_grad,
        down_grad.reshape(feed_down.shape),
    )


def solution(mesh):
    placed = (
        P(("fsdp", "dp"), None, None),
        P(("fsdp", "dp")),
        P(("fsdp", "dp"), None, None),
        P(("fsdp", "dp"), None, None),
        P(("fsdp", "dp")),
        P(("fsdp", "dp")),
        P(("fsdp", "dp")),
        P(("fsdp", "dp"), None),
        P(("fsdp", "dp"), None),
        P(("fsdp", "dp")),
        P(("fsdp", "dp")),
        P(("fsdp", "dp"), None),
        P(("fsdp", "dp"), None),
        P(("fsdp", "dp"), None),
        P(("fsdp", "dp")),
        P(("fsdp", "dp")),
        P(("fsdp", "dp"), None),
        P(("fsdp", "dp"), None),
        P(("fsdp", "dp"), None, None),
    )
    return jax.shard_map(
        local,
        mesh=mesh,
        in_specs=placed,
        out_specs=(
            P(("fsdp", "dp"), None, None),
            P(("fsdp", "dp"), None, None),
            P(("fsdp", "dp"), None, None),
            P(("fsdp", "dp")),
            P(("fsdp", "dp")),
            P(("fsdp", "dp"), None),
            P(("fsdp", "dp"), None),
            P(("fsdp", "dp")),
            P(("fsdp", "dp")),
            P(("fsdp", "dp"), None),
            P(("fsdp", "dp"), None),
            P(("fsdp", "dp"), None),
            P(("fsdp", "dp")),
            P(("fsdp", "dp")),
            P(("fsdp", "dp"), None),
            P(("fsdp", "dp"), None),
        ),
        check_vma=False,
    )
```

```python
import functools

import jax
import jax.numpy as jnp
from jax import lax
from jax.experimental import pallas as pl
from jax.experimental.pallas import tpu as pltpu
from jax.sharding import PartitionSpec as P

HEADS = 12
SPAN = 64
NEIGH = 2
LANES = 128
WIDE = 256
QBLOCK = 256

EPSILON = 1e-05
SCALE = 0.125
NEGATIVE = -1e30
BF16 = jnp.bfloat16
F32 = jnp.float32
NT = (((1,), (1,)), ((), ()))
NN = (((1,), (0,)), ((), ()))
TN = (((0,), (0,)), ((), ()))


def dot(left, right, dims=NN):
    return lax.dot_general(left, right, dims, preferred_element_type=F32)


def iota(shape, axis):
    return lax.broadcasted_iota(jnp.int32, shape, axis)


def cost(microseconds):
    return pl.CostEstimate(
        flops=int(microseconds * 1100000000.0), bytes_accessed=0, transcendentals=0
    )


def passing(kernel, before, given, *refs):
    return kernel(*refs[:before], *refs[before + given :])


def split_three(values):
    high = values.astype(BF16)
    rest = values - high.astype(F32)
    middle = rest.astype(BF16)
    low = (rest - middle.astype(F32)).astype(BF16)
    return (high, middle, low)


def self_forward_kernel(length_ref, query_ref, key_ref, value_ref, mixed_ref, exact_ref, logsum_ref):
    seq_len = query_ref.shape[0]
    length = length_ref[0]
    lane = iota((1, LANES), 1)
    first = lane < 64
    padded = jnp.where(iota((seq_len, 1), 0) < length, 0.0, NEGATIVE).astype(BF16)
    keys = key_ref[...]
    values = value_ref[...]
    one = jnp.ones((), BF16)
    keys_by_head = (
        jnp.where(first, keys, jnp.where(lane == 64, padded, 0)),
        jnp.where(first, jnp.where(lane == 0, padded, 0), keys),
    )
    values_by_head = (jnp.where(first, values, one), jnp.where(first, one, values))
    causal = iota((QBLOCK, QBLOCK), 1) <= iota((QBLOCK, QBLOCK), 0)

    def scores(block, head):
        start = block * QBLOCK
        query = query_ref[start : start + QBLOCK] * jnp.asarray(SCALE, BF16)
        if head == 0:
            query = jnp.where(first, query, jnp.where(lane == 64, one, 0))
        else:
            query = jnp.where(first, jnp.where(lane == 0, one, 0), query)
        diagonal = dot(query, keys_by_head[head][start : start + QBLOCK], NT)
        before = dot(query, keys_by_head[head][:start], NT) if block else None
        return (jnp.where(causal, diagonal, NEGATIVE), before)

    units = [(block, head) for block in reversed(range(seq_len // QBLOCK)) for head in range(2)]
    ahead = [scores(*unit) for unit in units[:AHEAD]]
    outs = []
    tops = []
    for place_at, (block, head) in enumerate(units):
        if place_at + AHEAD < len(units):
            ahead.append(scores(*units[place_at + AHEAD]))
        start = block * QBLOCK
        diagonal, before = ahead.pop(0)
        top = jnp.max(diagonal, axis=-1, keepdims=True)
        if block:
            top = jnp.maximum(top, jnp.max(before, axis=-1, keepdims=True))
        out = dot(
            jnp.exp(diagonal - top).astype(BF16), values_by_head[head][start : start + QBLOCK]
        )
        if block:
            out = out + dot(jnp.exp(before - top).astype(BF16), values_by_head[head][:start])
        outs.append(out)
        tops.append(top)
        if head == 0:
            continue
        total = pltpu.roll(jnp.where(first, outs[1], outs[0]), 64, 1)
        mixed = jnp.where(first, outs[0], outs[1]) / total
        mixed_ref[start : start + QBLOCK] = mixed.astype(BF16)
        exact_ref[start : start + QBLOCK] = mixed
        logsum = (jnp.where(first, tops[0], tops[1]) + jnp.log(total)).T
        logsum_ref[0, 0:1, start : start + QBLOCK] = logsum[0:1]
        logsum_ref[0, 1:2, start : start + QBLOCK] = logsum[64:65]
        outs = []
        tops = []


def self_forward(projected, lengths, first, count, earlier):
    seq_len = projected.shape[0]
    width = projected.shape[1] // 3
    pairs = width // LANES
    column = lambda offset: pl.BlockSpec((seq_len, LANES), lambda p: (0, p + offset))
    given = [] if earlier is None else list(earlier)
    return pl.pallas_call(
        functools.partial(passing, self_forward_kernel, 4, len(given)),
        grid=(count,),
        in_specs=[
            pl.BlockSpec(memory_space=pltpu.SMEM),
            column(first),
            column(pairs + first),
            column(2 * pairs + first),
        ]
        + [pl.BlockSpec(memory_space=pl.ANY)] * len(given),
        out_specs=[
            column(first),
            column(first),
            pl.BlockSpec((1, 8, seq_len), lambda p: (p + first, 0, 0)),
        ],
        out_shape=[
            jax.ShapeDtypeStruct((seq_len, width), BF16),
            jax.ShapeDtypeStruct((seq_len, width), F32),
            jax.ShapeDtypeStruct((pairs, 8, seq_len), F32),
        ],
        input_output_aliases={4 + i: i for i in range(len(given))},
        compiler_params=pltpu.CompilerParams(vmem_limit_bytes=48 * 2**20),
        cost_estimate=cost(8),
        name="self_forward",
    )(lengths, projected, projected, projected, *given)


AHEAD = 1
AHEAD_BACK = 2
AHEAD_CROSS = 2
SPANS_STEP = 8


def self_backward_kernel(
    length_ref,
    query_ref,
    key_ref,
    value_ref,
    grad_ref,
    exact_ref,
    logsum_ref,
    out_ref,
    key_grad_ref,
    value_grad_ref,
):
    seq_len = query_ref.shape[0]
    length = length_ref[0]
    lane = iota((1, LANES), 1)
    first = lane < 64
    row = iota((LANES, 1), 0)
    top_rows = row < 64
    padded = jnp.where(iota((seq_len, 1), 0) < length, 0.0, NEGATIVE).astype(BF16)
    keys = key_ref[...]
    values = value_ref[...]
    zero = jnp.zeros((), BF16)
    minus = -jnp.ones((), BF16)

    def beside(offset, head_lane):
        kept = (lane > head_lane) & (lane < head_lane + 4)
        return jnp.where(lane == head_lane, offset, jnp.where(kept, minus, zero))

    keys_by_head = (
        jnp.where(first, keys, beside(padded, 64)),
        jnp.where(first, beside(padded, 0), keys),
    )
    values_by_head = (
        jnp.where(first, values, beside(zero, 64)),
        jnp.where(first, beside(zero, 0), values),
    )
    keys_turned = keys.T
    turned_by_head = (
        jnp.where(top_rows, keys_turned, zero),
        jnp.where(top_rows, zero, keys_turned),
    )
    causal = iota((QBLOCK, QBLOCK), 0) <= iota((QBLOCK, QBLOCK), 1)

    def fill(turned, head, lead, parts):
        base = 64 if head == 0 else 0
        other = jnp.where(row == base, lead, zero)
        for place, part in enumerate(parts):
            other = jnp.where(row == base + 1 + place, part, other)
        own = top_rows if head == 0 else ~top_rows
        return jnp.where(own, turned, other)

    count = seq_len // QBLOCK
    units = [(block, head) for block in reversed(range(count)) for head in range(2)]
    loaded = {}

    def load(block):
        start = block * QBLOCK
        stop = start + QBLOCK
        query = query_ref[start:stop] * jnp.asarray(SCALE, BF16)
        grad = grad_ref[start:stop]
        weighted = (grad.astype(F32) * exact_ref[start:stop]).T
        return (query, grad, query.T, grad.T, weighted)

    def products(block, head):
        if head == 0:
            loaded[block] = load(block)
        _, _, query_turned, grad_turned, weighted = loaded[block]
        start = block * QBLOCK
        stop = start + QBLOCK
        delta = jnp.sum(weighted[head * 64 : head * 64 + 64], axis=0, keepdims=True)
        logsum = logsum_ref[0, head : head + 1, start:stop]
        score = dot(
            keys_by_head[head][:stop],
            fill(query_turned, head, jnp.ones((), BF16), split_three(logsum)),
        )
        centred = dot(
            values_by_head[head][:stop], fill(grad_turned, head, zero, split_three(delta))
        )
        return (score, centred)

    ahead = [products(*unit) for unit in units[:AHEAD_BACK]]
    probs_all = []
    scores_all = []
    query_grad = None
    for place_at, (block, head) in enumerate(units):
        if place_at + AHEAD_BACK < len(units):
            ahead.append(products(*units[place_at + AHEAD_BACK]))
        start = block * QBLOCK
        stop = start + QBLOCK
        score, centred = ahead.pop(0)
        prob = jnp.exp(score)
        last = jnp.where(causal, prob[start:], 0.0)
        prob = jnp.concatenate([prob[:start], last], axis=0) if block else last
        score_grad = (prob * centred).astype(BF16)
        scores_all.append(score_grad)
        probs_all.append(prob.astype(BF16))
        part = dot(turned_by_head[head][:, :stop], score_grad)
        query_grad = part if query_grad is None else query_grad + part
        if head == 0:
            continue
        query, grad = loaded[block][:2]
        out_ref[0, start:stop] = (query_grad.T * SCALE).astype(BF16)
        own_query = jnp.concatenate(
            [jnp.where(first, query, zero), jnp.where(first, zero, query)], axis=0
        )
        own_grad = jnp.concatenate(
            [jnp.where(first, grad, zero), jnp.where(first, zero, grad)], axis=0
        )
        key_part = dot(jnp.concatenate(scores_all, axis=1), own_query)
        value_part = dot(jnp.concatenate(probs_all, axis=1), own_grad)
        if block == count - 1:
            key_grad_ref[...] = key_part
            value_grad_ref[...] = value_part
        else:
            key_grad_ref[:stop] += key_part
            value_grad_ref[:stop] += value_part
        probs_all = []
        scores_all = []
        query_grad = None
    out_ref[1] = key_grad_ref[...].astype(BF16)
    out_ref[2] = value_grad_ref[...].astype(BF16)


def self_backward(projected, lengths, grad, exact, logsum, first, count, earlier):
    seq_len = projected.shape[0]
    width = projected.shape[1] // 3
    pairs = width // LANES
    column = lambda offset: pl.BlockSpec((seq_len, LANES), lambda p: (0, p + offset))
    given = [] if earlier is None else [earlier]
    return pl.pallas_call(
        functools.partial(passing, self_backward_kernel, 7, len(given)),
        grid=(count,),
        in_specs=[
            pl.BlockSpec(memory_space=pltpu.SMEM),
            column(first),
            column(pairs + first),
            column(2 * pairs + first),
            column(first),
            column(first),
            pl.BlockSpec((1, 8, seq_len), lambda p: (p + first, 0, 0)),
        ]
        + [pl.BlockSpec(memory_space=pl.ANY)] * len(given),
        out_specs=pl.BlockSpec((3, seq_len, LANES), lambda p: (0, 0, p + first)),
        out_shape=jax.ShapeDtypeStruct((3, seq_len, width), BF16),
        scratch_shapes=[pltpu.VMEM((seq_len, LANES), F32), pltpu.VMEM((seq_len, LANES), F32)],
        input_output_aliases={7: 0} if given else {},
        compiler_params=pltpu.CompilerParams(vmem_limit_bytes=48 * 2**20),
        cost_estimate=cost(12),
        name="self_backward",
    )(lengths, projected, projected, projected, grad, exact, logsum, *given)


def block_diagonal(rows):
    lane = iota((1, WIDE), 1)
    return jnp.concatenate(
        [jnp.where((lane >= h * 64) & (lane < h * 64 + 64), rows, 0) for h in range(4)], axis=0
    )


def take_diagonal(stacked):
    lane = iota((1, WIDE), 1)
    result = stacked[:SPAN]
    for h in range(1, 4):
        result = jnp.where(lane >= h * 64, stacked[h * SPAN : (h + 1) * SPAN], result)
    return result


def slot_bias(ids_ref, neighbour_lengths_ref, span, neigh_len, axis):
    shape = (1, NEIGH * neigh_len) if axis else (NEIGH * neigh_len, 1)
    place = iota(shape, axis)
    first = neighbour_lengths_ref[ids_ref[span * NEIGH]]
    second = neighbour_lengths_ref[ids_ref[span * NEIGH + 1]]
    limit = jnp.where(place < neigh_len, first, neigh_len + second)
    return jnp.where(place < limit, 0.0, NEGATIVE)


def cross_forward_kernel(ids_ref, neighbour_lengths_ref, query_ref, *refs):
    slots, mixed_ref = refs[:-1], refs[-1]
    step = pl.program_id(0)
    neigh_len = slots[0].shape[1]
    width = query_ref.shape[1]
    units = [(span, group) for span in range(SPANS_STEP) for group in range(width // WIDE)]

    def scores(span, group):
        rows = slice(span * SPAN, (span + 1) * SPAN)
        place = slice(group * WIDE, (group + 1) * WIDE)
        queries = block_diagonal(query_ref[rows, place] * jnp.asarray(SCALE, BF16))
        keys = jnp.concatenate([ref[0, :, place] for ref in slots[span * NEIGH :][:NEIGH]], axis=0)
        return dot(queries, keys, NT)

    ahead = [scores(*unit) for unit in units[:AHEAD_CROSS]]
    for place_at, (span, group) in enumerate(units):
        if place_at + AHEAD_CROSS < len(units):
            ahead.append(scores(*units[place_at + AHEAD_CROSS]))
        if group == 0:
            bias = slot_bias(
                ids_ref, neighbour_lengths_ref, step * SPANS_STEP + span, neigh_len, 1
            )
        score = ahead.pop(0) + bias
        expo = jnp.exp(score - jnp.max(score, axis=-1, keepdims=True))
        total = jnp.sum(expo, axis=-1, keepdims=True)
        place = slice(width + group * WIDE, width + (group + 1) * WIDE)
        values = jnp.concatenate(
            [ref[0, :, place] for ref in slots[span * NEIGH :][:NEIGH]], axis=0
        )
        out = dot(expo.astype(BF16), values) / total
        rows = slice(span * SPAN, (span + 1) * SPAN)
        mixed_ref[rows, group * WIDE : (group + 1) * WIDE] = take_diagonal(out).astype(BF16)


def cross_forward(queries, pool_keyval, ids, neighbour_lengths):
    seq_len, width = queries.shape
    neigh_len, both = pool_keyval.shape[1:]
    spans = seq_len // SPAN
    slots = SPANS_STEP * NEIGH
    rows = pl.BlockSpec((SPANS_STEP * SPAN, width), lambda c, ids, lens: (c, 0))
    slot = lambda j: pl.BlockSpec(
        (1, neigh_len, both), lambda c, ids, lens: (ids[c * slots + j], 0, 0)
    )
    return pl.pallas_call(
        cross_forward_kernel,
        grid_spec=pltpu.PrefetchScalarGridSpec(
            num_scalar_prefetch=2,
            grid=(spans // SPANS_STEP,),
            in_specs=[rows] + [slot(j) for j in range(slots)],
            out_specs=rows,
        ),
        out_shape=jax.ShapeDtypeStruct((seq_len, width), BF16),
        compiler_params=pltpu.CompilerParams(vmem_limit_bytes=56 * 2**20),
        cost_estimate=cost(12),
        name="cross_forward",
    )(ids, neighbour_lengths, queries, *[pool_keyval] * slots)


def cross_backward_kernel(
    ids_ref,
    neighbour_lengths_ref,
    query_ref,
    grad_ref,
    key_ref,
    value_ref,
    query_grad_ref,
    key_out_ref,
    value_out_ref,
    key_total,
    value_total,
):
    step = pl.program_id(1)
    neigh_len = key_ref.shape[1]

    @pl.when(step == 0)
    def _():
        key_total[...] = jnp.zeros_like(key_total)
        value_total[...] = jnp.zeros_like(value_total)

    def slots_of(span):
        place = (step * SPANS_STEP + span) * NEIGH
        return [ids_ref[place + slot] for slot in range(NEIGH)]

    def products(span):
        rows = slice(span * SPAN, (span + 1) * SPAN)
        queries = block_diagonal(query_ref[rows] * jnp.asarray(SCALE, BF16))
        grads = block_diagonal(grad_ref[rows])
        keys = jnp.concatenate([key_ref[ident] for ident in slots_of(span)], axis=0)
        values = jnp.concatenate([value_ref[ident] for ident in slots_of(span)], axis=0)
        return (queries, grads, keys, dot(keys, queries, NT), dot(values, grads, NT))

    ahead = [products(span) for span in range(AHEAD_CROSS)]
    for span in range(SPANS_STEP):
        if span + AHEAD_CROSS < SPANS_STEP:
            ahead.append(products(span + AHEAD_CROSS))
        queries, grads, keys, score, prob_grad = ahead.pop(0)
        bias = slot_bias(ids_ref, neighbour_lengths_ref, step * SPANS_STEP + span, neigh_len, 0)
        score = score + bias
        expo = jnp.exp(score - jnp.max(score, axis=0, keepdims=True))
        prob = expo * (1.0 / jnp.sum(expo, axis=0, keepdims=True))
        weighted = prob * prob_grad
        score_grad = (weighted - prob * jnp.sum(weighted, axis=0, keepdims=True)).astype(BF16)
        value_part = dot(prob.astype(BF16), grads)
        key_part = dot(score_grad, queries)
        query_part = dot(score_grad, keys, TN)
        rows = slice(span * SPAN, (span + 1) * SPAN)
        query_grad_ref[rows] = (take_diagonal(query_part) * SCALE).astype(BF16)
        for slot, ident in enumerate(slots_of(span)):
            part = slice(slot * neigh_len, (slot + 1) * neigh_len)
            key_total[ident] += key_part[part]
            value_total[ident] += value_part[part]

    @pl.when(step == pl.num_programs(1) - 1)
    def _():
        key_out_ref[...] = key_total[...].astype(BF16)
        value_out_ref[...] = value_total[...].astype(BF16)


def cross_backward(queries, grads, pool_keyval, ids, neighbour_lengths, first, count, earlier):
    seq_len, width = queries.shape
    pool_count, neigh_len, _ = pool_keyval.shape
    spans = seq_len // SPAN
    groups = width // WIDE
    rows = pl.BlockSpec((SPANS_STEP * SPAN, WIDE), lambda g, c, ids, lens: (c, g + first))
    pool = lambda offset: pl.BlockSpec(
        (pool_count, neigh_len, WIDE), lambda g, c, ids, lens: (0, 0, g + first + offset)
    )
    pool_shape = jax.ShapeDtypeStruct((pool_count, neigh_len, width), BF16)
    given = [] if earlier is None else list(earlier)
    return pl.pallas_call(
        functools.partial(passing, cross_backward_kernel, 6, len(given)),
        grid_spec=pltpu.PrefetchScalarGridSpec(
            num_scalar_prefetch=2,
            grid=(count, spans // SPANS_STEP),
            in_specs=[rows, rows, pool(0), pool(groups)]
            + [pl.BlockSpec(memory_space=pl.ANY)] * len(given),
            out_specs=[rows, pool(0), pool(0)],
            scratch_shapes=[
                pltpu.VMEM((pool_count, neigh_len, WIDE), F32),
                pltpu.VMEM((pool_count, neigh_len, WIDE), F32),
            ],
        ),
        out_shape=[jax.ShapeDtypeStruct((seq_len, width), BF16), pool_shape, pool_shape],
        input_output_aliases={6 + i: i for i in range(len(given))},
        compiler_params=pltpu.CompilerParams(vmem_limit_bytes=56 * 2**20),
        cost_estimate=cost(15),
        name="cross_backward",
    )(ids, neighbour_lengths, queries, grads, pool_keyval, pool_keyval, *given)

AXES = ("fsdp", "dp")
PIECES = 2
COPY_ROWS = 48
VMEM_FOLD = 32


def bits_of(size):
    return [1 << i for i in range(size.bit_length() - 1)]


def index_bits(count):
    return [1 << i for i in range(count.bit_length() - 2, -1, -1)]


class Line:
    def __init__(self):
        self.noted = []

    def note(self, *values):
        self.noted = [values[0]]

    def also(self, value):
        self.noted.append(value)

    def after(self, value):
        return self.after_all([value])[0]

    def after_all(self, values):
        if not self.noted:
            return values
        return lax.optimization_barrier((*values, *self.noted))[: len(values)]


class Plan:
    def __init__(self, rows, line):
        self.line = line
        self.inner = lax.axis_size("dp")
        self.outer = lax.axis_size("fsdp")
        self.count = self.inner * self.outer
        self.rows = rows
        self.core = [self.inner] if self.outer > 1 else []
        self.halves = 2 if self.core else 1
        self.across = self.outer // self.halves
        self.stripe = self.inner * rows
        self.half_rows = self.across * self.stripe
        self.copy_rows = min(self.stripe, COPY_ROWS)
        self.me = lax.axis_index(AXES)
        across = [bit * self.inner for bit in bits_of(self.outer)[1:]]
        along = bits_of(self.inner)
        near, far = along[: len(across)], along[len(across) :]
        self.orders = (far + near + across, far + across + near)
        self.natural = [mask for mask in index_bits(self.count) if mask not in self.core]
        self.odd = self.bit(self.core[0]) if self.core else jnp.zeros((), jnp.int32)
        self.odd_word = self.odd.reshape(1)
        self.steps = list(zip(*self.orders))
        self.places = self.arrival_places()

    def bit(self, mask):
        return (self.me // mask) % 2

    def by_core(self, even, odd):
        return jnp.where(self.odd == 0, even, odd)

    def exchange(self, values, masks):
        even, odd = masks
        pairs = []
        for index in range(self.count):
            is_odd = bool(self.core) and (index // self.core[0]) % 2 == 1
            pairs.append((index, index ^ (odd if is_odd else even)))
        return lax.ppermute(values, AXES, pairs)

    def swap(self, values):
        return self.exchange(values, (self.core[0], self.core[0])) if self.core else values

    def weight_of(self, mask):
        return 1 << (len(self.natural) - 1 - self.natural.index(mask))

    def arrival_places(self):
        blocks = jnp.arange(1 << len(self.natural), dtype=jnp.int32)
        found = []
        for order in self.orders:
            target = jnp.zeros_like(blocks)
            for place_at, mask in enumerate(order):
                flag = ((blocks >> place_at) & 1) ^ self.bit(mask)
                target = target + flag * self.weight_of(mask)
            found.append(target)
        return self.by_core(found[0], found[1])

    def fold_places(self, step):
        found = []
        for order in self.orders:
            gone = order[::-1][:step]
            left = [mask for mask in self.natural if mask not in gone]
            mask = order[::-1][step]
            high = 1 << (len(left) - 1 - left.index(mask))
            index = jnp.arange(1 << (len(left) - 1), dtype=jnp.int32)
            kept = (index // high) * (2 * high) + index % high
            own = self.bit(mask)
            found.append((kept + (1 - own) * high, kept + own * high))
        return tuple(self.by_core(found[0][i], found[1][i]) for i in range(2))


def reorder_kernel(places_ref, *refs):
    parts, (out_ref, buffer, sems) = refs[:-3], refs[-3:]
    blocks = buffer.shape[0]
    share = blocks // len(parts)

    def copies(block):
        return pltpu.make_async_copy(
            parts[block // share].at[block % share], buffer.at[places_ref[block]], sems.at[block]
        )

    for block in range(blocks):
        copies(block).start()
    for block in range(blocks):
        copies(block).wait()
    pltpu.sync_copy(buffer, out_ref)


def reorder(plan, parts):
    blocks = sum(part.shape[0] for part in parts)
    shape = (blocks,) + parts[0].shape[1:]
    return pl.pallas_call(
        reorder_kernel,
        in_specs=[pl.BlockSpec(memory_space=pltpu.SMEM)]
        + [pl.BlockSpec(memory_space=pl.ANY)] * len(parts),
        out_specs=pl.BlockSpec(memory_space=pl.ANY),
        out_shape=jax.ShapeDtypeStruct(shape, BF16),
        scratch_shapes=[pltpu.VMEM(shape, BF16), pltpu.SemaphoreType.DMA((blocks,))],
        compiler_params=pltpu.CompilerParams(vmem_limit_bytes=VMEM_FOLD * 2**20),
        cost_estimate=cost(0.1),
        name="reorder_blocks",
    )(plan.places, *parts)


class Gather:
    def __init__(self, plan, shard, pieces=PIECES):
        self.plan = plan
        self.pieces = pieces if plan.core else 1
        self.held = shard[None]
        self.at = 0
        self.other = None
        self.halves = None

    def launch(self):
        plan = self.plan
        self.held = plan.line.after(self.held)
        plan.line.also(self.held)
        if self.at < len(plan.steps):
            self.other = plan.exchange(self.held, plan.steps[self.at])
        else:
            blocks = self.held.shape[0] // self.pieces
            self.other = [
                plan.swap(self.held[i * blocks : (i + 1) * blocks]) for i in range(self.pieces)
            ]

    def land(self):
        plan = self.plan
        if self.at < len(plan.steps):
            other = plan.line.after(self.other)
            self.at += 1
            if self.at == len(plan.steps):
                self.held = reorder(plan, [self.held, other])
            else:
                self.held = jnp.concatenate([self.held, other], axis=0)
            plan.line.note(self.held)
        else:
            others = plan.line.after_all(self.other)
            plan.line.note(others[0])
            columns = self.held.shape[-1]
            self.halves = [self.held.reshape(plan.half_rows, columns)]
            self.halves += [other.reshape(-1, columns) for other in others]

    def done(self):
        return self.halves is not None

    def finish(self):
        while not self.done():
            self.land()
            if not self.done():
                self.launch()
        return self.halves


def fold_kernel(sent_places, kept_places, *refs):
    half = len(refs) // 2 - 1
    sent_in, kept_in, (sent_ref, kept_ref) = refs[:half], refs[half : 2 * half], refs[2 * half :]
    for source, target in ((sent_in, sent_ref), (kept_in, kept_ref)):
        total = source[0][...].astype(F32)
        for part in source[1:]:
            total = total + part[...].astype(F32)
        target[...] = total.astype(BF16)


def fold(places, parts):
    blocks, rows, columns = parts[0].shape
    shape = jax.ShapeDtypeStruct((blocks // 2, rows, columns), BF16)
    out = pl.BlockSpec((1, rows, columns), lambda i, sent, kept: (i, 0, 0))
    sent = pl.BlockSpec((1, rows, columns), lambda i, sent, kept: (sent[i], 0, 0))
    kept = pl.BlockSpec((1, rows, columns), lambda i, sent, kept: (kept[i], 0, 0))
    return pl.pallas_call(
        fold_kernel,
        grid_spec=pltpu.PrefetchScalarGridSpec(
            num_scalar_prefetch=2,
            grid=(blocks // 2,),
            in_specs=[sent] * len(parts) + [kept] * len(parts),
            out_specs=[out, out],
        ),
        out_shape=[shape, shape],
        compiler_params=pltpu.CompilerParams(vmem_limit_bytes=VMEM_FOLD * 2**20),
        cost_estimate=cost(0.1),
        name="fold_blocks",
    )(*places, *parts, *parts)


class Scatter:
    def __init__(self, plan, keep, send):
        self.plan = plan
        self.columns = keep.shape[1]
        shape = (1 << len(plan.natural), plan.rows, self.columns)
        self.kept = keep.reshape(shape)
        self.sent = send.reshape(shape) if plan.core else None
        self.at = -1
        self.other = None
        self.total = None

    def launch(self):
        plan = self.plan
        if self.sent is None:
            return
        self.sent = plan.line.after(self.sent)
        plan.line.also(self.sent)
        if self.at < 0:
            self.other = plan.swap(self.sent)
        else:
            self.other = plan.exchange(self.sent, plan.steps[::-1][self.at])

    def land(self):
        plan = self.plan
        parts = [self.kept] if self.other is None else [self.kept, plan.line.after(self.other)]
        self.at += 1
        if self.at < len(plan.steps):
            self.sent, self.kept = fold(plan.fold_places(self.at), parts)
            plan.line.note(self.sent)
        else:
            total = parts[0].astype(F32)
            for part in parts[1:]:
                total = total + part.astype(F32)
            self.total = total.reshape(plan.rows, self.columns)
            plan.line.note(self.total)

    def done(self):
        return self.total is not None

    def finish(self):
        while not self.done():
            self.land()
            if not self.done():
                self.launch()
        return self.total


def bundled(kernel, *spans):
    def call(*refs):
        refs = list(refs)
        for place, count in sorted(spans, reverse=True):
            refs[place : place + count] = [tuple(refs[place : place + count])]
        return kernel(*refs)

    return call


def column_copies(plan, odd, held_ref, other_refs, target, sems, start, width, rows=None):
    copies = []

    def add(ref, at, rows, first, half):
        across, rest = divmod(first, plan.stripe)
        place = across * plan.halves * plan.stripe + rest
        if plan.halves > 1:
            place = place + half * plan.stripe
            if plan.stripe % 16 == 0 and rest % 16 == 0:
                place = pl.multiple_of(place, 16)
        copies.append(
            pltpu.make_async_copy(
                ref.at[pl.ds(at, rows), pl.ds(start, width)],
                target.at[pl.ds(place, rows), :],
                sems.at[len(copies)],
            )
        )

    rows = rows or plan.copy_rows
    for first in range(0, plan.half_rows, rows):
        add(held_ref, first, rows, first, odd)
    if plan.halves > 1:
        for first in range(0, plan.half_rows, rows):
            piece = other_refs[0].shape[0]
            step = min(rows, piece)
            for rest in range(first, first + rows, step):
                add(other_refs[rest // piece], rest % piece, step, rest, 1 - odd)
    return copies


def store_halves(plan, odd, result, keep_ref, send_ref, columns):
    for across in range(plan.across):
        rows = slice(across * plan.stripe, (across + 1) * plan.stripe)
        parts = []
        for half in range(plan.halves):
            first = (across * plan.halves + half) * plan.stripe
            parts.append(result[first : first + plan.stripe])
        if plan.halves == 1:
            keep_ref[rows, columns] = parts[0].astype(BF16)
        else:
            keep_ref[rows, columns] = jnp.where(odd == 0, parts[0], parts[1]).astype(BF16)
            send_ref[rows, columns] = jnp.where(odd == 0, parts[1], parts[0]).astype(BF16)

ROWS = 512
FEED_ROWS = 256
BACK_ROWS = 256
POOL_BLOCK = 1024
BACK_BLOCK = 512
MEBI = 2**20
ANYWHERE = pl.BlockSpec(memory_space=pl.ANY)
SCALAR = pl.BlockSpec(memory_space=pltpu.SMEM)


def norm_parts(values):
    centre = jnp.mean(values, axis=-1, keepdims=True)
    centred = values - centre
    spread = jnp.mean(centred * centred, axis=-1, keepdims=True)
    inverse = lax.rsqrt(spread + EPSILON)
    return (centred * inverse, inverse)


def norm_back(values, gain, upstream):
    unit, inverse = norm_parts(values)
    gain_term = jnp.sum(upstream * unit, axis=0, keepdims=True)
    shift_term = jnp.sum(upstream, axis=0, keepdims=True)
    inner = upstream * gain
    mean_inner = jnp.mean(inner, axis=-1, keepdims=True)
    mean_both = jnp.mean(inner * unit, axis=-1, keepdims=True)
    return (inverse * (inner - mean_inner - unit * mean_both), gain_term, shift_term)


def add_terms(step, target_ref, gain_term, shift_term):
    @pl.when(step == 0)
    def _():
        target_ref[...] = jnp.zeros_like(target_ref)

    target_ref[0:1] += gain_term
    target_ref[1:2] += shift_term


def start_all(copies):
    for copy in copies:
        copy.start()


def wait_all(copies):
    for copy in copies:
        copy.wait()


def row_block(columns, last=None, block=ROWS):
    if last is None:
        return pl.BlockSpec((block, columns), lambda i: (i, 0))
    return pl.BlockSpec((block, columns), lambda i: (jnp.minimum(i, last), 0))


def params(megabytes):
    return pltpu.CompilerParams(vmem_limit_bytes=megabytes * MEBI)


def copy_sems(plan, *sets):
    return pltpu.SemaphoreType.DMA(sets + (plan.halves * plan.half_rows // min(plan.copy_rows, 48),))


def pool_kernel(plan, odd_ref, rows_ref, held_ref, other_ref, out_ref, weight_ref, sems):
    width = weight_ref.shape[1]

    @pl.when(pl.program_id(0) == 0)
    def _():
        copies = column_copies(plan, odd_ref[0], held_ref, other_ref, weight_ref, sems, 0, width)
        start_all(copies)
        wait_all(copies)

    out_ref[...] = dot(rows_ref[...], weight_ref[...]).astype(BF16)


def pool_project(plan, encoded, halves):
    rows, width = encoded.shape
    block = POOL_BLOCK
    return pl.pallas_call(
        bundled(functools.partial(pool_kernel, plan), (3, len(halves) - 1)),
        grid=(rows // block,),
        in_specs=[SCALAR, pl.BlockSpec((block, width), lambda i: (i, 0))]
        + [ANYWHERE] * len(halves),
        out_specs=[
            pl.BlockSpec((block, 2 * width), lambda i: (i, 0)),
            pl.BlockSpec((width, 2 * width), lambda i: (0, 0)),
        ],
        out_shape=[
            jax.ShapeDtypeStruct((rows, 2 * width), BF16),
            jax.ShapeDtypeStruct((width, 2 * width), BF16),
        ],
        scratch_shapes=[copy_sems(plan)],
        compiler_params=params(40),
        cost_estimate=cost(13),
        name="pool_project",
    )(plan.odd_word, encoded, *halves)


def project_kernel(
    plan,
    odd_ref,
    tokens_ref,
    held_ref,
    other_ref,
    unit_ref,
    projected_ref,
    vectors_ref,
    columns_ref,
    weight,
    pack,
    sems,
):
    width = tokens_ref.shape[1]

    @pl.when(pl.program_id(0) == 0)
    def _():
        copies = column_copies(plan, odd_ref[0], held_ref, other_ref, weight, sems.at[0], 0, 3 * width)
        copies += column_copies(
            plan, odd_ref[0], held_ref, other_ref, pack, sems.at[1], 3 * width, LANES
        )
        start_all(copies)
        wait_all(copies)
        columns_ref[...] = pack[...].astype(F32)
        vectors_ref[...] = columns_ref[...].T[:8]

    unit = norm_parts(tokens_ref[...].astype(F32))[0]
    first_in = (unit * vectors_ref[0:1] + vectors_ref[1:2]).astype(BF16)
    unit_ref[...] = unit.astype(BF16)
    projected_ref[...] = dot(first_in, weight[...]).astype(BF16)


def project(plan, tokens, halves):
    rows, width = tokens.shape
    return pl.pallas_call(
        bundled(functools.partial(project_kernel, plan), (3, len(halves) - 1)),
        grid=(rows // ROWS,),
        in_specs=[SCALAR, row_block(width)] + [ANYWHERE] * len(halves),
        out_specs=[
            row_block(width),
            row_block(3 * width),
            pl.BlockSpec((8, width), lambda i: (0, 0)),
            pl.BlockSpec((width, LANES), lambda i: (0, 0)),
            pl.BlockSpec((width, 3 * width), lambda i: (0, 0)),
        ],
        out_shape=[
            jax.ShapeDtypeStruct((rows, width), BF16),
            jax.ShapeDtypeStruct((rows, 3 * width), BF16),
            jax.ShapeDtypeStruct((8, width), F32),
            jax.ShapeDtypeStruct((width, LANES), F32),
            jax.ShapeDtypeStruct((width, 3 * width), BF16),
        ],
        scratch_shapes=[
            pltpu.VMEM((width, LANES), BF16),
            copy_sems(plan, 2),
        ],
        compiler_params=params(40),
        cost_estimate=cost(5),
        name="project",
    )(plan.odd_word, tokens, *halves)


def middle_kernel(
    plan,
    starts,
    odd_ref,
    tokens_ref,
    mixed_ref,
    vectors_ref,
    held_ref,
    other_ref,
    after_ref,
    second_in_ref,
    queries_ref,
    out_weight,
    query_weight,
    sems,
):
    width = tokens_ref.shape[1]

    @pl.when(pl.program_id(0) == 0)
    def _():
        copies = []
        for place_at, target in enumerate((out_weight, query_weight)):
            copies += column_copies(
                plan, odd_ref[0], held_ref, other_ref, target, sems.at[place_at], starts[place_at], width
            )
        start_all(copies)
        wait_all(copies)

    after = tokens_ref[...].astype(F32) + dot(mixed_ref[...], out_weight[...])
    after_ref[...] = after
    unit = norm_parts(after)[0]
    second_in = (unit * vectors_ref[2:3] + vectors_ref[3:4]).astype(BF16)
    second_in_ref[...] = second_in
    queries_ref[...] = dot(second_in, query_weight[...]).astype(BF16)


def middle(plan, starts, tokens, mixed, vectors, halves):
    rows, width = tokens.shape
    return pl.pallas_call(
        bundled(functools.partial(middle_kernel, plan, starts), (5, len(halves) - 1)),
        grid=(rows // ROWS,),
        in_specs=[
            SCALAR,
            row_block(width),
            row_block(width),
            pl.BlockSpec((8, width), lambda i: (0, 0)),
        ]
        + [ANYWHERE] * len(halves),
        out_specs=[row_block(width)] * 3 + [pl.BlockSpec((width, width), lambda i: (0, 0))] * 2,
        out_shape=[
            jax.ShapeDtypeStruct((rows, width), F32),
            jax.ShapeDtypeStruct((rows, width), BF16),
            jax.ShapeDtypeStruct((rows, width), BF16),
            jax.ShapeDtypeStruct((width, width), BF16),
            jax.ShapeDtypeStruct((width, width), BF16),
        ],
        scratch_shapes=[
            copy_sems(plan, 2),
        ],
        compiler_params=params(40),
        cost_estimate=cost(0.5),
        name="middle",
    )(plan.odd_word, tokens, mixed, vectors, *halves)


def segments_kernel(moves, in_ref, out_ref):
    lane = iota((1, LANES), 1)
    tiles = {}
    for place in range(out_ref.shape[1] // LANES):
        result = None
        for source, shift, first, last in moves[place]:
            if source not in tiles:
                tiles[source] = in_ref[:, source * LANES : (source + 1) * LANES].astype(F32)
            tile = pltpu.roll(tiles[source], shift, 1) if shift else tiles[source]
            if result is None:
                result = tile
            else:
                result = jnp.where((lane >= first) & (lane < last), tile, result)
        out_ref[:, place * LANES : (place + 1) * LANES] = result.astype(out_ref.dtype)


def swap_segments(matrix, outer, inner, size):
    rows, columns = matrix.shape
    moves = [[] for _ in range(columns // LANES)]
    for i in range(outer):
        for j in range(inner):
            source = (i * inner + j) * size
            target = (j * outer + i) * size
            done = 0
            while done < size:
                at, to = source + done, target + done
                count = min(size - done, LANES - at % LANES, LANES - to % LANES)
                shift = (to - at) % LANES
                moves[to // LANES].append((at // LANES, shift, to % LANES, to % LANES + count))
                done += count
    return pl.pallas_call(
        functools.partial(segments_kernel, moves),
        in_specs=[pl.BlockSpec(memory_space=pltpu.VMEM)],
        out_specs=pl.BlockSpec(memory_space=pltpu.VMEM),
        out_shape=jax.ShapeDtypeStruct((rows, columns), matrix.dtype),
        compiler_params=params(24),
        cost_estimate=cost(2),
        name="swap_segments",
    )(matrix)


GELU_SCALE = 0.7978845608028654
GELU_CUBE = 0.044715
TERMS_STEP = 3


def gelu_both(values):
    square = values * values
    bent = jnp.tanh(values * (GELU_SCALE + (GELU_SCALE * GELU_CUBE) * square))
    half = 0.5 + 0.5 * bent
    result = values * half
    slope = 2.0 * GELU_SCALE + (6.0 * GELU_SCALE * GELU_CUBE) * square
    return (result, half * (1.0 + (values - result) * slope))


def feed_kernel(
    plan,
    out_start,
    row_steps,
    odd_ref,
    after_ref,
    mixed_ref,
    cotangent_ref,
    vectors_ref,
    feed_held_ref,
    feed_other_ref,
    held_ref,
    other_ref,
    block_ref,
    grad_ref,
    mixed_grad_ref,
    terms_ref,
    keep_ref,
    send_ref,
    out_matrix,
    weights,
    lefts,
    rights,
    sems,
):
    step = pl.program_id(0)
    width = after_ref.shape[1]
    parts = weights.shape[1] // width // 2

    def copies():
        return column_copies(
            plan,
            odd_ref[0],
            held_ref,
            other_ref,
            out_matrix,
            sems.at[0],
            out_start,
            width,
            plan.stripe,
        ) + column_copies(
            plan,
            odd_ref[0],
            feed_held_ref,
            feed_other_ref,
            weights,
            sems.at[1],
            0,
            2 * parts * width,
            plan.stripe,
        )

    def ready(index):
        if index == 2 * parts:
            return out_matrix[...]
        return weights[:, index * width : (index + 1) * width]

    def rows_of(place_at):
        mixed = mixed_ref[...]
        cotangent = cotangent_ref[...]
        out_weight = ready(2 * parts)
        after_cross = after_ref[...] + dot(mixed, out_weight)
        unit, inverse = norm_parts(after_cross)
        gain = vectors_ref[4:5]
        third_in = (unit * gain + vectors_ref[5:6]).astype(BF16)
        up = ready(0)
        before = dot(third_in, up)
        lefts[parts, :, place_at] = third_in.T
        lefts[parts + 1, :, place_at] = mixed.T
        rights[0, place_at] = cotangent
        result = after_cross
        upstream = jnp.zeros_like(after_cross)
        for part in range(parts):
            down = ready(parts + part)
            back = dot(cotangent, down, NT)
            hidden, slope = gelu_both(before)
            hidden = hidden.astype(BF16)
            if part + 1 < parts:
                next_up = ready(part + 1)
                before = dot(third_in, next_up)
            result = result + dot(hidden, down)
            lefts[part, :, place_at] = hidden.T
            hidden_grad = (slope * back).astype(BF16)
            rights[1 + part, place_at] = hidden_grad
            upstream = upstream + dot(hidden_grad, up, NT)
            if part + 1 < parts:
                up = next_up
        block_ref[...] = result.astype(BF16)
        inner = upstream * gain
        mean_inner = jnp.mean(inner, axis=-1, keepdims=True)
        mean_both = jnp.mean(inner * unit, axis=-1, keepdims=True)
        grad = cotangent.astype(F32) + inverse * (inner - mean_inner - unit * mean_both)
        add_terms(
            step,
            terms_ref,
            jnp.sum(upstream * unit, axis=0, keepdims=True),
            jnp.sum(upstream, axis=0, keepdims=True),
        )
        grad_ref[...] = grad
        rounded = grad.astype(BF16)
        rights[parts + 1, place_at] = rounded
        mixed_grad_ref[...] = dot(rounded, out_weight, NT).astype(BF16)

    @pl.when(step == 0)
    def _():
        start_all(copies())
        wait_all(copies())

    @pl.when(step < row_steps)
    def _():
        rows_of(pl.ds(pl.multiple_of(step * FEED_ROWS, FEED_ROWS), FEED_ROWS))

    @pl.when(step >= row_steps)
    def _():
        for turn in range(TERMS_STEP):
            term = (step - row_steps) * TERMS_STEP + turn
            left = jnp.where(term < parts, term, jnp.where(term < 2 * parts, parts, parts + 1))
            right = jnp.where(term < parts, 0, term - parts + 1)
            result = dot(lefts[left], rights[right])
            columns = slice(turn * width, (turn + 1) * width)
            store_halves(plan, odd_ref[0], result, keep_ref, send_ref, columns)


def feed(plan, out_start, after, mixed, cotangent, vectors, feed_halves, halves):
    rows, width = after.shape
    parts = feed_halves[0].shape[1] // width // 2
    terms = 2 * parts + 1
    steps = rows // FEED_ROWS
    last = steps - 1
    rows_in = row_block(width, last, FEED_ROWS)
    whole = pl.BlockSpec((8, width), lambda i: (0, 0))
    slab = pl.BlockSpec(
        (plan.half_rows, TERMS_STEP * width), lambda i: (0, jnp.maximum(i - steps, 0))
    )
    slab_shape = jax.ShapeDtypeStruct((plan.half_rows, terms * width), BF16)
    return pl.pallas_call(
        bundled(
            functools.partial(feed_kernel, plan, out_start, steps),
            (6, len(feed_halves) - 1),
            (6 + len(feed_halves), len(halves) - 1),
        ),
        grid=(steps + terms // TERMS_STEP,),
        in_specs=[SCALAR, rows_in, rows_in, rows_in, whole]
        + [ANYWHERE] * (len(feed_halves) + len(halves)),
        out_specs=[rows_in, rows_in, rows_in, whole, slab, slab],
        out_shape=[
            jax.ShapeDtypeStruct((rows, width), BF16),
            jax.ShapeDtypeStruct((rows, width), F32),
            jax.ShapeDtypeStruct((rows, width), BF16),
            jax.ShapeDtypeStruct((8, width), F32),
            slab_shape,
            slab_shape,
        ],
        scratch_shapes=[
            pltpu.VMEM((width, width), BF16),
            pltpu.VMEM((width, 2 * parts * width), BF16),
            pltpu.VMEM((parts + 2, width, rows), BF16),
            pltpu.VMEM((parts + 2, rows, width), BF16),
            copy_sems(plan, 2),
        ],
        compiler_params=params(60),
        cost_estimate=cost(50),
        name="feed_forward",
    )(plan.odd_word, after, mixed, cotangent, vectors, *feed_halves, *halves)


def second_kernel(
    plan,
    row_steps,
    odd_ref,
    after_ref,
    grad_in_ref,
    query_grad_ref,
    second_in_ref,
    mixed_ref,
    vectors_ref,
    out_weight,
    query_weight,
    grad_ref,
    attend_ref,
    terms_ref,
    keep_ref,
    send_ref,
    lefts,
    rights,
):
    step = pl.program_id(0)
    width = after_ref.shape[1]

    place_at = pl.ds(pl.multiple_of(step * BACK_ROWS, BACK_ROWS), BACK_ROWS)
    query_grad = query_grad_ref[...]
    back, gain_term, shift_term = norm_back(
        after_ref[...], vectors_ref[2:3], dot(query_grad, query_weight[...], NT)
    )
    lefts[0, :, place_at] = second_in_ref[...].T
    lefts[1, :, place_at] = mixed_ref[...].T
    rights[0, place_at] = query_grad
    add_terms(step, terms_ref, gain_term, shift_term)
    grad = grad_in_ref[...] + back
    grad_ref[...] = grad
    rounded = grad.astype(BF16)
    attend_ref[...] = dot(rounded, out_weight[...], NT).astype(BF16)
    rights[1, place_at] = rounded

    @pl.when(step == row_steps - 1)
    def _():
        for term in range(2):
            result = dot(lefts[term], rights[term])
            columns = slice(term * width, (term + 1) * width)
            store_halves(plan, odd_ref[0], result, keep_ref, send_ref, columns)


def second_back(
    plan, after, grad_in, query_grad, second_in, mixed, vectors, out_weight, query_weight
):
    rows, width = after.shape
    steps = rows // BACK_ROWS
    rows_in = row_block(width, None, BACK_ROWS)
    whole = pl.BlockSpec((8, width), lambda i: (0, 0))
    matrix = pl.BlockSpec((width, width), lambda i: (0, 0))
    slab = pl.BlockSpec((plan.half_rows, 2 * width), lambda i: (0, 0))
    slab_shape = jax.ShapeDtypeStruct((plan.half_rows, 2 * width), BF16)
    return pl.pallas_call(
        functools.partial(second_kernel, plan, steps),
        grid=(steps,),
        in_specs=[SCALAR] + [rows_in] * 5 + [whole, matrix, matrix],
        out_specs=[rows_in, rows_in, whole, slab, slab],
        out_shape=[
            jax.ShapeDtypeStruct((rows, width), F32),
            jax.ShapeDtypeStruct((rows, width), BF16),
            jax.ShapeDtypeStruct((8, width), F32),
            slab_shape,
            slab_shape,
        ],
        scratch_shapes=[
            pltpu.VMEM((2, width, rows), BF16),
            pltpu.VMEM((2, rows, width), BF16),
        ],
        compiler_params=params(48),
        cost_estimate=cost(12),
        name="second_back",
    )(plan.odd_word, after, grad_in, query_grad, second_in, mixed, vectors, out_weight, query_weight)


def first_terms_kernel(
    plan,
    odd_ref,
    unit_ref,
    projected_grad_ref,
    columns_ref,
    second_terms_ref,
    third_terms_ref,
    weight,
    keep_ref,
    send_ref,
    terms,
):
    part = pl.program_id(0)
    width = unit_ref.shape[1]

    @pl.when(part == 0)
    def _():
        terms[...] = jnp.zeros_like(terms)

    grads = projected_grad_ref[0]
    plain = dot(unit_ref[...], grads, TN)
    sums = jnp.sum(grads.astype(F32), axis=0, keepdims=True)
    gain = columns_ref[:, 0:1]
    shift = columns_ref[:, 1:2]
    place = pl.ds(pl.multiple_of(part * width, LANES), width)
    store_halves(plan, odd_ref[0], gain * plain + shift * sums, keep_ref, send_ref, place)
    matrix = weight[...].astype(F32)
    terms[:, 0:1] += jnp.sum(matrix * plain, axis=1, keepdims=True)
    terms[:, 1:2] += jnp.sum(matrix * sums, axis=1, keepdims=True)

    @pl.when(part == 2)
    def _():
        rows = jnp.concatenate(
            [
                jnp.zeros((2, width), F32),
                second_terms_ref[0:2],
                third_terms_ref[0:2],
                jnp.zeros((LANES - 6, width), F32),
            ],
            axis=0,
        )
        lane = iota((1, LANES), 1)
        result = jnp.where(lane < 2, terms[...], rows.T)
        place = slice(3 * width, 3 * width + LANES)
        store_halves(plan, odd_ref[0], result, keep_ref, send_ref, place)


def first_terms(plan, unit, projected_grad, columns, second_terms, third_terms, weight):
    rows, width = unit.shape
    whole = pl.BlockSpec((8, width), lambda i: (0, 0))
    slab = pl.BlockSpec((plan.half_rows, 3 * width + LANES), lambda i: (0, 0))
    slab_shape = jax.ShapeDtypeStruct((plan.half_rows, 3 * width + LANES), BF16)
    return pl.pallas_call(
        functools.partial(first_terms_kernel, plan),
        grid=(3,),
        in_specs=[
            SCALAR,
            pl.BlockSpec((rows, width), lambda i: (0, 0)),
            pl.BlockSpec((1, rows, width), lambda i: (i, 0, 0)),
            pl.BlockSpec((width, LANES), lambda i: (0, 0)),
            whole,
            whole,
            pl.BlockSpec((width, width), lambda i: (0, i)),
        ],
        out_specs=[slab, slab],
        out_shape=[slab_shape, slab_shape],
        scratch_shapes=[
            pltpu.VMEM((width, LANES), F32),
        ],
        compiler_params=params(56),
        cost_estimate=cost(8),
        name="first_terms",
    )(plan.odd_word, unit, projected_grad, columns, second_terms, third_terms, weight)


def first_rows_kernel(
    tokens_ref,
    grad_in_ref,
    projected_grad_ref,
    vectors_ref,
    weight,
    grad_ref,
):
    width = tokens_ref.shape[1]

    upstream = None
    for part in range(3):
        product = dot(projected_grad_ref[part], weight[:, part * width : (part + 1) * width], NT)
        upstream = product if upstream is None else upstream + product
    unit, inverse = norm_parts(tokens_ref[...].astype(F32))
    inner = upstream * vectors_ref[0:1]
    mean_inner = jnp.mean(inner, axis=-1, keepdims=True)
    mean_both = jnp.mean(inner * unit, axis=-1, keepdims=True)
    grad_ref[...] = grad_in_ref[...] + inverse * (inner - mean_inner - unit * mean_both)


def first_rows(tokens, grad_in, projected_grad, vectors, weight):
    rows, width = tokens.shape
    rows_in = row_block(width, None, FEED_ROWS)
    return pl.pallas_call(
        first_rows_kernel,
        grid=(rows // FEED_ROWS,),
        in_specs=[
            rows_in,
            rows_in,
            pl.BlockSpec((3, FEED_ROWS, width), lambda i: (0, i, 0)),
            pl.BlockSpec((8, width), lambda i: (0, 0)),
            pl.BlockSpec((width, 3 * width), lambda i: (0, 0)),
        ],
        out_specs=rows_in,
        out_shape=jax.ShapeDtypeStruct((rows, width), F32),
        compiler_params=params(52),
        cost_estimate=cost(8),
        name="first_rows",
    )(tokens, grad_in, projected_grad, vectors, weight)


def keyval_kernel(
    plan, odd_ref, rows_ref, key_ref, value_ref, keep_ref, send_ref, key_total, value_total
):
    step = pl.program_id(0)
    width = rows_ref.shape[1]
    turned = rows_ref[...].T
    key_part = dot(turned, key_ref[...])
    value_part = dot(turned, value_ref[...])

    @pl.when(step == 0)
    def _():
        key_total[...] = key_part
        value_total[...] = value_part

    @pl.when(step > 0)
    def _():
        key_total[...] += key_part
        value_total[...] += value_part

    @pl.when(step == pl.num_programs(0) - 1)
    def _():
        for place_at, total in enumerate((key_total, value_total)):
            columns = slice(place_at * width, (place_at + 1) * width)
            store_halves(plan, odd_ref[0], total[...], keep_ref, send_ref, columns)


def keyval_terms(plan, encoded, pool_keys, pool_values):
    rows, width = encoded.shape
    block = 2048
    rows_in = pl.BlockSpec((block, width), lambda i: (i, 0))
    slab = pl.BlockSpec((plan.half_rows, 2 * width), lambda i: (0, 0))
    slab_shape = jax.ShapeDtypeStruct((plan.half_rows, 2 * width), BF16)
    return pl.pallas_call(
        functools.partial(keyval_kernel, plan),
        grid=(rows // block,),
        in_specs=[SCALAR, rows_in, rows_in, rows_in],
        out_specs=[slab, slab],
        out_shape=[slab_shape, slab_shape],
        scratch_shapes=[pltpu.VMEM((width, width), F32), pltpu.VMEM((width, width), F32)],
        compiler_params=params(48),
        cost_estimate=cost(14),
        name="keyval_terms",
    )(plan.odd_word, encoded, pool_keys, pool_values)


def neighbours_kernel(key_ref, value_ref, weight_ref, out_ref):
    width = key_ref.shape[1]
    out_ref[...] = dot(key_ref[...], weight_ref[:, :width], NT) + dot(
        value_ref[...], weight_ref[:, width:], NT
    )


def neighbours_back(pool_keys, pool_values, weight, first, count, earlier):
    rows, width = pool_keys.shape
    block = BACK_BLOCK
    rows_in = pl.BlockSpec((block, width), lambda i: (i + first, 0))
    given = [] if earlier is None else [earlier]
    return pl.pallas_call(
        functools.partial(passing, neighbours_kernel, 3, len(given)),
        grid=(count,),
        in_specs=[rows_in, rows_in, pl.BlockSpec((width, 2 * width), lambda i: (0, 0))]
        + [ANYWHERE] * len(given),
        out_specs=rows_in,
        out_shape=jax.ShapeDtypeStruct((rows, width), F32),
        input_output_aliases={3: 0} if given else {},
        compiler_params=params(40),
        cost_estimate=cost(5),
        name="neighbours_back",
    )(pool_keys, pool_values, weight, *given)

def local(
    tokens,
    lengths,
    neighbours,
    neighbour_ids,
    neighbour_lengths,
    first_gain,
    first_shift,
    self_input,
    self_output,
    second_gain,
    second_shift,
    cross_query,
    cross_keyval,
    cross_output,
    third_gain,
    third_shift,
    feed_up,
    feed_down,
    cotangent,
):
    rows, width = cross_query.shape
    line = Line()
    plan = Plan(rows, line)
    steps = len(plan.steps)
    parts = feed_down.shape[0] // rows
    pool_count, neigh_len = neighbours.shape[:2]
    vectors = (first_gain, first_shift, second_gain, second_shift, third_gain, third_shift)
    vector_pack = jnp.pad(jnp.stack(vectors, axis=1), ((0, 0), (0, LANES - len(vectors))))
    rows_in = tokens[0]
    encoded = neighbours.reshape(pool_count * neigh_len, width)
    ids = neighbour_ids.reshape(-1)
    pairs = width // LANES

    def advance(*chunks, after=()):
        moving = [chunk for chunk in chunks if not chunk.done()]
        for chunk in moving:
            chunk.land()
        for chunk in moving + list(after):
            if not chunk.done():
                chunk.launch()

    def run(kernel, first, *rest):
        results = kernel(line.after(first), *rest)
        line.note(results[0] if isinstance(results, (tuple, list)) else results)
        return results

    start = Gather(plan, jnp.concatenate([self_input, vector_pack], axis=1))
    start.launch()
    middle_part = Gather(
        plan,
        jnp.concatenate(
            [line.after(cross_keyval), self_output, cross_query, cross_output], axis=1
        ),
        4,
    )
    advance(start, after=[middle_part])
    advance(start, middle_part)
    up_shard = swap_segments(line.after(feed_up), plan.count, parts, rows)
    down_shard = line.after(feed_down).reshape(parts, rows, width)
    down_shard = down_shard.swapaxes(0, 1).reshape(rows, parts * width)
    feed_part = Gather(plan, jnp.concatenate([up_shard, down_shard], axis=1))
    advance(start, after=[feed_part])
    advance(start, middle_part, feed_part)
    start_halves = start.finish()
    unit, projected, vector_rows, vector_columns, input_weight = run(
        lambda values: project(plan, values, start_halves), rows_in
    )
    advance(middle_part)
    attended = None
    for turn in range(2):
        attended = run(self_forward, projected, lengths, turn * (pairs // 2), pairs // 2, attended)
    advance(feed_part)
    advance(middle_part)
    self_mixed, self_exact, logsum = attended
    middle_halves = middle_part.finish()
    advance(feed_part)
    after_self, second_in, cross_queries, output_weight, query_weight = run(
        lambda values: middle(
            plan, (2 * width, 3 * width), rows_in, values, vector_rows, middle_halves
        ),
        self_mixed,
    )
    pool_keyval, keyval_weight = run(
        lambda values: pool_project(plan, values, middle_halves), encoded
    )
    pool_keyval = pool_keyval.reshape(pool_count, neigh_len, 2 * width)
    advance(feed_part)
    cross_mixed = run(cross_forward, cross_queries, pool_keyval, ids, neighbour_lengths)
    feed_halves = feed_part.finish()
    block_out, after_cross_grad, mixed_grad, third_terms, feed_keep, feed_send = run(
        lambda values: feed(
            plan,
            4 * width,
            after_self,
            values,
            cotangent[0],
            vector_rows,
            feed_halves,
            middle_halves,
        ),
        cross_mixed,
    )
    feed_sum = Scatter(plan, feed_keep, feed_send)
    feed_sum.launch()

    groups = width // WIDE
    crossed = None
    for first, count in ((0, 1), (1, groups - 1)):
        crossed = run(
            cross_backward,
            cross_queries,
            mixed_grad,
            pool_keyval,
            ids,
            neighbour_lengths,
            first,
            count,
            crossed,
        )
        if first == 0:
            advance(feed_sum)
    query_grad, pool_keys, pool_values = crossed
    pool_keys = pool_keys.reshape(pool_count * neigh_len, width)
    pool_values = pool_values.reshape(pool_count * neigh_len, width)
    keyval_keep, keyval_send = run(
        lambda values: keyval_terms(plan, encoded, values, pool_values), pool_keys
    )
    advance(feed_sum)
    after_self_grad, attend_grad, second_terms, second_keep, second_send = run(
        lambda values: second_back(
            plan,
            after_self,
            after_cross_grad,
            values,
            second_in,
            self_mixed,
            vector_rows,
            output_weight,
            query_weight,
        ),
        query_grad,
    )
    middle_sum = Scatter(
        plan,
        jnp.concatenate([keyval_keep, second_keep], axis=1),
        jnp.concatenate([keyval_send, second_send], axis=1),
    )
    advance(feed_sum, after=[middle_sum])
    projected_grad = None
    for turn in range(2):
        projected_grad = run(
            lambda values: self_backward(
                projected,
                lengths,
                values,
                self_exact,
                logsum,
                turn * (pairs // 2),
                pairs // 2,
                projected_grad,
            ),
            attend_grad,
        )
        if turn == 0:
            advance(middle_sum)
    first_keep, first_send = run(
        lambda values: first_terms(
            plan, unit, values, vector_columns, second_terms, third_terms, input_weight
        ),
        projected_grad,
    )
    first_sum = Scatter(plan, first_keep, first_send)
    advance(feed_sum, middle_sum, after=[first_sum])
    blocks = pool_keys.shape[0] // BACK_BLOCK
    quarter = blocks // 4
    neighbours_grad = None

    def neighbours_turn(first, count, earlier):
        return run(
            lambda values: neighbours_back(
                values,
                pool_values,
                keyval_weight,
                first,
                count,
                earlier,
            ),
            pool_keys,
        )

    neighbours_grad = neighbours_turn(0, quarter, neighbours_grad)
    advance(feed_sum, middle_sum, first_sum)
    tokens_grad = run(
        lambda values: first_rows(
            rows_in, after_self_grad, values, vector_rows, input_weight
        ),
        projected_grad,
    )
    advance(middle_sum, first_sum)
    neighbours_grad = neighbours_turn(quarter, quarter, neighbours_grad)
    advance(middle_sum, first_sum)
    neighbours_grad = neighbours_turn(2 * quarter, blocks - 2 * quarter, neighbours_grad)
    middle_total = middle_sum.finish()
    feed_total = line.after(feed_sum.finish())
    first_total = first_sum.finish()

    down_grad = feed_total[:, : parts * width].reshape(rows, parts, width).swapaxes(0, 1)
    up_grad = swap_segments(
        feed_total[:, parts * width : 2 * parts * width], parts, plan.count, rows
    )
    vector_grads = [first_total[:, 3 * width + i] for i in range(len(vectors))]
    return (
        block_out[None],
        tokens_grad[None],
        neighbours_grad.reshape(neighbours.shape),
        vector_grads[0],
        vector_grads[1],
        first_total[:, : 3 * width],
        middle_total[:, 3 * width :],
        vector_grads[2],
        vector_grads[3],
        middle_total[:, 2 * width : 3 * width],
        middle_total[:, : 2 * width],
        feed_total[:, 2 * parts * width :],
        vector_grads[4],
        vector_grads[5],
        up_grad,
        down_grad.reshape(feed_down.shape),
    )


def solution(mesh):
    placed = (
        P(("fsdp", "dp"), None, None),
        P(("fsdp", "dp")),
        P(("fsdp", "dp"), None, None),
        P(("fsdp", "dp"), None, None),
        P(("fsdp", "dp")),
        P(("fsdp", "dp")),
        P(("fsdp", "dp")),
        P(("fsdp", "dp"), None),
        P(("fsdp", "dp"), None),
        P(("fsdp", "dp")),
        P(("fsdp", "dp")),
        P(("fsdp", "dp"), None),
        P(("fsdp", "dp"), None),
        P(("fsdp", "dp"), None),
        P(("fsdp", "dp")),
        P(("fsdp", "dp")),
        P(("fsdp", "dp"), None),
        P(("fsdp", "dp"), None),
        P(("fsdp", "dp"), None, None),
    )
    return jax.shard_map(
        local,
        mesh=mesh,
        in_specs=placed,
        out_specs=(
            P(("fsdp", "dp"), None, None),
            P(("fsdp", "dp"), None, None),
            P(("fsdp", "dp"), None, None),
            P(("fsdp", "dp")),
            P(("fsdp", "dp")),
            P(("fsdp", "dp"), None),
            P(("fsdp", "dp"), None),
            P(("fsdp", "dp")),
            P(("fsdp", "dp")),
            P(("fsdp", "dp"), None),
            P(("fsdp", "dp"), None),
            P(("fsdp", "dp"), None),
            P(("fsdp", "dp")),
            P(("fsdp", "dp")),
            P(("fsdp", "dp"), None),
            P(("fsdp", "dp"), None),
        ),
        check_vma=False,
    )
```

```python
import functools

import jax
import jax.numpy as jnp
from jax import lax
from jax.experimental import pallas as pl
from jax.experimental.pallas import tpu as pltpu
from jax.sharding import PartitionSpec as P

HEADS = 12
SPAN = 64
NEIGH = 2
LANES = 128
WIDE = 256
QBLOCK = 256

EPSILON = 1e-05
SCALE = 0.125
NEGATIVE = -1e30
BF16 = jnp.bfloat16
F32 = jnp.float32
NT = (((1,), (1,)), ((), ()))
NN = (((1,), (0,)), ((), ()))
TN = (((0,), (0,)), ((), ()))


def dot(left, right, dims=NN):
    return lax.dot_general(left, right, dims, preferred_element_type=F32)


def iota(shape, axis):
    return lax.broadcasted_iota(jnp.int32, shape, axis)


def cost(microseconds):
    return pl.CostEstimate(
        flops=int(microseconds * 1100000000.0), bytes_accessed=0, transcendentals=0
    )


def passing(kernel, before, given, *refs):
    return kernel(*refs[:before], *refs[before + given :])


def split_three(values):
    high = values.astype(BF16)
    rest = values - high.astype(F32)
    middle = rest.astype(BF16)
    low = (rest - middle.astype(F32)).astype(BF16)
    return (high, middle, low)


def self_forward_kernel(length_ref, query_ref, key_ref, value_ref, mixed_ref, exact_ref, logsum_ref):
    seq_len = query_ref.shape[0]
    length = length_ref[0]
    lane = iota((1, LANES), 1)
    first = lane < 64
    padded = jnp.where(iota((seq_len, 1), 0) < length, 0.0, NEGATIVE).astype(BF16)
    keys = key_ref[...]
    values = value_ref[...]
    one = jnp.ones((), BF16)
    keys_by_head = (
        jnp.where(first, keys, jnp.where(lane == 64, padded, 0)),
        jnp.where(first, jnp.where(lane == 0, padded, 0), keys),
    )
    values_by_head = (jnp.where(first, values, one), jnp.where(first, one, values))
    causal = iota((QBLOCK, QBLOCK), 1) <= iota((QBLOCK, QBLOCK), 0)

    def scores(block, head):
        start = block * QBLOCK
        query = query_ref[start : start + QBLOCK] * jnp.asarray(SCALE, BF16)
        if head == 0:
            query = jnp.where(first, query, jnp.where(lane == 64, one, 0))
        else:
            query = jnp.where(first, jnp.where(lane == 0, one, 0), query)
        diagonal = dot(query, keys_by_head[head][start : start + QBLOCK], NT)
        before = dot(query, keys_by_head[head][:start], NT) if block else None
        return (jnp.where(causal, diagonal, NEGATIVE), before)

    units = [(block, head) for block in reversed(range(seq_len // QBLOCK)) for head in range(2)]
    ahead = [scores(*unit) for unit in units[:AHEAD]]
    outs = []
    tops = []
    for place_at, (block, head) in enumerate(units):
        if place_at + AHEAD < len(units):
            ahead.append(scores(*units[place_at + AHEAD]))
        start = block * QBLOCK
        diagonal, before = ahead.pop(0)
        top = jnp.max(diagonal, axis=-1, keepdims=True)
        if block:
            top = jnp.maximum(top, jnp.max(before, axis=-1, keepdims=True))
        out = dot(
            jnp.exp(diagonal - top).astype(BF16), values_by_head[head][start : start + QBLOCK]
        )
        if block:
            out = out + dot(jnp.exp(before - top).astype(BF16), values_by_head[head][:start])
        outs.append(out)
        tops.append(top)
        if head == 0:
            continue
        total = pltpu.roll(jnp.where(first, outs[1], outs[0]), 64, 1)
        mixed = jnp.where(first, outs[0], outs[1]) / total
        mixed_ref[start : start + QBLOCK] = mixed.astype(BF16)
        exact_ref[start : start + QBLOCK] = mixed
        logsum = (jnp.where(first, tops[0], tops[1]) + jnp.log(total)).T
        logsum_ref[0, 0:1, start : start + QBLOCK] = logsum[0:1]
        logsum_ref[0, 1:2, start : start + QBLOCK] = logsum[64:65]
        outs = []
        tops = []


def self_forward(projected, lengths, first, count, earlier):
    seq_len = projected.shape[0]
    width = projected.shape[1] // 3
    pairs = width // LANES
    column = lambda offset: pl.BlockSpec((seq_len, LANES), lambda p: (0, p + offset))
    given = [] if earlier is None else list(earlier)
    return pl.pallas_call(
        functools.partial(passing, self_forward_kernel, 4, len(given)),
        grid=(count,),
        in_specs=[
            pl.BlockSpec(memory_space=pltpu.SMEM),
            column(first),
            column(pairs + first),
            column(2 * pairs + first),
        ]
        + [pl.BlockSpec(memory_space=pl.ANY)] * len(given),
        out_specs=[
            column(first),
            column(first),
            pl.BlockSpec((1, 8, seq_len), lambda p: (p + first, 0, 0)),
        ],
        out_shape=[
            jax.ShapeDtypeStruct((seq_len, width), BF16),
            jax.ShapeDtypeStruct((seq_len, width), F32),
            jax.ShapeDtypeStruct((pairs, 8, seq_len), F32),
        ],
        input_output_aliases={4 + i: i for i in range(len(given))},
        compiler_params=pltpu.CompilerParams(vmem_limit_bytes=48 * 2**20),
        cost_estimate=cost(8),
        name="self_forward",
    )(lengths, projected, projected, projected, *given)


AHEAD = 1
AHEAD_BACK = 2
AHEAD_CROSS = 2
SPANS_STEP = 8


def self_backward_kernel(
    length_ref,
    query_ref,
    key_ref,
    value_ref,
    grad_ref,
    exact_ref,
    logsum_ref,
    out_ref,
    key_grad_ref,
    value_grad_ref,
):
    seq_len = query_ref.shape[0]
    length = length_ref[0]
    lane = iota((1, LANES), 1)
    first = lane < 64
    row = iota((LANES, 1), 0)
    top_rows = row < 64
    padded = jnp.where(iota((seq_len, 1), 0) < length, 0.0, NEGATIVE).astype(BF16)
    keys = key_ref[...]
    values = value_ref[...]
    zero = jnp.zeros((), BF16)
    minus = -jnp.ones((), BF16)

    def beside(offset, head_lane):
        kept = (lane > head_lane) & (lane < head_lane + 4)
        return jnp.where(lane == head_lane, offset, jnp.where(kept, minus, zero))

    keys_by_head = (
        jnp.where(first, keys, beside(padded, 64)),
        jnp.where(first, beside(padded, 0), keys),
    )
    values_by_head = (
        jnp.where(first, values, beside(zero, 64)),
        jnp.where(first, beside(zero, 0), values),
    )
    keys_turned = keys.T
    turned_by_head = (
        jnp.where(top_rows, keys_turned, zero),
        jnp.where(top_rows, zero, keys_turned),
    )
    causal = iota((QBLOCK, QBLOCK), 0) <= iota((QBLOCK, QBLOCK), 1)

    def fill(turned, head, lead, parts):
        base = 64 if head == 0 else 0
        other = jnp.where(row == base, lead, zero)
        for place, part in enumerate(parts):
            other = jnp.where(row == base + 1 + place, part, other)
        own = top_rows if head == 0 else ~top_rows
        return jnp.where(own, turned, other)

    count = seq_len // QBLOCK
    units = [(block, head) for block in reversed(range(count)) for head in range(2)]
    loaded = {}

    def load(block):
        start = block * QBLOCK
        stop = start + QBLOCK
        query = query_ref[start:stop] * jnp.asarray(SCALE, BF16)
        grad = grad_ref[start:stop]
        weighted = (grad.astype(F32) * exact_ref[start:stop]).T
        return (query, grad, query.T, grad.T, weighted)

    def products(block, head):
        if head == 0:
            loaded[block] = load(block)
        _, _, query_turned, grad_turned, weighted = loaded[block]
        start = block * QBLOCK
        stop = start + QBLOCK
        delta = jnp.sum(weighted[head * 64 : head * 64 + 64], axis=0, keepdims=True)
        logsum = logsum_ref[0, head : head + 1, start:stop]
        score = dot(
            keys_by_head[head][:stop],
            fill(query_turned, head, jnp.ones((), BF16), split_three(logsum)),
        )
        centred = dot(
            values_by_head[head][:stop], fill(grad_turned, head, zero, split_three(delta))
        )
        return (score, centred)

    ahead = [products(*unit) for unit in units[:AHEAD_BACK]]
    probs_all = []
    scores_all = []
    query_grad = None
    for place_at, (block, head) in enumerate(units):
        if place_at + AHEAD_BACK < len(units):
            ahead.append(products(*units[place_at + AHEAD_BACK]))
        start = block * QBLOCK
        stop = start + QBLOCK
        score, centred = ahead.pop(0)
        prob = jnp.exp(score)
        last = jnp.where(causal, prob[start:], 0.0)
        prob = jnp.concatenate([prob[:start], last], axis=0) if block else last
        score_grad = (prob * centred).astype(BF16)
        scores_all.append(score_grad)
        probs_all.append(prob.astype(BF16))
        part = dot(turned_by_head[head][:, :stop], score_grad)
        query_grad = part if query_grad is None else query_grad + part
        if head == 0:
            continue
        query, grad = loaded[block][:2]
        out_ref[0, start:stop] = (query_grad.T * SCALE).astype(BF16)
        own_query = jnp.concatenate(
            [jnp.where(first, query, zero), jnp.where(first, zero, query)], axis=0
        )
        own_grad = jnp.concatenate(
            [jnp.where(first, grad, zero), jnp.where(first, zero, grad)], axis=0
        )
        key_part = dot(jnp.concatenate(scores_all, axis=1), own_query)
        value_part = dot(jnp.concatenate(probs_all, axis=1), own_grad)
        if block == count - 1:
            key_grad_ref[...] = key_part
            value_grad_ref[...] = value_part
        else:
            key_grad_ref[:stop] += key_part
            value_grad_ref[:stop] += value_part
        probs_all = []
        scores_all = []
        query_grad = None
    out_ref[1] = key_grad_ref[...].astype(BF16)
    out_ref[2] = value_grad_ref[...].astype(BF16)


def self_backward(projected, lengths, grad, exact, logsum, first, count, earlier):
    seq_len = projected.shape[0]
    width = projected.shape[1] // 3
    pairs = width // LANES
    column = lambda offset: pl.BlockSpec((seq_len, LANES), lambda p: (0, p + offset))
    given = [] if earlier is None else [earlier]
    return pl.pallas_call(
        functools.partial(passing, self_backward_kernel, 7, len(given)),
        grid=(count,),
        in_specs=[
            pl.BlockSpec(memory_space=pltpu.SMEM),
            column(first),
            column(pairs + first),
            column(2 * pairs + first),
            column(first),
            column(first),
            pl.BlockSpec((1, 8, seq_len), lambda p: (p + first, 0, 0)),
        ]
        + [pl.BlockSpec(memory_space=pl.ANY)] * len(given),
        out_specs=pl.BlockSpec((3, seq_len, LANES), lambda p: (0, 0, p + first)),
        out_shape=jax.ShapeDtypeStruct((3, seq_len, width), BF16),
        scratch_shapes=[pltpu.VMEM((seq_len, LANES), F32), pltpu.VMEM((seq_len, LANES), F32)],
        input_output_aliases={7: 0} if given else {},
        compiler_params=pltpu.CompilerParams(vmem_limit_bytes=48 * 2**20),
        cost_estimate=cost(12),
        name="self_backward",
    )(lengths, projected, projected, projected, grad, exact, logsum, *given)


def block_diagonal(rows):
    lane = iota((1, WIDE), 1)
    return jnp.concatenate(
        [jnp.where((lane >= h * 64) & (lane < h * 64 + 64), rows, 0) for h in range(4)], axis=0
    )


def take_diagonal(stacked):
    lane = iota((1, WIDE), 1)
    result = stacked[:SPAN]
    for h in range(1, 4):
        result = jnp.where(lane >= h * 64, stacked[h * SPAN : (h + 1) * SPAN], result)
    return result


def slot_bias(ids_ref, neighbour_lengths_ref, span, neigh_len, axis):
    shape = (1, NEIGH * neigh_len) if axis else (NEIGH * neigh_len, 1)
    place = iota(shape, axis)
    first = neighbour_lengths_ref[ids_ref[span * NEIGH]]
    second = neighbour_lengths_ref[ids_ref[span * NEIGH + 1]]
    limit = jnp.where(place < neigh_len, first, neigh_len + second)
    return jnp.where(place < limit, 0.0, NEGATIVE)


def cross_forward_kernel(ids_ref, neighbour_lengths_ref, query_ref, *refs):
    slots, mixed_ref, logsum_ref = refs[:-2], refs[-2], refs[-1]
    step = pl.program_id(0)
    neigh_len = slots[0].shape[1]
    width = query_ref.shape[1]
    units = [(span, group) for span in range(SPANS_STEP) for group in range(width // WIDE)]

    def scores(span, group):
        rows = slice(span * SPAN, (span + 1) * SPAN)
        place = slice(group * WIDE, (group + 1) * WIDE)
        queries = block_diagonal(query_ref[rows, place] * jnp.asarray(SCALE, BF16))
        keys = jnp.concatenate([ref[0, :, place] for ref in slots[span * NEIGH :][:NEIGH]], axis=0)
        return dot(queries, keys, NT)

    ahead = [scores(*unit) for unit in units[:AHEAD_CROSS]]
    for place_at, (span, group) in enumerate(units):
        if place_at + AHEAD_CROSS < len(units):
            ahead.append(scores(*units[place_at + AHEAD_CROSS]))
        if group == 0:
            bias = slot_bias(
                ids_ref, neighbour_lengths_ref, step * SPANS_STEP + span, neigh_len, 1
            )
        score = ahead.pop(0) + bias
        top = jnp.max(score, axis=-1, keepdims=True)
        expo = jnp.exp(score - top)
        total = jnp.sum(expo, axis=-1, keepdims=True)
        logsum = jnp.broadcast_to(top + jnp.log(total), (WIDE, LANES)).T
        logsum_ref[span, 0:1, group * WIDE : (group + 1) * WIDE] = logsum[0:1]
        place = slice(width + group * WIDE, width + (group + 1) * WIDE)
        values = jnp.concatenate(
            [ref[0, :, place] for ref in slots[span * NEIGH :][:NEIGH]], axis=0
        )
        out = dot(expo.astype(BF16), values) / total
        rows = slice(span * SPAN, (span + 1) * SPAN)
        mixed_ref[rows, group * WIDE : (group + 1) * WIDE] = take_diagonal(out).astype(BF16)


def cross_forward(queries, pool_keyval, ids, neighbour_lengths):
    seq_len, width = queries.shape
    neigh_len, both = pool_keyval.shape[1:]
    spans = seq_len // SPAN
    slots = SPANS_STEP * NEIGH
    rows = pl.BlockSpec((SPANS_STEP * SPAN, width), lambda c, ids, lens: (c, 0))
    slot = lambda j: pl.BlockSpec(
        (1, neigh_len, both), lambda c, ids, lens: (ids[c * slots + j], 0, 0)
    )
    return pl.pallas_call(
        cross_forward_kernel,
        grid_spec=pltpu.PrefetchScalarGridSpec(
            num_scalar_prefetch=2,
            grid=(spans // SPANS_STEP,),
            in_specs=[rows] + [slot(j) for j in range(slots)],
            out_specs=[rows, pl.BlockSpec((SPANS_STEP, 8, width), lambda c, ids, lens: (c, 0, 0))],
        ),
        out_shape=[
            jax.ShapeDtypeStruct((seq_len, width), BF16),
            jax.ShapeDtypeStruct((spans, 8, width), F32),
        ],
        compiler_params=pltpu.CompilerParams(vmem_limit_bytes=56 * 2**20),
        cost_estimate=cost(12),
        name="cross_forward",
    )(ids, neighbour_lengths, queries, *[pool_keyval] * slots)


def cross_backward_kernel(
    ids_ref,
    neighbour_lengths_ref,
    query_ref,
    grad_ref,
    key_ref,
    value_ref,
    logsum_ref,
    query_grad_ref,
    key_out_ref,
    value_out_ref,
    key_total,
    value_total,
):
    step = pl.program_id(1)
    neigh_len = key_ref.shape[1]

    @pl.when(step == 0)
    def _():
        key_total[...] = jnp.zeros_like(key_total)
        value_total[...] = jnp.zeros_like(value_total)

    def slots_of(span):
        place = (step * SPANS_STEP + span) * NEIGH
        return [ids_ref[place + slot] for slot in range(NEIGH)]

    def products(span):
        rows = slice(span * SPAN, (span + 1) * SPAN)
        queries = block_diagonal(query_ref[rows] * jnp.asarray(SCALE, BF16))
        grads = block_diagonal(grad_ref[rows])
        keys = jnp.concatenate([key_ref[ident] for ident in slots_of(span)], axis=0)
        values = jnp.concatenate([value_ref[ident] for ident in slots_of(span)], axis=0)
        return (queries, grads, keys, dot(keys, queries, NT), dot(values, grads, NT))

    place = iota((neigh_len, WIDE), 0)
    ahead = [products(span) for span in range(AHEAD_CROSS)]
    for span in range(SPANS_STEP):
        if span + AHEAD_CROSS < SPANS_STEP:
            ahead.append(products(span + AHEAD_CROSS))
        queries, grads, keys, score, prob_grad = ahead.pop(0)
        expo = jnp.exp(score - logsum_ref[span, 0:1])
        parts = []
        for slot, ident in enumerate(slots_of(span)):
            part = expo[slot * neigh_len : (slot + 1) * neigh_len]
            parts.append(jnp.where(place < neighbour_lengths_ref[ident], part, 0.0))
        prob = jnp.concatenate(parts, axis=0)
        weighted = prob * prob_grad
        score_grad = (weighted - prob * jnp.sum(weighted, axis=0, keepdims=True)).astype(BF16)
        value_part = dot(prob.astype(BF16), grads)
        key_part = dot(score_grad, queries)
        query_part = dot(score_grad, keys, TN)
        rows = slice(span * SPAN, (span + 1) * SPAN)
        query_grad_ref[rows] = (take_diagonal(query_part) * SCALE).astype(BF16)
        for slot, ident in enumerate(slots_of(span)):
            part = slice(slot * neigh_len, (slot + 1) * neigh_len)
            key_total[ident] += key_part[part]
            value_total[ident] += value_part[part]

    @pl.when(step == pl.num_programs(1) - 1)
    def _():
        key_out_ref[...] = key_total[...].astype(BF16)
        value_out_ref[...] = value_total[...].astype(BF16)


def cross_backward(
    queries, grads, pool_keyval, logsum, ids, neighbour_lengths, first, count, earlier
):
    seq_len, width = queries.shape
    pool_count, neigh_len, _ = pool_keyval.shape
    spans = seq_len // SPAN
    groups = width // WIDE
    rows = pl.BlockSpec((SPANS_STEP * SPAN, WIDE), lambda g, c, ids, lens: (c, g + first))
    pool = lambda offset: pl.BlockSpec(
        (pool_count, neigh_len, WIDE), lambda g, c, ids, lens: (0, 0, g + first + offset)
    )
    pool_shape = jax.ShapeDtypeStruct((pool_count, neigh_len, width), BF16)
    given = [] if earlier is None else list(earlier)
    return pl.pallas_call(
        functools.partial(passing, cross_backward_kernel, 7, len(given)),
        grid_spec=pltpu.PrefetchScalarGridSpec(
            num_scalar_prefetch=2,
            grid=(count, spans // SPANS_STEP),
            in_specs=[
                rows,
                rows,
                pool(0),
                pool(groups),
                pl.BlockSpec((SPANS_STEP, 8, WIDE), lambda g, c, ids, lens: (c, 0, g + first)),
            ]
            + [pl.BlockSpec(memory_space=pl.ANY)] * len(given),
            out_specs=[rows, pool(0), pool(0)],
            scratch_shapes=[
                pltpu.VMEM((pool_count, neigh_len, WIDE), F32),
                pltpu.VMEM((pool_count, neigh_len, WIDE), F32),
            ],
        ),
        out_shape=[jax.ShapeDtypeStruct((seq_len, width), BF16), pool_shape, pool_shape],
        input_output_aliases={7 + i: i for i in range(len(given))},
        compiler_params=pltpu.CompilerParams(vmem_limit_bytes=56 * 2**20),
        cost_estimate=cost(15),
        name="cross_backward",
    )(ids, neighbour_lengths, queries, grads, pool_keyval, pool_keyval, logsum, *given)

AXES = ("fsdp", "dp")
PIECES = 2
COPY_ROWS = 48
VMEM_FOLD = 32


def bits_of(size):
    return [1 << i for i in range(size.bit_length() - 1)]


def index_bits(count):
    return [1 << i for i in range(count.bit_length() - 2, -1, -1)]


class Line:
    def __init__(self):
        self.noted = []

    def note(self, *values):
        self.noted = [values[0]]

    def also(self, value):
        self.noted.append(value)

    def after(self, value):
        return self.after_all([value])[0]

    def after_all(self, values):
        if not self.noted:
            return values
        return lax.optimization_barrier((*values, *self.noted))[: len(values)]


class Plan:
    def __init__(self, rows, line):
        self.line = line
        self.inner = lax.axis_size("dp")
        self.outer = lax.axis_size("fsdp")
        self.count = self.inner * self.outer
        self.rows = rows
        self.core = [self.inner] if self.outer > 1 else []
        self.halves = 2 if self.core else 1
        self.across = self.outer // self.halves
        self.stripe = self.inner * rows
        self.half_rows = self.across * self.stripe
        self.copy_rows = min(self.stripe, COPY_ROWS)
        self.me = lax.axis_index(AXES)
        across = [bit * self.inner for bit in bits_of(self.outer)[1:]]
        along = bits_of(self.inner)
        near, far = along[: len(across)], along[len(across) :]
        self.orders = (far + near + across, far + across + near)
        self.natural = [mask for mask in index_bits(self.count) if mask not in self.core]
        self.odd = self.bit(self.core[0]) if self.core else jnp.zeros((), jnp.int32)
        self.odd_word = self.odd.reshape(1)
        self.steps = list(zip(*self.orders))
        self.places = self.arrival_places()

    def bit(self, mask):
        return (self.me // mask) % 2

    def by_core(self, even, odd):
        return jnp.where(self.odd == 0, even, odd)

    def exchange(self, values, masks):
        even, odd = masks
        pairs = []
        for index in range(self.count):
            is_odd = bool(self.core) and (index // self.core[0]) % 2 == 1
            pairs.append((index, index ^ (odd if is_odd else even)))
        return lax.ppermute(values, AXES, pairs)

    def swap(self, values):
        return self.exchange(values, (self.core[0], self.core[0])) if self.core else values

    def weight_of(self, mask):
        return 1 << (len(self.natural) - 1 - self.natural.index(mask))

    def arrival_places(self):
        blocks = jnp.arange(1 << len(self.natural), dtype=jnp.int32)
        found = []
        for order in self.orders:
            target = jnp.zeros_like(blocks)
            for place_at, mask in enumerate(order):
                flag = ((blocks >> place_at) & 1) ^ self.bit(mask)
                target = target + flag * self.weight_of(mask)
            found.append(target)
        return self.by_core(found[0], found[1])

    def fold_places(self, step):
        found = []
        for order in self.orders:
            gone = order[::-1][:step]
            left = [mask for mask in self.natural if mask not in gone]
            mask = order[::-1][step]
            high = 1 << (len(left) - 1 - left.index(mask))
            index = jnp.arange(1 << (len(left) - 1), dtype=jnp.int32)
            kept = (index // high) * (2 * high) + index % high
            own = self.bit(mask)
            found.append((kept + (1 - own) * high, kept + own * high))
        return tuple(self.by_core(found[0][i], found[1][i]) for i in range(2))


def reorder_kernel(pieces, places_ref, *refs):
    parts, outs, (buffer, sems) = refs[: -2 - pieces], refs[-2 - pieces : -2], refs[-2:]
    blocks = buffer.shape[0]
    share = blocks // len(parts)
    piece = blocks // pieces

    def copies(block):
        return pltpu.make_async_copy(
            parts[block // share].at[block % share], buffer.at[places_ref[block]], sems.at[block]
        )

    def going(index):
        return pltpu.make_async_copy(
            buffer.at[pl.ds(index * piece, piece)], outs[index], sems.at[index]
        )

    for block in range(blocks):
        copies(block).start()
    for block in range(blocks):
        copies(block).wait()
    for index in range(pieces):
        going(index).start()
    for index in range(pieces):
        going(index).wait()


def reorder(plan, parts, pieces):
    blocks = sum(part.shape[0] for part in parts)
    shape = (blocks,) + parts[0].shape[1:]
    piece = jax.ShapeDtypeStruct((blocks // pieces,) + shape[1:], BF16)
    return pl.pallas_call(
        functools.partial(reorder_kernel, pieces),
        in_specs=[pl.BlockSpec(memory_space=pltpu.SMEM)]
        + [pl.BlockSpec(memory_space=pl.ANY)] * len(parts),
        out_specs=[pl.BlockSpec(memory_space=pl.ANY)] * pieces,
        out_shape=[piece] * pieces,
        scratch_shapes=[pltpu.VMEM(shape, BF16), pltpu.SemaphoreType.DMA((blocks,))],
        compiler_params=pltpu.CompilerParams(vmem_limit_bytes=VMEM_FOLD * 2**20),
        cost_estimate=cost(0.1),
        name="reorder_blocks",
    )(plan.places, *parts)


class Gather:
    def __init__(self, plan, shard, pieces=PIECES):
        self.plan = plan
        self.pieces = pieces if plan.core else 1
        self.held = shard[None]
        self.at = 0
        self.other = None
        self.halves = None

    def launch(self):
        plan = self.plan
        if self.at < len(plan.steps):
            self.held = plan.line.after(self.held)
            plan.line.also(self.held)
            self.other = plan.exchange(self.held, plan.steps[self.at])
        else:
            held = self.held if isinstance(self.held, list) else [self.held]
            self.held = plan.line.after_all(held)
            plan.line.also(self.held[0])
            self.other = [plan.swap(piece) for piece in self.held]

    def land(self):
        plan = self.plan
        if self.at < len(plan.steps):
            other = plan.line.after(self.other)
            self.at += 1
            if self.at == len(plan.steps):
                self.held = list(reorder(plan, [self.held, other], self.pieces))
                plan.line.note(self.held[0])
            else:
                self.held = jnp.concatenate([self.held, other], axis=0)
                plan.line.note(self.held)
        else:
            others = plan.line.after_all(self.other)
            plan.line.note(others[0])
            columns = self.held[0].shape[-1]
            pieces = list(self.held) + list(others)
            self.halves = [piece.reshape(-1, columns) for piece in pieces]

    def done(self):
        return self.halves is not None

    def finish(self):
        while not self.done():
            self.land()
            if not self.done():
                self.launch()
        return self.halves


def fold_kernel(sent_places, kept_places, *refs):
    half = len(refs) // 2 - 1
    sent_in, kept_in, (sent_ref, kept_ref) = refs[:half], refs[half : 2 * half], refs[2 * half :]
    for source, target in ((sent_in, sent_ref), (kept_in, kept_ref)):
        total = source[0][...].astype(F32)
        for part in source[1:]:
            total = total + part[...].astype(F32)
        target[...] = total.astype(BF16)


def fold(places, parts):
    blocks, rows, columns = parts[0].shape
    shape = jax.ShapeDtypeStruct((blocks // 2, rows, columns), BF16)
    out = pl.BlockSpec((1, rows, columns), lambda i, sent, kept: (i, 0, 0))
    sent = pl.BlockSpec((1, rows, columns), lambda i, sent, kept: (sent[i], 0, 0))
    kept = pl.BlockSpec((1, rows, columns), lambda i, sent, kept: (kept[i], 0, 0))
    return pl.pallas_call(
        fold_kernel,
        grid_spec=pltpu.PrefetchScalarGridSpec(
            num_scalar_prefetch=2,
            grid=(blocks // 2,),
            in_specs=[sent] * len(parts) + [kept] * len(parts),
            out_specs=[out, out],
        ),
        out_shape=[shape, shape],
        compiler_params=pltpu.CompilerParams(vmem_limit_bytes=VMEM_FOLD * 2**20),
        cost_estimate=cost(0.1),
        name="fold_blocks",
    )(*places, *parts, *parts)


class Scatter:
    def __init__(self, plan, keep, send):
        self.plan = plan
        self.columns = keep.shape[1]
        shape = (1 << len(plan.natural), plan.rows, self.columns)
        self.kept = keep.reshape(shape)
        self.sent = send.reshape(shape) if plan.core else None
        self.at = -1
        self.other = None
        self.total = None

    def launch(self):
        plan = self.plan
        if self.sent is None:
            return
        self.sent = plan.line.after(self.sent)
        plan.line.also(self.sent)
        if self.at < 0:
            self.other = plan.swap(self.sent)
        else:
            self.other = plan.exchange(self.sent, plan.steps[::-1][self.at])

    def land(self):
        plan = self.plan
        parts = [self.kept] if self.other is None else [self.kept, plan.line.after(self.other)]
        self.at += 1
        if self.at < len(plan.steps):
            self.sent, self.kept = fold(plan.fold_places(self.at), parts)
            plan.line.note(self.sent)
        else:
            total = parts[0].astype(F32)
            for part in parts[1:]:
                total = total + part.astype(F32)
            self.total = total.reshape(plan.rows, self.columns)
            plan.line.note(self.total)

    def done(self):
        return self.total is not None

    def finish(self):
        while not self.done():
            self.land()
            if not self.done():
                self.launch()
        return self.total


def bundled(kernel, *spans):
    def call(*refs):
        refs = list(refs)
        for place, count in sorted(spans, reverse=True):
            middle = place + count // 2
            refs[place : place + count] = [tuple(refs[place:middle]), tuple(refs[middle : place + count])]
        return kernel(*refs)

    return call


def column_copies(plan, odd, held_refs, other_refs, target, sems, start, width, rows=None):
    copies = []

    def add(ref, at, rows, first, half):
        across, rest = divmod(first, plan.stripe)
        place = across * plan.halves * plan.stripe + rest
        if plan.halves > 1:
            place = place + half * plan.stripe
            if plan.stripe % 16 == 0 and rest % 16 == 0:
                place = pl.multiple_of(place, 16)
        copies.append(
            pltpu.make_async_copy(
                ref.at[pl.ds(at, rows), pl.ds(start, width)],
                target.at[pl.ds(place, rows), :],
                sems.at[len(copies)],
            )
        )

    rows = rows or plan.copy_rows
    for refs, half in ((held_refs, odd), (other_refs, 1 - odd))[: plan.halves]:
        piece = refs[0].shape[0]
        step = min(rows, piece)
        for first in range(0, plan.half_rows, step):
            add(refs[first // piece], first % piece, step, first, half)
    return copies


def store_halves(plan, odd, result, keep_ref, send_ref, columns):
    for across in range(plan.across):
        rows = slice(across * plan.stripe, (across + 1) * plan.stripe)
        parts = []
        for half in range(plan.halves):
            first = (across * plan.halves + half) * plan.stripe
            parts.append(result[first : first + plan.stripe])
        if plan.halves == 1:
            keep_ref[rows, columns] = parts[0].astype(BF16)
        else:
            keep_ref[rows, columns] = jnp.where(odd == 0, parts[0], parts[1]).astype(BF16)
            send_ref[rows, columns] = jnp.where(odd == 0, parts[1], parts[0]).astype(BF16)

ROWS = 512
FEED_ROWS = 256
BACK_ROWS = 256
POOL_BLOCK = 1024
BACK_BLOCK = 512
MEBI = 2**20
ANYWHERE = pl.BlockSpec(memory_space=pl.ANY)
SCALAR = pl.BlockSpec(memory_space=pltpu.SMEM)


def norm_parts(values):
    centre = jnp.mean(values, axis=-1, keepdims=True)
    centred = values - centre
    spread = jnp.mean(centred * centred, axis=-1, keepdims=True)
    inverse = lax.rsqrt(spread + EPSILON)
    return (centred * inverse, inverse)


def norm_back(values, gain, upstream):
    unit, inverse = norm_parts(values)
    gain_term = jnp.sum(upstream * unit, axis=0, keepdims=True)
    shift_term = jnp.sum(upstream, axis=0, keepdims=True)
    inner = upstream * gain
    mean_inner = jnp.mean(inner, axis=-1, keepdims=True)
    mean_both = jnp.mean(inner * unit, axis=-1, keepdims=True)
    return (inverse * (inner - mean_inner - unit * mean_both), gain_term, shift_term)


def add_terms(step, target_ref, gain_term, shift_term):
    @pl.when(step == 0)
    def _():
        target_ref[...] = jnp.zeros_like(target_ref)

    target_ref[0:1] += gain_term
    target_ref[1:2] += shift_term


def start_all(copies):
    for copy in copies:
        copy.start()


def wait_all(copies):
    for copy in copies:
        copy.wait()


def row_block(columns, last=None, block=ROWS):
    if last is None:
        return pl.BlockSpec((block, columns), lambda i: (i, 0))
    return pl.BlockSpec((block, columns), lambda i: (jnp.minimum(i, last), 0))


def params(megabytes):
    return pltpu.CompilerParams(vmem_limit_bytes=megabytes * MEBI)


def copy_sems(plan, *sets):
    return pltpu.SemaphoreType.DMA(sets + (plan.halves * plan.half_rows // min(plan.copy_rows, 48),))


def pool_kernel(plan, odd_ref, rows_ref, held_ref, other_ref, out_ref, weight_ref, sems):
    width = weight_ref.shape[1]

    @pl.when(pl.program_id(0) == 0)
    def _():
        copies = column_copies(plan, odd_ref[0], held_ref, other_ref, weight_ref, sems, 0, width)
        start_all(copies)
        wait_all(copies)

    out_ref[...] = dot(rows_ref[...], weight_ref[...]).astype(BF16)


def pool_project(plan, encoded, halves):
    rows, width = encoded.shape
    block = POOL_BLOCK
    return pl.pallas_call(
        bundled(functools.partial(pool_kernel, plan), (2, len(halves))),
        grid=(rows // block,),
        in_specs=[SCALAR, pl.BlockSpec((block, width), lambda i: (i, 0))]
        + [ANYWHERE] * len(halves),
        out_specs=[
            pl.BlockSpec((block, 2 * width), lambda i: (i, 0)),
            pl.BlockSpec((width, 2 * width), lambda i: (0, 0)),
        ],
        out_shape=[
            jax.ShapeDtypeStruct((rows, 2 * width), BF16),
            jax.ShapeDtypeStruct((width, 2 * width), BF16),
        ],
        scratch_shapes=[copy_sems(plan)],
        compiler_params=params(40),
        cost_estimate=cost(13),
        name="pool_project",
    )(plan.odd_word, encoded, *halves)


def project_kernel(
    plan,
    odd_ref,
    tokens_ref,
    held_ref,
    other_ref,
    unit_ref,
    projected_ref,
    vectors_ref,
    columns_ref,
    weight,
    pack,
    sems,
):
    width = tokens_ref.shape[1]

    @pl.when(pl.program_id(0) == 0)
    def _():
        copies = column_copies(plan, odd_ref[0], held_ref, other_ref, weight, sems.at[0], 0, 3 * width)
        copies += column_copies(
            plan, odd_ref[0], held_ref, other_ref, pack, sems.at[1], 3 * width, LANES
        )
        start_all(copies)
        wait_all(copies)
        columns_ref[...] = pack[...].astype(F32)
        vectors_ref[...] = columns_ref[...].T[:8]

    unit = norm_parts(tokens_ref[...].astype(F32))[0]
    first_in = (unit * vectors_ref[0:1] + vectors_ref[1:2]).astype(BF16)
    unit_ref[...] = unit.astype(BF16)
    projected_ref[...] = dot(first_in, weight[...]).astype(BF16)


def project(plan, tokens, halves):
    rows, width = tokens.shape
    return pl.pallas_call(
        bundled(functools.partial(project_kernel, plan), (2, len(halves))),
        grid=(rows // ROWS,),
        in_specs=[SCALAR, row_block(width)] + [ANYWHERE] * len(halves),
        out_specs=[
            row_block(width),
            row_block(3 * width),
            pl.BlockSpec((8, width), lambda i: (0, 0)),
            pl.BlockSpec((width, LANES), lambda i: (0, 0)),
            pl.BlockSpec((width, 3 * width), lambda i: (0, 0)),
        ],
        out_shape=[
            jax.ShapeDtypeStruct((rows, width), BF16),
            jax.ShapeDtypeStruct((rows, 3 * width), BF16),
            jax.ShapeDtypeStruct((8, width), F32),
            jax.ShapeDtypeStruct((width, LANES), F32),
            jax.ShapeDtypeStruct((width, 3 * width), BF16),
        ],
        scratch_shapes=[
            pltpu.VMEM((width, LANES), BF16),
            copy_sems(plan, 2),
        ],
        compiler_params=params(40),
        cost_estimate=cost(5),
        name="project",
    )(plan.odd_word, tokens, *halves)


def middle_kernel(
    plan,
    starts,
    odd_ref,
    tokens_ref,
    mixed_ref,
    vectors_ref,
    held_ref,
    other_ref,
    after_ref,
    second_in_ref,
    queries_ref,
    out_weight,
    query_weight,
    sems,
):
    width = tokens_ref.shape[1]

    @pl.when(pl.program_id(0) == 0)
    def _():
        copies = []
        for place_at, target in enumerate((out_weight, query_weight)):
            copies += column_copies(
                plan, odd_ref[0], held_ref, other_ref, target, sems.at[place_at], starts[place_at], width
            )
        start_all(copies)
        wait_all(copies)

    after = tokens_ref[...].astype(F32) + dot(mixed_ref[...], out_weight[...])
    after_ref[...] = after
    unit = norm_parts(after)[0]
    second_in = (unit * vectors_ref[2:3] + vectors_ref[3:4]).astype(BF16)
    second_in_ref[...] = second_in
    queries_ref[...] = dot(second_in, query_weight[...]).astype(BF16)


def middle(plan, starts, tokens, mixed, vectors, halves):
    rows, width = tokens.shape
    return pl.pallas_call(
        bundled(functools.partial(middle_kernel, plan, starts), (4, len(halves))),
        grid=(rows // ROWS,),
        in_specs=[
            SCALAR,
            row_block(width),
            row_block(width),
            pl.BlockSpec((8, width), lambda i: (0, 0)),
        ]
        + [ANYWHERE] * len(halves),
        out_specs=[row_block(width)] * 3 + [pl.BlockSpec((width, width), lambda i: (0, 0))] * 2,
        out_shape=[
            jax.ShapeDtypeStruct((rows, width), F32),
            jax.ShapeDtypeStruct((rows, width), BF16),
            jax.ShapeDtypeStruct((rows, width), BF16),
            jax.ShapeDtypeStruct((width, width), BF16),
            jax.ShapeDtypeStruct((width, width), BF16),
        ],
        scratch_shapes=[
            copy_sems(plan, 2),
        ],
        compiler_params=params(40),
        cost_estimate=cost(0.5),
        name="middle",
    )(plan.odd_word, tokens, mixed, vectors, *halves)


def segments_kernel(moves, in_ref, out_ref):
    lane = iota((1, LANES), 1)
    tiles = {}
    for place in range(out_ref.shape[1] // LANES):
        result = None
        for source, shift, first, last in moves[place]:
            if source not in tiles:
                tiles[source] = in_ref[:, source * LANES : (source + 1) * LANES].astype(F32)
            tile = pltpu.roll(tiles[source], shift, 1) if shift else tiles[source]
            if result is None:
                result = tile
            else:
                result = jnp.where((lane >= first) & (lane < last), tile, result)
        out_ref[:, place * LANES : (place + 1) * LANES] = result.astype(out_ref.dtype)


def swap_segments(matrix, outer, inner, size):
    rows, columns = matrix.shape
    moves = [[] for _ in range(columns // LANES)]
    for i in range(outer):
        for j in range(inner):
            source = (i * inner + j) * size
            target = (j * outer + i) * size
            done = 0
            while done < size:
                at, to = source + done, target + done
                count = min(size - done, LANES - at % LANES, LANES - to % LANES)
                shift = (to - at) % LANES
                moves[to // LANES].append((at // LANES, shift, to % LANES, to % LANES + count))
                done += count
    return pl.pallas_call(
        functools.partial(segments_kernel, moves),
        in_specs=[pl.BlockSpec(memory_space=pltpu.VMEM)],
        out_specs=pl.BlockSpec(memory_space=pltpu.VMEM),
        out_shape=jax.ShapeDtypeStruct((rows, columns), matrix.dtype),
        compiler_params=params(24),
        cost_estimate=cost(2),
        name="swap_segments",
    )(matrix)


GELU_SCALE = 0.7978845608028654
GELU_CUBE = 0.044715
TERMS_STEP = 3


def gelu_both(values):
    square = values * values
    bent = jnp.tanh(values * (GELU_SCALE + (GELU_SCALE * GELU_CUBE) * square))
    half = 0.5 + 0.5 * bent
    result = values * half
    slope = 2.0 * GELU_SCALE + (6.0 * GELU_SCALE * GELU_CUBE) * square
    return (result, half * (1.0 + (values - result) * slope))


def feed_kernel(
    plan,
    out_start,
    row_steps,
    odd_ref,
    after_ref,
    mixed_ref,
    cotangent_ref,
    vectors_ref,
    feed_held_ref,
    feed_other_ref,
    held_ref,
    other_ref,
    block_ref,
    grad_ref,
    mixed_grad_ref,
    terms_ref,
    keep_ref,
    send_ref,
    out_matrix,
    weights,
    lefts,
    rights,
    sems,
):
    step = pl.program_id(0)
    width = after_ref.shape[1]
    parts = weights.shape[1] // width // 2

    def copies():
        return column_copies(
            plan,
            odd_ref[0],
            held_ref,
            other_ref,
            out_matrix,
            sems.at[0],
            out_start,
            width,
            plan.stripe,
        ) + column_copies(
            plan,
            odd_ref[0],
            feed_held_ref,
            feed_other_ref,
            weights,
            sems.at[1],
            0,
            2 * parts * width,
            plan.stripe,
        )

    def ready(index):
        if index == 2 * parts:
            return out_matrix[...]
        return weights[:, index * width : (index + 1) * width]

    def rows_of(place_at):
        mixed = mixed_ref[...]
        cotangent = cotangent_ref[...]
        out_weight = ready(2 * parts)
        after_cross = after_ref[...] + dot(mixed, out_weight)
        unit, inverse = norm_parts(after_cross)
        gain = vectors_ref[4:5]
        third_in = (unit * gain + vectors_ref[5:6]).astype(BF16)
        up = ready(0)
        before = dot(third_in, up)
        lefts[parts, :, place_at] = third_in.T
        lefts[parts + 1, :, place_at] = mixed.T
        rights[0, place_at] = cotangent
        result = after_cross
        upstream = jnp.zeros_like(after_cross)
        for part in range(parts):
            down = ready(parts + part)
            back = dot(cotangent, down, NT)
            hidden, slope = gelu_both(before)
            hidden = hidden.astype(BF16)
            if part + 1 < parts:
                next_up = ready(part + 1)
                before = dot(third_in, next_up)
            result = result + dot(hidden, down)
            lefts[part, :, place_at] = hidden.T
            hidden_grad = (slope * back).astype(BF16)
            rights[1 + part, place_at] = hidden_grad
            upstream = upstream + dot(hidden_grad, up, NT)
            if part + 1 < parts:
                up = next_up
        block_ref[...] = result.astype(BF16)
        inner = upstream * gain
        mean_inner = jnp.mean(inner, axis=-1, keepdims=True)
        mean_both = jnp.mean(inner * unit, axis=-1, keepdims=True)
        grad = cotangent.astype(F32) + inverse * (inner - mean_inner - unit * mean_both)
        add_terms(
            step,
            terms_ref,
            jnp.sum(upstream * unit, axis=0, keepdims=True),
            jnp.sum(upstream, axis=0, keepdims=True),
        )
        grad_ref[...] = grad
        rounded = grad.astype(BF16)
        rights[parts + 1, place_at] = rounded
        mixed_grad_ref[...] = dot(rounded, out_weight, NT).astype(BF16)

    @pl.when(step == 0)
    def _():
        start_all(copies())
        wait_all(copies())

    @pl.when(step < row_steps)
    def _():
        rows_of(pl.ds(pl.multiple_of(step * FEED_ROWS, FEED_ROWS), FEED_ROWS))

    @pl.when(step >= row_steps)
    def _():
        for turn in range(TERMS_STEP):
            term = (step - row_steps) * TERMS_STEP + turn
            left = jnp.where(term < parts, term, jnp.where(term < 2 * parts, parts, parts + 1))
            right = jnp.where(term < parts, 0, term - parts + 1)
            result = dot(lefts[left], rights[right])
            columns = slice(turn * width, (turn + 1) * width)
            store_halves(plan, odd_ref[0], result, keep_ref, send_ref, columns)


def feed(plan, out_start, after, mixed, cotangent, vectors, feed_halves, halves):
    rows, width = after.shape
    parts = feed_halves[0].shape[1] // width // 2
    terms = 2 * parts + 1
    steps = rows // FEED_ROWS
    last = steps - 1
    rows_in = row_block(width, last, FEED_ROWS)
    whole = pl.BlockSpec((8, width), lambda i: (0, 0))
    slab = pl.BlockSpec(
        (plan.half_rows, TERMS_STEP * width), lambda i: (0, jnp.maximum(i - steps, 0))
    )
    slab_shape = jax.ShapeDtypeStruct((plan.half_rows, terms * width), BF16)
    return pl.pallas_call(
        bundled(
            functools.partial(feed_kernel, plan, out_start, steps),
            (5, len(feed_halves)),
            (5 + len(feed_halves), len(halves)),
        ),
        grid=(steps + terms // TERMS_STEP,),
        in_specs=[SCALAR, rows_in, rows_in, rows_in, whole]
        + [ANYWHERE] * (len(feed_halves) + len(halves)),
        out_specs=[rows_in, rows_in, rows_in, whole, slab, slab],
        out_shape=[
            jax.ShapeDtypeStruct((rows, width), BF16),
            jax.ShapeDtypeStruct((rows, width), F32),
            jax.ShapeDtypeStruct((rows, width), BF16),
            jax.ShapeDtypeStruct((8, width), F32),
            slab_shape,
            slab_shape,
        ],
        scratch_shapes=[
            pltpu.VMEM((width, width), BF16),
            pltpu.VMEM((width, 2 * parts * width), BF16),
            pltpu.VMEM((parts + 2, width, rows), BF16),
            pltpu.VMEM((parts + 2, rows, width), BF16),
            copy_sems(plan, 2),
        ],
        compiler_params=params(60),
        cost_estimate=cost(50),
        name="feed_forward",
    )(plan.odd_word, after, mixed, cotangent, vectors, *feed_halves, *halves)


def second_kernel(
    plan,
    row_steps,
    odd_ref,
    after_ref,
    grad_in_ref,
    query_grad_ref,
    second_in_ref,
    mixed_ref,
    vectors_ref,
    out_weight,
    query_weight,
    grad_ref,
    attend_ref,
    terms_ref,
    keep_ref,
    send_ref,
    lefts,
    rights,
):
    step = pl.program_id(0)
    width = after_ref.shape[1]

    place_at = pl.ds(pl.multiple_of(step * BACK_ROWS, BACK_ROWS), BACK_ROWS)
    query_grad = query_grad_ref[...]
    back, gain_term, shift_term = norm_back(
        after_ref[...], vectors_ref[2:3], dot(query_grad, query_weight[...], NT)
    )
    lefts[0, :, place_at] = second_in_ref[...].T
    lefts[1, :, place_at] = mixed_ref[...].T
    rights[0, place_at] = query_grad
    add_terms(step, terms_ref, gain_term, shift_term)
    grad = grad_in_ref[...] + back
    grad_ref[...] = grad
    rounded = grad.astype(BF16)
    attend_ref[...] = dot(rounded, out_weight[...], NT).astype(BF16)
    rights[1, place_at] = rounded

    @pl.when(step == row_steps - 1)
    def _():
        for term in range(2):
            result = dot(lefts[term], rights[term])
            columns = slice(term * width, (term + 1) * width)
            store_halves(plan, odd_ref[0], result, keep_ref, send_ref, columns)


def second_back(
    plan, after, grad_in, query_grad, second_in, mixed, vectors, out_weight, query_weight, *given
):
    rows, width = after.shape
    steps = rows // BACK_ROWS
    rows_in = row_block(width, None, BACK_ROWS)
    whole = pl.BlockSpec((8, width), lambda i: (0, 0))
    matrix = pl.BlockSpec((width, width), lambda i: (0, 0))
    slab = pl.BlockSpec((plan.half_rows, 2 * width), lambda i: (0, 1))
    slab_shape = jax.ShapeDtypeStruct((plan.half_rows, 4 * width), BF16)
    return pl.pallas_call(
        functools.partial(passing, functools.partial(second_kernel, plan, steps), 9, len(given)),
        grid=(steps,),
        in_specs=[SCALAR] + [rows_in] * 5 + [whole, matrix, matrix] + [ANYWHERE] * len(given),
        out_specs=[rows_in, rows_in, whole, slab, slab],
        out_shape=[
            jax.ShapeDtypeStruct((rows, width), F32),
            jax.ShapeDtypeStruct((rows, width), BF16),
            jax.ShapeDtypeStruct((8, width), F32),
            slab_shape,
            slab_shape,
        ],
        scratch_shapes=[
            pltpu.VMEM((2, width, rows), BF16),
            pltpu.VMEM((2, rows, width), BF16),
        ],
        input_output_aliases={9: 3, 10: 4},
        compiler_params=params(48),
        cost_estimate=cost(12),
        name="second_back",
    )(plan.odd_word, after, grad_in, query_grad, second_in, mixed, vectors, out_weight, query_weight, *given)


def first_terms_kernel(
    plan,
    odd_ref,
    unit_ref,
    projected_grad_ref,
    columns_ref,
    second_terms_ref,
    third_terms_ref,
    weight,
    keep_ref,
    send_ref,
    terms,
):
    part = pl.program_id(0)
    width = unit_ref.shape[1]

    @pl.when(part == 0)
    def _():
        terms[...] = jnp.zeros_like(terms)

    grads = projected_grad_ref[0]
    plain = dot(unit_ref[...], grads, TN)
    sums = jnp.sum(grads.astype(F32), axis=0, keepdims=True)
    gain = columns_ref[:, 0:1]
    shift = columns_ref[:, 1:2]
    place = pl.ds(pl.multiple_of(part * width, LANES), width)
    store_halves(plan, odd_ref[0], gain * plain + shift * sums, keep_ref, send_ref, place)
    matrix = weight[...].astype(F32)
    terms[:, 0:1] += jnp.sum(matrix * plain, axis=1, keepdims=True)
    terms[:, 1:2] += jnp.sum(matrix * sums, axis=1, keepdims=True)

    @pl.when(part == 2)
    def _():
        rows = jnp.concatenate(
            [
                jnp.zeros((2, width), F32),
                second_terms_ref[0:2],
                third_terms_ref[0:2],
                jnp.zeros((LANES - 6, width), F32),
            ],
            axis=0,
        )
        lane = iota((1, LANES), 1)
        result = jnp.where(lane < 2, terms[...], rows.T)
        place = slice(3 * width, 3 * width + LANES)
        store_halves(plan, odd_ref[0], result, keep_ref, send_ref, place)


def first_terms(plan, unit, projected_grad, columns, second_terms, third_terms, weight):
    rows, width = unit.shape
    whole = pl.BlockSpec((8, width), lambda i: (0, 0))
    slab = pl.BlockSpec((plan.half_rows, 3 * width + LANES), lambda i: (0, 0))
    slab_shape = jax.ShapeDtypeStruct((plan.half_rows, 3 * width + LANES), BF16)
    return pl.pallas_call(
        functools.partial(first_terms_kernel, plan),
        grid=(3,),
        in_specs=[
            SCALAR,
            pl.BlockSpec((rows, width), lambda i: (0, 0)),
            pl.BlockSpec((1, rows, width), lambda i: (i, 0, 0)),
            pl.BlockSpec((width, LANES), lambda i: (0, 0)),
            whole,
            whole,
            pl.BlockSpec((width, width), lambda i: (0, i)),
        ],
        out_specs=[slab, slab],
        out_shape=[slab_shape, slab_shape],
        scratch_shapes=[
            pltpu.VMEM((width, LANES), F32),
        ],
        compiler_params=params(56),
        cost_estimate=cost(8),
        name="first_terms",
    )(plan.odd_word, unit, projected_grad, columns, second_terms, third_terms, weight)


def first_rows_kernel(
    tokens_ref,
    grad_in_ref,
    projected_grad_ref,
    vectors_ref,
    weight,
    grad_ref,
):
    width = tokens_ref.shape[1]

    upstream = None
    for part in range(3):
        product = dot(projected_grad_ref[part], weight[:, part * width : (part + 1) * width], NT)
        upstream = product if upstream is None else upstream + product
    unit, inverse = norm_parts(tokens_ref[...].astype(F32))
    inner = upstream * vectors_ref[0:1]
    mean_inner = jnp.mean(inner, axis=-1, keepdims=True)
    mean_both = jnp.mean(inner * unit, axis=-1, keepdims=True)
    grad_ref[...] = grad_in_ref[...] + inverse * (inner - mean_inner - unit * mean_both)


def first_rows(tokens, grad_in, projected_grad, vectors, weight):
    rows, width = tokens.shape
    rows_in = row_block(width, None, FEED_ROWS)
    return pl.pallas_call(
        first_rows_kernel,
        grid=(rows // FEED_ROWS,),
        in_specs=[
            rows_in,
            rows_in,
            pl.BlockSpec((3, FEED_ROWS, width), lambda i: (0, i, 0)),
            pl.BlockSpec((8, width), lambda i: (0, 0)),
            pl.BlockSpec((width, 3 * width), lambda i: (0, 0)),
        ],
        out_specs=rows_in,
        out_shape=jax.ShapeDtypeStruct((rows, width), F32),
        compiler_params=params(52),
        cost_estimate=cost(8),
        name="first_rows",
    )(tokens, grad_in, projected_grad, vectors, weight)


def keyval_kernel(
    plan, odd_ref, rows_ref, key_ref, value_ref, keep_ref, send_ref, key_total, value_total
):
    step = pl.program_id(0)
    width = rows_ref.shape[1]
    turned = rows_ref[...].T
    key_part = dot(turned, key_ref[...])
    value_part = dot(turned, value_ref[...])

    @pl.when(step == 0)
    def _():
        key_total[...] = key_part
        value_total[...] = value_part

    @pl.when(step > 0)
    def _():
        key_total[...] += key_part
        value_total[...] += value_part

    @pl.when(step == pl.num_programs(0) - 1)
    def _():
        for place_at, total in enumerate((key_total, value_total)):
            columns = slice(place_at * width, (place_at + 1) * width)
            store_halves(plan, odd_ref[0], total[...], keep_ref, send_ref, columns)


def keyval_terms(plan, encoded, pool_keys, pool_values):
    rows, width = encoded.shape
    block = 2048
    rows_in = pl.BlockSpec((block, width), lambda i: (i, 0))
    slab = pl.BlockSpec((plan.half_rows, 2 * width), lambda i: (0, 0))
    slab_shape = jax.ShapeDtypeStruct((plan.half_rows, 4 * width), BF16)
    return pl.pallas_call(
        functools.partial(keyval_kernel, plan),
        grid=(rows // block,),
        in_specs=[SCALAR, rows_in, rows_in, rows_in],
        out_specs=[slab, slab],
        out_shape=[slab_shape, slab_shape],
        scratch_shapes=[pltpu.VMEM((width, width), F32), pltpu.VMEM((width, width), F32)],
        compiler_params=params(48),
        cost_estimate=cost(14),
        name="keyval_terms",
    )(plan.odd_word, encoded, pool_keys, pool_values)


def neighbours_kernel(key_ref, value_ref, weight_ref, out_ref):
    width = key_ref.shape[1]
    out_ref[...] = dot(key_ref[...], weight_ref[:, :width], NT) + dot(
        value_ref[...], weight_ref[:, width:], NT
    )


def neighbours_back(pool_keys, pool_values, weight, first, count, earlier):
    rows, width = pool_keys.shape
    block = BACK_BLOCK
    rows_in = pl.BlockSpec((block, width), lambda i: (i + first, 0))
    given = [] if earlier is None else [earlier]
    return pl.pallas_call(
        functools.partial(passing, neighbours_kernel, 3, len(given)),
        grid=(count,),
        in_specs=[rows_in, rows_in, pl.BlockSpec((width, 2 * width), lambda i: (0, 0))]
        + [ANYWHERE] * len(given),
        out_specs=rows_in,
        out_shape=jax.ShapeDtypeStruct((rows, width), F32),
        input_output_aliases={3: 0} if given else {},
        compiler_params=params(40),
        cost_estimate=cost(5),
        name="neighbours_back",
    )(pool_keys, pool_values, weight, *given)

def local(
    tokens,
    lengths,
    neighbours,
    neighbour_ids,
    neighbour_lengths,
    first_gain,
    first_shift,
    self_input,
    self_output,
    second_gain,
    second_shift,
    cross_query,
    cross_keyval,
    cross_output,
    third_gain,
    third_shift,
    feed_up,
    feed_down,
    cotangent,
):
    rows, width = cross_query.shape
    line = Line()
    plan = Plan(rows, line)
    steps = len(plan.steps)
    parts = feed_down.shape[0] // rows
    pool_count, neigh_len = neighbours.shape[:2]
    vectors = (first_gain, first_shift, second_gain, second_shift, third_gain, third_shift)
    vector_pack = jnp.pad(jnp.stack(vectors, axis=1), ((0, 0), (0, LANES - len(vectors))))
    rows_in = tokens[0]
    encoded = neighbours.reshape(pool_count * neigh_len, width)
    ids = neighbour_ids.reshape(-1)
    pairs = width // LANES

    def advance(*chunks, after=()):
        moving = [chunk for chunk in chunks if not chunk.done()]
        for chunk in moving:
            chunk.land()
        for chunk in moving + list(after):
            if not chunk.done():
                chunk.launch()

    def run(kernel, first, *rest):
        results = kernel(line.after(first), *rest)
        line.note(results[0] if isinstance(results, (tuple, list)) else results)
        return results

    start = Gather(plan, jnp.concatenate([self_input, vector_pack], axis=1))
    start.launch()
    middle_part = Gather(
        plan,
        jnp.concatenate(
            [line.after(cross_keyval), self_output, cross_query, cross_output], axis=1
        ),
        4,
    )
    advance(start, after=[middle_part])
    advance(start, middle_part)
    up_shard = swap_segments(line.after(feed_up), plan.count, parts, rows)
    down_shard = line.after(feed_down).reshape(parts, rows, width)
    down_shard = down_shard.swapaxes(0, 1).reshape(rows, parts * width)
    feed_part = Gather(plan, jnp.concatenate([up_shard, down_shard], axis=1))
    advance(start, after=[feed_part])
    advance(start, middle_part, feed_part)
    start_halves = start.finish()
    unit, projected, vector_rows, vector_columns, input_weight = run(
        lambda values: project(plan, values, start_halves), rows_in
    )
    advance(middle_part)
    attended = None
    for turn in range(2):
        attended = run(self_forward, projected, lengths, turn * (pairs // 2), pairs // 2, attended)
    advance(feed_part)
    advance(middle_part)
    self_mixed, self_exact, logsum = attended
    middle_halves = middle_part.finish()
    advance(feed_part)
    after_self, second_in, cross_queries, output_weight, query_weight = run(
        lambda values: middle(
            plan, (2 * width, 3 * width), rows_in, values, vector_rows, middle_halves
        ),
        self_mixed,
    )
    pool_keyval, keyval_weight = run(
        lambda values: pool_project(plan, values, middle_halves), encoded
    )
    pool_keyval = pool_keyval.reshape(pool_count, neigh_len, 2 * width)
    advance(feed_part)
    cross_mixed, cross_logsum = run(cross_forward, cross_queries, pool_keyval, ids, neighbour_lengths)
    feed_halves = feed_part.finish()
    block_out, after_cross_grad, mixed_grad, third_terms, feed_keep, feed_send = run(
        lambda values: feed(
            plan,
            4 * width,
            after_self,
            values,
            cotangent[0],
            vector_rows,
            feed_halves,
            middle_halves,
        ),
        cross_mixed,
    )
    feed_sum = Scatter(plan, feed_keep, feed_send)
    feed_sum.launch()

    crossed = run(
        cross_backward,
        cross_queries,
        mixed_grad,
        pool_keyval,
        cross_logsum,
        ids,
        neighbour_lengths,
        0,
        width // WIDE,
        None,
    )
    advance(feed_sum)
    query_grad, pool_keys, pool_values = crossed
    pool_keys = pool_keys.reshape(pool_count * neigh_len, width)
    pool_values = pool_values.reshape(pool_count * neigh_len, width)
    middle_keep, middle_send = run(
        lambda values: keyval_terms(plan, encoded, values, pool_values), pool_keys
    )
    after_self_grad, attend_grad, second_terms, middle_keep, middle_send = run(
        lambda values: second_back(
            plan,
            after_self,
            after_cross_grad,
            values,
            second_in,
            self_mixed,
            vector_rows,
            output_weight,
            query_weight,
            middle_keep,
            middle_send,
        ),
        query_grad,
    )
    middle_sum = Scatter(plan, middle_keep, middle_send)
    advance(feed_sum, after=[middle_sum])
    projected_grad = None
    for turn in range(2):
        projected_grad = run(
            lambda values: self_backward(
                projected,
                lengths,
                values,
                self_exact,
                logsum,
                turn * (pairs // 2),
                pairs // 2,
                projected_grad,
            ),
            attend_grad,
        )
        if turn == 0:
            advance(feed_sum, middle_sum)
    first_keep, first_send = run(
        lambda values: first_terms(
            plan, unit, values, vector_columns, second_terms, third_terms, input_weight
        ),
        projected_grad,
    )
    first_sum = Scatter(plan, first_keep, first_send)
    advance(feed_sum, middle_sum, after=[first_sum])
    blocks = pool_keys.shape[0] // BACK_BLOCK
    quarter = blocks // 4
    neighbours_grad = None

    def neighbours_turn(first, count, earlier):
        return run(
            lambda values: neighbours_back(
                values,
                pool_values,
                keyval_weight,
                first,
                count,
                earlier,
            ),
            pool_keys,
        )

    neighbours_grad = neighbours_turn(0, quarter, neighbours_grad)
    advance(feed_sum, middle_sum, first_sum)
    tokens_grad = run(
        lambda values: first_rows(
            rows_in, after_self_grad, values, vector_rows, input_weight
        ),
        projected_grad,
    )
    advance(middle_sum, first_sum)
    neighbours_grad = neighbours_turn(quarter, quarter, neighbours_grad)
    advance(middle_sum, first_sum)
    neighbours_grad = neighbours_turn(2 * quarter, blocks - 2 * quarter, neighbours_grad)
    middle_total = middle_sum.finish()
    feed_total = line.after(feed_sum.finish())
    first_total = first_sum.finish()

    down_grad = feed_total[:, : parts * width].reshape(rows, parts, width).swapaxes(0, 1)
    up_grad = swap_segments(
        feed_total[:, parts * width : 2 * parts * width], parts, plan.count, rows
    )
    vector_grads = [first_total[:, 3 * width + i] for i in range(len(vectors))]
    return (
        block_out[None],
        tokens_grad[None],
        neighbours_grad.reshape(neighbours.shape),
        vector_grads[0],
        vector_grads[1],
        first_total[:, : 3 * width],
        middle_total[:, 3 * width :],
        vector_grads[2],
        vector_grads[3],
        middle_total[:, 2 * width : 3 * width],
        middle_total[:, : 2 * width],
        feed_total[:, 2 * parts * width :],
        vector_grads[4],
        vector_grads[5],
        up_grad,
        down_grad.reshape(feed_down.shape),
    )


def solution(mesh):
    placed = (
        P(("fsdp", "dp"), None, None),
        P(("fsdp", "dp")),
        P(("fsdp", "dp"), None, None),
        P(("fsdp", "dp"), None, None),
        P(("fsdp", "dp")),
        P(("fsdp", "dp")),
        P(("fsdp", "dp")),
        P(("fsdp", "dp"), None),
        P(("fsdp", "dp"), None),
        P(("fsdp", "dp")),
        P(("fsdp", "dp")),
        P(("fsdp", "dp"), None),
        P(("fsdp", "dp"), None),
        P(("fsdp", "dp"), None),
        P(("fsdp", "dp")),
        P(("fsdp", "dp")),
        P(("fsdp", "dp"), None),
        P(("fsdp", "dp"), None),
        P(("fsdp", "dp"), None, None),
    )
    return jax.shard_map(
        local,
        mesh=mesh,
        in_specs=placed,
        out_specs=(
            P(("fsdp", "dp"), None, None),
            P(("fsdp", "dp"), None, None),
            P(("fsdp", "dp"), None, None),
            P(("fsdp", "dp")),
            P(("fsdp", "dp")),
            P(("fsdp", "dp"), None),
            P(("fsdp", "dp"), None),
            P(("fsdp", "dp")),
            P(("fsdp", "dp")),
            P(("fsdp", "dp"), None),
            P(("fsdp", "dp"), None),
            P(("fsdp", "dp"), None),
            P(("fsdp", "dp")),
            P(("fsdp", "dp")),
            P(("fsdp", "dp"), None),
            P(("fsdp", "dp"), None),
        ),
        check_vma=False,
    )
```

```python
import functools

import jax
import jax.numpy as jnp
from jax import lax
from jax.experimental import pallas as pl
from jax.experimental.pallas import tpu as pltpu
from jax.sharding import PartitionSpec as P

HEADS = 12
SPAN = 64
NEIGH = 2
LANES = 128
WIDE = 256
QBLOCK = 256

EPSILON = 1e-05
SCALE = 0.125
NEGATIVE = -1e30
BF16 = jnp.bfloat16
F32 = jnp.float32
NT = (((1,), (1,)), ((), ()))
NN = (((1,), (0,)), ((), ()))
TN = (((0,), (0,)), ((), ()))


def dot(left, right, dims=NN):
    return lax.dot_general(left, right, dims, preferred_element_type=F32)


def iota(shape, axis):
    return lax.broadcasted_iota(jnp.int32, shape, axis)


def cost(microseconds):
    return pl.CostEstimate(
        flops=int(microseconds * 1100000000.0), bytes_accessed=0, transcendentals=0
    )


def passing(kernel, before, given, *refs):
    return kernel(*refs[:before], *refs[before + given :])


def split_three(values):
    high = values.astype(BF16)
    rest = values - high.astype(F32)
    middle = rest.astype(BF16)
    low = (rest - middle.astype(F32)).astype(BF16)
    return (high, middle, low)


def self_forward_kernel(length_ref, query_ref, key_ref, value_ref, mixed_ref, exact_ref, logsum_ref):
    seq_len = query_ref.shape[0]
    length = length_ref[0]
    lane = iota((1, LANES), 1)
    first = lane < 64
    padded = jnp.where(iota((seq_len, 1), 0) < length, 0.0, NEGATIVE).astype(BF16)
    keys = key_ref[...]
    values = value_ref[...]
    one = jnp.ones((), BF16)
    keys_by_head = (
        jnp.where(first, keys, jnp.where(lane == 64, padded, 0)),
        jnp.where(first, jnp.where(lane == 0, padded, 0), keys),
    )
    values_by_head = (jnp.where(first, values, one), jnp.where(first, one, values))
    causal = iota((QBLOCK, QBLOCK), 1) <= iota((QBLOCK, QBLOCK), 0)

    def scores(block, head):
        start = block * QBLOCK
        query = query_ref[start : start + QBLOCK] * jnp.asarray(SCALE, BF16)
        if head == 0:
            query = jnp.where(first, query, jnp.where(lane == 64, one, 0))
        else:
            query = jnp.where(first, jnp.where(lane == 0, one, 0), query)
        diagonal = dot(query, keys_by_head[head][start : start + QBLOCK], NT)
        before = dot(query, keys_by_head[head][:start], NT) if block else None
        return (jnp.where(causal, diagonal, NEGATIVE), before)

    units = [(block, head) for block in reversed(range(seq_len // QBLOCK)) for head in range(2)]
    ahead = [scores(*unit) for unit in units[:AHEAD]]
    outs = []
    tops = []
    for place_at, (block, head) in enumerate(units):
        if place_at + AHEAD < len(units):
            ahead.append(scores(*units[place_at + AHEAD]))
        start = block * QBLOCK
        diagonal, before = ahead.pop(0)
        top = jnp.max(diagonal, axis=-1, keepdims=True)
        if block:
            top = jnp.maximum(top, jnp.max(before, axis=-1, keepdims=True))
        out = dot(
            jnp.exp(diagonal - top).astype(BF16), values_by_head[head][start : start + QBLOCK]
        )
        if block:
            out = out + dot(jnp.exp(before - top).astype(BF16), values_by_head[head][:start])
        outs.append(out)
        tops.append(top)
        if head == 0:
            continue
        total = pltpu.roll(jnp.where(first, outs[1], outs[0]), 64, 1)
        mixed = jnp.where(first, outs[0], outs[1]) / total
        mixed_ref[start : start + QBLOCK] = mixed.astype(BF16)
        exact_ref[start : start + QBLOCK] = mixed
        logsum = (jnp.where(first, tops[0], tops[1]) + jnp.log(total)).T
        logsum_ref[0, 0:1, start : start + QBLOCK] = logsum[0:1]
        logsum_ref[0, 1:2, start : start + QBLOCK] = logsum[64:65]
        outs = []
        tops = []


def self_forward(projected, lengths, first, count, earlier):
    seq_len = projected.shape[0]
    width = projected.shape[1] // 3
    pairs = width // LANES
    column = lambda offset: pl.BlockSpec((seq_len, LANES), lambda p: (0, p + offset))
    given = [] if earlier is None else list(earlier)
    return pl.pallas_call(
        functools.partial(passing, self_forward_kernel, 4, len(given)),
        grid=(count,),
        in_specs=[
            pl.BlockSpec(memory_space=pltpu.SMEM),
            column(first),
            column(pairs + first),
            column(2 * pairs + first),
        ]
        + [pl.BlockSpec(memory_space=pl.ANY)] * len(given),
        out_specs=[
            column(first),
            column(first),
            pl.BlockSpec((1, 8, seq_len), lambda p: (p + first, 0, 0)),
        ],
        out_shape=[
            jax.ShapeDtypeStruct((seq_len, width), BF16),
            jax.ShapeDtypeStruct((seq_len, width), F32),
            jax.ShapeDtypeStruct((pairs, 8, seq_len), F32),
        ],
        input_output_aliases={4 + i: i for i in range(len(given))},
        compiler_params=pltpu.CompilerParams(vmem_limit_bytes=48 * 2**20),
        cost_estimate=cost(8),
        name="self_forward",
    )(lengths, projected, projected, projected, *given)


AHEAD = 1
AHEAD_BACK = 2
AHEAD_CROSS = 2
SPANS_STEP = 8


def self_backward_kernel(
    length_ref,
    query_ref,
    key_ref,
    value_ref,
    grad_ref,
    exact_ref,
    logsum_ref,
    out_ref,
    key_grad_ref,
    value_grad_ref,
):
    seq_len = query_ref.shape[0]
    length = length_ref[0]
    lane = iota((1, LANES), 1)
    first = lane < 64
    row = iota((LANES, 1), 0)
    top_rows = row < 64
    padded = jnp.where(iota((seq_len, 1), 0) < length, 0.0, NEGATIVE).astype(BF16)
    keys = key_ref[...]
    values = value_ref[...]
    zero = jnp.zeros((), BF16)
    minus = -jnp.ones((), BF16)

    def beside(offset, head_lane):
        kept = (lane > head_lane) & (lane < head_lane + 4)
        return jnp.where(lane == head_lane, offset, jnp.where(kept, minus, zero))

    keys_by_head = (
        jnp.where(first, keys, beside(padded, 64)),
        jnp.where(first, beside(padded, 0), keys),
    )
    values_by_head = (
        jnp.where(first, values, beside(zero, 64)),
        jnp.where(first, beside(zero, 0), values),
    )
    keys_turned = keys.T
    turned_by_head = (
        jnp.where(top_rows, keys_turned, zero),
        jnp.where(top_rows, zero, keys_turned),
    )
    causal = iota((QBLOCK, QBLOCK), 0) <= iota((QBLOCK, QBLOCK), 1)

    def fill(turned, head, lead, parts):
        base = 64 if head == 0 else 0
        other = jnp.where(row == base, lead, zero)
        for place, part in enumerate(parts):
            other = jnp.where(row == base + 1 + place, part, other)
        own = top_rows if head == 0 else ~top_rows
        return jnp.where(own, turned, other)

    count = seq_len // QBLOCK
    units = [(block, head) for block in reversed(range(count)) for head in range(2)]
    loaded = {}

    def load(block):
        start = block * QBLOCK
        stop = start + QBLOCK
        query = query_ref[start:stop] * jnp.asarray(SCALE, BF16)
        grad = grad_ref[start:stop]
        weighted = (grad.astype(F32) * exact_ref[start:stop]).T
        return (query, grad, query.T, grad.T, weighted)

    def products(block, head):
        if head == 0:
            loaded[block] = load(block)
        _, _, query_turned, grad_turned, weighted = loaded[block]
        start = block * QBLOCK
        stop = start + QBLOCK
        delta = jnp.sum(weighted[head * 64 : head * 64 + 64], axis=0, keepdims=True)
        logsum = logsum_ref[0, head : head + 1, start:stop]
        score = dot(
            keys_by_head[head][:stop],
            fill(query_turned, head, jnp.ones((), BF16), split_three(logsum)),
        )
        centred = dot(
            values_by_head[head][:stop], fill(grad_turned, head, zero, split_three(delta))
        )
        return (score, centred)

    ahead = [products(*unit) for unit in units[:AHEAD_BACK]]
    probs_all = []
    scores_all = []
    query_grad = None
    for place_at, (block, head) in enumerate(units):
        if place_at + AHEAD_BACK < len(units):
            ahead.append(products(*units[place_at + AHEAD_BACK]))
        start = block * QBLOCK
        stop = start + QBLOCK
        score, centred = ahead.pop(0)
        prob = jnp.exp(score)
        last = jnp.where(causal, prob[start:], 0.0)
        prob = jnp.concatenate([prob[:start], last], axis=0) if block else last
        score_grad = (prob * centred).astype(BF16)
        scores_all.append(score_grad)
        probs_all.append(prob.astype(BF16))
        part = dot(turned_by_head[head][:, :stop], score_grad)
        query_grad = part if query_grad is None else query_grad + part
        if head == 0:
            continue
        query, grad = loaded[block][:2]
        out_ref[0, start:stop] = (query_grad.T * SCALE).astype(BF16)
        own_query = jnp.concatenate(
            [jnp.where(first, query, zero), jnp.where(first, zero, query)], axis=0
        )
        own_grad = jnp.concatenate(
            [jnp.where(first, grad, zero), jnp.where(first, zero, grad)], axis=0
        )
        key_part = dot(jnp.concatenate(scores_all, axis=1), own_query)
        value_part = dot(jnp.concatenate(probs_all, axis=1), own_grad)
        if block == count - 1:
            key_grad_ref[...] = key_part
            value_grad_ref[...] = value_part
        else:
            key_grad_ref[:stop] += key_part
            value_grad_ref[:stop] += value_part
        probs_all = []
        scores_all = []
        query_grad = None
    out_ref[1] = key_grad_ref[...].astype(BF16)
    out_ref[2] = value_grad_ref[...].astype(BF16)


def self_backward(projected, lengths, grad, exact, logsum, first, count, earlier):
    seq_len = projected.shape[0]
    width = projected.shape[1] // 3
    pairs = width // LANES
    column = lambda offset: pl.BlockSpec((seq_len, LANES), lambda p: (0, p + offset))
    given = [] if earlier is None else [earlier]
    return pl.pallas_call(
        functools.partial(passing, self_backward_kernel, 7, len(given)),
        grid=(count,),
        in_specs=[
            pl.BlockSpec(memory_space=pltpu.SMEM),
            column(first),
            column(pairs + first),
            column(2 * pairs + first),
            column(first),
            column(first),
            pl.BlockSpec((1, 8, seq_len), lambda p: (p + first, 0, 0)),
        ]
        + [pl.BlockSpec(memory_space=pl.ANY)] * len(given),
        out_specs=pl.BlockSpec((3, seq_len, LANES), lambda p: (0, 0, p + first)),
        out_shape=jax.ShapeDtypeStruct((3, seq_len, width), BF16),
        scratch_shapes=[pltpu.VMEM((seq_len, LANES), F32), pltpu.VMEM((seq_len, LANES), F32)],
        input_output_aliases={7: 0} if given else {},
        compiler_params=pltpu.CompilerParams(vmem_limit_bytes=48 * 2**20),
        cost_estimate=cost(12),
        name="self_backward",
    )(lengths, projected, projected, projected, grad, exact, logsum, *given)


def block_diagonal(rows):
    lane = iota((1, WIDE), 1)
    return jnp.concatenate(
        [jnp.where((lane >= h * 64) & (lane < h * 64 + 64), rows, 0) for h in range(4)], axis=0
    )


def take_diagonal(stacked):
    lane = iota((1, WIDE), 1)
    result = stacked[:SPAN]
    for h in range(1, 4):
        result = jnp.where(lane >= h * 64, stacked[h * SPAN : (h + 1) * SPAN], result)
    return result


def slot_bias(ids_ref, neighbour_lengths_ref, span, neigh_len, axis):
    shape = (1, NEIGH * neigh_len) if axis else (NEIGH * neigh_len, 1)
    place = iota(shape, axis)
    first = neighbour_lengths_ref[ids_ref[span * NEIGH]]
    second = neighbour_lengths_ref[ids_ref[span * NEIGH + 1]]
    limit = jnp.where(place < neigh_len, first, neigh_len + second)
    return jnp.where(place < limit, 0.0, NEGATIVE)


def cross_forward_kernel(ids_ref, neighbour_lengths_ref, query_ref, *refs):
    slots, mixed_ref, logsum_ref = refs[:-2], refs[-2], refs[-1]
    step = pl.program_id(0)
    neigh_len = slots[0].shape[1]
    width = query_ref.shape[1]
    units = [(span, group) for span in range(SPANS_STEP) for group in range(width // WIDE)]

    def scores(span, group):
        rows = slice(span * SPAN, (span + 1) * SPAN)
        place = slice(group * WIDE, (group + 1) * WIDE)
        queries = block_diagonal(query_ref[rows, place] * jnp.asarray(SCALE, BF16))
        keys = jnp.concatenate([ref[0, :, place] for ref in slots[span * NEIGH :][:NEIGH]], axis=0)
        return dot(queries, keys, NT)

    ahead = [scores(*unit) for unit in units[:AHEAD_CROSS]]
    for place_at, (span, group) in enumerate(units):
        if place_at + AHEAD_CROSS < len(units):
            ahead.append(scores(*units[place_at + AHEAD_CROSS]))
        if group == 0:
            bias = slot_bias(
                ids_ref, neighbour_lengths_ref, step * SPANS_STEP + span, neigh_len, 1
            )
        score = ahead.pop(0) + bias
        top = jnp.max(score, axis=-1, keepdims=True)
        expo = jnp.exp(score - top)
        total = jnp.sum(expo, axis=-1, keepdims=True)
        logsum = jnp.broadcast_to(top + jnp.log(total), (WIDE, LANES)).T
        logsum_ref[span, 0:1, group * WIDE : (group + 1) * WIDE] = logsum[0:1]
        place = slice(width + group * WIDE, width + (group + 1) * WIDE)
        values = jnp.concatenate(
            [ref[0, :, place] for ref in slots[span * NEIGH :][:NEIGH]], axis=0
        )
        out = dot(expo.astype(BF16), values) / total
        rows = slice(span * SPAN, (span + 1) * SPAN)
        mixed_ref[rows, group * WIDE : (group + 1) * WIDE] = take_diagonal(out).astype(BF16)


def cross_forward(queries, pool_keyval, ids, neighbour_lengths):
    seq_len, width = queries.shape
    neigh_len, both = pool_keyval.shape[1:]
    spans = seq_len // SPAN
    slots = SPANS_STEP * NEIGH
    rows = pl.BlockSpec((SPANS_STEP * SPAN, width), lambda c, ids, lens: (c, 0))
    slot = lambda j: pl.BlockSpec(
        (1, neigh_len, both), lambda c, ids, lens: (ids[c * slots + j], 0, 0)
    )
    return pl.pallas_call(
        cross_forward_kernel,
        grid_spec=pltpu.PrefetchScalarGridSpec(
            num_scalar_prefetch=2,
            grid=(spans // SPANS_STEP,),
            in_specs=[rows] + [slot(j) for j in range(slots)],
            out_specs=[rows, pl.BlockSpec((SPANS_STEP, 8, width), lambda c, ids, lens: (c, 0, 0))],
        ),
        out_shape=[
            jax.ShapeDtypeStruct((seq_len, width), BF16),
            jax.ShapeDtypeStruct((spans, 8, width), F32),
        ],
        compiler_params=pltpu.CompilerParams(vmem_limit_bytes=56 * 2**20),
        cost_estimate=cost(12),
        name="cross_forward",
    )(ids, neighbour_lengths, queries, *[pool_keyval] * slots)


def cross_backward_kernel(
    ids_ref,
    neighbour_lengths_ref,
    query_ref,
    grad_ref,
    key_ref,
    value_ref,
    logsum_ref,
    query_grad_ref,
    key_out_ref,
    value_out_ref,
    key_total,
    value_total,
):
    step = pl.program_id(1)
    neigh_len = key_ref.shape[1]

    @pl.when(step == 0)
    def _():
        key_total[...] = jnp.zeros_like(key_total)
        value_total[...] = jnp.zeros_like(value_total)

    def slots_of(span):
        place = (step * SPANS_STEP + span) * NEIGH
        return [ids_ref[place + slot] for slot in range(NEIGH)]

    def products(span):
        rows = slice(span * SPAN, (span + 1) * SPAN)
        queries = block_diagonal(query_ref[rows] * jnp.asarray(SCALE, BF16))
        grads = block_diagonal(grad_ref[rows])
        keys = jnp.concatenate([key_ref[ident] for ident in slots_of(span)], axis=0)
        values = jnp.concatenate([value_ref[ident] for ident in slots_of(span)], axis=0)
        return (queries, grads, keys, dot(keys, queries, NT), dot(values, grads, NT))

    place = iota((neigh_len, WIDE), 0)
    ahead = [products(span) for span in range(AHEAD_CROSS)]
    for span in range(SPANS_STEP):
        if span + AHEAD_CROSS < SPANS_STEP:
            ahead.append(products(span + AHEAD_CROSS))
        queries, grads, keys, score, prob_grad = ahead.pop(0)
        expo = jnp.exp(score - logsum_ref[span, 0:1])
        parts = []
        for slot, ident in enumerate(slots_of(span)):
            part = expo[slot * neigh_len : (slot + 1) * neigh_len]
            parts.append(jnp.where(place < neighbour_lengths_ref[ident], part, 0.0))
        prob = jnp.concatenate(parts, axis=0)
        weighted = prob * prob_grad
        score_grad = (weighted - prob * jnp.sum(weighted, axis=0, keepdims=True)).astype(BF16)
        value_part = dot(prob.astype(BF16), grads)
        key_part = dot(score_grad, queries)
        query_part = dot(score_grad, keys, TN)
        rows = slice(span * SPAN, (span + 1) * SPAN)
        query_grad_ref[rows] = (take_diagonal(query_part) * SCALE).astype(BF16)
        for slot, ident in enumerate(slots_of(span)):
            part = slice(slot * neigh_len, (slot + 1) * neigh_len)
            key_total[ident] += key_part[part]
            value_total[ident] += value_part[part]

    @pl.when(step == pl.num_programs(1) - 1)
    def _():
        key_out_ref[...] = key_total[...].astype(BF16)
        value_out_ref[...] = value_total[...].astype(BF16)


def cross_backward(
    queries, grads, pool_keyval, logsum, ids, neighbour_lengths, first, count, earlier
):
    seq_len, width = queries.shape
    pool_count, neigh_len, _ = pool_keyval.shape
    spans = seq_len // SPAN
    groups = width // WIDE
    rows = pl.BlockSpec((SPANS_STEP * SPAN, WIDE), lambda g, c, ids, lens: (c, g + first))
    pool = lambda offset: pl.BlockSpec(
        (pool_count, neigh_len, WIDE), lambda g, c, ids, lens: (0, 0, g + first + offset)
    )
    pool_shape = jax.ShapeDtypeStruct((pool_count, neigh_len, width), BF16)
    given = [] if earlier is None else list(earlier)
    return pl.pallas_call(
        functools.partial(passing, cross_backward_kernel, 7, len(given)),
        grid_spec=pltpu.PrefetchScalarGridSpec(
            num_scalar_prefetch=2,
            grid=(count, spans // SPANS_STEP),
            in_specs=[
                rows,
                rows,
                pool(0),
                pool(groups),
                pl.BlockSpec((SPANS_STEP, 8, WIDE), lambda g, c, ids, lens: (c, 0, g + first)),
            ]
            + [pl.BlockSpec(memory_space=pl.ANY)] * len(given),
            out_specs=[rows, pool(0), pool(0)],
            scratch_shapes=[
                pltpu.VMEM((pool_count, neigh_len, WIDE), F32),
                pltpu.VMEM((pool_count, neigh_len, WIDE), F32),
            ],
        ),
        out_shape=[jax.ShapeDtypeStruct((seq_len, width), BF16), pool_shape, pool_shape],
        input_output_aliases={7 + i: i for i in range(len(given))},
        compiler_params=pltpu.CompilerParams(vmem_limit_bytes=56 * 2**20),
        cost_estimate=cost(15),
        name="cross_backward",
    )(ids, neighbour_lengths, queries, grads, pool_keyval, pool_keyval, logsum, *given)

AXES = ("fsdp", "dp")
PIECES = 2
COPY_ROWS = 48
VMEM_FOLD = 32


def bits_of(size):
    return [1 << i for i in range(size.bit_length() - 1)]


def index_bits(count):
    return [1 << i for i in range(count.bit_length() - 2, -1, -1)]


class Line:
    def __init__(self):
        self.noted = []

    def note(self, *values):
        self.noted = [values[0]]

    def also(self, value):
        self.noted.append(value)

    def after(self, value):
        return self.after_all([value])[0]

    def after_all(self, values):
        if not self.noted:
            return values
        return lax.optimization_barrier((*values, *self.noted))[: len(values)]


class Plan:
    def __init__(self, rows, line):
        self.line = line
        self.inner = lax.axis_size("dp")
        self.outer = lax.axis_size("fsdp")
        self.count = self.inner * self.outer
        self.rows = rows
        self.core = [self.inner] if self.outer > 1 else []
        self.halves = 2 if self.core else 1
        self.across = self.outer // self.halves
        self.stripe = self.inner * rows
        self.half_rows = self.across * self.stripe
        self.copy_rows = min(self.stripe, COPY_ROWS)
        self.me = lax.axis_index(AXES)
        across = [bit * self.inner for bit in bits_of(self.outer)[1:]]
        along = bits_of(self.inner)
        near, far = along[: len(across)], along[len(across) :]
        self.orders = (far + near + across, far + across + near)
        self.natural = [mask for mask in index_bits(self.count) if mask not in self.core]
        self.odd = self.bit(self.core[0]) if self.core else jnp.zeros((), jnp.int32)
        self.odd_word = self.odd.reshape(1)
        self.steps = list(zip(*self.orders))
        self.places = self.arrival_places()

    def bit(self, mask):
        return (self.me // mask) % 2

    def by_core(self, even, odd):
        return jnp.where(self.odd == 0, even, odd)

    def exchange(self, values, masks):
        even, odd = masks
        pairs = []
        for index in range(self.count):
            is_odd = bool(self.core) and (index // self.core[0]) % 2 == 1
            pairs.append((index, index ^ (odd if is_odd else even)))
        return lax.ppermute(values, AXES, pairs)

    def swap(self, values):
        return self.exchange(values, (self.core[0], self.core[0])) if self.core else values

    def weight_of(self, mask):
        return 1 << (len(self.natural) - 1 - self.natural.index(mask))

    def arrival_places(self):
        blocks = jnp.arange(1 << len(self.natural), dtype=jnp.int32)
        found = []
        for order in self.orders:
            target = jnp.zeros_like(blocks)
            for place_at, mask in enumerate(order):
                flag = ((blocks >> place_at) & 1) ^ self.bit(mask)
                target = target + flag * self.weight_of(mask)
            found.append(target)
        return self.by_core(found[0], found[1])

    def fold_places(self, step):
        found = []
        for order in self.orders:
            gone = order[::-1][:step]
            left = [mask for mask in self.natural if mask not in gone]
            mask = order[::-1][step]
            high = 1 << (len(left) - 1 - left.index(mask))
            index = jnp.arange(1 << (len(left) - 1), dtype=jnp.int32)
            kept = (index // high) * (2 * high) + index % high
            own = self.bit(mask)
            found.append((kept + (1 - own) * high, kept + own * high))
        return tuple(self.by_core(found[0][i], found[1][i]) for i in range(2))


def reorder_kernel(pieces, places_ref, *refs):
    parts, outs, (buffer, sems) = refs[: -2 - pieces], refs[-2 - pieces : -2], refs[-2:]
    blocks = buffer.shape[0]
    share = blocks // len(parts)
    piece = blocks // pieces

    def copies(block):
        return pltpu.make_async_copy(
            parts[block // share].at[block % share], buffer.at[places_ref[block]], sems.at[block]
        )

    def going(index):
        return pltpu.make_async_copy(
            buffer.at[pl.ds(index * piece, piece)], outs[index], sems.at[index]
        )

    for block in range(blocks):
        copies(block).start()
    for block in range(blocks):
        copies(block).wait()
    for index in range(pieces):
        going(index).start()
    for index in range(pieces):
        going(index).wait()


def reorder(plan, parts, pieces):
    blocks = sum(part.shape[0] for part in parts)
    shape = (blocks,) + parts[0].shape[1:]
    piece = jax.ShapeDtypeStruct((blocks // pieces,) + shape[1:], BF16)
    return pl.pallas_call(
        functools.partial(reorder_kernel, pieces),
        in_specs=[pl.BlockSpec(memory_space=pltpu.SMEM)]
        + [pl.BlockSpec(memory_space=pl.ANY)] * len(parts),
        out_specs=[pl.BlockSpec(memory_space=pl.ANY)] * pieces,
        out_shape=[piece] * pieces,
        scratch_shapes=[pltpu.VMEM(shape, BF16), pltpu.SemaphoreType.DMA((blocks,))],
        compiler_params=pltpu.CompilerParams(vmem_limit_bytes=VMEM_FOLD * 2**20),
        cost_estimate=cost(0.1),
        name="reorder_blocks",
    )(plan.places, *parts)


class Gather:
    def __init__(self, plan, shard, pieces=PIECES):
        self.plan = plan
        self.pieces = pieces if plan.core else 1
        self.held = shard[None]
        self.at = 0
        self.other = None
        self.halves = None

    def launch(self):
        plan = self.plan
        if self.at < len(plan.steps):
            self.held = plan.line.after(self.held)
            plan.line.also(self.held)
            self.other = plan.exchange(self.held, plan.steps[self.at])
        else:
            held = self.held if isinstance(self.held, list) else [self.held]
            self.held = plan.line.after_all(held)
            plan.line.also(self.held[0])
            self.other = [plan.swap(piece) for piece in self.held]

    def land(self):
        plan = self.plan
        if self.at < len(plan.steps):
            other = plan.line.after(self.other)
            self.at += 1
            if self.at == len(plan.steps):
                self.held = list(reorder(plan, [self.held, other], self.pieces))
                plan.line.note(self.held[0])
            else:
                self.held = jnp.concatenate([self.held, other], axis=0)
                plan.line.note(self.held)
        else:
            others = plan.line.after_all(self.other)
            plan.line.note(others[0])
            columns = self.held[0].shape[-1]
            pieces = list(self.held) + list(others)
            self.halves = [piece.reshape(-1, columns) for piece in pieces]

    def done(self):
        return self.halves is not None

    def finish(self):
        while not self.done():
            self.land()
            if not self.done():
                self.launch()
        return self.halves


def fold_kernel(sent_places, kept_places, *refs):
    half = len(refs) // 2 - 1
    sent_in, kept_in, (sent_ref, kept_ref) = refs[:half], refs[half : 2 * half], refs[2 * half :]
    for source, target in ((sent_in, sent_ref), (kept_in, kept_ref)):
        total = source[0][...].astype(F32)
        for part in source[1:]:
            total = total + part[...].astype(F32)
        target[...] = total.astype(BF16)


def fold(places, parts):
    blocks, rows, columns = parts[0].shape
    shape = jax.ShapeDtypeStruct((blocks // 2, rows, columns), BF16)
    out = pl.BlockSpec((1, rows, columns), lambda i, sent, kept: (i, 0, 0))
    sent = pl.BlockSpec((1, rows, columns), lambda i, sent, kept: (sent[i], 0, 0))
    kept = pl.BlockSpec((1, rows, columns), lambda i, sent, kept: (kept[i], 0, 0))
    return pl.pallas_call(
        fold_kernel,
        grid_spec=pltpu.PrefetchScalarGridSpec(
            num_scalar_prefetch=2,
            grid=(blocks // 2,),
            in_specs=[sent] * len(parts) + [kept] * len(parts),
            out_specs=[out, out],
        ),
        out_shape=[shape, shape],
        compiler_params=pltpu.CompilerParams(vmem_limit_bytes=VMEM_FOLD * 2**20),
        cost_estimate=cost(0.1),
        name="fold_blocks",
    )(*places, *parts, *parts)


class Scatter:
    def __init__(self, plan, keep, send):
        self.plan = plan
        self.columns = keep.shape[1]
        shape = (1 << len(plan.natural), plan.rows, self.columns)
        self.kept = keep.reshape(shape)
        self.sent = send.reshape(shape) if plan.core else None
        self.at = -1
        self.other = None
        self.total = None

    def launch(self):
        plan = self.plan
        if self.sent is None:
            return
        self.sent = plan.line.after(self.sent)
        plan.line.also(self.sent)
        if self.at < 0:
            self.other = plan.swap(self.sent)
        else:
            self.other = plan.exchange(self.sent, plan.steps[::-1][self.at])

    def land(self):
        plan = self.plan
        parts = [self.kept] if self.other is None else [self.kept, plan.line.after(self.other)]
        self.at += 1
        if self.at < len(plan.steps):
            self.sent, self.kept = fold(plan.fold_places(self.at), parts)
            plan.line.note(self.sent)
        else:
            total = parts[0].astype(F32)
            for part in parts[1:]:
                total = total + part.astype(F32)
            self.total = total.reshape(plan.rows, self.columns)
            plan.line.note(self.total)

    def done(self):
        return self.total is not None

    def finish(self):
        while not self.done():
            self.land()
            if not self.done():
                self.launch()
        return self.total


def bundled(kernel, *spans):
    def call(*refs):
        refs = list(refs)
        for place, count in sorted(spans, reverse=True):
            middle = place + count // 2
            refs[place : place + count] = [tuple(refs[place:middle]), tuple(refs[middle : place + count])]
        return kernel(*refs)

    return call


def column_copies(plan, odd, held_refs, other_refs, target, sems, start, width, rows=None):
    copies = []

    def add(ref, at, rows, first, half):
        across, rest = divmod(first, plan.stripe)
        place = across * plan.halves * plan.stripe + rest
        if plan.halves > 1:
            place = place + half * plan.stripe
            if plan.stripe % 16 == 0 and rest % 16 == 0:
                place = pl.multiple_of(place, 16)
        copies.append(
            pltpu.make_async_copy(
                ref.at[pl.ds(at, rows), pl.ds(start, width)],
                target.at[pl.ds(place, rows), :],
                sems.at[len(copies)],
            )
        )

    rows = rows or plan.copy_rows
    for refs, half in ((held_refs, odd), (other_refs, 1 - odd))[: plan.halves]:
        piece = refs[0].shape[0]
        step = min(rows, piece)
        for first in range(0, plan.half_rows, step):
            add(refs[first // piece], first % piece, step, first, half)
    return copies


def store_halves(plan, odd, result, keep_ref, send_ref, columns):
    for across in range(plan.across):
        rows = slice(across * plan.stripe, (across + 1) * plan.stripe)
        parts = []
        for half in range(plan.halves):
            first = (across * plan.halves + half) * plan.stripe
            parts.append(result[first : first + plan.stripe])
        if plan.halves == 1:
            keep_ref[rows, columns] = parts[0].astype(BF16)
        else:
            keep_ref[rows, columns] = jnp.where(odd == 0, parts[0], parts[1]).astype(BF16)
            send_ref[rows, columns] = jnp.where(odd == 0, parts[1], parts[0]).astype(BF16)

ROWS = 512
FEED_ROWS = 256
BACK_ROWS = 256
POOL_BLOCK = 1024
BACK_BLOCK = 512
MEBI = 2**20
ANYWHERE = pl.BlockSpec(memory_space=pl.ANY)
SCALAR = pl.BlockSpec(memory_space=pltpu.SMEM)


def norm_parts(values):
    centre = jnp.mean(values, axis=-1, keepdims=True)
    centred = values - centre
    spread = jnp.mean(centred * centred, axis=-1, keepdims=True)
    inverse = lax.rsqrt(spread + EPSILON)
    return (centred * inverse, inverse)


def norm_back(values, gain, upstream):
    unit, inverse = norm_parts(values)
    gain_term = jnp.sum(upstream * unit, axis=0, keepdims=True)
    shift_term = jnp.sum(upstream, axis=0, keepdims=True)
    inner = upstream * gain
    mean_inner = jnp.mean(inner, axis=-1, keepdims=True)
    mean_both = jnp.mean(inner * unit, axis=-1, keepdims=True)
    return (inverse * (inner - mean_inner - unit * mean_both), gain_term, shift_term)


def add_terms(step, target_ref, gain_term, shift_term):
    @pl.when(step == 0)
    def _():
        target_ref[...] = jnp.zeros_like(target_ref)

    target_ref[0:1] += gain_term
    target_ref[1:2] += shift_term


def start_all(copies):
    for copy in copies:
        copy.start()


def wait_all(copies):
    for copy in copies:
        copy.wait()


def row_block(columns, last=None, block=ROWS):
    if last is None:
        return pl.BlockSpec((block, columns), lambda i: (i, 0))
    return pl.BlockSpec((block, columns), lambda i: (jnp.minimum(i, last), 0))


def params(megabytes):
    return pltpu.CompilerParams(vmem_limit_bytes=megabytes * MEBI)


def copy_sems(plan, *sets):
    return pltpu.SemaphoreType.DMA(sets + (plan.halves * plan.half_rows // min(plan.copy_rows, 48),))


def pool_kernel(plan, odd_ref, rows_ref, held_ref, other_ref, out_ref, weight_ref, sems):
    width = weight_ref.shape[1]

    @pl.when(pl.program_id(0) == 0)
    def _():
        copies = column_copies(plan, odd_ref[0], held_ref, other_ref, weight_ref, sems, 0, width)
        start_all(copies)
        wait_all(copies)

    out_ref[...] = dot(rows_ref[...], weight_ref[...]).astype(BF16)


def pool_project(plan, encoded, halves):
    rows, width = encoded.shape
    block = POOL_BLOCK
    return pl.pallas_call(
        bundled(functools.partial(pool_kernel, plan), (2, len(halves))),
        grid=(rows // block,),
        in_specs=[SCALAR, pl.BlockSpec((block, width), lambda i: (i, 0))]
        + [ANYWHERE] * len(halves),
        out_specs=[
            pl.BlockSpec((block, 2 * width), lambda i: (i, 0)),
            pl.BlockSpec((width, 2 * width), lambda i: (0, 0)),
        ],
        out_shape=[
            jax.ShapeDtypeStruct((rows, 2 * width), BF16),
            jax.ShapeDtypeStruct((width, 2 * width), BF16),
        ],
        scratch_shapes=[copy_sems(plan)],
        compiler_params=params(40),
        cost_estimate=cost(13),
        name="pool_project",
    )(plan.odd_word, encoded, *halves)


def project_kernel(
    plan,
    odd_ref,
    tokens_ref,
    held_ref,
    other_ref,
    unit_ref,
    projected_ref,
    vectors_ref,
    columns_ref,
    weight,
    pack,
    sems,
):
    width = tokens_ref.shape[1]

    @pl.when(pl.program_id(0) == 0)
    def _():
        copies = column_copies(plan, odd_ref[0], held_ref, other_ref, weight, sems.at[0], 0, 3 * width)
        copies += column_copies(
            plan, odd_ref[0], held_ref, other_ref, pack, sems.at[1], 3 * width, LANES
        )
        start_all(copies)
        wait_all(copies)
        columns_ref[...] = pack[...].astype(F32)
        vectors_ref[...] = columns_ref[...].T[:8]

    unit = norm_parts(tokens_ref[...].astype(F32))[0]
    first_in = (unit * vectors_ref[0:1] + vectors_ref[1:2]).astype(BF16)
    unit_ref[...] = unit.astype(BF16)
    projected_ref[...] = dot(first_in, weight[...]).astype(BF16)


def project(plan, tokens, halves):
    rows, width = tokens.shape
    return pl.pallas_call(
        bundled(functools.partial(project_kernel, plan), (2, len(halves))),
        grid=(rows // ROWS,),
        in_specs=[SCALAR, row_block(width)] + [ANYWHERE] * len(halves),
        out_specs=[
            row_block(width),
            row_block(3 * width),
            pl.BlockSpec((8, width), lambda i: (0, 0)),
            pl.BlockSpec((width, LANES), lambda i: (0, 0)),
            pl.BlockSpec((width, 3 * width), lambda i: (0, 0)),
        ],
        out_shape=[
            jax.ShapeDtypeStruct((rows, width), BF16),
            jax.ShapeDtypeStruct((rows, 3 * width), BF16),
            jax.ShapeDtypeStruct((8, width), F32),
            jax.ShapeDtypeStruct((width, LANES), F32),
            jax.ShapeDtypeStruct((width, 3 * width), BF16),
        ],
        scratch_shapes=[
            pltpu.VMEM((width, LANES), BF16),
            copy_sems(plan, 2),
        ],
        compiler_params=params(40),
        cost_estimate=cost(5),
        name="project",
    )(plan.odd_word, tokens, *halves)


def middle_kernel(
    plan,
    starts,
    odd_ref,
    tokens_ref,
    mixed_ref,
    vectors_ref,
    held_ref,
    other_ref,
    after_ref,
    second_in_ref,
    queries_ref,
    out_weight,
    query_weight,
    sems,
):
    width = tokens_ref.shape[1]

    @pl.when(pl.program_id(0) == 0)
    def _():
        copies = []
        for place_at, target in enumerate((out_weight, query_weight)):
            copies += column_copies(
                plan, odd_ref[0], held_ref, other_ref, target, sems.at[place_at], starts[place_at], width
            )
        start_all(copies)
        wait_all(copies)

    after = tokens_ref[...].astype(F32) + dot(mixed_ref[...], out_weight[...])
    after_ref[...] = after
    unit = norm_parts(after)[0]
    second_in = (unit * vectors_ref[2:3] + vectors_ref[3:4]).astype(BF16)
    second_in_ref[...] = second_in
    queries_ref[...] = dot(second_in, query_weight[...]).astype(BF16)


def middle(plan, starts, tokens, mixed, vectors, halves):
    rows, width = tokens.shape
    return pl.pallas_call(
        bundled(functools.partial(middle_kernel, plan, starts), (4, len(halves))),
        grid=(rows // ROWS,),
        in_specs=[
            SCALAR,
            row_block(width),
            row_block(width),
            pl.BlockSpec((8, width), lambda i: (0, 0)),
        ]
        + [ANYWHERE] * len(halves),
        out_specs=[row_block(width)] * 3 + [pl.BlockSpec((width, width), lambda i: (0, 0))] * 2,
        out_shape=[
            jax.ShapeDtypeStruct((rows, width), F32),
            jax.ShapeDtypeStruct((rows, width), BF16),
            jax.ShapeDtypeStruct((rows, width), BF16),
            jax.ShapeDtypeStruct((width, width), BF16),
            jax.ShapeDtypeStruct((width, width), BF16),
        ],
        scratch_shapes=[
            copy_sems(plan, 2),
        ],
        compiler_params=params(40),
        cost_estimate=cost(0.5),
        name="middle",
    )(plan.odd_word, tokens, mixed, vectors, *halves)


def segments_kernel(moves, in_ref, out_ref):
    lane = iota((1, LANES), 1)
    tiles = {}
    for place in range(out_ref.shape[1] // LANES):
        result = None
        for source, shift, first, last in moves[place]:
            if source not in tiles:
                tiles[source] = in_ref[:, source * LANES : (source + 1) * LANES].astype(F32)
            tile = pltpu.roll(tiles[source], shift, 1) if shift else tiles[source]
            if result is None:
                result = tile
            else:
                result = jnp.where((lane >= first) & (lane < last), tile, result)
        out_ref[:, place * LANES : (place + 1) * LANES] = result.astype(out_ref.dtype)


def swap_segments(matrix, outer, inner, size):
    rows, columns = matrix.shape
    moves = [[] for _ in range(columns // LANES)]
    for i in range(outer):
        for j in range(inner):
            source = (i * inner + j) * size
            target = (j * outer + i) * size
            done = 0
            while done < size:
                at, to = source + done, target + done
                count = min(size - done, LANES - at % LANES, LANES - to % LANES)
                shift = (to - at) % LANES
                moves[to // LANES].append((at // LANES, shift, to % LANES, to % LANES + count))
                done += count
    return pl.pallas_call(
        functools.partial(segments_kernel, moves),
        in_specs=[pl.BlockSpec(memory_space=pltpu.VMEM)],
        out_specs=pl.BlockSpec(memory_space=pltpu.VMEM),
        out_shape=jax.ShapeDtypeStruct((rows, columns), matrix.dtype),
        compiler_params=params(24),
        cost_estimate=cost(2),
        name="swap_segments",
    )(matrix)


GELU_SCALE = 0.7978845608028654
GELU_CUBE = 0.044715
TERMS_STEP = 3


def gelu_both(values):
    square = values * values
    bent = jnp.tanh(values * (GELU_SCALE + (GELU_SCALE * GELU_CUBE) * square))
    half = 0.5 + 0.5 * bent
    result = values * half
    slope = 2.0 * GELU_SCALE + (6.0 * GELU_SCALE * GELU_CUBE) * square
    return (result, half * (1.0 + (values - result) * slope))


def feed_kernel(
    plan,
    out_start,
    row_steps,
    odd_ref,
    after_ref,
    mixed_ref,
    cotangent_ref,
    vectors_ref,
    feed_held_ref,
    feed_other_ref,
    held_ref,
    other_ref,
    block_ref,
    grad_ref,
    mixed_grad_ref,
    terms_ref,
    keep_ref,
    send_ref,
    out_matrix,
    weights,
    lefts,
    rights,
    sems,
):
    step = pl.program_id(0)
    width = after_ref.shape[1]
    parts = weights.shape[1] // width // 2

    def copies(which):
        if which == 0:
            return column_copies(
                plan,
                odd_ref[0],
                held_ref,
                other_ref,
                out_matrix,
                sems.at[0],
                out_start,
                width,
                plan.stripe,
            )
        start = (which - 1) * parts * width
        return column_copies(
            plan,
            odd_ref[0],
            feed_held_ref,
            feed_other_ref,
            weights.at[:, pl.ds(start, parts * width)],
            sems.at[which],
            start,
            parts * width,
            plan.stripe,
        )

    def ready(index):
        if index == 2 * parts:
            return out_matrix[...]
        return weights[:, index * width : (index + 1) * width]

    def rows_of(place_at, await_copies):
        mixed = mixed_ref[...]
        cotangent = cotangent_ref[...]
        await_copies(0)
        out_weight = ready(2 * parts)
        after_cross = after_ref[...] + dot(mixed, out_weight)
        unit, inverse = norm_parts(after_cross)
        gain = vectors_ref[4:5]
        third_in = (unit * gain + vectors_ref[5:6]).astype(BF16)
        await_copies(1)
        up = ready(0)
        before = dot(third_in, up)
        lefts[parts, :, place_at] = third_in.T
        lefts[parts + 1, :, place_at] = mixed.T
        rights[0, place_at] = cotangent
        result = after_cross
        upstream = jnp.zeros_like(after_cross)
        await_copies(2)
        for part in range(parts):
            down = ready(parts + part)
            back = dot(cotangent, down, NT)
            hidden, slope = gelu_both(before)
            hidden = hidden.astype(BF16)
            if part + 1 < parts:
                next_up = ready(part + 1)
                before = dot(third_in, next_up)
            result = result + dot(hidden, down)
            lefts[part, :, place_at] = hidden.T
            hidden_grad = (slope * back).astype(BF16)
            rights[1 + part, place_at] = hidden_grad
            upstream = upstream + dot(hidden_grad, up, NT)
            if part + 1 < parts:
                up = next_up
        block_ref[...] = result.astype(BF16)
        inner = upstream * gain
        mean_inner = jnp.mean(inner, axis=-1, keepdims=True)
        mean_both = jnp.mean(inner * unit, axis=-1, keepdims=True)
        grad = cotangent.astype(F32) + inverse * (inner - mean_inner - unit * mean_both)
        add_terms(
            step,
            terms_ref,
            jnp.sum(upstream * unit, axis=0, keepdims=True),
            jnp.sum(upstream, axis=0, keepdims=True),
        )
        grad_ref[...] = grad
        rounded = grad.astype(BF16)
        rights[parts + 1, place_at] = rounded
        mixed_grad_ref[...] = dot(rounded, out_weight, NT).astype(BF16)

    @pl.when(step == 0)
    def _():
        for which in range(3):
            start_all(copies(which))
        rows_of(pl.ds(0, FEED_ROWS), lambda which: wait_all(copies(which)))

    @pl.when((step > 0) & (step < row_steps))
    def _():
        rows_of(
            pl.ds(pl.multiple_of(step * FEED_ROWS, FEED_ROWS), FEED_ROWS), lambda which: None
        )

    @pl.when(step >= row_steps)
    def _():
        for turn in range(TERMS_STEP):
            term = (step - row_steps) * TERMS_STEP + turn
            left = jnp.where(term < parts, term, jnp.where(term < 2 * parts, parts, parts + 1))
            right = jnp.where(term < parts, 0, term - parts + 1)
            result = dot(lefts[left], rights[right])
            columns = slice(turn * width, (turn + 1) * width)
            store_halves(plan, odd_ref[0], result, keep_ref, send_ref, columns)


def feed(plan, out_start, after, mixed, cotangent, vectors, feed_halves, halves):
    rows, width = after.shape
    parts = feed_halves[0].shape[1] // width // 2
    terms = 2 * parts + 1
    steps = rows // FEED_ROWS
    last = steps - 1
    rows_in = row_block(width, last, FEED_ROWS)
    whole = pl.BlockSpec((8, width), lambda i: (0, 0))
    slab = pl.BlockSpec(
        (plan.half_rows, TERMS_STEP * width), lambda i: (0, jnp.maximum(i - steps, 0))
    )
    slab_shape = jax.ShapeDtypeStruct((plan.half_rows, terms * width), BF16)
    return pl.pallas_call(
        bundled(
            functools.partial(feed_kernel, plan, out_start, steps),
            (5, len(feed_halves)),
            (5 + len(feed_halves), len(halves)),
        ),
        grid=(steps + terms // TERMS_STEP,),
        in_specs=[SCALAR, rows_in, rows_in, rows_in, whole]
        + [ANYWHERE] * (len(feed_halves) + len(halves)),
        out_specs=[rows_in, rows_in, rows_in, whole, slab, slab],
        out_shape=[
            jax.ShapeDtypeStruct((rows, width), BF16),
            jax.ShapeDtypeStruct((rows, width), F32),
            jax.ShapeDtypeStruct((rows, width), BF16),
            jax.ShapeDtypeStruct((8, width), F32),
            slab_shape,
            slab_shape,
        ],
        scratch_shapes=[
            pltpu.VMEM((width, width), BF16),
            pltpu.VMEM((width, 2 * parts * width), BF16),
            pltpu.VMEM((parts + 2, width, rows), BF16),
            pltpu.VMEM((parts + 2, rows, width), BF16),
            copy_sems(plan, 3),
        ],
        compiler_params=params(60),
        cost_estimate=cost(50),
        name="feed_forward",
    )(plan.odd_word, after, mixed, cotangent, vectors, *feed_halves, *halves)


def second_kernel(
    plan,
    row_steps,
    odd_ref,
    after_ref,
    grad_in_ref,
    query_grad_ref,
    second_in_ref,
    mixed_ref,
    vectors_ref,
    out_weight,
    query_weight,
    grad_ref,
    attend_ref,
    terms_ref,
    keep_ref,
    send_ref,
    lefts,
    rights,
):
    step = pl.program_id(0)
    width = after_ref.shape[1]

    place_at = pl.ds(pl.multiple_of(step * BACK_ROWS, BACK_ROWS), BACK_ROWS)
    query_grad = query_grad_ref[...]
    back, gain_term, shift_term = norm_back(
        after_ref[...], vectors_ref[2:3], dot(query_grad, query_weight[...], NT)
    )
    lefts[0, :, place_at] = second_in_ref[...].T
    lefts[1, :, place_at] = mixed_ref[...].T
    rights[0, place_at] = query_grad
    add_terms(step, terms_ref, gain_term, shift_term)
    grad = grad_in_ref[...] + back
    grad_ref[...] = grad
    rounded = grad.astype(BF16)
    attend_ref[...] = dot(rounded, out_weight[...], NT).astype(BF16)
    rights[1, place_at] = rounded

    @pl.when(step == row_steps - 1)
    def _():
        for term in range(2):
            result = dot(lefts[term], rights[term])
            columns = slice(term * width, (term + 1) * width)
            store_halves(plan, odd_ref[0], result, keep_ref, send_ref, columns)


def second_back(
    plan, after, grad_in, query_grad, second_in, mixed, vectors, out_weight, query_weight, *given
):
    rows, width = after.shape
    steps = rows // BACK_ROWS
    rows_in = row_block(width, None, BACK_ROWS)
    whole = pl.BlockSpec((8, width), lambda i: (0, 0))
    matrix = pl.BlockSpec((width, width), lambda i: (0, 0))
    slab = pl.BlockSpec((plan.half_rows, 2 * width), lambda i: (0, 1))
    slab_shape = jax.ShapeDtypeStruct((plan.half_rows, 4 * width), BF16)
    return pl.pallas_call(
        functools.partial(passing, functools.partial(second_kernel, plan, steps), 9, len(given)),
        grid=(steps,),
        in_specs=[SCALAR] + [rows_in] * 5 + [whole, matrix, matrix] + [ANYWHERE] * len(given),
        out_specs=[rows_in, rows_in, whole, slab, slab],
        out_shape=[
            jax.ShapeDtypeStruct((rows, width), F32),
            jax.ShapeDtypeStruct((rows, width), BF16),
            jax.ShapeDtypeStruct((8, width), F32),
            slab_shape,
            slab_shape,
        ],
        scratch_shapes=[
            pltpu.VMEM((2, width, rows), BF16),
            pltpu.VMEM((2, rows, width), BF16),
        ],
        input_output_aliases={9: 3, 10: 4},
        compiler_params=params(48),
        cost_estimate=cost(12),
        name="second_back",
    )(plan.odd_word, after, grad_in, query_grad, second_in, mixed, vectors, out_weight, query_weight, *given)


def first_terms_kernel(
    plan,
    odd_ref,
    unit_ref,
    projected_grad_ref,
    columns_ref,
    second_terms_ref,
    third_terms_ref,
    weight,
    keep_ref,
    send_ref,
    terms,
):
    part = pl.program_id(0)
    width = unit_ref.shape[1]

    @pl.when(part == 0)
    def _():
        terms[...] = jnp.zeros_like(terms)

    grads = projected_grad_ref[0]
    plain = dot(unit_ref[...], grads, TN)
    sums = jnp.sum(grads.astype(F32), axis=0, keepdims=True)
    gain = columns_ref[:, 0:1]
    shift = columns_ref[:, 1:2]
    place = pl.ds(pl.multiple_of(part * width, LANES), width)
    store_halves(plan, odd_ref[0], gain * plain + shift * sums, keep_ref, send_ref, place)
    matrix = weight[...].astype(F32)
    terms[:, 0:1] += jnp.sum(matrix * plain, axis=1, keepdims=True)
    terms[:, 1:2] += jnp.sum(matrix * sums, axis=1, keepdims=True)

    @pl.when(part == 2)
    def _():
        rows = jnp.concatenate(
            [
                jnp.zeros((2, width), F32),
                second_terms_ref[0:2],
                third_terms_ref[0:2],
                jnp.zeros((LANES - 6, width), F32),
            ],
            axis=0,
        )
        lane = iota((1, LANES), 1)
        result = jnp.where(lane < 2, terms[...], rows.T)
        place = slice(3 * width, 3 * width + LANES)
        store_halves(plan, odd_ref[0], result, keep_ref, send_ref, place)


def first_terms(plan, unit, projected_grad, columns, second_terms, third_terms, weight):
    rows, width = unit.shape
    whole = pl.BlockSpec((8, width), lambda i: (0, 0))
    slab = pl.BlockSpec((plan.half_rows, 3 * width + LANES), lambda i: (0, 0))
    slab_shape = jax.ShapeDtypeStruct((plan.half_rows, 3 * width + LANES), BF16)
    return pl.pallas_call(
        functools.partial(first_terms_kernel, plan),
        grid=(3,),
        in_specs=[
            SCALAR,
            pl.BlockSpec((rows, width), lambda i: (0, 0)),
            pl.BlockSpec((1, rows, width), lambda i: (i, 0, 0)),
            pl.BlockSpec((width, LANES), lambda i: (0, 0)),
            whole,
            whole,
            pl.BlockSpec((width, width), lambda i: (0, i)),
        ],
        out_specs=[slab, slab],
        out_shape=[slab_shape, slab_shape],
        scratch_shapes=[
            pltpu.VMEM((width, LANES), F32),
        ],
        compiler_params=params(56),
        cost_estimate=cost(8),
        name="first_terms",
    )(plan.odd_word, unit, projected_grad, columns, second_terms, third_terms, weight)


def first_rows_kernel(
    tokens_ref,
    grad_in_ref,
    projected_grad_ref,
    vectors_ref,
    weight,
    grad_ref,
):
    width = tokens_ref.shape[1]

    upstream = None
    for part in range(3):
        product = dot(projected_grad_ref[part], weight[:, part * width : (part + 1) * width], NT)
        upstream = product if upstream is None else upstream + product
    unit, inverse = norm_parts(tokens_ref[...].astype(F32))
    inner = upstream * vectors_ref[0:1]
    mean_inner = jnp.mean(inner, axis=-1, keepdims=True)
    mean_both = jnp.mean(inner * unit, axis=-1, keepdims=True)
    grad_ref[...] = grad_in_ref[...] + inverse * (inner - mean_inner - unit * mean_both)


def first_rows(tokens, grad_in, projected_grad, vectors, weight):
    rows, width = tokens.shape
    rows_in = row_block(width, None, FEED_ROWS)
    return pl.pallas_call(
        first_rows_kernel,
        grid=(rows // FEED_ROWS,),
        in_specs=[
            rows_in,
            rows_in,
            pl.BlockSpec((3, FEED_ROWS, width), lambda i: (0, i, 0)),
            pl.BlockSpec((8, width), lambda i: (0, 0)),
            pl.BlockSpec((width, 3 * width), lambda i: (0, 0)),
        ],
        out_specs=rows_in,
        out_shape=jax.ShapeDtypeStruct((rows, width), F32),
        compiler_params=params(52),
        cost_estimate=cost(8),
        name="first_rows",
    )(tokens, grad_in, projected_grad, vectors, weight)


def keyval_kernel(
    plan, odd_ref, rows_ref, key_ref, value_ref, keep_ref, send_ref, key_total, value_total
):
    step = pl.program_id(0)
    width = rows_ref.shape[1]
    turned = rows_ref[...].T
    key_part = dot(turned, key_ref[...])
    value_part = dot(turned, value_ref[...])

    @pl.when(step == 0)
    def _():
        key_total[...] = key_part
        value_total[...] = value_part

    @pl.when(step > 0)
    def _():
        key_total[...] += key_part
        value_total[...] += value_part

    @pl.when(step == pl.num_programs(0) - 1)
    def _():
        for place_at, total in enumerate((key_total, value_total)):
            columns = slice(place_at * width, (place_at + 1) * width)
            store_halves(plan, odd_ref[0], total[...], keep_ref, send_ref, columns)


def keyval_terms(plan, encoded, pool_keys, pool_values):
    rows, width = encoded.shape
    block = 2048
    rows_in = pl.BlockSpec((block, width), lambda i: (i, 0))
    slab = pl.BlockSpec((plan.half_rows, 2 * width), lambda i: (0, 0))
    slab_shape = jax.ShapeDtypeStruct((plan.half_rows, 4 * width), BF16)
    return pl.pallas_call(
        functools.partial(keyval_kernel, plan),
        grid=(rows // block,),
        in_specs=[SCALAR, rows_in, rows_in, rows_in],
        out_specs=[slab, slab],
        out_shape=[slab_shape, slab_shape],
        scratch_shapes=[pltpu.VMEM((width, width), F32), pltpu.VMEM((width, width), F32)],
        compiler_params=params(48),
        cost_estimate=cost(14),
        name="keyval_terms",
    )(plan.odd_word, encoded, pool_keys, pool_values)


def neighbours_kernel(key_ref, value_ref, weight_ref, out_ref):
    width = key_ref.shape[1]
    out_ref[...] = dot(key_ref[...], weight_ref[:, :width], NT) + dot(
        value_ref[...], weight_ref[:, width:], NT
    )


def neighbours_back(pool_keys, pool_values, weight, first, count, earlier):
    rows, width = pool_keys.shape
    block = BACK_BLOCK
    rows_in = pl.BlockSpec((block, width), lambda i: (i + first, 0))
    given = [] if earlier is None else [earlier]
    return pl.pallas_call(
        functools.partial(passing, neighbours_kernel, 3, len(given)),
        grid=(count,),
        in_specs=[rows_in, rows_in, pl.BlockSpec((width, 2 * width), lambda i: (0, 0))]
        + [ANYWHERE] * len(given),
        out_specs=rows_in,
        out_shape=jax.ShapeDtypeStruct((rows, width), F32),
        input_output_aliases={3: 0} if given else {},
        compiler_params=params(56),
        cost_estimate=cost(5),
        name="neighbours_back",
    )(pool_keys, pool_values, weight, *given)

def local(
    tokens,
    lengths,
    neighbours,
    neighbour_ids,
    neighbour_lengths,
    first_gain,
    first_shift,
    self_input,
    self_output,
    second_gain,
    second_shift,
    cross_query,
    cross_keyval,
    cross_output,
    third_gain,
    third_shift,
    feed_up,
    feed_down,
    cotangent,
):
    rows, width = cross_query.shape
    line = Line()
    plan = Plan(rows, line)
    steps = len(plan.steps)
    parts = feed_down.shape[0] // rows
    pool_count, neigh_len = neighbours.shape[:2]
    vectors = (first_gain, first_shift, second_gain, second_shift, third_gain, third_shift)
    vector_pack = jnp.pad(jnp.stack(vectors, axis=1), ((0, 0), (0, LANES - len(vectors))))
    rows_in = tokens[0]
    encoded = neighbours.reshape(pool_count * neigh_len, width)
    ids = neighbour_ids.reshape(-1)
    pairs = width // LANES

    def advance(*chunks, after=()):
        moving = [chunk for chunk in chunks if not chunk.done()]
        for chunk in moving:
            chunk.land()
        for chunk in moving + list(after):
            if not chunk.done():
                chunk.launch()

    def run(kernel, first, *rest):
        results = kernel(line.after(first), *rest)
        line.note(results[0] if isinstance(results, (tuple, list)) else results)
        return results

    start = Gather(plan, jnp.concatenate([self_input, vector_pack], axis=1))
    start.launch()
    middle_part = Gather(
        plan,
        jnp.concatenate(
            [line.after(cross_keyval), self_output, cross_query, cross_output], axis=1
        ),
        4,
    )
    advance(start, after=[middle_part])
    advance(start, middle_part)
    up_shard = swap_segments(line.after(feed_up), plan.count, parts, rows)
    down_shard = line.after(feed_down).reshape(parts, rows, width)
    down_shard = down_shard.swapaxes(0, 1).reshape(rows, parts * width)
    feed_part = Gather(plan, jnp.concatenate([up_shard, down_shard], axis=1))
    advance(start, after=[feed_part])
    advance(start, middle_part, feed_part)
    start_halves = start.finish()
    unit, projected, vector_rows, vector_columns, input_weight = run(
        lambda values: project(plan, values, start_halves), rows_in
    )
    advance(middle_part)
    attended = None
    for turn in range(2):
        attended = run(self_forward, projected, lengths, turn * (pairs // 2), pairs // 2, attended)
    advance(feed_part)
    advance(middle_part)
    self_mixed, self_exact, logsum = attended
    middle_halves = middle_part.finish()
    advance(feed_part)
    after_self, second_in, cross_queries, output_weight, query_weight = run(
        lambda values: middle(
            plan, (2 * width, 3 * width), rows_in, values, vector_rows, middle_halves
        ),
        self_mixed,
    )
    pool_keyval, keyval_weight = run(
        lambda values: pool_project(plan, values, middle_halves), encoded
    )
    pool_keyval = pool_keyval.reshape(pool_count, neigh_len, 2 * width)
    advance(feed_part)
    cross_mixed, cross_logsum = run(cross_forward, cross_queries, pool_keyval, ids, neighbour_lengths)
    feed_halves = feed_part.finish()
    block_out, after_cross_grad, mixed_grad, third_terms, feed_keep, feed_send = run(
        lambda values: feed(
            plan,
            4 * width,
            after_self,
            values,
            cotangent[0],
            vector_rows,
            feed_halves,
            middle_halves,
        ),
        cross_mixed,
    )
    feed_sum = Scatter(plan, feed_keep, feed_send)
    feed_sum.launch()

    crossed = run(
        cross_backward,
        cross_queries,
        mixed_grad,
        pool_keyval,
        cross_logsum,
        ids,
        neighbour_lengths,
        0,
        width // WIDE,
        None,
    )
    advance(feed_sum)
    query_grad, pool_keys, pool_values = crossed
    pool_keys = pool_keys.reshape(pool_count * neigh_len, width)
    pool_values = pool_values.reshape(pool_count * neigh_len, width)
    middle_keep, middle_send = run(
        lambda values: keyval_terms(plan, encoded, values, pool_values), pool_keys
    )
    after_self_grad, attend_grad, second_terms, middle_keep, middle_send = run(
        lambda values: second_back(
            plan,
            after_self,
            after_cross_grad,
            values,
            second_in,
            self_mixed,
            vector_rows,
            output_weight,
            query_weight,
            middle_keep,
            middle_send,
        ),
        query_grad,
    )
    middle_sum = Scatter(plan, middle_keep, middle_send)
    advance(feed_sum, after=[middle_sum])
    projected_grad = None
    for turn in range(2):
        projected_grad = run(
            lambda values: self_backward(
                projected,
                lengths,
                values,
                self_exact,
                logsum,
                turn * (pairs // 2),
                pairs // 2,
                projected_grad,
            ),
            attend_grad,
        )
        if turn == 0:
            advance(feed_sum, middle_sum)
    first_keep, first_send = run(
        lambda values: first_terms(
            plan, unit, values, vector_columns, second_terms, third_terms, input_weight
        ),
        projected_grad,
    )
    first_sum = Scatter(plan, first_keep, first_send)
    advance(feed_sum, middle_sum, after=[first_sum])
    blocks = pool_keys.shape[0] // BACK_BLOCK
    quarter = blocks // 4
    neighbours_grad = None

    def neighbours_turn(first, count, earlier):
        return run(
            lambda values: neighbours_back(
                values,
                pool_values,
                keyval_weight,
                first,
                count,
                earlier,
            ),
            pool_keys,
        )

    advance(first_sum)
    tokens_grad = run(
        lambda values: first_rows(
            rows_in, after_self_grad, values, vector_rows, input_weight
        ),
        projected_grad,
    )
    advance(feed_sum, middle_sum, first_sum)
    neighbours_grad = neighbours_turn(0, quarter, neighbours_grad)
    advance(first_sum)
    neighbours_grad = neighbours_turn(quarter, quarter, neighbours_grad)
    advance(middle_sum)
    neighbours_grad = neighbours_turn(2 * quarter, blocks - 2 * quarter, neighbours_grad)
    middle_total = middle_sum.finish()
    feed_total = line.after(feed_sum.finish())
    first_total = first_sum.finish()

    down_grad = feed_total[:, : parts * width].reshape(rows, parts, width).swapaxes(0, 1)
    up_grad = swap_segments(
        feed_total[:, parts * width : 2 * parts * width], parts, plan.count, rows
    )
    vector_grads = [first_total[:, 3 * width + i] for i in range(len(vectors))]
    return (
        block_out[None],
        tokens_grad[None],
        neighbours_grad.reshape(neighbours.shape),
        vector_grads[0],
        vector_grads[1],
        first_total[:, : 3 * width],
        middle_total[:, 3 * width :],
        vector_grads[2],
        vector_grads[3],
        middle_total[:, 2 * width : 3 * width],
        middle_total[:, : 2 * width],
        feed_total[:, 2 * parts * width :],
        vector_grads[4],
        vector_grads[5],
        up_grad,
        down_grad.reshape(feed_down.shape),
    )


def solution(mesh):
    placed = (
        P(("fsdp", "dp"), None, None),
        P(("fsdp", "dp")),
        P(("fsdp", "dp"), None, None),
        P(("fsdp", "dp"), None, None),
        P(("fsdp", "dp")),
        P(("fsdp", "dp")),
        P(("fsdp", "dp")),
        P(("fsdp", "dp"), None),
        P(("fsdp", "dp"), None),
        P(("fsdp", "dp")),
        P(("fsdp", "dp")),
        P(("fsdp", "dp"), None),
        P(("fsdp", "dp"), None),
        P(("fsdp", "dp"), None),
        P(("fsdp", "dp")),
        P(("fsdp", "dp")),
        P(("fsdp", "dp"), None),
        P(("fsdp", "dp"), None),
        P(("fsdp", "dp"), None, None),
    )
    return jax.shard_map(
        local,
        mesh=mesh,
        in_specs=placed,
        out_specs=(
            P(("fsdp", "dp"), None, None),
            P(("fsdp", "dp"), None, None),
            P(("fsdp", "dp"), None, None),
            P(("fsdp", "dp")),
            P(("fsdp", "dp")),
            P(("fsdp", "dp"), None),
            P(("fsdp", "dp"), None),
            P(("fsdp", "dp")),
            P(("fsdp", "dp")),
            P(("fsdp", "dp"), None),
            P(("fsdp", "dp"), None),
            P(("fsdp", "dp"), None),
            P(("fsdp", "dp")),
            P(("fsdp", "dp")),
            P(("fsdp", "dp"), None),
            P(("fsdp", "dp"), None),
        ),
        check_vma=False,
    )
```

```python
import functools

import jax
import jax.numpy as jnp
from jax import lax
from jax.experimental import pallas as pl
from jax.experimental.pallas import tpu as pltpu
from jax.sharding import PartitionSpec as P

HEADS = 12
SPAN = 64
NEIGH = 2
LANES = 128
WIDE = 256
QBLOCK = 256

EPSILON = 1e-05
SCALE = 0.125
NEGATIVE = -1e30
BF16 = jnp.bfloat16
F32 = jnp.float32
NT = (((1,), (1,)), ((), ()))
NN = (((1,), (0,)), ((), ()))
TN = (((0,), (0,)), ((), ()))


def dot(left, right, dims=NN):
    return lax.dot_general(left, right, dims, preferred_element_type=F32)


def iota(shape, axis):
    return lax.broadcasted_iota(jnp.int32, shape, axis)


def cost(microseconds):
    return pl.CostEstimate(
        flops=int(microseconds * 1100000000.0), bytes_accessed=0, transcendentals=0
    )


def passing(kernel, before, given, *refs):
    return kernel(*refs[:before], *refs[before + given :])


def split_three(values):
    high = values.astype(BF16)
    rest = values - high.astype(F32)
    middle = rest.astype(BF16)
    low = (rest - middle.astype(F32)).astype(BF16)
    return (high, middle, low)


def self_forward_kernel(length_ref, query_ref, key_ref, value_ref, mixed_ref, exact_ref, logsum_ref):
    seq_len = query_ref.shape[0]
    length = length_ref[0]
    lane = iota((1, LANES), 1)
    first = lane < 64
    padded = jnp.where(iota((seq_len, 1), 0) < length, 0.0, NEGATIVE).astype(BF16)
    keys = key_ref[...]
    values = value_ref[...]
    one = jnp.ones((), BF16)
    keys_by_head = (
        jnp.where(first, keys, jnp.where(lane == 64, padded, 0)),
        jnp.where(first, jnp.where(lane == 0, padded, 0), keys),
    )
    values_by_head = (jnp.where(first, values, one), jnp.where(first, one, values))
    causal = iota((QBLOCK, QBLOCK), 1) <= iota((QBLOCK, QBLOCK), 0)

    def scores(block, head):
        start = block * QBLOCK
        query = query_ref[start : start + QBLOCK] * jnp.asarray(SCALE, BF16)
        if head == 0:
            query = jnp.where(first, query, jnp.where(lane == 64, one, 0))
        else:
            query = jnp.where(first, jnp.where(lane == 0, one, 0), query)
        diagonal = dot(query, keys_by_head[head][start : start + QBLOCK], NT)
        before = dot(query, keys_by_head[head][:start], NT) if block else None
        return (jnp.where(causal, diagonal, NEGATIVE), before)

    units = [(block, head) for block in reversed(range(seq_len // QBLOCK)) for head in range(2)]
    ahead = [scores(*unit) for unit in units[:AHEAD]]
    outs = []
    tops = []
    for place_at, (block, head) in enumerate(units):
        if place_at + AHEAD < len(units):
            ahead.append(scores(*units[place_at + AHEAD]))
        start = block * QBLOCK
        diagonal, before = ahead.pop(0)
        top = jnp.max(diagonal, axis=-1, keepdims=True)
        if block:
            top = jnp.maximum(top, jnp.max(before, axis=-1, keepdims=True))
        out = dot(
            jnp.exp(diagonal - top).astype(BF16), values_by_head[head][start : start + QBLOCK]
        )
        if block:
            out = out + dot(jnp.exp(before - top).astype(BF16), values_by_head[head][:start])
        outs.append(out)
        tops.append(top)
        if head == 0:
            continue
        total = pltpu.roll(jnp.where(first, outs[1], outs[0]), 64, 1)
        mixed = jnp.where(first, outs[0], outs[1]) / total
        mixed_ref[start : start + QBLOCK] = mixed.astype(BF16)
        exact_ref[start : start + QBLOCK] = mixed
        logsum = (jnp.where(first, tops[0], tops[1]) + jnp.log(total)).T
        logsum_ref[0, 0:1, start : start + QBLOCK] = logsum[0:1]
        logsum_ref[0, 1:2, start : start + QBLOCK] = logsum[64:65]
        outs = []
        tops = []


def self_forward(projected, lengths, first, count, earlier):
    seq_len = projected.shape[0]
    width = projected.shape[1] // 3
    pairs = width // LANES
    column = lambda offset: pl.BlockSpec((seq_len, LANES), lambda p: (0, p + offset))
    given = [] if earlier is None else list(earlier)
    return pl.pallas_call(
        functools.partial(passing, self_forward_kernel, 4, len(given)),
        grid=(count,),
        in_specs=[
            pl.BlockSpec(memory_space=pltpu.SMEM),
            column(first),
            column(pairs + first),
            column(2 * pairs + first),
        ]
        + [pl.BlockSpec(memory_space=pl.ANY)] * len(given),
        out_specs=[
            column(first),
            column(first),
            pl.BlockSpec((1, 8, seq_len), lambda p: (p + first, 0, 0)),
        ],
        out_shape=[
            jax.ShapeDtypeStruct((seq_len, width), BF16),
            jax.ShapeDtypeStruct((seq_len, width), F32),
            jax.ShapeDtypeStruct((pairs, 8, seq_len), F32),
        ],
        input_output_aliases={4 + i: i for i in range(len(given))},
        compiler_params=pltpu.CompilerParams(vmem_limit_bytes=48 * 2**20),
        cost_estimate=cost(8),
        name="self_forward",
    )(lengths, projected, projected, projected, *given)


AHEAD = 1
AHEAD_BACK = 2
AHEAD_CROSS = 2
SPANS_STEP = 8
SPANS_BACK = 16


def self_backward_kernel(
    length_ref,
    query_ref,
    key_ref,
    value_ref,
    grad_ref,
    exact_ref,
    logsum_ref,
    out_ref,
    key_grad_ref,
    value_grad_ref,
):
    seq_len = query_ref.shape[0]
    length = length_ref[0]
    lane = iota((1, LANES), 1)
    first = lane < 64
    row = iota((LANES, 1), 0)
    top_rows = row < 64
    padded = jnp.where(iota((seq_len, 1), 0) < length, 0.0, NEGATIVE).astype(BF16)
    keys = key_ref[...]
    values = value_ref[...]
    zero = jnp.zeros((), BF16)
    minus = -jnp.ones((), BF16)

    def beside(offset, head_lane):
        kept = (lane > head_lane) & (lane < head_lane + 4)
        return jnp.where(lane == head_lane, offset, jnp.where(kept, minus, zero))

    keys_by_head = (
        jnp.where(first, keys, beside(padded, 64)),
        jnp.where(first, beside(padded, 0), keys),
    )
    values_by_head = (
        jnp.where(first, values, beside(zero, 64)),
        jnp.where(first, beside(zero, 0), values),
    )
    keys_turned = keys.T
    turned_by_head = (
        jnp.where(top_rows, keys_turned, zero),
        jnp.where(top_rows, zero, keys_turned),
    )
    causal = iota((QBLOCK, QBLOCK), 0) <= iota((QBLOCK, QBLOCK), 1)

    def fill(turned, head, lead, parts):
        base = 64 if head == 0 else 0
        other = jnp.where(row == base, lead, zero)
        for place, part in enumerate(parts):
            other = jnp.where(row == base + 1 + place, part, other)
        own = top_rows if head == 0 else ~top_rows
        return jnp.where(own, turned, other)

    count = seq_len // QBLOCK
    units = [(block, head) for block in reversed(range(count)) for head in range(2)]
    loaded = {}

    def load(block):
        start = block * QBLOCK
        stop = start + QBLOCK
        query = query_ref[start:stop] * jnp.asarray(SCALE, BF16)
        grad = grad_ref[start:stop]
        weighted = (grad.astype(F32) * exact_ref[start:stop]).T
        return (query, grad, query.T, grad.T, weighted)

    def products(block, head):
        if head == 0:
            loaded[block] = load(block)
        _, _, query_turned, grad_turned, weighted = loaded[block]
        start = block * QBLOCK
        stop = start + QBLOCK
        delta = jnp.sum(weighted[head * 64 : head * 64 + 64], axis=0, keepdims=True)
        logsum = logsum_ref[0, head : head + 1, start:stop]
        score = dot(
            keys_by_head[head][:stop],
            fill(query_turned, head, jnp.ones((), BF16), split_three(logsum)),
        )
        centred = dot(
            values_by_head[head][:stop], fill(grad_turned, head, zero, split_three(delta))
        )
        return (score, centred)

    ahead = [products(*unit) for unit in units[:AHEAD_BACK]]
    probs_all = []
    scores_all = []
    query_grad = None
    for place_at, (block, head) in enumerate(units):
        if place_at + AHEAD_BACK < len(units):
            ahead.append(products(*units[place_at + AHEAD_BACK]))
        start = block * QBLOCK
        stop = start + QBLOCK
        score, centred = ahead.pop(0)
        prob = jnp.exp(score)
        last = jnp.where(causal, prob[start:], 0.0)
        prob = jnp.concatenate([prob[:start], last], axis=0) if block else last
        score_grad = (prob * centred).astype(BF16)
        scores_all.append(score_grad)
        probs_all.append(prob.astype(BF16))
        part = dot(turned_by_head[head][:, :stop], score_grad)
        query_grad = part if query_grad is None else query_grad + part
        if head == 0:
            continue
        query, grad = loaded[block][:2]
        out_ref[0, start:stop] = (query_grad.T * SCALE).astype(BF16)
        own_query = jnp.concatenate(
            [jnp.where(first, query, zero), jnp.where(first, zero, query)], axis=0
        )
        own_grad = jnp.concatenate(
            [jnp.where(first, grad, zero), jnp.where(first, zero, grad)], axis=0
        )
        key_part = dot(jnp.concatenate(scores_all, axis=1), own_query)
        value_part = dot(jnp.concatenate(probs_all, axis=1), own_grad)
        if block == count - 1:
            key_grad_ref[...] = key_part
            value_grad_ref[...] = value_part
        else:
            key_grad_ref[:stop] += key_part
            value_grad_ref[:stop] += value_part
        probs_all = []
        scores_all = []
        query_grad = None
    out_ref[1] = key_grad_ref[...].astype(BF16)
    out_ref[2] = value_grad_ref[...].astype(BF16)


def self_backward(projected, lengths, grad, exact, logsum, first, count, earlier):
    seq_len = projected.shape[0]
    width = projected.shape[1] // 3
    pairs = width // LANES
    column = lambda offset: pl.BlockSpec((seq_len, LANES), lambda p: (0, p + offset))
    given = [] if earlier is None else [earlier]
    return pl.pallas_call(
        functools.partial(passing, self_backward_kernel, 7, len(given)),
        grid=(count,),
        in_specs=[
            pl.BlockSpec(memory_space=pltpu.SMEM),
            column(first),
            column(pairs + first),
            column(2 * pairs + first),
            column(first),
            column(first),
            pl.BlockSpec((1, 8, seq_len), lambda p: (p + first, 0, 0)),
        ]
        + [pl.BlockSpec(memory_space=pl.ANY)] * len(given),
        out_specs=pl.BlockSpec((3, seq_len, LANES), lambda p: (0, 0, p + first)),
        out_shape=jax.ShapeDtypeStruct((3, seq_len, width), BF16),
        scratch_shapes=[pltpu.VMEM((seq_len, LANES), F32), pltpu.VMEM((seq_len, LANES), F32)],
        input_output_aliases={7: 0} if given else {},
        compiler_params=pltpu.CompilerParams(vmem_limit_bytes=48 * 2**20),
        cost_estimate=cost(12),
        name="self_backward",
    )(lengths, projected, projected, projected, grad, exact, logsum, *given)


def block_diagonal(rows):
    lane = iota((1, WIDE), 1)
    return jnp.concatenate(
        [jnp.where((lane >= h * 64) & (lane < h * 64 + 64), rows, 0) for h in range(4)], axis=0
    )


def take_diagonal(stacked):
    lane = iota((1, WIDE), 1)
    result = stacked[:SPAN]
    for h in range(1, 4):
        result = jnp.where(lane >= h * 64, stacked[h * SPAN : (h + 1) * SPAN], result)
    return result


def slot_bias(ids_ref, neighbour_lengths_ref, span, neigh_len, axis):
    shape = (1, NEIGH * neigh_len) if axis else (NEIGH * neigh_len, 1)
    place = iota(shape, axis)
    first = neighbour_lengths_ref[ids_ref[span * NEIGH]]
    second = neighbour_lengths_ref[ids_ref[span * NEIGH + 1]]
    limit = jnp.where(place < neigh_len, first, neigh_len + second)
    return jnp.where(place < limit, 0.0, NEGATIVE)


def cross_forward_kernel(ids_ref, neighbour_lengths_ref, query_ref, *refs):
    slots, mixed_ref, logsum_ref = refs[:-2], refs[-2], refs[-1]
    step = pl.program_id(0)
    neigh_len = slots[0].shape[1]
    width = query_ref.shape[1]
    units = [(span, group) for span in range(SPANS_STEP) for group in range(width // WIDE)]

    def scores(span, group):
        rows = slice(span * SPAN, (span + 1) * SPAN)
        place = slice(group * WIDE, (group + 1) * WIDE)
        queries = block_diagonal(query_ref[rows, place] * jnp.asarray(SCALE, BF16))
        keys = jnp.concatenate([ref[0, :, place] for ref in slots[span * NEIGH :][:NEIGH]], axis=0)
        return dot(queries, keys, NT)

    ahead = [scores(*unit) for unit in units[:AHEAD_CROSS]]
    for place_at, (span, group) in enumerate(units):
        if place_at + AHEAD_CROSS < len(units):
            ahead.append(scores(*units[place_at + AHEAD_CROSS]))
        if group == 0:
            bias = slot_bias(
                ids_ref, neighbour_lengths_ref, step * SPANS_STEP + span, neigh_len, 1
            )
        score = ahead.pop(0) + bias
        top = jnp.max(score, axis=-1, keepdims=True)
        expo = jnp.exp(score - top)
        total = jnp.sum(expo, axis=-1, keepdims=True)
        logsum = jnp.broadcast_to(top + jnp.log(total), (WIDE, LANES)).T
        logsum_ref[span, 0:1, group * WIDE : (group + 1) * WIDE] = logsum[0:1]
        place = slice(width + group * WIDE, width + (group + 1) * WIDE)
        values = jnp.concatenate(
            [ref[0, :, place] for ref in slots[span * NEIGH :][:NEIGH]], axis=0
        )
        out = dot(expo.astype(BF16), values) / total
        rows = slice(span * SPAN, (span + 1) * SPAN)
        mixed_ref[rows, group * WIDE : (group + 1) * WIDE] = take_diagonal(out).astype(BF16)


def cross_forward(queries, pool_keyval, ids, neighbour_lengths):
    seq_len, width = queries.shape
    neigh_len, both = pool_keyval.shape[1:]
    spans = seq_len // SPAN
    slots = SPANS_STEP * NEIGH
    rows = pl.BlockSpec((SPANS_STEP * SPAN, width), lambda c, ids, lens: (c, 0))
    slot = lambda j: pl.BlockSpec(
        (1, neigh_len, both), lambda c, ids, lens: (ids[c * slots + j], 0, 0)
    )
    return pl.pallas_call(
        cross_forward_kernel,
        grid_spec=pltpu.PrefetchScalarGridSpec(
            num_scalar_prefetch=2,
            grid=(spans // SPANS_STEP,),
            in_specs=[rows] + [slot(j) for j in range(slots)],
            out_specs=[rows, pl.BlockSpec((SPANS_STEP, 8, width), lambda c, ids, lens: (c, 0, 0))],
        ),
        out_shape=[
            jax.ShapeDtypeStruct((seq_len, width), BF16),
            jax.ShapeDtypeStruct((spans, 8, width), F32),
        ],
        compiler_params=pltpu.CompilerParams(vmem_limit_bytes=56 * 2**20),
        cost_estimate=cost(12),
        name="cross_forward",
    )(ids, neighbour_lengths, queries, *[pool_keyval] * slots)


def cross_backward_kernel(
    ids_ref,
    neighbour_lengths_ref,
    query_ref,
    grad_ref,
    key_ref,
    value_ref,
    logsum_ref,
    query_grad_ref,
    key_out_ref,
    value_out_ref,
    key_total,
    value_total,
):
    step = pl.program_id(1)
    neigh_len = key_ref.shape[1]

    @pl.when(step == 0)
    def _():
        key_total[...] = jnp.zeros_like(key_total)
        value_total[...] = jnp.zeros_like(value_total)

    def slots_of(span):
        place = (step * SPANS_BACK + span) * NEIGH
        return [ids_ref[place + slot] for slot in range(NEIGH)]

    def products(span):
        rows = slice(span * SPAN, (span + 1) * SPAN)
        queries = block_diagonal(query_ref[rows] * jnp.asarray(SCALE, BF16))
        grads = block_diagonal(grad_ref[rows])
        keys = jnp.concatenate([key_ref[ident] for ident in slots_of(span)], axis=0)
        values = jnp.concatenate([value_ref[ident] for ident in slots_of(span)], axis=0)
        return (queries, grads, keys, dot(keys, queries, NT), dot(values, grads, NT))

    place = iota((neigh_len, WIDE), 0)
    ahead = [products(span) for span in range(AHEAD_CROSS)]
    for span in range(SPANS_BACK):
        if span + AHEAD_CROSS < SPANS_BACK:
            ahead.append(products(span + AHEAD_CROSS))
        queries, grads, keys, score, prob_grad = ahead.pop(0)
        expo = jnp.exp(score - logsum_ref[span, 0:1])
        parts = []
        for slot, ident in enumerate(slots_of(span)):
            part = expo[slot * neigh_len : (slot + 1) * neigh_len]
            parts.append(jnp.where(place < neighbour_lengths_ref[ident], part, 0.0))
        prob = jnp.concatenate(parts, axis=0)
        weighted = prob * prob_grad
        score_grad = (weighted - prob * jnp.sum(weighted, axis=0, keepdims=True)).astype(BF16)
        value_part = dot(prob.astype(BF16), grads)
        key_part = dot(score_grad, queries)
        query_part = dot(score_grad, keys, TN)
        rows = slice(span * SPAN, (span + 1) * SPAN)
        query_grad_ref[rows] = (take_diagonal(query_part) * SCALE).astype(BF16)
        for slot, ident in enumerate(slots_of(span)):
            part = slice(slot * neigh_len, (slot + 1) * neigh_len)
            key_total[ident] += key_part[part]
            value_total[ident] += value_part[part]

    @pl.when(step == pl.num_programs(1) - 1)
    def _():
        key_out_ref[...] = key_total[...].astype(BF16)
        value_out_ref[...] = value_total[...].astype(BF16)


def cross_backward(
    queries, grads, pool_keyval, logsum, ids, neighbour_lengths, first, count, earlier
):
    seq_len, width = queries.shape
    pool_count, neigh_len, _ = pool_keyval.shape
    spans = seq_len // SPAN
    groups = width // WIDE
    rows = pl.BlockSpec((SPANS_BACK * SPAN, WIDE), lambda g, c, ids, lens: (c, g + first))
    pool = lambda offset: pl.BlockSpec(
        (pool_count, neigh_len, WIDE), lambda g, c, ids, lens: (0, 0, g + first + offset)
    )
    pool_shape = jax.ShapeDtypeStruct((pool_count, neigh_len, width), BF16)
    given = [] if earlier is None else list(earlier)
    return pl.pallas_call(
        functools.partial(passing, cross_backward_kernel, 7, len(given)),
        grid_spec=pltpu.PrefetchScalarGridSpec(
            num_scalar_prefetch=2,
            grid=(count, spans // SPANS_BACK),
            in_specs=[
                rows,
                rows,
                pool(0),
                pool(groups),
                pl.BlockSpec((SPANS_BACK, 8, WIDE), lambda g, c, ids, lens: (c, 0, g + first)),
            ]
            + [pl.BlockSpec(memory_space=pl.ANY)] * len(given),
            out_specs=[rows, pool(0), pool(0)],
            scratch_shapes=[
                pltpu.VMEM((pool_count, neigh_len, WIDE), F32),
                pltpu.VMEM((pool_count, neigh_len, WIDE), F32),
            ],
        ),
        out_shape=[jax.ShapeDtypeStruct((seq_len, width), BF16), pool_shape, pool_shape],
        input_output_aliases={7 + i: i for i in range(len(given))},
        compiler_params=pltpu.CompilerParams(vmem_limit_bytes=56 * 2**20),
        cost_estimate=cost(15),
        name="cross_backward",
    )(ids, neighbour_lengths, queries, grads, pool_keyval, pool_keyval, logsum, *given)

AXES = ("fsdp", "dp")
PIECES = 2
COPY_ROWS = 48
VMEM_FOLD = 32


def bits_of(size):
    return [1 << i for i in range(size.bit_length() - 1)]


def index_bits(count):
    return [1 << i for i in range(count.bit_length() - 2, -1, -1)]


class Line:
    def __init__(self):
        self.noted = []

    def note(self, *values):
        self.noted = [values[0]]

    def also(self, value):
        self.noted.append(value)

    def after(self, value):
        return self.after_all([value])[0]

    def after_all(self, values):
        if not self.noted:
            return values
        return lax.optimization_barrier((*values, *self.noted))[: len(values)]


class Plan:
    def __init__(self, rows, line):
        self.line = line
        self.inner = lax.axis_size("dp")
        self.outer = lax.axis_size("fsdp")
        self.count = self.inner * self.outer
        self.rows = rows
        self.core = [self.inner] if self.outer > 1 else []
        self.halves = 2 if self.core else 1
        self.across = self.outer // self.halves
        self.stripe = self.inner * rows
        self.half_rows = self.across * self.stripe
        self.copy_rows = min(self.stripe, COPY_ROWS)
        self.me = lax.axis_index(AXES)
        across = [bit * self.inner for bit in bits_of(self.outer)[1:]]
        along = bits_of(self.inner)
        near, far = along[: len(across)], along[len(across) :]
        self.orders = (far + near + across, far + across + near)
        self.natural = [mask for mask in index_bits(self.count) if mask not in self.core]
        self.odd = self.bit(self.core[0]) if self.core else jnp.zeros((), jnp.int32)
        self.odd_word = self.odd.reshape(1)
        self.steps = list(zip(*self.orders))
        self.places = self.arrival_places()

    def bit(self, mask):
        return (self.me // mask) % 2

    def by_core(self, even, odd):
        return jnp.where(self.odd == 0, even, odd)

    def exchange(self, values, masks):
        even, odd = masks
        pairs = []
        for index in range(self.count):
            is_odd = bool(self.core) and (index // self.core[0]) % 2 == 1
            pairs.append((index, index ^ (odd if is_odd else even)))
        return lax.ppermute(values, AXES, pairs)

    def swap(self, values):
        return self.exchange(values, (self.core[0], self.core[0])) if self.core else values

    def weight_of(self, mask):
        return 1 << (len(self.natural) - 1 - self.natural.index(mask))

    def arrival_places(self):
        blocks = jnp.arange(1 << len(self.natural), dtype=jnp.int32)
        found = []
        for order in self.orders:
            target = jnp.zeros_like(blocks)
            for place_at, mask in enumerate(order):
                flag = ((blocks >> place_at) & 1) ^ self.bit(mask)
                target = target + flag * self.weight_of(mask)
            found.append(target)
        return self.by_core(found[0], found[1])

    def fold_places(self, step):
        found = []
        for order in self.orders:
            gone = order[::-1][:step]
            left = [mask for mask in self.natural if mask not in gone]
            mask = order[::-1][step]
            high = 1 << (len(left) - 1 - left.index(mask))
            index = jnp.arange(1 << (len(left) - 1), dtype=jnp.int32)
            kept = (index // high) * (2 * high) + index % high
            own = self.bit(mask)
            found.append((kept + (1 - own) * high, kept + own * high))
        return tuple(self.by_core(found[0][i], found[1][i]) for i in range(2))


def reorder_kernel(pieces, places_ref, *refs):
    parts, outs, (buffer, sems) = refs[: -2 - pieces], refs[-2 - pieces : -2], refs[-2:]
    blocks = buffer.shape[0]
    share = blocks // len(parts)
    piece = blocks // pieces

    def copies(block):
        return pltpu.make_async_copy(
            parts[block // share].at[block % share], buffer.at[places_ref[block]], sems.at[block]
        )

    def going(index):
        return pltpu.make_async_copy(
            buffer.at[pl.ds(index * piece, piece)], outs[index], sems.at[index]
        )

    for block in range(blocks):
        copies(block).start()
    for block in range(blocks):
        copies(block).wait()
    for index in range(pieces):
        going(index).start()
    for index in range(pieces):
        going(index).wait()


def reorder(plan, parts, pieces):
    blocks = sum(part.shape[0] for part in parts)
    shape = (blocks,) + parts[0].shape[1:]
    piece = jax.ShapeDtypeStruct((blocks // pieces,) + shape[1:], BF16)
    return pl.pallas_call(
        functools.partial(reorder_kernel, pieces),
        in_specs=[pl.BlockSpec(memory_space=pltpu.SMEM)]
        + [pl.BlockSpec(memory_space=pl.ANY)] * len(parts),
        out_specs=[pl.BlockSpec(memory_space=pl.ANY)] * pieces,
        out_shape=[piece] * pieces,
        scratch_shapes=[pltpu.VMEM(shape, BF16), pltpu.SemaphoreType.DMA((blocks,))],
        compiler_params=pltpu.CompilerParams(vmem_limit_bytes=VMEM_FOLD * 2**20),
        cost_estimate=cost(0.1),
        name="reorder_blocks",
    )(plan.places, *parts)


class Gather:
    def __init__(self, plan, shard, pieces=PIECES):
        self.plan = plan
        self.pieces = pieces if plan.core else 1
        self.held = shard[None]
        self.at = 0
        self.other = None
        self.halves = None

    def launch(self):
        plan = self.plan
        if self.at < len(plan.steps):
            self.held = plan.line.after(self.held)
            plan.line.also(self.held)
            self.other = plan.exchange(self.held, plan.steps[self.at])
        else:
            held = self.held if isinstance(self.held, list) else [self.held]
            self.held = plan.line.after_all(held)
            plan.line.also(self.held[0])
            self.other = [plan.swap(piece) for piece in self.held]

    def land(self):
        plan = self.plan
        if self.at < len(plan.steps):
            other = plan.line.after(self.other)
            self.at += 1
            if self.at == len(plan.steps):
                self.held = list(reorder(plan, [self.held, other], self.pieces))
                plan.line.note(self.held[0])
            else:
                self.held = jnp.concatenate([self.held, other], axis=0)
                plan.line.note(self.held)
        else:
            others = plan.line.after_all(self.other)
            plan.line.note(others[0])
            columns = self.held[0].shape[-1]
            pieces = list(self.held) + list(others)
            self.halves = [piece.reshape(-1, columns) for piece in pieces]

    def done(self):
        return self.halves is not None

    def finish(self):
        while not self.done():
            self.land()
            if not self.done():
                self.launch()
        return self.halves


def fold_kernel(sent_places, kept_places, *refs):
    half = len(refs) // 2 - 1
    sent_in, kept_in, (sent_ref, kept_ref) = refs[:half], refs[half : 2 * half], refs[2 * half :]
    for source, target in ((sent_in, sent_ref), (kept_in, kept_ref)):
        total = source[0][...].astype(F32)
        for part in source[1:]:
            total = total + part[...].astype(F32)
        target[...] = total.astype(BF16)


def fold(places, parts):
    blocks, rows, columns = parts[0].shape
    shape = jax.ShapeDtypeStruct((blocks // 2, rows, columns), BF16)
    out = pl.BlockSpec((1, rows, columns), lambda i, sent, kept: (i, 0, 0))
    sent = pl.BlockSpec((1, rows, columns), lambda i, sent, kept: (sent[i], 0, 0))
    kept = pl.BlockSpec((1, rows, columns), lambda i, sent, kept: (kept[i], 0, 0))
    return pl.pallas_call(
        fold_kernel,
        grid_spec=pltpu.PrefetchScalarGridSpec(
            num_scalar_prefetch=2,
            grid=(blocks // 2,),
            in_specs=[sent] * len(parts) + [kept] * len(parts),
            out_specs=[out, out],
        ),
        out_shape=[shape, shape],
        compiler_params=pltpu.CompilerParams(vmem_limit_bytes=VMEM_FOLD * 2**20),
        cost_estimate=cost(0.1),
        name="fold_blocks",
    )(*places, *parts, *parts)


class Scatter:
    def __init__(self, plan, keep, send):
        self.plan = plan
        self.columns = keep.shape[1]
        shape = (1 << len(plan.natural), plan.rows, self.columns)
        self.kept = keep.reshape(shape)
        self.sent = send.reshape(shape) if plan.core else None
        self.at = -1
        self.other = None
        self.total = None

    def launch(self):
        plan = self.plan
        if self.sent is None:
            return
        self.sent = plan.line.after(self.sent)
        plan.line.also(self.sent)
        if self.at < 0:
            self.other = plan.swap(self.sent)
        else:
            self.other = plan.exchange(self.sent, plan.steps[::-1][self.at])

    def land(self):
        plan = self.plan
        parts = [self.kept] if self.other is None else [self.kept, plan.line.after(self.other)]
        self.at += 1
        if self.at < len(plan.steps):
            self.sent, self.kept = fold(plan.fold_places(self.at), parts)
            plan.line.note(self.sent)
        else:
            total = parts[0].astype(F32)
            for part in parts[1:]:
                total = total + part.astype(F32)
            self.total = total.reshape(plan.rows, self.columns)
            plan.line.note(self.total)

    def done(self):
        return self.total is not None

    def finish(self):
        while not self.done():
            self.land()
            if not self.done():
                self.launch()
        return self.total


def bundled(kernel, *spans):
    def call(*refs):
        refs = list(refs)
        for place, count in sorted(spans, reverse=True):
            middle = place + count // 2
            refs[place : place + count] = [tuple(refs[place:middle]), tuple(refs[middle : place + count])]
        return kernel(*refs)

    return call


def column_copies(plan, odd, held_refs, other_refs, target, sems, start, width, rows=None):
    copies = []

    def add(ref, at, rows, first, half):
        across, rest = divmod(first, plan.stripe)
        place = across * plan.halves * plan.stripe + rest
        if plan.halves > 1:
            place = place + half * plan.stripe
            if plan.stripe % 16 == 0 and rest % 16 == 0:
                place = pl.multiple_of(place, 16)
        copies.append(
            pltpu.make_async_copy(
                ref.at[pl.ds(at, rows), pl.ds(start, width)],
                target.at[pl.ds(place, rows), :],
                sems.at[len(copies)],
            )
        )

    rows = rows or plan.copy_rows
    for refs, half in ((held_refs, odd), (other_refs, 1 - odd))[: plan.halves]:
        piece = refs[0].shape[0]
        step = min(rows, piece)
        for first in range(0, plan.half_rows, step):
            add(refs[first // piece], first % piece, step, first, half)
    return copies


def store_halves(plan, odd, result, keep_ref, send_ref, columns):
    for across in range(plan.across):
        rows = slice(across * plan.stripe, (across + 1) * plan.stripe)
        parts = []
        for half in range(plan.halves):
            first = (across * plan.halves + half) * plan.stripe
            parts.append(result[first : first + plan.stripe])
        if plan.halves == 1:
            keep_ref[rows, columns] = parts[0].astype(BF16)
        else:
            keep_ref[rows, columns] = jnp.where(odd == 0, parts[0], parts[1]).astype(BF16)
            send_ref[rows, columns] = jnp.where(odd == 0, parts[1], parts[0]).astype(BF16)

ROWS = 512
FEED_ROWS = 256
BACK_ROWS = 256
POOL_BLOCK = 1024
BACK_BLOCK = 512
MEBI = 2**20
ANYWHERE = pl.BlockSpec(memory_space=pl.ANY)
SCALAR = pl.BlockSpec(memory_space=pltpu.SMEM)


def norm_parts(values):
    centre = jnp.mean(values, axis=-1, keepdims=True)
    centred = values - centre
    spread = jnp.mean(centred * centred, axis=-1, keepdims=True)
    inverse = lax.rsqrt(spread + EPSILON)
    return (centred * inverse, inverse)


def norm_back(values, gain, upstream):
    unit, inverse = norm_parts(values)
    gain_term = jnp.sum(upstream * unit, axis=0, keepdims=True)
    shift_term = jnp.sum(upstream, axis=0, keepdims=True)
    inner = upstream * gain
    mean_inner = jnp.mean(inner, axis=-1, keepdims=True)
    mean_both = jnp.mean(inner * unit, axis=-1, keepdims=True)
    return (inverse * (inner - mean_inner - unit * mean_both), gain_term, shift_term)


def add_terms(step, target_ref, gain_term, shift_term):
    @pl.when(step == 0)
    def _():
        target_ref[...] = jnp.zeros_like(target_ref)

    target_ref[0:1] += gain_term
    target_ref[1:2] += shift_term


def start_all(copies):
    for copy in copies:
        copy.start()


def wait_all(copies):
    for copy in copies:
        copy.wait()


def row_block(columns, last=None, block=ROWS):
    if last is None:
        return pl.BlockSpec((block, columns), lambda i: (i, 0))
    return pl.BlockSpec((block, columns), lambda i: (jnp.minimum(i, last), 0))


def params(megabytes):
    return pltpu.CompilerParams(vmem_limit_bytes=megabytes * MEBI)


def copy_sems(plan, *sets):
    return pltpu.SemaphoreType.DMA(sets + (plan.halves * plan.half_rows // min(plan.copy_rows, 48),))


def pool_kernel(plan, odd_ref, rows_ref, held_ref, other_ref, out_ref, weight_ref, sems):
    width = weight_ref.shape[1]

    @pl.when(pl.program_id(0) == 0)
    def _():
        copies = column_copies(plan, odd_ref[0], held_ref, other_ref, weight_ref, sems, 0, width)
        start_all(copies)
        wait_all(copies)

    out_ref[...] = dot(rows_ref[...], weight_ref[...]).astype(BF16)


def pool_project(plan, encoded, halves):
    rows, width = encoded.shape
    block = POOL_BLOCK
    return pl.pallas_call(
        bundled(functools.partial(pool_kernel, plan), (2, len(halves))),
        grid=(rows // block,),
        in_specs=[SCALAR, pl.BlockSpec((block, width), lambda i: (i, 0))]
        + [ANYWHERE] * len(halves),
        out_specs=[
            pl.BlockSpec((block, 2 * width), lambda i: (i, 0)),
            pl.BlockSpec((width, 2 * width), lambda i: (0, 0)),
        ],
        out_shape=[
            jax.ShapeDtypeStruct((rows, 2 * width), BF16),
            jax.ShapeDtypeStruct((width, 2 * width), BF16),
        ],
        scratch_shapes=[copy_sems(plan)],
        compiler_params=params(40),
        cost_estimate=cost(13),
        name="pool_project",
    )(plan.odd_word, encoded, *halves)


def project_kernel(
    plan,
    odd_ref,
    tokens_ref,
    held_ref,
    other_ref,
    unit_ref,
    projected_ref,
    vectors_ref,
    columns_ref,
    weight,
    pack,
    sems,
):
    width = tokens_ref.shape[1]

    @pl.when(pl.program_id(0) == 0)
    def _():
        copies = column_copies(plan, odd_ref[0], held_ref, other_ref, weight, sems.at[0], 0, 3 * width)
        copies += column_copies(
            plan, odd_ref[0], held_ref, other_ref, pack, sems.at[1], 3 * width, LANES
        )
        start_all(copies)
        wait_all(copies)
        columns_ref[...] = pack[...].astype(F32)
        vectors_ref[...] = columns_ref[...].T[:8]

    unit = norm_parts(tokens_ref[...].astype(F32))[0]
    first_in = (unit * vectors_ref[0:1] + vectors_ref[1:2]).astype(BF16)
    unit_ref[...] = unit.astype(BF16)
    projected_ref[...] = dot(first_in, weight[...]).astype(BF16)


def project(plan, tokens, halves):
    rows, width = tokens.shape
    return pl.pallas_call(
        bundled(functools.partial(project_kernel, plan), (2, len(halves))),
        grid=(rows // ROWS,),
        in_specs=[SCALAR, row_block(width)] + [ANYWHERE] * len(halves),
        out_specs=[
            row_block(width),
            row_block(3 * width),
            pl.BlockSpec((8, width), lambda i: (0, 0)),
            pl.BlockSpec((width, LANES), lambda i: (0, 0)),
            pl.BlockSpec((width, 3 * width), lambda i: (0, 0)),
        ],
        out_shape=[
            jax.ShapeDtypeStruct((rows, width), BF16),
            jax.ShapeDtypeStruct((rows, 3 * width), BF16),
            jax.ShapeDtypeStruct((8, width), F32),
            jax.ShapeDtypeStruct((width, LANES), F32),
            jax.ShapeDtypeStruct((width, 3 * width), BF16),
        ],
        scratch_shapes=[
            pltpu.VMEM((width, LANES), BF16),
            copy_sems(plan, 2),
        ],
        compiler_params=params(40),
        cost_estimate=cost(5),
        name="project",
    )(plan.odd_word, tokens, *halves)


def middle_kernel(
    plan,
    starts,
    odd_ref,
    tokens_ref,
    mixed_ref,
    vectors_ref,
    held_ref,
    other_ref,
    after_ref,
    second_in_ref,
    queries_ref,
    out_weight,
    query_weight,
    sems,
):
    width = tokens_ref.shape[1]

    @pl.when(pl.program_id(0) == 0)
    def _():
        copies = []
        for place_at, target in enumerate((out_weight, query_weight)):
            copies += column_copies(
                plan, odd_ref[0], held_ref, other_ref, target, sems.at[place_at], starts[place_at], width
            )
        start_all(copies)
        wait_all(copies)

    after = tokens_ref[...].astype(F32) + dot(mixed_ref[...], out_weight[...])
    after_ref[...] = after
    unit = norm_parts(after)[0]
    second_in = (unit * vectors_ref[2:3] + vectors_ref[3:4]).astype(BF16)
    second_in_ref[...] = second_in
    queries_ref[...] = dot(second_in, query_weight[...]).astype(BF16)


def middle(plan, starts, tokens, mixed, vectors, halves):
    rows, width = tokens.shape
    return pl.pallas_call(
        bundled(functools.partial(middle_kernel, plan, starts), (4, len(halves))),
        grid=(rows // ROWS,),
        in_specs=[
            SCALAR,
            row_block(width),
            row_block(width),
            pl.BlockSpec((8, width), lambda i: (0, 0)),
        ]
        + [ANYWHERE] * len(halves),
        out_specs=[row_block(width)] * 3 + [pl.BlockSpec((width, width), lambda i: (0, 0))] * 2,
        out_shape=[
            jax.ShapeDtypeStruct((rows, width), F32),
            jax.ShapeDtypeStruct((rows, width), BF16),
            jax.ShapeDtypeStruct((rows, width), BF16),
            jax.ShapeDtypeStruct((width, width), BF16),
            jax.ShapeDtypeStruct((width, width), BF16),
        ],
        scratch_shapes=[
            copy_sems(plan, 2),
        ],
        compiler_params=params(40),
        cost_estimate=cost(0.5),
        name="middle",
    )(plan.odd_word, tokens, mixed, vectors, *halves)


def segments_kernel(moves, in_ref, out_ref):
    lane = iota((1, LANES), 1)
    tiles = {}
    for place in range(out_ref.shape[1] // LANES):
        result = None
        for source, shift, first, last in moves[place]:
            if source not in tiles:
                tiles[source] = in_ref[:, source * LANES : (source + 1) * LANES].astype(F32)
            tile = pltpu.roll(tiles[source], shift, 1) if shift else tiles[source]
            if result is None:
                result = tile
            else:
                result = jnp.where((lane >= first) & (lane < last), tile, result)
        out_ref[:, place * LANES : (place + 1) * LANES] = result.astype(out_ref.dtype)


def swap_segments(matrix, outer, inner, size):
    rows, columns = matrix.shape
    moves = [[] for _ in range(columns // LANES)]
    for i in range(outer):
        for j in range(inner):
            source = (i * inner + j) * size
            target = (j * outer + i) * size
            done = 0
            while done < size:
                at, to = source + done, target + done
                count = min(size - done, LANES - at % LANES, LANES - to % LANES)
                shift = (to - at) % LANES
                moves[to // LANES].append((at // LANES, shift, to % LANES, to % LANES + count))
                done += count
    return pl.pallas_call(
        functools.partial(segments_kernel, moves),
        in_specs=[pl.BlockSpec(memory_space=pltpu.VMEM)],
        out_specs=pl.BlockSpec(memory_space=pltpu.VMEM),
        out_shape=jax.ShapeDtypeStruct((rows, columns), matrix.dtype),
        compiler_params=params(24),
        cost_estimate=cost(2),
        name="swap_segments",
    )(matrix)


GELU_SCALE = 0.7978845608028654
GELU_CUBE = 0.044715
TERMS_STEP = 3


def gelu_both(values):
    square = values * values
    bent = jnp.tanh(values * (GELU_SCALE + (GELU_SCALE * GELU_CUBE) * square))
    half = 0.5 + 0.5 * bent
    result = values * half
    slope = 2.0 * GELU_SCALE + (6.0 * GELU_SCALE * GELU_CUBE) * square
    return (result, half * (1.0 + (values - result) * slope))


def feed_kernel(
    plan,
    out_start,
    row_steps,
    odd_ref,
    after_ref,
    mixed_ref,
    cotangent_ref,
    vectors_ref,
    feed_held_ref,
    feed_other_ref,
    held_ref,
    other_ref,
    block_ref,
    grad_ref,
    mixed_grad_ref,
    terms_ref,
    keep_ref,
    send_ref,
    out_matrix,
    weights,
    lefts,
    rights,
    sems,
):
    step = pl.program_id(0)
    width = after_ref.shape[1]
    parts = weights.shape[1] // width // 2

    def copies(which):
        if which == 0:
            return column_copies(
                plan,
                odd_ref[0],
                held_ref,
                other_ref,
                out_matrix,
                sems.at[0],
                out_start,
                width,
                plan.stripe,
            )
        start = (which - 1) * parts * width
        return column_copies(
            plan,
            odd_ref[0],
            feed_held_ref,
            feed_other_ref,
            weights.at[:, pl.ds(start, parts * width)],
            sems.at[which],
            start,
            parts * width,
            plan.stripe,
        )

    def ready(index):
        if index == 2 * parts:
            return out_matrix[...]
        return weights[:, index * width : (index + 1) * width]

    def rows_of(place_at, await_copies):
        mixed = mixed_ref[...]
        cotangent = cotangent_ref[...]
        await_copies(0)
        out_weight = ready(2 * parts)
        after_cross = after_ref[...] + dot(mixed, out_weight)
        unit, inverse = norm_parts(after_cross)
        gain = vectors_ref[4:5]
        third_in = (unit * gain + vectors_ref[5:6]).astype(BF16)
        await_copies(1)
        up = ready(0)
        before = dot(third_in, up)
        lefts[parts, :, place_at] = third_in.T
        lefts[parts + 1, :, place_at] = mixed.T
        rights[0, place_at] = cotangent
        result = after_cross
        upstream = jnp.zeros_like(after_cross)
        await_copies(2)
        for part in range(parts):
            down = ready(parts + part)
            back = dot(cotangent, down, NT)
            hidden, slope = gelu_both(before)
            hidden = hidden.astype(BF16)
            if part + 1 < parts:
                next_up = ready(part + 1)
                before = dot(third_in, next_up)
            result = result + dot(hidden, down)
            lefts[part, :, place_at] = hidden.T
            hidden_grad = (slope * back).astype(BF16)
            rights[1 + part, place_at] = hidden_grad
            upstream = upstream + dot(hidden_grad, up, NT)
            if part + 1 < parts:
                up = next_up
        block_ref[...] = result.astype(BF16)
        inner = upstream * gain
        mean_inner = jnp.mean(inner, axis=-1, keepdims=True)
        mean_both = jnp.mean(inner * unit, axis=-1, keepdims=True)
        grad = cotangent.astype(F32) + inverse * (inner - mean_inner - unit * mean_both)
        add_terms(
            step,
            terms_ref,
            jnp.sum(upstream * unit, axis=0, keepdims=True),
            jnp.sum(upstream, axis=0, keepdims=True),
        )
        grad_ref[...] = grad
        rounded = grad.astype(BF16)
        rights[parts + 1, place_at] = rounded
        mixed_grad_ref[...] = dot(rounded, out_weight, NT).astype(BF16)

    @pl.when(step == 0)
    def _():
        for which in range(3):
            start_all(copies(which))
        rows_of(pl.ds(0, FEED_ROWS), lambda which: wait_all(copies(which)))

    @pl.when((step > 0) & (step < row_steps))
    def _():
        rows_of(
            pl.ds(pl.multiple_of(step * FEED_ROWS, FEED_ROWS), FEED_ROWS), lambda which: None
        )

    @pl.when(step >= row_steps)
    def _():
        for turn in range(TERMS_STEP):
            term = (step - row_steps) * TERMS_STEP + turn
            left = jnp.where(term < parts, term, jnp.where(term < 2 * parts, parts, parts + 1))
            right = jnp.where(term < parts, 0, term - parts + 1)
            result = dot(lefts[left], rights[right])
            columns = slice(turn * width, (turn + 1) * width)
            store_halves(plan, odd_ref[0], result, keep_ref, send_ref, columns)


def feed(plan, out_start, after, mixed, cotangent, vectors, feed_halves, halves):
    rows, width = after.shape
    parts = feed_halves[0].shape[1] // width // 2
    terms = 2 * parts + 1
    steps = rows // FEED_ROWS
    last = steps - 1
    rows_in = row_block(width, last, FEED_ROWS)
    whole = pl.BlockSpec((8, width), lambda i: (0, 0))
    slab = pl.BlockSpec(
        (plan.half_rows, TERMS_STEP * width), lambda i: (0, jnp.maximum(i - steps, 0))
    )
    slab_shape = jax.ShapeDtypeStruct((plan.half_rows, terms * width), BF16)
    return pl.pallas_call(
        bundled(
            functools.partial(feed_kernel, plan, out_start, steps),
            (5, len(feed_halves)),
            (5 + len(feed_halves), len(halves)),
        ),
        grid=(steps + terms // TERMS_STEP,),
        in_specs=[SCALAR, rows_in, rows_in, rows_in, whole]
        + [ANYWHERE] * (len(feed_halves) + len(halves)),
        out_specs=[rows_in, rows_in, rows_in, whole, slab, slab],
        out_shape=[
            jax.ShapeDtypeStruct((rows, width), BF16),
            jax.ShapeDtypeStruct((rows, width), F32),
            jax.ShapeDtypeStruct((rows, width), BF16),
            jax.ShapeDtypeStruct((8, width), F32),
            slab_shape,
            slab_shape,
        ],
        scratch_shapes=[
            pltpu.VMEM((width, width), BF16),
            pltpu.VMEM((width, 2 * parts * width), BF16),
            pltpu.VMEM((parts + 2, width, rows), BF16),
            pltpu.VMEM((parts + 2, rows, width), BF16),
            copy_sems(plan, 3),
        ],
        compiler_params=params(60),
        cost_estimate=cost(50),
        name="feed_forward",
    )(plan.odd_word, after, mixed, cotangent, vectors, *feed_halves, *halves)


def second_kernel(
    plan,
    row_steps,
    odd_ref,
    after_ref,
    grad_in_ref,
    query_grad_ref,
    second_in_ref,
    mixed_ref,
    vectors_ref,
    out_weight,
    query_weight,
    grad_ref,
    attend_ref,
    terms_ref,
    keep_ref,
    send_ref,
    lefts,
    rights,
):
    step = pl.program_id(0)
    width = after_ref.shape[1]

    place_at = pl.ds(pl.multiple_of(step * BACK_ROWS, BACK_ROWS), BACK_ROWS)
    query_grad = query_grad_ref[...]
    back, gain_term, shift_term = norm_back(
        after_ref[...], vectors_ref[2:3], dot(query_grad, query_weight[...], NT)
    )
    lefts[0, :, place_at] = second_in_ref[...].T
    lefts[1, :, place_at] = mixed_ref[...].T
    rights[0, place_at] = query_grad
    add_terms(step, terms_ref, gain_term, shift_term)
    grad = grad_in_ref[...] + back
    grad_ref[...] = grad
    rounded = grad.astype(BF16)
    attend_ref[...] = dot(rounded, out_weight[...], NT).astype(BF16)
    rights[1, place_at] = rounded

    @pl.when(step == row_steps - 1)
    def _():
        for term in range(2):
            result = dot(lefts[term], rights[term])
            columns = slice(term * width, (term + 1) * width)
            store_halves(plan, odd_ref[0], result, keep_ref, send_ref, columns)


def second_back(
    plan, after, grad_in, query_grad, second_in, mixed, vectors, out_weight, query_weight, *given
):
    rows, width = after.shape
    steps = rows // BACK_ROWS
    rows_in = row_block(width, None, BACK_ROWS)
    whole = pl.BlockSpec((8, width), lambda i: (0, 0))
    matrix = pl.BlockSpec((width, width), lambda i: (0, 0))
    slab = pl.BlockSpec((plan.half_rows, 2 * width), lambda i: (0, 1))
    slab_shape = jax.ShapeDtypeStruct((plan.half_rows, 4 * width), BF16)
    return pl.pallas_call(
        functools.partial(passing, functools.partial(second_kernel, plan, steps), 9, len(given)),
        grid=(steps,),
        in_specs=[SCALAR] + [rows_in] * 5 + [whole, matrix, matrix] + [ANYWHERE] * len(given),
        out_specs=[rows_in, rows_in, whole, slab, slab],
        out_shape=[
            jax.ShapeDtypeStruct((rows, width), F32),
            jax.ShapeDtypeStruct((rows, width), BF16),
            jax.ShapeDtypeStruct((8, width), F32),
            slab_shape,
            slab_shape,
        ],
        scratch_shapes=[
            pltpu.VMEM((2, width, rows), BF16),
            pltpu.VMEM((2, rows, width), BF16),
        ],
        input_output_aliases={9: 3, 10: 4},
        compiler_params=params(48),
        cost_estimate=cost(12),
        name="second_back",
    )(plan.odd_word, after, grad_in, query_grad, second_in, mixed, vectors, out_weight, query_weight, *given)


def first_terms_kernel(
    plan,
    odd_ref,
    unit_ref,
    projected_grad_ref,
    columns_ref,
    second_terms_ref,
    third_terms_ref,
    weight,
    keep_ref,
    send_ref,
    terms,
):
    part = pl.program_id(0)
    width = unit_ref.shape[1]

    @pl.when(part == 0)
    def _():
        terms[...] = jnp.zeros_like(terms)

    grads = projected_grad_ref[0]
    plain = dot(unit_ref[...], grads, TN)
    sums = jnp.sum(grads.astype(F32), axis=0, keepdims=True)
    gain = columns_ref[:, 0:1]
    shift = columns_ref[:, 1:2]
    place = pl.ds(pl.multiple_of(part * width, LANES), width)
    store_halves(plan, odd_ref[0], gain * plain + shift * sums, keep_ref, send_ref, place)
    matrix = weight[...].astype(F32)
    terms[:, 0:1] += jnp.sum(matrix * plain, axis=1, keepdims=True)
    terms[:, 1:2] += jnp.sum(matrix * sums, axis=1, keepdims=True)

    @pl.when(part == 2)
    def _():
        rows = jnp.concatenate(
            [
                jnp.zeros((2, width), F32),
                second_terms_ref[0:2],
                third_terms_ref[0:2],
                jnp.zeros((LANES - 6, width), F32),
            ],
            axis=0,
        )
        lane = iota((1, LANES), 1)
        result = jnp.where(lane < 2, terms[...], rows.T)
        place = slice(3 * width, 3 * width + LANES)
        store_halves(plan, odd_ref[0], result, keep_ref, send_ref, place)


def first_terms(plan, unit, projected_grad, columns, second_terms, third_terms, weight):
    rows, width = unit.shape
    whole = pl.BlockSpec((8, width), lambda i: (0, 0))
    slab = pl.BlockSpec((plan.half_rows, 3 * width + LANES), lambda i: (0, 0))
    slab_shape = jax.ShapeDtypeStruct((plan.half_rows, 3 * width + LANES), BF16)
    return pl.pallas_call(
        functools.partial(first_terms_kernel, plan),
        grid=(3,),
        in_specs=[
            SCALAR,
            pl.BlockSpec((rows, width), lambda i: (0, 0)),
            pl.BlockSpec((1, rows, width), lambda i: (i, 0, 0)),
            pl.BlockSpec((width, LANES), lambda i: (0, 0)),
            whole,
            whole,
            pl.BlockSpec((width, width), lambda i: (0, i)),
        ],
        out_specs=[slab, slab],
        out_shape=[slab_shape, slab_shape],
        scratch_shapes=[
            pltpu.VMEM((width, LANES), F32),
        ],
        compiler_params=params(56),
        cost_estimate=cost(8),
        name="first_terms",
    )(plan.odd_word, unit, projected_grad, columns, second_terms, third_terms, weight)


def first_rows_kernel(
    tokens_ref,
    grad_in_ref,
    projected_grad_ref,
    vectors_ref,
    weight,
    grad_ref,
):
    width = tokens_ref.shape[1]

    upstream = None
    for part in range(3):
        product = dot(projected_grad_ref[part], weight[:, part * width : (part + 1) * width], NT)
        upstream = product if upstream is None else upstream + product
    unit, inverse = norm_parts(tokens_ref[...].astype(F32))
    inner = upstream * vectors_ref[0:1]
    mean_inner = jnp.mean(inner, axis=-1, keepdims=True)
    mean_both = jnp.mean(inner * unit, axis=-1, keepdims=True)
    grad_ref[...] = grad_in_ref[...] + inverse * (inner - mean_inner - unit * mean_both)


def first_rows(tokens, grad_in, projected_grad, vectors, weight):
    rows, width = tokens.shape
    rows_in = row_block(width, None, FEED_ROWS)
    return pl.pallas_call(
        first_rows_kernel,
        grid=(rows // FEED_ROWS,),
        in_specs=[
            rows_in,
            rows_in,
            pl.BlockSpec((3, FEED_ROWS, width), lambda i: (0, i, 0)),
            pl.BlockSpec((8, width), lambda i: (0, 0)),
            pl.BlockSpec((width, 3 * width), lambda i: (0, 0)),
        ],
        out_specs=rows_in,
        out_shape=jax.ShapeDtypeStruct((rows, width), F32),
        compiler_params=params(52),
        cost_estimate=cost(8),
        name="first_rows",
    )(tokens, grad_in, projected_grad, vectors, weight)


def keyval_kernel(
    plan, odd_ref, rows_ref, key_ref, value_ref, keep_ref, send_ref, key_total, value_total
):
    step = pl.program_id(0)
    width = rows_ref.shape[1]
    turned = rows_ref[...].T
    key_part = dot(turned, key_ref[...])
    value_part = dot(turned, value_ref[...])

    @pl.when(step == 0)
    def _():
        key_total[...] = key_part
        value_total[...] = value_part

    @pl.when(step > 0)
    def _():
        key_total[...] += key_part
        value_total[...] += value_part

    @pl.when(step == pl.num_programs(0) - 1)
    def _():
        for place_at, total in enumerate((key_total, value_total)):
            columns = slice(place_at * width, (place_at + 1) * width)
            store_halves(plan, odd_ref[0], total[...], keep_ref, send_ref, columns)


def keyval_terms(plan, encoded, pool_keys, pool_values):
    rows, width = encoded.shape
    block = 2048
    rows_in = pl.BlockSpec((block, width), lambda i: (i, 0))
    slab = pl.BlockSpec((plan.half_rows, 2 * width), lambda i: (0, 0))
    slab_shape = jax.ShapeDtypeStruct((plan.half_rows, 4 * width), BF16)
    return pl.pallas_call(
        functools.partial(keyval_kernel, plan),
        grid=(rows // block,),
        in_specs=[SCALAR, rows_in, rows_in, rows_in],
        out_specs=[slab, slab],
        out_shape=[slab_shape, slab_shape],
        scratch_shapes=[pltpu.VMEM((width, width), F32), pltpu.VMEM((width, width), F32)],
        compiler_params=params(48),
        cost_estimate=cost(14),
        name="keyval_terms",
    )(plan.odd_word, encoded, pool_keys, pool_values)


def neighbours_kernel(key_ref, value_ref, weight_ref, out_ref):
    width = key_ref.shape[1]
    out_ref[...] = dot(key_ref[...], weight_ref[:, :width], NT) + dot(
        value_ref[...], weight_ref[:, width:], NT
    )


def neighbours_back(pool_keys, pool_values, weight, first, count, earlier):
    rows, width = pool_keys.shape
    block = BACK_BLOCK
    rows_in = pl.BlockSpec((block, width), lambda i: (i + first, 0))
    given = [] if earlier is None else [earlier]
    return pl.pallas_call(
        functools.partial(passing, neighbours_kernel, 3, len(given)),
        grid=(count,),
        in_specs=[rows_in, rows_in, pl.BlockSpec((width, 2 * width), lambda i: (0, 0))]
        + [ANYWHERE] * len(given),
        out_specs=rows_in,
        out_shape=jax.ShapeDtypeStruct((rows, width), F32),
        input_output_aliases={3: 0} if given else {},
        compiler_params=params(56),
        cost_estimate=cost(5),
        name="neighbours_back",
    )(pool_keys, pool_values, weight, *given)

def local(
    tokens,
    lengths,
    neighbours,
    neighbour_ids,
    neighbour_lengths,
    first_gain,
    first_shift,
    self_input,
    self_output,
    second_gain,
    second_shift,
    cross_query,
    cross_keyval,
    cross_output,
    third_gain,
    third_shift,
    feed_up,
    feed_down,
    cotangent,
):
    rows, width = cross_query.shape
    line = Line()
    plan = Plan(rows, line)
    steps = len(plan.steps)
    parts = feed_down.shape[0] // rows
    pool_count, neigh_len = neighbours.shape[:2]
    vectors = (first_gain, first_shift, second_gain, second_shift, third_gain, third_shift)
    vector_pack = jnp.pad(jnp.stack(vectors, axis=1), ((0, 0), (0, LANES - len(vectors))))
    rows_in = tokens[0]
    encoded = neighbours.reshape(pool_count * neigh_len, width)
    ids = neighbour_ids.reshape(-1)
    pairs = width // LANES

    def advance(*chunks, after=()):
        moving = [chunk for chunk in chunks if not chunk.done()]
        for chunk in moving:
            chunk.land()
        for chunk in moving + list(after):
            if not chunk.done():
                chunk.launch()

    def run(kernel, first, *rest):
        results = kernel(line.after(first), *rest)
        line.note(results[0] if isinstance(results, (tuple, list)) else results)
        return results

    start = Gather(plan, jnp.concatenate([self_input, vector_pack], axis=1))
    start.launch()
    middle_part = Gather(
        plan,
        jnp.concatenate(
            [line.after(cross_keyval), self_output, cross_query, cross_output], axis=1
        ),
        4,
    )
    advance(start, after=[middle_part])
    advance(start, middle_part)
    up_shard = swap_segments(line.after(feed_up), plan.count, parts, rows)
    down_shard = line.after(feed_down).reshape(parts, rows, width)
    down_shard = down_shard.swapaxes(0, 1).reshape(rows, parts * width)
    feed_part = Gather(plan, jnp.concatenate([up_shard, down_shard], axis=1))
    advance(start, after=[feed_part])
    advance(start, middle_part, feed_part)
    start_halves = start.finish()
    unit, projected, vector_rows, vector_columns, input_weight = run(
        lambda values: project(plan, values, start_halves), rows_in
    )
    advance(middle_part)
    attended = None
    for turn in range(2):
        attended = run(self_forward, projected, lengths, turn * (pairs // 2), pairs // 2, attended)
    advance(feed_part)
    advance(middle_part)
    self_mixed, self_exact, logsum = attended
    middle_halves = middle_part.finish()
    advance(feed_part)
    after_self, second_in, cross_queries, output_weight, query_weight = run(
        lambda values: middle(
            plan, (2 * width, 3 * width), rows_in, values, vector_rows, middle_halves
        ),
        self_mixed,
    )
    pool_keyval, keyval_weight = run(
        lambda values: pool_project(plan, values, middle_halves), encoded
    )
    pool_keyval = pool_keyval.reshape(pool_count, neigh_len, 2 * width)
    advance(feed_part)
    cross_mixed, cross_logsum = run(cross_forward, cross_queries, pool_keyval, ids, neighbour_lengths)
    feed_halves = feed_part.finish()
    block_out, after_cross_grad, mixed_grad, third_terms, feed_keep, feed_send = run(
        lambda values: feed(
            plan,
            4 * width,
            after_self,
            values,
            cotangent[0],
            vector_rows,
            feed_halves,
            middle_halves,
        ),
        cross_mixed,
    )
    feed_sum = Scatter(plan, feed_keep, feed_send)
    feed_sum.launch()

    crossed = run(
        cross_backward,
        cross_queries,
        mixed_grad,
        pool_keyval,
        cross_logsum,
        ids,
        neighbour_lengths,
        0,
        width // WIDE,
        None,
    )
    advance(feed_sum)
    query_grad, pool_keys, pool_values = crossed
    pool_keys = pool_keys.reshape(pool_count * neigh_len, width)
    pool_values = pool_values.reshape(pool_count * neigh_len, width)
    middle_keep, middle_send = run(
        lambda values: keyval_terms(plan, encoded, values, pool_values), pool_keys
    )
    after_self_grad, attend_grad, second_terms, middle_keep, middle_send = run(
        lambda values: second_back(
            plan,
            after_self,
            after_cross_grad,
            values,
            second_in,
            self_mixed,
            vector_rows,
            output_weight,
            query_weight,
            middle_keep,
            middle_send,
        ),
        query_grad,
    )
    middle_sum = Scatter(plan, middle_keep, middle_send)
    advance(feed_sum, after=[middle_sum])
    projected_grad = None
    for turn in range(2):
        projected_grad = run(
            lambda values: self_backward(
                projected,
                lengths,
                values,
                self_exact,
                logsum,
                turn * (pairs // 2),
                pairs // 2,
                projected_grad,
            ),
            attend_grad,
        )
        if turn == 0:
            advance(feed_sum, middle_sum)
    first_keep, first_send = run(
        lambda values: first_terms(
            plan, unit, values, vector_columns, second_terms, third_terms, input_weight
        ),
        projected_grad,
    )
    first_sum = Scatter(plan, first_keep, first_send)
    advance(feed_sum, middle_sum, after=[first_sum])
    blocks = pool_keys.shape[0] // BACK_BLOCK
    quarter = blocks // 4
    neighbours_grad = None

    def neighbours_turn(first, count, earlier):
        return run(
            lambda values: neighbours_back(
                values,
                pool_values,
                keyval_weight,
                first,
                count,
                earlier,
            ),
            pool_keys,
        )

    advance(first_sum)
    tokens_grad = run(
        lambda values: first_rows(
            rows_in, after_self_grad, values, vector_rows, input_weight
        ),
        projected_grad,
    )
    advance(feed_sum, middle_sum, first_sum)
    neighbours_grad = neighbours_turn(0, quarter, neighbours_grad)
    advance(first_sum)
    neighbours_grad = neighbours_turn(quarter, quarter, neighbours_grad)
    advance(middle_sum)
    neighbours_grad = neighbours_turn(2 * quarter, blocks - 2 * quarter, neighbours_grad)
    middle_total = middle_sum.finish()
    feed_total = line.after(feed_sum.finish())
    first_total = first_sum.finish()

    down_grad = feed_total[:, : parts * width].reshape(rows, parts, width).swapaxes(0, 1)
    up_grad = swap_segments(
        feed_total[:, parts * width : 2 * parts * width], parts, plan.count, rows
    )
    vector_grads = [first_total[:, 3 * width + i] for i in range(len(vectors))]
    return (
        block_out[None],
        tokens_grad[None],
        neighbours_grad.reshape(neighbours.shape),
        vector_grads[0],
        vector_grads[1],
        first_total[:, : 3 * width],
        middle_total[:, 3 * width :],
        vector_grads[2],
        vector_grads[3],
        middle_total[:, 2 * width : 3 * width],
        middle_total[:, : 2 * width],
        feed_total[:, 2 * parts * width :],
        vector_grads[4],
        vector_grads[5],
        up_grad,
        down_grad.reshape(feed_down.shape),
    )


def solution(mesh):
    placed = (
        P(("fsdp", "dp"), None, None),
        P(("fsdp", "dp")),
        P(("fsdp", "dp"), None, None),
        P(("fsdp", "dp"), None, None),
        P(("fsdp", "dp")),
        P(("fsdp", "dp")),
        P(("fsdp", "dp")),
        P(("fsdp", "dp"), None),
        P(("fsdp", "dp"), None),
        P(("fsdp", "dp")),
        P(("fsdp", "dp")),
        P(("fsdp", "dp"), None),
        P(("fsdp", "dp"), None),
        P(("fsdp", "dp"), None),
        P(("fsdp", "dp")),
        P(("fsdp", "dp")),
        P(("fsdp", "dp"), None),
        P(("fsdp", "dp"), None),
        P(("fsdp", "dp"), None, None),
    )
    return jax.shard_map(
        local,
        mesh=mesh,
        in_specs=placed,
        out_specs=(
            P(("fsdp", "dp"), None, None),
            P(("fsdp", "dp"), None, None),
            P(("fsdp", "dp"), None, None),
            P(("fsdp", "dp")),
            P(("fsdp", "dp")),
            P(("fsdp", "dp"), None),
            P(("fsdp", "dp"), None),
            P(("fsdp", "dp")),
            P(("fsdp", "dp")),
            P(("fsdp", "dp"), None),
            P(("fsdp", "dp"), None),
            P(("fsdp", "dp"), None),
            P(("fsdp", "dp")),
            P(("fsdp", "dp")),
            P(("fsdp", "dp"), None),
            P(("fsdp", "dp"), None),
        ),
        check_vma=False,
    )
```
